32 devices in a mesh: section: 2 (over x), dp: 8 (over z, core), tensor: 2 (over y).
Axes of the slice: x: 2, y: 2, z: 4, core: 2. Of those that a mesh axis runs over, the one named last changes fastest.
Arguments:
- layer_input: bfloat16 [2, 2048, 2048], P(None, ('dp', 'tensor')), may hold values from -6 to 6
- segment_ids: int32 [2, 2048], P(None, 'dp'), may hold values from 0 to 2, as said below
- output_grad: bfloat16 [2, 2048, 2048], P(None, ('dp', 'tensor')), may hold values from -6 to 6
- query_weight: bfloat16 [2, 2048, 2048], P('section', 'dp', 'tensor'), may hold values from -0.125 to 0.125
- key_weight: bfloat16 [2, 2048, 2048], P('section', 'dp', 'tensor'), may hold values from -0.125 to 0.125
- value_weight: bfloat16 [2, 2048, 4096], P('section', 'dp', 'tensor'), may hold values from -0.125 to 0.125
- swish_weight: bfloat16 [2, 2048, 4096], P('section', 'dp', 'tensor'), may hold values from -0.125 to 0.125
- output_weight: bfloat16 [2, 4096, 2048], P('section', 'tensor', 'dp'), may hold values from -0.09375 to 0.09375
- gate_weight: bfloat16 [2, 2048, 4096], P('section', 'dp', 'tensor'), may hold values from -0.125 to 0.125
- up_weight: bfloat16 [2, 2048, 4096], P('section', 'dp', 'tensor'), may hold values from -0.125 to 0.125
- down_weight: bfloat16 [2, 4096, 2048], P('section', 'tensor', 'dp'), may hold values from -0.09375 to 0.09375
- mixer_gain: float32 [2, 2048], P('section'), may hold values from 0.25 to 1.75
- ffn_gain: float32 [2, 2048], P('section'), may hold values from 0.25 to 1.75
Outputs:
- layer_outputs: bfloat16 [2, 2, 2048, 2048], P('section', None, ('dp', 'tensor'))
- input_grads: bfloat16 [2, 2, 2048, 2048], P('section', None, ('dp', 'tensor'))
- grad_query: float32 [2, 2048, 2048], P('section', 'dp', 'tensor')
- grad_key: float32 [2, 2048, 2048], P('section', 'dp', 'tensor')
- grad_value: float32 [2, 2048, 4096], P('section', 'dp', 'tensor')
- grad_swish: float32 [2, 2048, 4096], P('section', 'dp', 'tensor')
- grad_output: float32 [2, 4096, 2048], P('section', 'tensor', 'dp')
- grad_gate: float32 [2, 2048, 4096], P('section', 'dp', 'tensor')
- grad_up: float32 [2, 2048, 4096], P('section', 'dp', 'tensor')
- grad_down: float32 [2, 4096, 2048], P('section', 'tensor', 'dp')
- grad_mixer_gain: float32 [2, 2048], P('section')
- grad_ffn_gain: float32 [2, 2048], P('section')
The draws below stay inside these ranges and needn't reach their ends.
Inputs may be any that keep to these rules, and one draw needn't show every extreme that they name: `segment_ids`: within each sequence of 256 tokens the numbers start at 0 and rise by one at each of exactly two document boundaries: one among positions 64 to 95, one among positions 160 to 192.
All inputs are finite; a program needn't handle non-finite values.
Results may differ from the reference program's by a relative error of at most 0.03.
Values may be sent and summed in bfloat16 or wider, within the bound.
A program may use at most 576 MiB of HBM per device.

```python
import jax
import jax.numpy as jnp
from jax import lax

D = 2048
HEADS = 8
HEAD_K = 256
HEAD_V = 512
FF = 4096
LEN = 256
M = 2
QK = 2048
VD = 4096
TOKENS_MB = 2048
N_DP = 8


def draw_segment_ids(key, part):
    key = jax.random.fold_in(key, 11)
    position = jnp.arange(LEN)

    def one_sequence(index):
        seq_key = jax.random.fold_in(key, index)
        early_key, late_key = jax.random.split(seq_key)
        early = jax.random.randint(early_key, (1,), 0, LEN // 8) + LEN // 4
        late = jax.random.randint(late_key, (1,), 0, LEN // 8 + 1) + 5 * (LEN // 8)
        starts = jnp.concatenate([early, late]).astype(jnp.int32)
        marks = jnp.sum((position[None, :] == starts[:, None]).astype(jnp.int32), axis=0)
        return jnp.cumsum(marks).astype(jnp.int32)
    numbers = jax.vmap(one_sequence)(jnp.arange(M * N_DP))
    return numbers.reshape(M, N_DP * LEN).astype(jnp.int32)


def block_scale(stream_key, extent, shards, least, top_value):
    loudness, own = 1.0, jax.random.fold_in(stream_key, 6)
    for axis_at, shards_of in shards:
        draws = jnp.exp(jax.random.uniform(jax.random.fold_in(own, axis_at), (shards_of,), jnp.float32, least / len(shards), top_value / len(shards)))
        loudness = loudness * jnp.repeat(draws, extent[axis_at] // shards_of).reshape([-1 if axis == axis_at else 1 for axis in range(len(extent))])
    return loudness


def gaussian(rng, extent, scale, limit, cuts=(), kind=jnp.bfloat16):
    array = scale * jax.random.normal(rng, extent, jnp.float32)
    if cuts:
        array = array * block_scale(rng, extent, cuts, -0.22, 0.18)
    return jnp.clip(array, -limit, limit).astype(kind)


def setup_inputs(seed: int = 0) -> dict:
    seeds = jax.random.split(jax.random.key(seed), 14)
    layer_input = gaussian(seeds[0], (M, TOKENS_MB, D), 1.0, 6.0, ((1, 16),))
    segment_ids = draw_segment_ids(jax.random.fold_in(seeds[13], 71), 0)
    output_grad = gaussian(seeds[2], (M, TOKENS_MB, D), 1.0, 6.0, ((1, 16),))
    query_weight = gaussian(seeds[3], (2, D, QK), D ** -0.5, 0.125, ((0, 2), (1, 8), (2, 2)))
    key_weight = gaussian(seeds[4], (2, D, QK), D ** -0.5, 0.125, ((0, 2), (1, 8), (2, 2)))
    value_weight = gaussian(seeds[5], (2, D, VD), D ** -0.5, 0.125, ((0, 2), (1, 8), (2, 2)))
    swish_weight = gaussian(seeds[6], (2, D, VD), D ** -0.5, 0.125, ((0, 2), (1, 8), (2, 2)))
    output_weight = gaussian(seeds[7], (2, VD, D), VD ** -0.5, 0.09375, ((0, 2), (1, 2), (2, 8)))
    gate_weight = gaussian(seeds[8], (2, D, FF), D ** -0.5, 0.125, ((0, 2), (1, 8), (2, 2)))
    up_weight = gaussian(seeds[9], (2, D, FF), D ** -0.5, 0.125, ((0, 2), (1, 8), (2, 2)))
    down_weight = gaussian(seeds[10], (2, FF, D), FF ** -0.5, 0.09375, ((0, 2), (1, 2), (2, 8)))
    mixer_gain = jnp.clip(1.0 + 0.15 * jax.random.normal(seeds[11], (2, D), jnp.float32), 0.25, 1.75)
    ffn_gain = jnp.clip(1.0 + 0.15 * jax.random.normal(seeds[12], (2, D), jnp.float32), 0.25, 1.75)
    return dict(layer_input=layer_input, segment_ids=segment_ids, output_grad=output_grad, query_weight=query_weight, key_weight=key_weight, value_weight=value_weight, swish_weight=swish_weight, output_weight=output_weight, gate_weight=gate_weight, up_weight=up_weight, down_weight=down_weight, mixer_gain=mixer_gain, ffn_gain=ffn_gain)


@jax.custom_vjp
def low(v):
    return lax.optimization_barrier(v.astype(jnp.bfloat16)).astype(jnp.float32)

@jax.custom_vjp
def low_back(v):
    return v

def low_keep(v):
    return (low(v), None)

def low_pass(kept, grad):
    return (grad,)

def back_keep(v):
    return (v, None)

def back_low(kept, grad):
    return (low(grad),)
low.defvjp(low_keep, low_pass)
low_back.defvjp(back_keep, back_low)
epsilon = 1e-05
group_guard = 1.0
highest = lax.Precision.HIGHEST

def layer_norm(values, gain):
    centred = values - lax.optimization_barrier(jnp.mean(values, axis=-1, keepdims=True))
    spread = lax.optimization_barrier(jnp.mean(centred * centred, axis=-1, keepdims=True))
    return centred * lax.rsqrt(spread + epsilon) * gain

def group_norm(mixed):
    centred = mixed - lax.optimization_barrier(jnp.mean(mixed, axis=-1, keepdims=True))
    spread = lax.optimization_barrier(jnp.mean(centred * centred, axis=-1, keepdims=True))
    return centred * lax.rsqrt(spread + group_guard)

def rotation_tables(length, half_width):
    pair_index = jnp.arange(half_width).astype(jnp.float32)
    position = jnp.arange(length).astype(jnp.float32)[:, None]
    angle = position * jnp.exp(-jnp.log(10000.0) * pair_index / half_width)
    zeta = (pair_index / half_width + 0.4) / 1.4
    growth = jnp.exp(position / 512.0 * jnp.log(zeta))
    return (jnp.cos(angle), jnp.sin(angle), growth)

def rotate(values, cosine, sine, growth):
    half_width = values.shape[-1] // 2
    first_half = values[..., :half_width]
    second_half = values[..., half_width:]
    cos_table = cosine[:, None, :]
    sin_table = sine[:, None, :]
    scale_table = growth[:, None, :]
    return jnp.concatenate([(first_half * cos_table - second_half * sin_table) * scale_table, (first_half * sin_table + second_half * cos_table) * scale_table], axis=-1)

def decay_mask(segments, first_head, heads):
    length = segments.shape[-1]
    position = jnp.arange(length)
    earlier = position[:, None] >= position[None, :]
    same_doc = (segments[:, None] == segments[None, :]) & earlier
    distance = jnp.maximum(position[:, None] - position[None, :], 0).astype(jnp.float32)
    head_index = (first_head + jnp.arange(heads)).astype(jnp.float32)
    log_rate = jnp.log(1.0 - jnp.exp2(-5.0 - head_index))
    return jnp.where(same_doc[None], jnp.exp(log_rate[:, None, None] * distance[None]), 0.0)

def layer(hidden_in, masks, tables, weights):
    query_weight, key_weight, value_weight, swish_weight, output_weight, gate_weight, up_weight, down_weight, mixer_gain, ffn_gain = weights
    cosine, sine, growth = tables
    batch, length, width = hidden_in.shape
    normed_in = low(layer_norm(hidden_in, mixer_gain))
    query = low_back(jnp.matmul(normed_in, query_weight, precision=highest)).reshape(batch, length, HEADS, HEAD_K)
    key_proj = low_back(jnp.matmul(normed_in, key_weight, precision=highest)).reshape(batch, length, HEADS, HEAD_K)
    value = low_back(low(jnp.matmul(normed_in, value_weight, precision=highest))).reshape(batch, length, HEADS, HEAD_V)
    gate_pre = low_back(jnp.matmul(normed_in, swish_weight, precision=highest))
    query_rot = low(rotate(query, cosine, sine, growth))
    key_rot = low(rotate(key_proj, cosine, sine, 1.0 / growth))
    product = low_back(jnp.einsum('bthd,bshd->bhts', query_rot, key_rot, precision=highest))
    weight = low(product * HEAD_K ** (-0.5) * masks)
    mixed = low_back(jnp.einsum('bhts,bshv->bthv', weight, value, precision=highest))
    merged = low(group_norm(mixed).reshape(batch, length, -1) * jax.nn.silu(gate_pre))
    middle = hidden_in + low_back(jnp.matmul(merged, output_weight, precision=highest))
    normed_mid = low(layer_norm(middle, ffn_gain))
    gate = low_back(jnp.matmul(normed_mid, gate_weight, precision=highest))
    up_part = low_back(jnp.matmul(normed_mid, up_weight, precision=highest))
    hidden = low(jax.nn.gelu(gate) * up_part)
    return middle + low_back(jnp.matmul(hidden, down_weight, precision=highest))

def reference(layer_input, segment_ids, output_grad, query_weight, key_weight, value_weight, swish_weight, output_weight, gate_weight, up_weight, down_weight, mixer_gain, ffn_gain):
    sequences = M * N_DP
    inputs = layer_input.astype(jnp.float32).reshape(sequences, LEN, D)
    cotangent = output_grad.astype(jnp.float32).reshape(sequences, LEN, D)
    segments = segment_ids.reshape(sequences, LEN)
    masks = jax.vmap(lambda sequence_ids: decay_mask(sequence_ids, 0, HEADS))(segments)
    tables = rotation_tables(LEN, HEAD_K // 2)
    params = tuple((weight_array.astype(jnp.float32) for weight_array in (query_weight, key_weight, value_weight, swish_weight, output_weight, gate_weight, up_weight, down_weight, mixer_gain, ffn_gain)))

    def forward(first_in, probe, layer_params):
        first_out = layer(first_in, masks, tables, tuple((param_array[0] for param_array in layer_params)))
        passed = low_back(low(first_out))
        second_out = layer(passed + probe, masks, tables, tuple((param_array[1] for param_array in layer_params)))
        return (second_out, first_out)
    second_out, pullback, first_out = jax.vjp(forward, inputs, jnp.zeros_like(inputs), params, has_aux=True)
    input_grad, probe_grad, param_grads = pullback(cotangent)
    shape = (2, M, N_DP * LEN, D)
    outputs = jnp.stack([first_out, second_out]).astype(jnp.bfloat16).reshape(shape)
    grads_in = jnp.stack([input_grad, probe_grad]).astype(jnp.bfloat16).reshape(shape)
    return (outputs, grads_in, param_grads[0], param_grads[1], param_grads[2], param_grads[3], param_grads[4], param_grads[5], param_grads[6], param_grads[7], param_grads[8], param_grads[9])
```

```python
import functools

import jax
import jax.numpy as jnp
from jax import lax
from jax.experimental import pallas as pl
from jax.experimental.pallas import tpu as pltpu
from jax.sharding import PartitionSpec as P

HEAD_K = 256
HEAD_V = 512
MESH = pl.DeviceIdType.MESH

epsilon = 1e-05
group_guard = 1.0
bf16 = jnp.bfloat16
f32 = jnp.float32


def rotation_tables(length, half_width):
    pair_index = jnp.arange(half_width).astype(f32)
    position = jnp.arange(length).astype(f32)[:, None]
    angle = position * jnp.exp(-jnp.log(10000.0) * pair_index / half_width)
    zeta = (pair_index / half_width + 0.4) / 1.4
    growth = jnp.exp(position / 512.0 * jnp.log(zeta))
    return (jnp.cos(angle), jnp.sin(angle), growth)


def decay_mask(segments, first_head, heads):
    length = segments.shape[-1]
    position = jnp.arange(length)
    earlier = position[:, None] >= position[None, :]
    same_doc = (segments[:, :, None] == segments[:, None, :]) & earlier[None]
    distance = jnp.maximum(position[:, None] - position[None, :], 0).astype(f32)
    head_index = (first_head + jnp.arange(heads)).astype(f32)
    log_rate = jnp.log(1.0 - jnp.exp2(-5.0 - head_index))
    decay = jnp.exp(log_rate[:, None, None] * distance[None])
    return jnp.where(same_doc[:, None], decay[None], 0.0)


class Place:
    def __init__(self, dp_size):
        self.groups = dp_size // 4
        self.section = lax.axis_index("section")
        self.dp = lax.axis_index("dp")
        self.tensor = lax.axis_index("tensor")
        self.core = self.dp % 2
        self.low = (self.dp // 2) % 2
        self.group = self.dp // 4

    def dp_at(self, group_step, low_step):
        group = (self.group + group_step + self.groups) % self.groups
        return (group * 2 + (self.low + low_step) % 2) * 2 + self.core

    def sibling(self):
        return self.dp + 1 - 2 * self.core


SQUARE = ((0, 1), (1, 0), (1, 1))
TILE = 512
VMEM_LIMIT = 63 * 1024 * 1024


def mm(left, right):
    return lax.dot_general(left, right, (((1,), (0,)), ((), ())), preferred_element_type=f32)


def mm_nt(left, right):
    return lax.dot_general(left, right, (((1,), (1,)), ((), ())), preferred_element_type=f32)


def mm_tn(left, right):
    return lax.dot_general(left, right, (((0,), (0,)), ((), ())), preferred_element_type=f32)


class Square:
    def __init__(self, dp_size, rows):
        self.at = Place(dp_size)
        self.rows = rows
        self.own = self.at.low
        self.next = 1 - self.at.low

    def device(self, low_step, tensor_step):
        return (self.at.section, self.at.dp_at(0, low_step), (self.at.tensor + tensor_step) % 2)

    def barrier(self):
        barrier = pltpu.get_barrier_semaphore()
        for step in SQUARE:
            pl.semaphore_signal(barrier, inc=1, device_id=self.device(*step), device_id_type=MESH)
        pl.semaphore_wait(barrier, len(SQUARE))

    def chunk(self, ref, low_step=0, tensor_step=0):
        start = pl.multiple_of((self.at.tensor + tensor_step) % 2 * self.rows, self.rows)
        return ref.at[(self.at.low + low_step) % 2, pl.ds(start, self.rows)]

    def copy(self, src, dst, send, recv, step):
        return pltpu.make_async_remote_copy(
            src_ref=src,
            dst_ref=dst,
            send_sem=send,
            recv_sem=recv,
            device_id=self.device(*step),
            device_id_type=MESH,
        )

    def spread(self, ref, send, recv):
        pushes = []
        for j, step in enumerate(SQUARE):
            push = self.copy(self.chunk(ref), self.chunk(ref), send.at[j], recv.at[j], step)
            push.start()
            pushes.append(push)
        return pushes

    def spread_from(self, own, ref, send, recv, here):
        local = pltpu.make_async_copy(own, self.chunk(ref), here)
        local.start()
        pushes = [local]
        for j, step in enumerate(SQUARE):
            push = self.copy(own, self.chunk(ref), send.at[j], recv.at[j], step)
            push.start()
            pushes.append(push)
        return pushes

    def give(self, parts, landed, send, recv, j):
        push = self.copy(self.chunk(parts, *SQUARE[j]), landed.at[j], send.at[j], recv.at[j], SQUARE[j])
        push.start()
        return push


def row_blocks(rows, body, block=32):
    block = min(block, rows)

    @pl.loop(0, rows // block)
    def _(i):
        body(pl.ds(pl.multiple_of(i * block, block), block))


def norm_parts(values):
    centred = values - jnp.mean(values, axis=-1, keepdims=True)
    scale = lax.rsqrt(jnp.mean(centred * centred, axis=-1, keepdims=True) + epsilon)
    return centred * scale, scale


def norm_grad(normed, scale, upstream, gain):
    through = upstream * gain
    return scale * (
        through
        - jnp.mean(through, axis=-1, keepdims=True)
        - normed * jnp.mean(through * normed, axis=-1, keepdims=True)
    )


def turn(values, cosine, sine, scale):
    half = values.shape[-1] // 2
    a, b = values[:, :half], values[:, half:]
    return jnp.concatenate([(a * cosine - b * sine) * scale, (a * sine + b * cosine) * scale], axis=-1)


def turn_back(values, cosine, sine, scale):
    half = values.shape[-1] // 2
    a, b = values[:, :half] * scale, values[:, half:] * scale
    return jnp.concatenate([a * cosine + b * sine, b * cosine - a * sine], axis=-1)


def transpose_into(target, source):
    _, length, width = source.shape
    for s in range(2):
        for start in range(0, width, TILE):
            target[start : start + TILE, s * length : (s + 1) * length] = source[s, :, start : start + TILE].T


def forward_kernel(dp_size, layer, *refs):
    streams = layer == 0
    v = Refs()
    if streams:
        (v.x, v.own_gains, v.tables, v.masks, v.out_grad, *refs) = refs
        shards, refs = refs[:8], refs[8:]
        stored, refs = refs[:4], refs[4:]
        (v.gains, *refs) = refs
    else:
        (v.x, v.gains, v.tables, v.masks, *refs) = refs
        stored, refs = refs[:4], refs[4:]
    (middle, normed_in_t, query_rot, key_rot, value, unit, inverse, opened, slope_open, merged, normed_mid_t, act, slope,
     hidden, *refs) = refs
    if streams:
        (v.grad_down, result, *refs) = refs
    held, refs = refs[:4], refs[4:]
    (w_sem, normed_in, normed_mid, parts, landed, s_send, s_recv, g_send, g_recv, *refs) = refs
    x, tables, masks = v.x, v.tables, v.masks
    rows, width = x.shape
    sq = Square(dp_size, rows)
    at = sq.at
    qkvs, out_t, gate_up, down_t = held
    wide_k = query_rot.shape[-1]
    wide_v = value.shape[-1]
    wide_f = hidden.shape[-1]
    heads = wide_k // HEAD_K
    slices = dp_size // 2
    other = 1 - at.section
    groups = [(0, 0, wide_k), (0, wide_k, wide_k), (0, 2 * wide_k, wide_v), (0, 2 * wide_k + wide_v, wide_v),
              (1, 0, wide_v), (2, 0, wide_f), (2, wide_f, wide_f), (3, 0, wide_f)]
    loads = {}

    def load(i):
        which, first, size = groups[i]
        columns = pl.ds(first, size)
        loads[i] = pltpu.make_async_copy(
            stored[which].at[layer, :, :, :, columns], held[which].at[:, :, :, columns], w_sem.at[i]
        )
        loads[i].start()

    def weight(which, first, size):
        return held[which][:, :, :, first : first + size].reshape(width, size)

    def first_norm(block):
        unit_rows, _ = norm_parts(x[block].astype(f32))
        sq.chunk(normed_in)[block] = (unit_rows * v.gains[layer, 0:1]).astype(bf16)

    def project(i, s):
        loads_wait(i)
        first, size = groups[i][1:]
        tokens = normed_in[s]
        for start in range(0, size, TILE):
            wide = mm(tokens, weight(0, first + start, TILE))
            cols = slice(start, start + TILE)
            if i < 2:
                dest = (query_rot, key_rot)[i]
                for head in range(TILE // HEAD_K):
                    part = wide[:, head * HEAD_K : (head + 1) * HEAD_K]
                    dest[s, :, start + head * HEAD_K : start + (head + 1) * HEAD_K] = turn(
                        part, tables[0], tables[1], tables[2 + i]
                    ).astype(bf16)
            elif i == 2:
                value[s, :, cols] = wide.astype(bf16)
            else:
                sigmoid = 1.0 / (1.0 + jnp.exp(-wide))
                opened[s, :, cols] = (wide * sigmoid).astype(bf16)
                slope_open[s, :, cols] = (sigmoid * (1.0 + wide * (1.0 - sigmoid))).astype(bf16)

    waited = []

    def loads_wait(i):
        if i not in waited:
            waited.append(i)
            loads[i].wait()

    def retain(s):
        for head in range(heads):
            cols_k = slice(head * HEAD_K, (head + 1) * HEAD_K)
            cols_v = slice(head * HEAD_V, (head + 1) * HEAD_V)
            product = mm_nt(query_rot[s, :, cols_k], key_rot[s, :, cols_k])
            weights = (product * masks[s, head]).astype(bf16)
            mixed = mm(weights, value[s, :, cols_v])
            centred = mixed - jnp.mean(mixed, axis=-1, keepdims=True)
            scale = lax.rsqrt(jnp.mean(centred * centred, axis=-1, keepdims=True) + group_guard)
            unit_rows = centred * scale
            inverse[s, head] = scale
            unit[s, :, cols_v] = unit_rows.astype(bf16)
            merged[s, :, cols_v] = (unit_rows * opened[s, :, cols_v].astype(f32)).astype(bf16)

    def give_back(s, source, weight_t):
        tokens = source[s]
        step = width // slices
        for i in range(slices):
            parts[s, :, i * step : (i + 1) * step] = mm_nt(tokens, weight_t[i].reshape(step, -1)).astype(bf16)

    def collected(block, which):
        total = sq.chunk(parts)[block].astype(f32)
        for j in range(len(SQUARE)):
            total = total + landed[which, j, block].astype(f32)
        return total

    def give(s, which):
        send, recv = g_send.at[which], g_recv.at[which]
        return [sq.give(parts, landed.at[which], send, recv, j) for j in ((1, 2) if s == 1 else (0,))]

    def second_norm(block):
        middle_rows = x[block].astype(f32) + collected(block, 0)
        middle[block] = middle_rows
        unit_rows, _ = norm_parts(middle_rows)
        sq.chunk(normed_mid)[block] = (unit_rows * v.gains[layer, 1:2]).astype(bf16)

    def feed(s):
        loads_wait(5)
        loads_wait(6)
        tokens = normed_mid[s]
        for start in range(0, wide_f, TILE):
            cols = slice(start, start + TILE)
            gate = mm(tokens, weight(2, start, TILE))
            up = mm(tokens, weight(2, wide_f + start, TILE))
            square = gate * gate
            bend = jnp.tanh(0.7978845608028654 * gate * (1.0 + 0.044715 * square))
            half = 0.5 * (1.0 + bend)
            gelu = gate * half
            slope_gelu = half + 0.5 * gate * (1.0 - bend * bend) * (
                0.7978845608028654 * (1.0 + 3 * 0.044715 * square)
            )
            act[s, :, cols] = gelu.astype(bf16)
            slope[s, :, cols] = (slope_gelu * up).astype(bf16)
            hidden[s, :, cols] = (gelu * up).astype(bf16)

    if not streams:
        for i in range(7):
            load(i)
        row_blocks(rows, first_norm)
        sq.barrier()
        ins = sq.spread(normed_in, s_send.at[0], s_recv.at[0])
        ins[0].wait_recv()
        for i in range(4):
            project(i, sq.own)
        ins[1].wait_recv()
        ins[2].wait_recv()
        for i in range(4):
            project(i, sq.next)
        retain(sq.next)
        loads_wait(4)
        give_back(sq.next, merged, out_t)
        gives = give(1, 0)
        retain(sq.own)
        give_back(sq.own, merged, out_t)
        gives += give(0, 0)
        transpose_into(normed_in_t, normed_in)
        for push in gives:
            push.wait_recv()
        row_blocks(rows, second_norm)
        mids = sq.spread(normed_mid, s_send.at[1], s_recv.at[1])
        mids[0].wait_recv()
        feed(sq.own)
        mids[1].wait_recv()
        mids[2].wait_recv()
        feed(sq.next)
        transpose_into(normed_mid_t, normed_mid)
        for push in ins + mids + gives:
            push.wait_send()
        return

    (z_send, z_recv, x_send, x_recv, c_send, c_recv, o_send, o_recv, here_sem, gain_send, gain_recv, d_send, d_recv,
     d_sem) = refs
    steps = [(k, b) for k in range(at.groups) for b in range(2)][1:]

    def place(section=None, dp=None):
        return (at.section if section is None else section, at.dp if dp is None else dp, at.tensor)

    def copy(src, dst, send, recv, device):
        return pltpu.make_async_remote_copy(
            src_ref=src, dst_ref=dst, send_sem=send, recv_sem=recv, device_id=device, device_id_type=MESH
        )

    partners = [sq.device(*step) for step in SQUARE] + [place(dp=at.sibling()), place(section=other)]
    partners += [place(dp=at.dp_at(k, b)) for k, b in steps if (k, b) != (0, 1)]
    barrier = pltpu.get_barrier_semaphore()
    for partner in partners:
        pl.semaphore_signal(barrier, inc=1, device_id=partner, device_id_type=MESH)
    pl.semaphore_wait(barrier, len(partners))

    gain_copy = copy(v.own_gains, v.gains.at[at.section], gain_send, gain_recv, place(section=other))
    gain_copy.start()
    v.gains[at.section] = v.own_gains[...]

    def slot(i, section, dp):
        which, first, size = groups[i]
        return stored[which].at[section, dp // 2, dp % 2, :, pl.ds(first, size)]

    def block(i, section, core):
        which, first, size = groups[i]
        return stored[which].at[section, :, core, :, pl.ds(first, size)]

    def part(i, b):
        size = groups[i][2]
        return shards[i].at[:, pl.ds(pl.multiple_of((at.low + b) % 2 * size, size), size)]

    z_copies, x_copies, here, core_own, core_other = {}, {}, {}, {}, {}

    def push_own(i):
        mine = slot(i, at.section, at.dp)
        for j, (k, b) in enumerate(steps):
            z_copies[i, j] = copy(part(i, b), mine, z_send.at[i, j], z_recv.at[i, j], place(dp=at.dp_at(k, b)))
            z_copies[i, j].start()
        x_copies[i, 0] = copy(part(i, 0), mine, x_send.at[i, 0], x_recv.at[i, 0], place(section=other))
        x_copies[i, 0].start()
        here[i] = pltpu.make_async_copy(part(i, 0), mine, here_sem.at[i])
        here[i].start()

    def pass_on(i):
        for j, (k, b) in enumerate(steps):
            z_copies[i, j].wait_recv()
            arrived = slot(i, at.section, at.dp_at(-k, b))
            x_copies[i, j + 1] = copy(arrived, arrived, x_send.at[i, j + 1], x_recv.at[i, j + 1], place(section=other))
            x_copies[i, j + 1].start()
        here[i].wait()
        mine = block(i, at.section, at.core)
        core_own[i] = copy(mine, mine, c_send.at[i], c_recv.at[i], place(dp=at.sibling()))
        core_own[i].start()

    def share_other(i):
        for j in range(slices):
            x_copies[i, j].wait_recv()
        theirs = block(i, other, at.core)
        core_other[i] = copy(theirs, theirs, o_send.at[i], o_recv.at[i], place(dp=at.sibling()))
        core_other[i].start()

    def arrive(i):
        @pl.when(at.section == 0)
        def _():
            core_own[i].wait_recv()

        @pl.when(at.section == 1)
        def _():
            core_other[i].wait_recv()

        load(i)

    ahead = 3
    for i in range(ahead):
        push_own(i)
    gain_copy.wait_recv()
    row_blocks(rows, first_norm)
    ins = sq.spread(normed_in, s_send.at[0], s_recv.at[0])

    def advance(i):
        pass_on(i)
        if i + ahead < 8:
            push_own(i + ahead)
        if i > 0:
            share_other(i - 1)
            arrive(i - 1)

    advance(0)
    downs = sq.spread_from(v.out_grad, v.grad_down, d_send, d_recv, d_sem)
    advance(1)
    for push in ins:
        push.wait_recv()
    transpose_into(normed_in_t, normed_in)
    for i in range(2, 5):
        advance(i)
        for s in (sq.own, sq.next):
            project(i - 2, s)
    advance(5)
    for s in (sq.own, sq.next):
        project(3, s)
    retain(sq.next)
    loads_wait(4)
    give_back(sq.next, merged, out_t)
    gives = give(1, 0)
    retain(sq.own)
    give_back(sq.own, merged, out_t)
    gives += give(0, 0)
    advance(6)
    for push in gives:
        push.wait_recv()
    row_blocks(rows, second_norm)
    mids = sq.spread(normed_mid, s_send.at[1], s_recv.at[1])
    advance(7)
    for push in mids:
        push.wait_recv()
    transpose_into(normed_mid_t, normed_mid)
    feed(sq.next)
    feed(sq.own)
    for push in gives:
        push.wait_send()

    def last_group():
        for j in range(slices):
            x_copies[7, j].wait_recv()
        core_other[7].start()

    theirs = block(7, other, at.core)
    core_other[7] = copy(theirs, theirs, o_send.at[7], o_recv.at[7], place(dp=at.sibling()))

    @pl.when(at.section == 1)
    def _():
        last_group()

    arrive(7)
    loads_wait(7)
    give_back(sq.next, hidden, down_t)
    ends = give(1, 1)
    give_back(sq.own, hidden, down_t)
    ends += give(0, 1)

    @pl.when(at.section == 0)
    def _():
        last_group()

    for push in ends:
        push.wait_recv()

    def last(block):
        result[block] = (middle[block] + collected(block, 1)).astype(bf16)

    row_blocks(rows, last)

    @pl.when(at.section == 0)
    def _():
        for i in range(8):
            core_other[i].wait_recv()

    @pl.when(at.section == 1)
    def _():
        for i in range(8):
            core_own[i].wait_recv()

    for push in downs:
        push.wait()
    for push in ins + mids + ends + list(z_copies.values()) + list(x_copies.values()):
        push.wait_send()
    for i in range(8):
        core_own[i].wait_send()
        core_other[i].wait_send()
    gain_copy.wait_send()


def forward_layer(layer, x, gains, tables, masks, weights, dp_size, out_grad=None):
    rows, width = x.shape
    length = masks.shape[-1]
    heads = masks.shape[1]
    streams = layer == 0
    slices = dp_size // 2
    quarter_k = heads * HEAD_K
    quarter_v = heads * HEAD_V
    quarter_f = weights[-1].shape[-1] // 2 if streams else weights[-1].shape[-1]
    vmem = pl.BlockSpec(memory_space=pltpu.VMEM)
    any_spec = pl.BlockSpec(memory_space=pl.ANY)
    wides = (2 * quarter_k + 2 * quarter_v, quarter_v, 2 * quarter_f, quarter_f)

    def tokens(wide, kind=bf16):
        return jax.ShapeDtypeStruct((2, length, wide), kind)

    turned = jax.ShapeDtypeStruct((width, 2 * length), bf16)
    dma = pltpu.SemaphoreType.DMA
    out_shape = [
        jax.ShapeDtypeStruct((rows, width), f32),
        turned,
        tokens(quarter_k),
        tokens(quarter_k),
        tokens(quarter_v),
        tokens(quarter_v),
        jax.ShapeDtypeStruct((2, heads, length, 1), f32),
        tokens(quarter_v),
        tokens(quarter_v),
        tokens(quarter_v),
        turned,
        tokens(quarter_f),
        tokens(quarter_f),
        tokens(quarter_f),
    ]
    out_specs = [vmem] * len(out_shape)
    scratch = [pltpu.VMEM((slices, 2, width // dp_size, wide), bf16) for wide in wides] + [
        dma((8,)),
        pltpu.VMEM((2, length, width), bf16),
        pltpu.VMEM((2, length, width), bf16),
        pltpu.VMEM((2, length, width), bf16),
        pltpu.VMEM((2, 3, rows, width), bf16),
        dma((2, 3)),
        dma((2, 3)),
        dma((2, 3)),
        dma((2, 3)),
    ]
    if streams:
        out_shape = (
            [jax.ShapeDtypeStruct((2, slices, 2, width // dp_size, wide), bf16) for wide in wides]
            + [jax.ShapeDtypeStruct((2,) + gains.shape, f32)]
            + out_shape
            + [tokens(width), jax.ShapeDtypeStruct((rows, width), bf16)]
        )
        out_specs = [any_spec] * 4 + [vmem] + out_specs + [any_spec, vmem]
        scratch += [
            dma((8, slices - 1)),
            dma((8, slices - 1)),
            dma((8, slices)),
            dma((8, slices)),
            dma((8,)),
            dma((8,)),
            dma((8,)),
            dma((8,)),
            dma((8,)),
            dma,
            dma,
            dma((3,)),
            dma((3,)),
            dma,
        ]
    operands = [x, gains, tables, masks] + ([out_grad] if streams else [])
    return pl.pallas_call(
        functools.partial(forward_kernel, dp_size, layer),
        out_shape=out_shape,
        in_specs=[vmem] * len(operands) + [any_spec] * len(weights),
        out_specs=out_specs,
        scratch_shapes=scratch,
        compiler_params=pltpu.CompilerParams(
            collective_id=1 + layer, has_side_effects=True, vmem_limit_bytes=VMEM_LIMIT
        ),
        name="forward_layer",
    )(*operands, *weights)


class Refs:
    pass


GROUPS = 7


def backward_kernel(dp_size, layer, *refs):
    final_layer = layer == 0
    v = Refs()
    (v.grad_out, v.gains, v.tables, v.masks, v.x, v.middle, v.normed_in_t, v.query_rot, v.key_rot, v.value, v.unit,
     v.inverse, v.opened, v.slope_open, v.merged, v.normed_mid_t, v.act, v.slope, v.hidden,
     v.qkvs_all, v.out_all, v.gate_up_all, v.down_all, v.down_in, *refs) = refs
    if final_layer:
        v.later_chip, v.later_terms, v.first_rows, v.second_rows, *refs = refs
    v.grad_in, v.chip, v.core_land, *refs = refs
    if final_layer:
        v.x_land, v.final, v.gain_sums, v.taken_rows, v.taken_grads, *refs = refs
    else:
        v.terms, v.result, v.next_down, *refs = refs
    (v.big, v.out_t, v.query_v, v.key_v, v.value_v, v.wide_a, v.wide_b, v.wide_c, v.inverse_v, v.x_v, v.middle_v,
     v.normed_t, v.outer, v.grad_down, v.grad_gate_up, v.grad_branch, v.grad_qkvs, v.turned, v.parts, v.landed,
     v.grad_middle, v.stage_given, v.stage_own, v.core_part, v.load_sem, v.s_send, v.s_recv, v.g_send, v.g_recv,
     v.c_send, v.c_recv, v.local_sem, *refs) = refs
    if final_layer:
        (v.left, v.right, v.sums, v.r_sem, v.x_send, v.x_recv, v.z_send, v.z_recv, v.terms, v.held, v.hop_land,
         v.t_send, v.t_recv, v.row_send, v.row_recv) = refs
    else:
        v.parts_y, v.landed_y, v.d_send, v.d_recv, v.d_sem = refs
    at = Place(dp_size)
    rows, width = v.x.shape
    sq = Square(dp_size, rows)
    masks, tables, gains = v.masks, v.tables, v.gains
    query_v, key_v, value_v = v.query_v, v.key_v, v.value_v
    wide_a, wide_b, wide_c = v.wide_a, v.wide_b, v.wide_c
    grad_down, grad_gate_up, grad_branch, grad_qkvs = v.grad_down, v.grad_gate_up, v.grad_branch, v.grad_qkvs
    big, out_t, outer, parts, landed, terms = v.big, v.out_t, v.outer, v.parts, v.landed, v.terms
    wide_k = query_v.shape[-1]
    wide_v = value_v.shape[-1]
    wide_f = outer.shape[-1]
    heads = wide_k // HEAD_K
    slices = dp_size // 2
    slice_rows = width // dp_size
    gain_in = gains[layer, 0:1]
    gain_mid = gains[layer, 1:2]
    other = 1 - at.section
    steps = [(k, b) for k in range(at.groups) for b in range(2)]
    steps = steps[1:] + steps[:1]

    def load(index, source, target):
        copy = pltpu.make_async_copy(source, target, v.load_sem.at[index])
        copy.start()
        return copy

    def remote(src, dst, send, recv, device):
        return pltpu.make_async_remote_copy(
            src_ref=src, dst_ref=dst, send_sem=send, recv_sem=recv, device_id=device, device_id_type=MESH
        )

    def place(section=None, dp=None, tensor=None):
        return (
            at.section if section is None else section,
            at.dp if dp is None else dp,
            at.tensor if tensor is None else tensor,
        )

    sibling = place(dp=at.sibling())
    across = place(section=other)

    token_load = load(14, v.down_in, grad_down)
    down_load = load(0, v.down_all.at[layer], big.at[:, pl.ds(2 * wide_f, wide_f)])
    act_load = load(1, v.act, wide_a)
    slope_load = load(2, v.slope, wide_b)
    gate_load = load(3, v.gate_up_all.at[layer], big.at[:, pl.ds(0, 2 * wide_f)])
    hidden_load = load(4, v.hidden, outer)
    mid_load = load(5, v.normed_mid_t, v.normed_t)
    early = [
        load(6, v.middle, v.middle_v),
        load(7, v.x, v.x_v),
        load(8, v.out_all.at[layer], out_t),
        load(9, v.query_rot, query_v),
        load(10, v.key_rot, key_v),
        load(11, v.value, value_v),
        load(12, v.inverse, v.inverse_v),
        load(13, v.opened, wide_c),
    ]
    terms[...] = jnp.zeros_like(terms)

    partners = [sq.device(*step) for step in SQUARE] + [sibling]
    if final_layer:
        partners.append(across)
        partners += [place(dp=at.dp_at(k, b)) for k, b in steps[:-1] if (k, b) != (0, 1)]
    barrier = pltpu.get_barrier_semaphore()
    for partner in partners:
        pl.semaphore_signal(barrier, inc=1, device_id=partner, device_id_type=MESH)
    pl.semaphore_wait(barrier, len(partners))

    def x_copy(e, j, source):
        block = source.at[e, j]
        return remote(block, v.x_land.at[e, j], v.x_send.at[e, j], v.x_recv.at[e, j], across)

    def start_x(e, source):
        @pl.loop(0, slices)
        def _(j):
            x_copy(e, j, source).start()

    row_copies = []
    if final_layer:

        @pl.when(at.section == 0)
        def _():
            remote(v.second_rows, v.taken_rows, v.row_send.at[0], v.row_recv.at[0], across).start()

            @pl.loop(0, GROUPS)
            def _(e):
                start_x(e, v.later_chip)

            remote(v.grad_out, v.taken_grads, v.row_send.at[1], v.row_recv.at[1], across).start()

        @pl.when(at.section == 1)
        def _():
            remote(v.first_rows, v.taken_rows, v.row_send.at[0], v.row_recv.at[0], across).start()

    def through_down(s):
        tokens = grad_down[s]
        for start in range(0, wide_f, TILE):
            cols = slice(start, start + TILE)
            grad_hidden = mm(tokens, big[:, 2 * wide_f + start : 2 * wide_f + start + TILE])
            grad_gate_up[s, :, cols] = (grad_hidden * wide_b[s, :, cols].astype(f32)).astype(bf16)
            grad_gate_up[s, :, wide_f + start : wide_f + start + TILE] = (
                grad_hidden * wide_a[s, :, cols].astype(f32)
            ).astype(bf16)

    def give_back(s, source, weight, first, size, target):
        tokens = source[s]
        for start in range(0, width, TILE):
            target[s, :, start : start + TILE] = mm_nt(
                tokens, weight[start : start + TILE, first : first + size]
            ).astype(bf16)

    def collected(block, given, land):
        total = sq.chunk(given)[block].astype(f32)
        for j in range(len(SQUARE)):
            total = total + land[j, block].astype(f32)
        return total

    def exchange(source, weight, first, size, target, land, which):
        give_back(sq.next, source, weight, first, size, target)
        send, recv = v.g_send.at[which], v.g_recv.at[which]
        pushes = [sq.give(target, land, send, recv, j) for j in (1, 2)]
        give_back(sq.own, source, weight, first, size, target)
        pushes.append(sq.give(target, land, send, recv, 0))
        return pushes

    members = [
        (v.turned, outer, 0, wide_f),
        (v.normed_t, grad_gate_up, 0, wide_f),
        (v.normed_t, grad_gate_up, wide_f, wide_f),
        (v.turned, outer, 0, wide_v),
        (v.normed_t, grad_qkvs, 0, 2 * wide_k),
        (v.normed_t, grad_qkvs, 2 * wide_k, wide_v),
        (v.normed_t, grad_qkvs, 2 * wide_k + wide_v, wide_v),
    ]
    given_copies, own_copies, fetches = {}, {}, {}

    def product(e, dp):
        left, right, first, size = members[e]
        start = pl.multiple_of(dp * slice_rows, slice_rows)
        wide = right[:, :, first : first + size].reshape(-1, size)
        return mm(left[pl.ds(start, slice_rows), :], wide)

    def given(e):
        if e >= 2:
            given_copies[e - 2].wait_send()
        stage = v.stage_given.at[e % 2]

        @pl.loop(0, slices)
        def _(j):
            stage[j] = product(e, j * 2 + 1 - at.core).astype(bf16)

        given_copies[e] = remote(stage, v.core_land.at[e], v.c_send.at[e], v.c_recv.at[e], sibling)
        given_copies[e].start()

    def fetch(e):
        given_copies[e].wait_recv()
        fetches[e] = pltpu.make_async_copy(v.core_land.at[e], v.core_part, v.local_sem.at[0])
        fetches[e].start()

    def settle(e):
        if e in settled:
            return
        settled.append(e)
        own_copies[e].wait()
        if final_layer:

            @pl.when(at.section == 1)
            def _():
                start_x(e, v.chip)

    def own(e):
        if e >= 1:
            settle(e - 1)
        fetches[e].wait()

        @pl.loop(0, slices)
        def _(j):
            v.stage_own[j] = (product(e, j * 2 + at.core) + v.core_part[j].astype(f32)).astype(bf16)

        own_copies[e] = pltpu.make_async_copy(v.stage_own, v.chip.at[e], v.local_sem.at[1])
        own_copies[e].start()

    settled = []

    def index(k, b):
        return ((at.group + k) % at.groups) * 2 + (at.low + b) % 2

    def z_copy(e, j):
        k, b = steps[j]
        return remote(
            v.sums.at[j], v.final.at[e, k, at.low], v.z_send.at[e, j], v.z_recv.at[e, j], place(dp=at.dp_at(k, b))
        )

    def home_copy(e):
        return pltpu.make_async_copy(v.sums.at[slices - 1], v.final.at[e, 0, at.low], v.r_sem.at[2, 0])

    def reduce_group(e, source, wait_previous):
        def loads(j):
            here = index(*steps[j])
            return (
                pltpu.make_async_copy(source.at[e, here], v.left.at[j % 2], v.r_sem.at[0, j % 2]),
                pltpu.make_async_copy(v.x_land.at[e, here], v.right.at[j % 2], v.r_sem.at[1, j % 2]),
            )

        def begin(j):
            x_copy(e, index(*steps[j]), source).wait_recv()
            for copy in loads(j):
                copy.start()

        begin(0)
        for j in range(slices):
            if j + 1 < slices:
                begin(j + 1)
            for copy in loads(j):
                copy.wait()
            if wait_previous is not None:
                last = j == slices - 1

                @pl.when(wait_previous)
                def _():
                    if last:
                        home_copy(e).wait()
                    else:
                        z_copy(e - 1, j).wait_send()

            v.sums[j] = (v.left[j % 2].astype(f32) + v.right[j % 2].astype(f32)).astype(bf16)
            if j == slices - 1:
                home_copy(e).start()
            else:
                z_copy(e, j).start()

    def reduce_for(section, source, first, stop):
        @pl.when(at.section == section)
        def _():
            @pl.loop(first, stop)
            def _(e):
                reduce_group(e, source, e > 0)

    token_load.wait()
    if final_layer:
        hidden_load.wait()
        transpose_into(v.turned, grad_down)
        given(0)
    down_load.wait()
    act_load.wait()
    slope_load.wait()
    through_down(sq.next)
    through_down(sq.own)
    unit_load = load(1, v.unit, wide_a)
    bend_load = load(2, v.slope_open, wide_b)
    gate_load.wait()
    gives = exchange(grad_gate_up, big, 0, 2 * wide_f, parts, landed, 0)
    if not final_layer:
        hidden_load.wait()
        transpose_into(v.turned, grad_down)
        given(0)
        for s in (sq.next, sq.own):
            give_back(s, outer, big, 2 * wide_f, wide_f, v.parts_y)
    fetch(0)
    own(0)
    mid_load.wait()
    given(1)
    qkvs_load = load(3, v.qkvs_all.at[layer], big)
    merged_load = load(4, v.merged, outer)
    for copy in early:
        copy.wait()
    settle(0)
    for push in gives:
        push.wait_recv()

    def through_mid(block):
        upstream = collected(block, parts, landed)
        normed, scale = norm_parts(v.middle_v[block])
        grad_rows = v.grad_out[block].astype(f32) + norm_grad(normed, scale, upstream, gain_mid)
        v.grad_middle[block] = grad_rows
        sq.chunk(grad_branch)[block] = grad_rows.astype(bf16)
        terms[1:2] = terms[1:2] + jnp.sum(upstream * normed, axis=0, keepdims=True)

    row_blocks(rows, through_mid)
    mids = sq.spread(grad_branch, v.s_send, v.s_recv)
    given(2)
    fetch(1)
    own(1)
    unit_load.wait()
    bend_load.wait()
    settle(1)

    def through_heads(s):
        tokens = grad_branch[s]
        for head in range(heads):
            cols_k = slice(head * HEAD_K, (head + 1) * HEAD_K)
            cols_v = slice(head * HEAD_V, (head + 1) * HEAD_V)
            grad_merged = mm(tokens, out_t[:, cols_v])
            unit_rows = wide_a[s, :, cols_v].astype(f32)
            first = 2 * wide_k + wide_v + head * HEAD_V
            grad_qkvs[s, :, first : first + HEAD_V] = (
                grad_merged * unit_rows * wide_b[s, :, cols_v].astype(f32)
            ).astype(bf16)
            grad_unit = grad_merged * wide_c[s, :, cols_v].astype(f32)
            grad_mixed = (
                v.inverse_v[s, head]
                * (
                    grad_unit
                    - jnp.mean(grad_unit, axis=-1, keepdims=True)
                    - unit_rows * jnp.mean(grad_unit * unit_rows, axis=-1, keepdims=True)
                )
            ).astype(bf16)
            query, key, val = query_v[s, :, cols_k], key_v[s, :, cols_k], value_v[s, :, cols_v]
            mask = masks[s, head]
            weight = (mm_nt(query, key) * mask).astype(bf16)
            grad_product = (mm_nt(grad_mixed, val) * mask).astype(bf16)
            first = 2 * wide_k + head * HEAD_V
            grad_qkvs[s, :, first : first + HEAD_V] = mm_tn(weight, grad_mixed).astype(bf16)
            grad_qkvs[s, :, cols_k] = turn_back(mm(grad_product, key), tables[0], tables[1], tables[2]).astype(bf16)
            first = wide_k + head * HEAD_K
            grad_qkvs[s, :, first : first + HEAD_K] = turn_back(
                mm_tn(grad_product, query), tables[0], tables[1], tables[3]
            ).astype(bf16)

    mids[0].wait_recv()
    through_heads(sq.own)
    mids[1].wait_recv()
    mids[2].wait_recv()
    if not final_layer:
        gives_y = [sq.give(v.parts_y, v.landed_y, v.g_send.at[2], v.g_recv.at[2], j) for j in range(3)]
    through_heads(sq.next)
    qkvs_load.wait()
    for push in gives:
        push.wait_send()
    ends = exchange(grad_qkvs, big, 0, grad_qkvs.shape[-1], parts, landed, 1)
    fetch(2)
    own(2)
    in_load = load(5, v.normed_in_t, v.normed_t)
    transpose_into(v.turned, grad_branch)
    settle(2)
    merged_load.wait()
    given(3)
    in_load.wait()
    given(4)
    fetch(3)
    own(3)
    if final_layer:
        reduce_for(1, v.later_chip, 0, 1)
        reduce_for(0, v.chip, 0, 1)
    settle(3)
    for push in ends:
        push.wait_recv()

    def through_in(block):
        upstream = collected(block, parts, landed)
        normed, scale = norm_parts(v.x_v[block].astype(f32))
        v.grad_in[block] = (v.grad_middle[block] + norm_grad(normed, scale, upstream, gain_in)).astype(bf16)
        terms[0:1] = terms[0:1] + jnp.sum(upstream * normed, axis=0, keepdims=True)

    row_blocks(rows, through_in)
    if final_layer:

        @pl.when(at.section == 1)
        def _():
            remote(v.grad_in, v.taken_grads, v.row_send.at[1], v.row_recv.at[1], across).start()

    else:
        downs = sq.spread_from(v.grad_in, v.next_down, v.d_send, v.d_recv, v.d_sem)

    given(5)
    fetch(4)
    own(4)
    given(6)
    settle(4)
    fetch(5)
    own(5)
    if not final_layer:
        for push in gives_y:
            push.wait_recv()

        def last(block):
            v.result[block] = (
                v.middle_v[block] + collected(block, v.parts_y, v.landed_y)
            ).astype(bf16)

        row_blocks(rows, last)
    fetch(6)
    own(6)
    settle(6)
    for push in mids + ends:
        push.wait_send()
    for e in (5, 6):
        given_copies[e].wait_send()
    if not final_layer:
        for push in gives_y:
            push.wait_send()
        for push in downs:
            push.wait()
        return

    reduce_for(1, v.later_chip, 1, GROUPS)
    reduce_for(0, v.chip, 1, GROUPS)

    held, hop_land, mine = v.held, v.hop_land, v.held.at[at.section]
    held[0] = terms[...]
    held[1] = v.later_terms[...]
    hop = remote(held, hop_land.at[0], v.t_send.at[0], v.t_recv.at[0], sibling)
    hop.start()
    hop.wait()
    held[...] = held[...] + hop_land[0]
    hop = remote(held.at[other], hop_land.at[1, other], v.t_send.at[1], v.t_recv.at[1], across)
    hop.start()
    hop.wait_send()
    remote(held.at[other], hop_land.at[1, at.section], v.t_send.at[1], v.t_recv.at[1], across).wait_recv()
    mine[...] = mine[...] + hop_land[1, at.section]
    for h, device in ((2, place(tensor=1 - at.tensor)), (3, place(dp=at.dp_at(0, 1)))):
        hop = remote(mine, hop_land.at[h, 0], v.t_send.at[h], v.t_recv.at[h], device)
        hop.start()
        hop.wait()
        mine[...] = mine[...] + hop_land[h, 0]
    hops = []
    for k in range(1, at.groups):
        hop = remote(mine, hop_land.at[3 + k, 0], v.t_send.at[3 + k], v.t_recv.at[3 + k], place(dp=at.dp_at(k, 0)))
        hop.start()
        hops.append(hop)
    total = mine[...]
    for k, hop in zip(range(1, at.groups), hops):
        hop.wait()
        total = total + hop_land[3 + k, 0]
    v.gain_sums[...] = total

    for which, rows_sent in ((0, v.second_rows), (1, v.grad_in)):
        target = v.taken_rows if which == 0 else v.taken_grads
        copy = remote(rows_sent, target, v.row_send.at[which], v.row_recv.at[which], across)
        copy.wait_recv()
        copy.wait_send()

    home_copy(0).wait()
    for j in range(slices - 1):
        z_copy(GROUPS - 1, j).wait_send()

        @pl.loop(0, GROUPS)
        def _(e):
            z_copy(e, j).wait_recv()

    @pl.loop(0, GROUPS)
    def _(e):
        @pl.loop(0, slices)
        def _(j):
            x_copy(e, j, v.chip).wait_send()


def backward_layer(layer, grad_out, down, x, gains, tables, masks, saved, gathered, dp_size, later=None, rows_out=None):
    rows, width = x.shape
    length = masks.shape[-1]
    (middle, normed_in_t, query_rot, key_rot, value, unit, inverse, opened, slope_open, merged, normed_mid_t, act, slope,
     hidden) = saved
    vmem = pl.BlockSpec(memory_space=pltpu.VMEM)
    any_spec = pl.BlockSpec(memory_space=pl.ANY)
    final_layer = layer == 0
    slices = dp_size // 2
    slice_rows = width // dp_size
    size = hidden.shape[-1]
    assert value.shape[-1] == size and 2 * query_rot.shape[-1] == size
    block = (slices, slice_rows, size)

    def held(*shape, kind=bf16):
        return pltpu.VMEM(shape, kind)

    def stored(*shape, kind=bf16):
        return jax.ShapeDtypeStruct(shape, kind)

    dma = pltpu.SemaphoreType.DMA
    operands = [grad_out, gains, tables, masks]
    operands += [x, middle, normed_in_t, query_rot, key_rot, value, unit, inverse, opened, slope_open, merged, normed_mid_t,
                 act, slope, hidden]
    operands += [*gathered, down]
    in_specs = [vmem] * 4 + [any_spec] * (len(operands) - 4)
    out_shape = [stored(rows, width), stored(GROUPS, *block), stored(GROUPS, *block)]
    out_specs = [vmem, any_spec, any_spec]
    if final_layer:
        later_chip, later_terms = later
        operands += [later_chip, later_terms, *rows_out]
        in_specs += [any_spec, vmem, any_spec, any_spec]
        out_shape += [stored(GROUPS, *block), stored(GROUPS, dp_size // 4, 2, slice_rows, size), stored(2, width, kind=f32),
                      stored(rows, width), stored(rows, width)]
        out_specs += [any_spec, any_spec, vmem, any_spec, any_spec]
    else:
        out_shape += [stored(2, width, kind=f32), stored(rows, width), stored(2, length, width)]
        out_specs += [vmem, vmem, any_spec]
    scratch = [
        held(width, 3 * size),
        held(width, size),
        held(*query_rot.shape),
        held(*key_rot.shape),
        held(*value.shape),
        held(2, length, size),
        held(2, length, size),
        held(2, length, size),
        held(*inverse.shape, kind=f32),
        held(rows, width),
        held(rows, width, kind=f32),
        held(width, 2 * length),
        held(2, length, size),
        held(2, length, width),
        held(2, length, 2 * size),
        held(2, length, width),
        held(2, length, 3 * size),
        held(width, 2 * length),
        held(2, length, width),
        held(3, rows, width),
        held(rows, width, kind=f32),
        held(2, *block),
        held(*block),
        held(*block),
        dma((15,)),
        dma((3,)),
        dma((3,)),
        dma((3, 3)),
        dma((3, 3)),
        dma((GROUPS,)),
        dma((GROUPS,)),
        dma((2,)),
    ]
    if final_layer:
        hops = 3 + dp_size // 4
        scratch += [
            held(2, slice_rows, size),
            held(2, slice_rows, size),
            held(*block),
            dma((3, 2)),
            dma((GROUPS, slices)),
            dma((GROUPS, slices)),
            dma((GROUPS, slices - 1)),
            dma((GROUPS, slices - 1)),
            held(2, width, kind=f32),
            held(2, 2, width, kind=f32),
            held(hops, 2, 2, width, kind=f32),
            dma((hops,)),
            dma((hops,)),
            dma((2,)),
            dma((2,)),
        ]
    else:
        scratch += [held(2, length, width), held(3, rows, width), dma((3,)), dma((3,)), dma]
    return pl.pallas_call(
        functools.partial(backward_kernel, dp_size, layer),
        out_shape=out_shape,
        in_specs=in_specs,
        out_specs=out_specs,
        scratch_shapes=scratch,
        compiler_params=pltpu.CompilerParams(
            collective_id=4 + layer, has_side_effects=True, vmem_limit_bytes=VMEM_LIMIT
        ),
        name="backward_layer",
    )(*operands)


def nested(outs):
    return (*outs[:5], outs[5:-2], *outs[-2:])


def on_device(
    dp_size,
    layer_input,
    segment_ids,
    output_grad,
    query_weight,
    key_weight,
    value_weight,
    swish_weight,
    output_weight,
    gate_weight,
    up_weight,
    down_weight,
    mixer_gain,
    ffn_gain,
):
    at = Place(dp_size)
    section_first = at.section == 0
    rows_here, width = layer_input.shape[1:]
    length = segment_ids.shape[1]
    score_scale = HEAD_K ** (-0.5)

    quarter_k = query_weight.shape[2] // 2
    quarter_v = value_weight.shape[2] // 2
    quarter_f = gate_weight.shape[2] // 2
    heads_here = quarter_k // HEAD_K
    first_head = (at.tensor * 2 + at.low) * heads_here
    cosine, sine, growth = rotation_tables(length, HEAD_K // 2)

    ids_mine = lax.dynamic_index_in_dim(segment_ids, at.section, 0, keepdims=False)
    ids_pair = lax.ppermute(ids_mine, "dp", [(i, i ^ 2) for i in range(dp_size)])
    ids = jnp.where(at.low == 0, jnp.stack([ids_mine, ids_pair]), jnp.stack([ids_pair, ids_mine]))
    masks = decay_mask(ids, first_head, heads_here) * score_scale
    tables = jnp.stack([cosine, sine, growth, 1.0 / growth])

    first_in = lax.dynamic_index_in_dim(layer_input, at.section, 0, keepdims=False)
    out_grad = lax.dynamic_index_in_dim(output_grad, at.section, 0, keepdims=False)
    shards = (query_weight[0], key_weight[0], value_weight[0], swish_weight[0], output_weight[0].T, gate_weight[0],
              up_weight[0], down_weight[0].T)
    own_gains = jnp.concatenate([mixer_gain, ffn_gain], axis=0)
    *gathered, all_gains, first_saved, second_down, first_sent = nested(
        forward_layer(0, first_in, own_gains, tables, masks, shards, dp_size, out_grad)
    )
    second_saved = forward_layer(1, first_sent, all_gains, tables, masks, gathered, dp_size)
    gathered = [g.reshape(2, width, g.shape[-1]) for g in gathered]
    second_grad, later_chip, _, later_terms, second_sent, first_down = backward_layer(
        1, out_grad, second_down, first_sent, all_gains, tables, masks, second_saved, gathered, dp_size
    )
    first_grad, _, _, _, landed, my_gains, taken_rows, taken_grads = backward_layer(
        0, second_grad, first_down, first_in, all_gains, tables, masks, first_saved, gathered, dp_size,
        (later_chip, later_terms), (first_sent, second_sent),
    )

    def by_layer(first, second, taken):
        return jnp.where(section_first, jnp.stack([first, taken]), jnp.stack([taken, second]))[None]

    def natural(e, start, size):
        part = jnp.sum(landed[e, :, :, :, start : start + size].astype(f32), axis=0)
        return part.swapaxes(0, 1).reshape(part.shape[1], -1)

    def tall(e):
        part = jnp.sum(landed[e].astype(f32), axis=0)
        return part.swapaxes(1, 2).reshape(-1, part.shape[1])

    return (
        by_layer(first_sent, second_sent, taken_rows),
        by_layer(first_grad, second_grad, taken_grads),
        natural(4, 0, quarter_k)[None],
        natural(4, quarter_k, quarter_k)[None],
        natural(5, 0, quarter_v)[None],
        natural(6, 0, quarter_v)[None],
        tall(3)[None],
        natural(1, 0, quarter_f)[None],
        natural(2, 0, quarter_f)[None],
        tall(0)[None],
        my_gains[0][None],
        my_gains[1][None],
    )


def solution(mesh):
    in_specs = (
        P(None, ("dp", "tensor"), None),
        P(None, "dp"),
        P(None, ("dp", "tensor"), None),
        P("section", "dp", "tensor"),
        P("section", "dp", "tensor"),
        P("section", "dp", "tensor"),
        P("section", "dp", "tensor"),
        P("section", "tensor", "dp"),
        P("section", "dp", "tensor"),
        P("section", "dp", "tensor"),
        P("section", "tensor", "dp"),
        P("section", None),
        P("section", None),
    )
    out_specs = (
        P("section", None, ("dp", "tensor"), None),
        P("section", None, ("dp", "tensor"), None),
        P("section", "dp", "tensor"),
        P("section", "dp", "tensor"),
        P("section", "dp", "tensor"),
        P("section", "dp", "tensor"),
        P("section", "tensor", "dp"),
        P("section", "dp", "tensor"),
        P("section", "dp", "tensor"),
        P("section", "tensor", "dp"),
        P("section", None),
        P("section", None),
    )
    return jax.shard_map(
        functools.partial(on_device, mesh.shape["dp"]),
        mesh=mesh,
        in_specs=in_specs,
        out_specs=out_specs,
        check_vma=False,
    )
```

```python
import functools

import jax
import jax.numpy as jnp
from jax import lax
from jax.experimental import pallas as pl
from jax.experimental.pallas import tpu as pltpu
from jax.sharding import PartitionSpec as P

HEAD_K = 256
HEAD_V = 512
MESH = pl.DeviceIdType.MESH

epsilon = 1e-05
group_guard = 1.0
bf16 = jnp.bfloat16
f32 = jnp.float32


def rotation_tables(length, half_width):
    pair_index = jnp.arange(half_width).astype(f32)
    position = jnp.arange(length).astype(f32)[:, None]
    angle = position * jnp.exp(-jnp.log(10000.0) * pair_index / half_width)
    zeta = (pair_index / half_width + 0.4) / 1.4
    growth = jnp.exp(position / 512.0 * jnp.log(zeta))
    return (jnp.cos(angle), jnp.sin(angle), growth)


def decay_mask(segments, first_head, heads):
    length = segments.shape[-1]
    position = jnp.arange(length)
    earlier = position[:, None] >= position[None, :]
    same_doc = (segments[:, :, None] == segments[:, None, :]) & earlier[None]
    distance = jnp.maximum(position[:, None] - position[None, :], 0).astype(f32)
    head_index = (first_head + jnp.arange(heads)).astype(f32)
    log_rate = jnp.log(1.0 - jnp.exp2(-5.0 - head_index))
    decay = jnp.exp(log_rate[:, None, None] * distance[None])
    return jnp.where(same_doc[:, None], decay[None], 0.0)


class Place:
    def __init__(self, dp_size):
        self.groups = dp_size // 4
        self.section = lax.axis_index("section")
        self.dp = lax.axis_index("dp")
        self.tensor = lax.axis_index("tensor")
        self.core = self.dp % 2
        self.low = (self.dp // 2) % 2
        self.group = self.dp // 4

    def dp_at(self, group_step, low_step):
        group = (self.group + group_step + self.groups) % self.groups
        return (group * 2 + (self.low + low_step) % 2) * 2 + self.core

    def sibling(self):
        return self.dp + 1 - 2 * self.core


SQUARE = ((0, 1), (1, 0), (1, 1))
TILE = 512
VMEM_LIMIT = 63 * 1024 * 1024


def mm(left, right):
    return lax.dot_general(left, right, (((1,), (0,)), ((), ())), preferred_element_type=f32)


def mm_nt(left, right):
    return lax.dot_general(left, right, (((1,), (1,)), ((), ())), preferred_element_type=f32)


def mm_tn(left, right):
    return lax.dot_general(left, right, (((0,), (0,)), ((), ())), preferred_element_type=f32)


class Square:
    def __init__(self, dp_size, rows):
        self.at = Place(dp_size)
        self.rows = rows
        self.own = self.at.low
        self.next = 1 - self.at.low

    def device(self, low_step, tensor_step):
        return (self.at.section, self.at.dp_at(0, low_step), (self.at.tensor + tensor_step) % 2)

    def barrier(self):
        barrier = pltpu.get_barrier_semaphore()
        for step in SQUARE:
            pl.semaphore_signal(barrier, inc=1, device_id=self.device(*step), device_id_type=MESH)
        pl.semaphore_wait(barrier, len(SQUARE))

    def chunk(self, ref, low_step=0, tensor_step=0):
        start = pl.multiple_of((self.at.tensor + tensor_step) % 2 * self.rows, self.rows)
        return ref.at[(self.at.low + low_step) % 2, pl.ds(start, self.rows)]

    def copy(self, src, dst, send, recv, step):
        return pltpu.make_async_remote_copy(
            src_ref=src,
            dst_ref=dst,
            send_sem=send,
            recv_sem=recv,
            device_id=self.device(*step),
            device_id_type=MESH,
        )

    def spread(self, ref, send, recv):
        pushes = []
        for j, step in enumerate(SQUARE):
            push = self.copy(self.chunk(ref), self.chunk(ref), send.at[j], recv.at[j], step)
            push.start()
            pushes.append(push)
        return pushes

    def spread_from(self, own, ref, send, recv, here):
        local = pltpu.make_async_copy(own, self.chunk(ref), here)
        local.start()
        pushes = [local]
        for j, step in enumerate(SQUARE):
            push = self.copy(own, self.chunk(ref), send.at[j], recv.at[j], step)
            push.start()
            pushes.append(push)
        return pushes

    def give(self, parts, landed, send, recv, j):
        push = self.copy(self.chunk(parts, *SQUARE[j]), landed.at[j], send.at[j], recv.at[j], SQUARE[j])
        push.start()
        return push


def row_blocks(rows, body, block=32):
    block = min(block, rows)

    @pl.loop(0, rows // block)
    def _(i):
        body(pl.ds(pl.multiple_of(i * block, block), block))


def norm_parts(values):
    centred = values - jnp.mean(values, axis=-1, keepdims=True)
    scale = lax.rsqrt(jnp.mean(centred * centred, axis=-1, keepdims=True) + epsilon)
    return centred * scale, scale


def norm_grad(normed, scale, upstream, gain):
    through = upstream * gain
    return scale * (
        through
        - jnp.mean(through, axis=-1, keepdims=True)
        - normed * jnp.mean(through * normed, axis=-1, keepdims=True)
    )


def turn(values, cosine, sine, scale):
    half = values.shape[-1] // 2
    a, b = values[:, :half], values[:, half:]
    return jnp.concatenate([(a * cosine - b * sine) * scale, (a * sine + b * cosine) * scale], axis=-1)


def turn_back(values, cosine, sine, scale):
    half = values.shape[-1] // 2
    a, b = values[:, :half] * scale, values[:, half:] * scale
    return jnp.concatenate([a * cosine + b * sine, b * cosine - a * sine], axis=-1)


def transpose_into(target, source):
    _, length, width = source.shape
    for s in range(2):
        for start in range(0, width, TILE):
            target[start : start + TILE, s * length : (s + 1) * length] = source[s, :, start : start + TILE].T


def forward_kernel(dp_size, layer, *refs):
    streams = layer == 0
    v = Refs()
    if streams:
        (v.x, v.own_gains, v.tables, v.masks, v.out_grad, *refs) = refs
        shards, refs = refs[:8], refs[8:]
        stored, refs = refs[:4], refs[4:]
        (v.gains, *refs) = refs
    else:
        (v.x, v.gains, v.tables, v.masks, *refs) = refs
        stored, refs = refs[:4], refs[4:]
    (middle, normed_in_t, query_rot, key_rot, value, unit, inverse, opened, slope_open, merged, normed_mid_t, act, slope,
     hidden, *refs) = refs
    if streams:
        (v.grad_down, result, *refs) = refs
    held, refs = refs[:4], refs[4:]
    (w_sem, normed_in, normed_mid, parts, landed, s_send, s_recv, g_send, g_recv, *refs) = refs
    x, tables, masks = v.x, v.tables, v.masks
    rows, width = x.shape
    sq = Square(dp_size, rows)
    at = sq.at
    qkvs, out_t, gate_up, down_t = held
    wide_k = query_rot.shape[-1]
    wide_v = value.shape[-1]
    wide_f = hidden.shape[-1]
    heads = wide_k // HEAD_K
    slices = dp_size // 2
    other = 1 - at.section
    groups = [(0, 0, wide_k), (0, wide_k, wide_k), (0, 2 * wide_k, wide_v), (0, 2 * wide_k + wide_v, wide_v),
              (1, 0, wide_v), (2, 0, wide_f), (2, wide_f, wide_f), (3, 0, wide_f)]
    loads = {}

    def load(i):
        which, first, size = groups[i]
        columns = pl.ds(first, size)
        loads[i] = pltpu.make_async_copy(
            stored[which].at[layer, :, :, :, columns], held[which].at[:, :, :, columns], w_sem.at[i]
        )
        loads[i].start()

    def weight(which, first, size):
        return held[which][:, :, :, first : first + size].reshape(width, size)

    def first_norm(block):
        unit_rows, _ = norm_parts(x[block].astype(f32))
        sq.chunk(normed_in)[block] = (unit_rows * v.gains[layer, 0:1]).astype(bf16)

    def project(i, s):
        loads_wait(i)
        first, size = groups[i][1:]
        tokens = normed_in[s]
        for start in range(0, size, TILE):
            wide = mm(tokens, weight(0, first + start, TILE))
            cols = slice(start, start + TILE)
            if i < 2:
                dest = (query_rot, key_rot)[i]
                for head in range(TILE // HEAD_K):
                    part = wide[:, head * HEAD_K : (head + 1) * HEAD_K]
                    dest[s, :, start + head * HEAD_K : start + (head + 1) * HEAD_K] = turn(
                        part, tables[0], tables[1], tables[2 + i]
                    ).astype(bf16)
            elif i == 2:
                value[s, :, cols] = wide.astype(bf16)
            else:
                sigmoid = 1.0 / (1.0 + jnp.exp(-wide))
                opened[s, :, cols] = (wide * sigmoid).astype(bf16)
                slope_open[s, :, cols] = (sigmoid * (1.0 + wide * (1.0 - sigmoid))).astype(bf16)

    waited = []

    def loads_wait(i):
        if i not in waited:
            waited.append(i)
            loads[i].wait()

    def retain(s):
        for head in range(heads):
            cols_k = slice(head * HEAD_K, (head + 1) * HEAD_K)
            cols_v = slice(head * HEAD_V, (head + 1) * HEAD_V)
            product = mm_nt(query_rot[s, :, cols_k], key_rot[s, :, cols_k])
            weights = (product * masks[s, head]).astype(bf16)
            mixed = mm(weights, value[s, :, cols_v])
            centred = mixed - jnp.mean(mixed, axis=-1, keepdims=True)
            scale = lax.rsqrt(jnp.mean(centred * centred, axis=-1, keepdims=True) + group_guard)
            unit_rows = centred * scale
            inverse[s, head] = scale
            unit[s, :, cols_v] = unit_rows.astype(bf16)
            merged[s, :, cols_v] = (unit_rows * opened[s, :, cols_v].astype(f32)).astype(bf16)

    def give_back(s, source, weight_t):
        tokens = source[s]
        step = width // slices
        for i in range(slices):
            parts[s, :, i * step : (i + 1) * step] = mm_nt(tokens, weight_t[i].reshape(step, -1)).astype(bf16)

    def collected(block, which):
        total = sq.chunk(parts)[block].astype(f32)
        for j in range(len(SQUARE)):
            total = total + landed[which, j, block].astype(f32)
        return total

    def give(s, which):
        send, recv = g_send.at[which], g_recv.at[which]
        return [sq.give(parts, landed.at[which], send, recv, j) for j in ((1, 2) if s == 1 else (0,))]

    def second_norm(block):
        middle_rows = x[block].astype(f32) + collected(block, 0)
        middle[block] = middle_rows
        unit_rows, _ = norm_parts(middle_rows)
        sq.chunk(normed_mid)[block] = (unit_rows * v.gains[layer, 1:2]).astype(bf16)

    def feed(s):
        loads_wait(5)
        loads_wait(6)
        tokens = normed_mid[s]
        for start in range(0, wide_f, TILE):
            cols = slice(start, start + TILE)
            gate = mm(tokens, weight(2, start, TILE))
            up = mm(tokens, weight(2, wide_f + start, TILE))
            square = gate * gate
            bend = jnp.tanh(0.7978845608028654 * gate * (1.0 + 0.044715 * square))
            half = 0.5 * (1.0 + bend)
            gelu = gate * half
            slope_gelu = half + 0.5 * gate * (1.0 - bend * bend) * (
                0.7978845608028654 * (1.0 + 3 * 0.044715 * square)
            )
            act[s, :, cols] = gelu.astype(bf16)
            slope[s, :, cols] = (slope_gelu * up).astype(bf16)
            hidden[s, :, cols] = (gelu * up).astype(bf16)

    if not streams:
        for i in range(7):
            load(i)
        row_blocks(rows, first_norm)
        sq.barrier()
        ins = sq.spread(normed_in, s_send.at[0], s_recv.at[0])
        ins[0].wait_recv()
        for i in range(4):
            project(i, sq.own)
        ins[1].wait_recv()
        ins[2].wait_recv()
        for i in range(4):
            project(i, sq.next)
        retain(sq.next)
        loads_wait(4)
        give_back(sq.next, merged, out_t)
        gives = give(1, 0)
        retain(sq.own)
        give_back(sq.own, merged, out_t)
        gives += give(0, 0)
        transpose_into(normed_in_t, normed_in)
        for push in gives:
            push.wait_recv()
        row_blocks(rows, second_norm)
        mids = sq.spread(normed_mid, s_send.at[1], s_recv.at[1])
        mids[0].wait_recv()
        feed(sq.own)
        mids[1].wait_recv()
        mids[2].wait_recv()
        feed(sq.next)
        transpose_into(normed_mid_t, normed_mid)
        for push in ins + mids + gives:
            push.wait_send()
        return

    (z_send, z_recv, x_send, x_recv, c_send, c_recv, o_send, o_recv, here_sem, gain_send, gain_recv, d_send, d_recv,
     d_sem) = refs
    steps = [(k, b) for k in range(at.groups) for b in range(2)][1:]

    def place(section=None, dp=None):
        return (at.section if section is None else section, at.dp if dp is None else dp, at.tensor)

    def copy(src, dst, send, recv, device):
        return pltpu.make_async_remote_copy(
            src_ref=src, dst_ref=dst, send_sem=send, recv_sem=recv, device_id=device, device_id_type=MESH
        )

    partners = [sq.device(*step) for step in SQUARE] + [place(dp=at.sibling()), place(section=other)]
    partners += [place(dp=at.dp_at(k, b)) for k, b in steps if (k, b) != (0, 1)]
    barrier = pltpu.get_barrier_semaphore()
    for partner in partners:
        pl.semaphore_signal(barrier, inc=1, device_id=partner, device_id_type=MESH)
    pl.semaphore_wait(barrier, len(partners))

    gain_copy = copy(v.own_gains, v.gains.at[at.section], gain_send, gain_recv, place(section=other))
    gain_copy.start()
    v.gains[at.section] = v.own_gains[...]

    def slot(i, section, dp):
        which, first, size = groups[i]
        return stored[which].at[section, dp // 2, dp % 2, :, pl.ds(first, size)]

    def block(i, section, core):
        which, first, size = groups[i]
        return stored[which].at[section, :, core, :, pl.ds(first, size)]

    def part(i, b):
        size = groups[i][2]
        return shards[i].at[:, pl.ds(pl.multiple_of((at.low + b) % 2 * size, size), size)]

    z_copies, x_copies, here, core_own, core_other = {}, {}, {}, {}, {}

    def push_own(i):
        mine = slot(i, at.section, at.dp)
        for j, (k, b) in enumerate(steps):
            z_copies[i, j] = copy(part(i, b), mine, z_send.at[i, j], z_recv.at[i, j], place(dp=at.dp_at(k, b)))
            z_copies[i, j].start()
        x_copies[i, 0] = copy(part(i, 0), mine, x_send.at[i, 0], x_recv.at[i, 0], place(section=other))
        x_copies[i, 0].start()
        here[i] = pltpu.make_async_copy(part(i, 0), mine, here_sem.at[i])
        here[i].start()

    def pass_on(i):
        for j, (k, b) in enumerate(steps):
            z_copies[i, j].wait_recv()
            arrived = slot(i, at.section, at.dp_at(-k, b))
            x_copies[i, j + 1] = copy(arrived, arrived, x_send.at[i, j + 1], x_recv.at[i, j + 1], place(section=other))
            x_copies[i, j + 1].start()
        here[i].wait()
        mine = block(i, at.section, at.core)
        core_own[i] = copy(mine, mine, c_send.at[i], c_recv.at[i], place(dp=at.sibling()))
        core_own[i].start()

    def share_other(i):
        for j in range(slices):
            x_copies[i, j].wait_recv()
        theirs = block(i, other, at.core)
        core_other[i] = copy(theirs, theirs, o_send.at[i], o_recv.at[i], place(dp=at.sibling()))
        core_other[i].start()

    def arrive(i):
        @pl.when(at.section == 0)
        def _():
            core_own[i].wait_recv()

        @pl.when(at.section == 1)
        def _():
            core_other[i].wait_recv()

        load(i)

    ahead = 3
    for i in range(ahead):
        push_own(i)
    gain_copy.wait_recv()
    row_blocks(rows, first_norm)
    ins = sq.spread(normed_in, s_send.at[0], s_recv.at[0])

    def advance(i):
        pass_on(i)
        if i + ahead < 8:
            push_own(i + ahead)
        if i > 0:
            share_other(i - 1)
            arrive(i - 1)

    advance(0)
    downs = sq.spread_from(v.out_grad, v.grad_down, d_send, d_recv, d_sem)
    advance(1)
    for push in ins:
        push.wait_recv()
    transpose_into(normed_in_t, normed_in)
    for i in range(2, 5):
        advance(i)
        for s in (sq.own, sq.next):
            project(i - 2, s)
    advance(5)
    for s in (sq.own, sq.next):
        project(3, s)
    retain(sq.next)
    loads_wait(4)
    give_back(sq.next, merged, out_t)
    gives = give(1, 0)
    retain(sq.own)
    give_back(sq.own, merged, out_t)
    gives += give(0, 0)
    advance(6)
    for push in gives:
        push.wait_recv()
    row_blocks(rows, second_norm)
    mids = sq.spread(normed_mid, s_send.at[1], s_recv.at[1])
    advance(7)
    for push in mids:
        push.wait_recv()
    transpose_into(normed_mid_t, normed_mid)
    feed(sq.next)
    feed(sq.own)
    for push in gives:
        push.wait_send()

    def last_group():
        for j in range(slices):
            x_copies[7, j].wait_recv()
        core_other[7].start()

    theirs = block(7, other, at.core)
    core_other[7] = copy(theirs, theirs, o_send.at[7], o_recv.at[7], place(dp=at.sibling()))

    @pl.when(at.section == 1)
    def _():
        last_group()

    arrive(7)
    loads_wait(7)
    give_back(sq.next, hidden, down_t)
    ends = give(1, 1)
    give_back(sq.own, hidden, down_t)
    ends += give(0, 1)

    @pl.when(at.section == 0)
    def _():
        last_group()

    for push in ends:
        push.wait_recv()

    def last(block):
        result[block] = (middle[block] + collected(block, 1)).astype(bf16)

    row_blocks(rows, last)

    @pl.when(at.section == 0)
    def _():
        for i in range(8):
            core_other[i].wait_recv()

    @pl.when(at.section == 1)
    def _():
        for i in range(8):
            core_own[i].wait_recv()

    for push in downs:
        push.wait()
    for push in ins + mids + ends + list(z_copies.values()) + list(x_copies.values()):
        push.wait_send()
    for i in range(8):
        core_own[i].wait_send()
        core_other[i].wait_send()
    gain_copy.wait_send()


def forward_layer(layer, x, gains, tables, masks, weights, dp_size, out_grad=None):
    rows, width = x.shape
    length = masks.shape[-1]
    heads = masks.shape[1]
    streams = layer == 0
    slices = dp_size // 2
    quarter_k = heads * HEAD_K
    quarter_v = heads * HEAD_V
    quarter_f = weights[-1].shape[-1] // 2 if streams else weights[-1].shape[-1]
    vmem = pl.BlockSpec(memory_space=pltpu.VMEM)
    any_spec = pl.BlockSpec(memory_space=pl.ANY)
    wides = (2 * quarter_k + 2 * quarter_v, quarter_v, 2 * quarter_f, quarter_f)

    def tokens(wide, kind=bf16):
        return jax.ShapeDtypeStruct((2, length, wide), kind)

    turned = jax.ShapeDtypeStruct((width, 2 * length), bf16)
    dma = pltpu.SemaphoreType.DMA
    out_shape = [
        jax.ShapeDtypeStruct((rows, width), f32),
        turned,
        tokens(quarter_k),
        tokens(quarter_k),
        tokens(quarter_v),
        tokens(quarter_v),
        jax.ShapeDtypeStruct((2, heads, length, 1), f32),
        tokens(quarter_v),
        tokens(quarter_v),
        tokens(quarter_v),
        turned,
        tokens(quarter_f),
        tokens(quarter_f),
        tokens(quarter_f),
    ]
    out_specs = [vmem] * len(out_shape)
    scratch = [pltpu.VMEM((slices, 2, width // dp_size, wide), bf16) for wide in wides] + [
        dma((8,)),
        pltpu.VMEM((2, length, width), bf16),
        pltpu.VMEM((2, length, width), bf16),
        pltpu.VMEM((2, length, width), bf16),
        pltpu.VMEM((2, 3, rows, width), bf16),
        dma((2, 3)),
        dma((2, 3)),
        dma((2, 3)),
        dma((2, 3)),
    ]
    if streams:
        out_shape = (
            [jax.ShapeDtypeStruct((2, slices, 2, width // dp_size, wide), bf16) for wide in wides]
            + [jax.ShapeDtypeStruct((2,) + gains.shape, f32)]
            + out_shape
            + [tokens(width), jax.ShapeDtypeStruct((rows, width), bf16)]
        )
        out_specs = [any_spec] * 4 + [vmem] + out_specs + [any_spec, vmem]
        scratch += [
            dma((8, slices - 1)),
            dma((8, slices - 1)),
            dma((8, slices)),
            dma((8, slices)),
            dma((8,)),
            dma((8,)),
            dma((8,)),
            dma((8,)),
            dma((8,)),
            dma,
            dma,
            dma((3,)),
            dma((3,)),
            dma,
        ]
    operands = [x, gains, tables, masks] + ([out_grad] if streams else [])
    return pl.pallas_call(
        functools.partial(forward_kernel, dp_size, layer),
        out_shape=out_shape,
        in_specs=[vmem] * len(operands) + [any_spec] * len(weights),
        out_specs=out_specs,
        scratch_shapes=scratch,
        compiler_params=pltpu.CompilerParams(
            collective_id=1 + layer, has_side_effects=True, vmem_limit_bytes=VMEM_LIMIT
        ),
        name="forward_layer",
    )(*operands, *weights)


class Refs:
    pass


GROUPS = 7


def backward_kernel(dp_size, layer, *refs):
    final_layer = layer == 0
    v = Refs()
    (v.grad_out, v.gains, v.tables, v.masks, v.x, v.middle, v.normed_in_t, v.query_rot, v.key_rot, v.value, v.unit,
     v.inverse, v.opened, v.slope_open, v.merged, v.normed_mid_t, v.act, v.slope, v.hidden,
     v.qkvs_all, v.out_all, v.gate_up_all, v.down_all, v.down_in, *refs) = refs
    if final_layer:
        v.later_chip, v.later_terms, v.first_rows, v.second_rows, *refs = refs
    v.grad_in, v.chip, v.core_land, *refs = refs
    if final_layer:
        v.x_land, v.final, v.gain_sums, v.taken_rows, v.taken_grads, *refs = refs
    else:
        v.terms, v.result, v.next_down, *refs = refs
    (v.big, v.out_t, v.query_v, v.key_v, v.value_v, v.wide_a, v.wide_b, v.wide_c, v.inverse_v, v.x_v, v.middle_v,
     v.normed_t, v.outer, v.grad_down, v.grad_gate_up, v.grad_branch, v.grad_qkvs, v.turned, v.parts, v.landed,
     v.grad_middle, v.stage_given, v.stage_own, v.core_part, v.load_sem, v.s_send, v.s_recv, v.g_send, v.g_recv,
     v.c_send, v.c_recv, v.local_sem, *refs) = refs
    if final_layer:
        (v.left, v.right, v.sums, v.r_sem, v.x_send, v.x_recv, v.z_send, v.z_recv, v.terms, v.held, v.hop_land,
         v.t_send, v.t_recv, v.row_send, v.row_recv) = refs
    else:
        v.parts_y, v.landed_y, v.d_send, v.d_recv, v.d_sem = refs
    at = Place(dp_size)
    rows, width = v.x.shape
    sq = Square(dp_size, rows)
    masks, tables, gains = v.masks, v.tables, v.gains
    query_v, key_v, value_v = v.query_v, v.key_v, v.value_v
    wide_a, wide_b, wide_c = v.wide_a, v.wide_b, v.wide_c
    grad_down, grad_gate_up, grad_branch, grad_qkvs = v.grad_down, v.grad_gate_up, v.grad_branch, v.grad_qkvs
    big, out_t, outer, parts, landed, terms = v.big, v.out_t, v.outer, v.parts, v.landed, v.terms
    wide_k = query_v.shape[-1]
    wide_v = value_v.shape[-1]
    wide_f = outer.shape[-1]
    heads = wide_k // HEAD_K
    slices = dp_size // 2
    slice_rows = width // dp_size
    gain_in = gains[layer, 0:1]
    gain_mid = gains[layer, 1:2]
    other = 1 - at.section
    steps = [(k, b) for k in range(at.groups) for b in range(2)]
    steps = steps[1:] + steps[:1]

    def load(index, source, target):
        copy = pltpu.make_async_copy(source, target, v.load_sem.at[index])
        copy.start()
        return copy

    def remote(src, dst, send, recv, device):
        return pltpu.make_async_remote_copy(
            src_ref=src, dst_ref=dst, send_sem=send, recv_sem=recv, device_id=device, device_id_type=MESH
        )

    def place(section=None, dp=None, tensor=None):
        return (
            at.section if section is None else section,
            at.dp if dp is None else dp,
            at.tensor if tensor is None else tensor,
        )

    sibling = place(dp=at.sibling())
    across = place(section=other)

    token_load = load(14, v.down_in, grad_down)
    down_load = load(0, v.down_all.at[layer], big.at[:, pl.ds(2 * wide_f, wide_f)])
    act_load = load(1, v.act, wide_a)
    slope_load = load(2, v.slope, wide_b)
    gate_load = load(3, v.gate_up_all.at[layer], big.at[:, pl.ds(0, 2 * wide_f)])
    hidden_load = load(4, v.hidden, outer)
    mid_load = load(5, v.normed_mid_t, v.normed_t)
    early = [
        load(6, v.middle, v.middle_v),
        load(7, v.x, v.x_v),
        load(8, v.out_all.at[layer], out_t),
        load(9, v.query_rot, query_v),
        load(10, v.key_rot, key_v),
        load(11, v.value, value_v),
        load(12, v.inverse, v.inverse_v),
        load(13, v.opened, wide_c),
    ]
    terms[...] = jnp.zeros_like(terms)

    partners = [sq.device(*step) for step in SQUARE] + [sibling]
    if final_layer:
        partners.append(across)
        partners += [place(dp=at.dp_at(k, b)) for k, b in steps[:-1] if (k, b) != (0, 1)]
    barrier = pltpu.get_barrier_semaphore()
    for partner in partners:
        pl.semaphore_signal(barrier, inc=1, device_id=partner, device_id_type=MESH)
    pl.semaphore_wait(barrier, len(partners))

    def x_copy(e, j, source):
        block = source.at[e, j]
        return remote(block, v.x_land.at[e, j], v.x_send.at[e, j], v.x_recv.at[e, j], across)

    def start_x(e, source):
        @pl.loop(0, slices)
        def _(j):
            x_copy(e, j, source).start()

    row_copies = []
    if final_layer:

        @pl.when(at.section == 0)
        def _():
            remote(v.second_rows, v.taken_rows, v.row_send.at[0], v.row_recv.at[0], across).start()

            @pl.loop(0, GROUPS)
            def _(e):
                start_x(e, v.later_chip)

            remote(v.grad_out, v.taken_grads, v.row_send.at[1], v.row_recv.at[1], across).start()

        @pl.when(at.section == 1)
        def _():
            remote(v.first_rows, v.taken_rows, v.row_send.at[0], v.row_recv.at[0], across).start()

    def through_down(s):
        tokens = grad_down[s]
        for start in range(0, wide_f, TILE):
            cols = slice(start, start + TILE)
            grad_hidden = mm(tokens, big[:, 2 * wide_f + start : 2 * wide_f + start + TILE])
            grad_gate_up[s, :, cols] = (grad_hidden * wide_b[s, :, cols].astype(f32)).astype(bf16)
            grad_gate_up[s, :, wide_f + start : wide_f + start + TILE] = (
                grad_hidden * wide_a[s, :, cols].astype(f32)
            ).astype(bf16)

    def give_back(s, source, weight, first, size, target):
        tokens = source[s]
        for start in range(0, width, TILE):
            target[s, :, start : start + TILE] = mm_nt(
                tokens, weight[start : start + TILE, first : first + size]
            ).astype(bf16)

    def collected(block, given, land):
        total = sq.chunk(given)[block].astype(f32)
        for j in range(len(SQUARE)):
            total = total + land[j, block].astype(f32)
        return total

    def exchange(source, weight, first, size, target, land, which):
        give_back(sq.next, source, weight, first, size, target)
        send, recv = v.g_send.at[which], v.g_recv.at[which]
        pushes = [sq.give(target, land, send, recv, j) for j in (1, 2)]
        give_back(sq.own, source, weight, first, size, target)
        pushes.append(sq.give(target, land, send, recv, 0))
        return pushes

    members = [
        (v.turned, outer, 0, wide_f),
        (v.normed_t, grad_gate_up, 0, wide_f),
        (v.normed_t, grad_gate_up, wide_f, wide_f),
        (v.turned, outer, 0, wide_v),
        (v.normed_t, grad_qkvs, 0, 2 * wide_k),
        (v.normed_t, grad_qkvs, 2 * wide_k, wide_v),
        (v.normed_t, grad_qkvs, 2 * wide_k + wide_v, wide_v),
    ]
    given_copies, own_copies, fetches = {}, {}, {}

    def product(e, dp):
        left, right, first, size = members[e]
        start = pl.multiple_of(dp * slice_rows, slice_rows)
        wide = right[:, :, first : first + size].reshape(-1, size)
        return mm(left[pl.ds(start, slice_rows), :], wide)

    def given(e):
        if e >= 2:
            given_copies[e - 2].wait_send()
        stage = v.stage_given.at[e % 2]

        @pl.loop(0, slices)
        def _(j):
            stage[j] = product(e, j * 2 + 1 - at.core).astype(bf16)

        given_copies[e] = remote(stage, v.core_land.at[e], v.c_send.at[e], v.c_recv.at[e], sibling)
        given_copies[e].start()

    def fetch(e):
        given_copies[e].wait_recv()
        fetches[e] = pltpu.make_async_copy(v.core_land.at[e], v.core_part, v.local_sem.at[0])
        fetches[e].start()

    def settle(e):
        if e in settled:
            return
        settled.append(e)
        own_copies[e].wait()
        if final_layer:

            @pl.when(at.section == 1)
            def _():
                start_x(e, v.chip)

    def own(e):
        if e >= 1:
            settle(e - 1)
        fetches[e].wait()

        @pl.loop(0, slices)
        def _(j):
            v.stage_own[j] = (product(e, j * 2 + at.core) + v.core_part[j].astype(f32)).astype(bf16)

        own_copies[e] = pltpu.make_async_copy(v.stage_own, v.chip.at[e], v.local_sem.at[1])
        own_copies[e].start()

    settled = []

    def index(k, b):
        return ((at.group + k) % at.groups) * 2 + (at.low + b) % 2

    def piece(e, k):
        start = pl.multiple_of(at.low * wide_f, wide_f)
        return v.final.at[e, k, :, pl.ds(start, wide_f)]

    def z_copy(e, j):
        k, b = steps[j]
        return remote(v.sums.at[j], piece(e, k), v.z_send.at[e, j], v.z_recv.at[e, j], place(dp=at.dp_at(k, b)))

    def home_copy(e):
        return pltpu.make_async_copy(v.sums.at[slices - 1], piece(e, 0), v.r_sem.at[2, 0])

    def reduce_slices(e, source, first, stop, wait_previous):
        def loads(j):
            here = index(*steps[j])
            return (
                pltpu.make_async_copy(source.at[e, here], v.left.at[j % 2], v.r_sem.at[0, j % 2]),
                pltpu.make_async_copy(v.x_land.at[e, here], v.right.at[j % 2], v.r_sem.at[1, j % 2]),
            )

        def begin(j):
            x_copy(e, index(*steps[j]), source).wait_recv()
            for copy in loads(j):
                copy.start()

        begin(first)
        for j in range(first, stop):
            if j + 1 < stop:
                begin(j + 1)
            for copy in loads(j):
                copy.wait()

            @pl.when(wait_previous)
            def _():
                if j == slices - 1:
                    home_copy(e).wait()
                else:
                    z_copy(e - 1, j).wait_send()

            v.sums[j] = (v.left[j % 2].astype(f32) + v.right[j % 2].astype(f32)).astype(bf16)
            if j == slices - 1:
                home_copy(e).start()
            else:
                z_copy(e, j).start()

    reduced = [0, 0]

    def sources(section):
        return v.later_chip if section == 1 else v.chip

    def reduce_some(section, count):
        if not final_layer:
            return

        @pl.when(at.section == section)
        def _():
            done = reduced[section]
            while done < reduced[section] + count:
                e, first = divmod(done, slices)
                stop = min(slices, first + reduced[section] + count - done)
                reduce_slices(e, sources(section), first, stop, e > 0)
                done += stop - first

        reduced[section] += count

    def reduce_rest(section):
        @pl.when(at.section == section)
        def _():
            e, first = divmod(reduced[section], slices)
            if first > 0:
                reduce_slices(e, sources(section), first, slices, e > 0)
                e += 1

            @pl.loop(e, GROUPS)
            def _(e):
                reduce_slices(e, sources(section), 0, slices, e > 0)

    token_load.wait()
    if final_layer:
        hidden_load.wait()
        transpose_into(v.turned, grad_down)
        given(0)
    down_load.wait()
    act_load.wait()
    slope_load.wait()
    through_down(sq.next)
    through_down(sq.own)
    unit_load = load(1, v.unit, wide_a)
    bend_load = load(2, v.slope_open, wide_b)
    gate_load.wait()
    gives = exchange(grad_gate_up, big, 0, 2 * wide_f, parts, landed, 0)
    if not final_layer:
        hidden_load.wait()
        transpose_into(v.turned, grad_down)
        given(0)
        for s in (sq.next, sq.own):
            give_back(s, outer, big, 2 * wide_f, wide_f, v.parts_y)
    fetch(0)
    own(0)
    mid_load.wait()
    settle(0)
    given(1)
    qkvs_load = load(3, v.qkvs_all.at[layer], big)
    merged_load = load(4, v.merged, outer)
    for copy in early:
        copy.wait()
    for push in gives:
        push.wait_recv()

    def through_mid(block):
        upstream = collected(block, parts, landed)
        normed, scale = norm_parts(v.middle_v[block])
        grad_rows = v.grad_out[block].astype(f32) + norm_grad(normed, scale, upstream, gain_mid)
        v.grad_middle[block] = grad_rows
        sq.chunk(grad_branch)[block] = grad_rows.astype(bf16)
        terms[1:2] = terms[1:2] + jnp.sum(upstream * normed, axis=0, keepdims=True)

    row_blocks(rows, through_mid)
    mids = sq.spread(grad_branch, v.s_send, v.s_recv)
    reduce_some(0, 1)
    given(2)
    fetch(1)
    own(1)
    unit_load.wait()
    bend_load.wait()
    settle(1)
    reduce_some(1, slices)
    reduce_some(0, 1)

    def through_heads(s):
        tokens = grad_branch[s]
        for head in range(heads):
            cols_k = slice(head * HEAD_K, (head + 1) * HEAD_K)
            cols_v = slice(head * HEAD_V, (head + 1) * HEAD_V)
            grad_merged = mm(tokens, out_t[:, cols_v])
            unit_rows = wide_a[s, :, cols_v].astype(f32)
            first = 2 * wide_k + wide_v + head * HEAD_V
            grad_qkvs[s, :, first : first + HEAD_V] = (
                grad_merged * unit_rows * wide_b[s, :, cols_v].astype(f32)
            ).astype(bf16)
            grad_unit = grad_merged * wide_c[s, :, cols_v].astype(f32)
            grad_mixed = (
                v.inverse_v[s, head]
                * (
                    grad_unit
                    - jnp.mean(grad_unit, axis=-1, keepdims=True)
                    - unit_rows * jnp.mean(grad_unit * unit_rows, axis=-1, keepdims=True)
                )
            ).astype(bf16)
            query, key, val = query_v[s, :, cols_k], key_v[s, :, cols_k], value_v[s, :, cols_v]
            mask = masks[s, head]
            weight = (mm_nt(query, key) * mask).astype(bf16)
            grad_product = (mm_nt(grad_mixed, val) * mask).astype(bf16)
            first = 2 * wide_k + head * HEAD_V
            grad_qkvs[s, :, first : first + HEAD_V] = mm_tn(weight, grad_mixed).astype(bf16)
            grad_qkvs[s, :, cols_k] = turn_back(mm(grad_product, key), tables[0], tables[1], tables[2]).astype(bf16)
            first = wide_k + head * HEAD_K
            grad_qkvs[s, :, first : first + HEAD_K] = turn_back(
                mm_tn(grad_product, query), tables[0], tables[1], tables[3]
            ).astype(bf16)

    mids[0].wait_recv()
    through_heads(sq.own)
    mids[1].wait_recv()
    mids[2].wait_recv()
    if not final_layer:
        gives_y = [sq.give(v.parts_y, v.landed_y, v.g_send.at[2], v.g_recv.at[2], j) for j in range(3)]
    through_heads(sq.next)
    qkvs_load.wait()
    reduce_some(0, 1)
    for push in gives:
        push.wait_send()
    ends = exchange(grad_qkvs, big, 0, grad_qkvs.shape[-1], parts, landed, 1)
    fetch(2)
    own(2)
    in_load = load(5, v.normed_in_t, v.normed_t)
    transpose_into(v.turned, grad_branch)
    settle(2)
    merged_load.wait()
    given(3)
    in_load.wait()
    given(4)
    fetch(3)
    own(3)
    reduce_some(1, slices)
    reduce_some(0, 1)
    settle(3)
    for push in ends:
        push.wait_recv()

    def through_in(block):
        upstream = collected(block, parts, landed)
        normed, scale = norm_parts(v.x_v[block].astype(f32))
        v.grad_in[block] = (v.grad_middle[block] + norm_grad(normed, scale, upstream, gain_in)).astype(bf16)
        terms[0:1] = terms[0:1] + jnp.sum(upstream * normed, axis=0, keepdims=True)

    row_blocks(rows, through_in)
    if final_layer:

        @pl.when(at.section == 1)
        def _():
            remote(v.grad_in, v.taken_grads, v.row_send.at[1], v.row_recv.at[1], across).start()

    else:
        downs = sq.spread_from(v.grad_in, v.next_down, v.d_send, v.d_recv, v.d_sem)

    reduce_some(0, 1)
    given(5)
    fetch(4)
    own(4)
    reduce_some(0, 1)
    given(6)
    settle(4)
    reduce_some(1, slices)
    reduce_some(0, 1)
    fetch(5)
    own(5)
    reduce_some(0, 1)
    if not final_layer:
        for push in gives_y:
            push.wait_recv()

        def last(block):
            v.result[block] = (
                v.middle_v[block] + collected(block, v.parts_y, v.landed_y)
            ).astype(bf16)

        row_blocks(rows, last)
    fetch(6)
    own(6)
    settle(6)
    for push in mids + ends:
        push.wait_send()
    for e in (5, 6):
        given_copies[e].wait_send()
    if not final_layer:
        for push in gives_y:
            push.wait_send()
        for push in downs:
            push.wait()
        return

    reduce_rest(1)
    reduce_rest(0)

    held, hop_land, mine = v.held, v.hop_land, v.held.at[at.section]
    held[0] = terms[...]
    held[1] = v.later_terms[...]
    hop = remote(held, hop_land.at[0], v.t_send.at[0], v.t_recv.at[0], sibling)
    hop.start()
    hop.wait()
    held[...] = held[...] + hop_land[0]
    hop = remote(held.at[other], hop_land.at[1, other], v.t_send.at[1], v.t_recv.at[1], across)
    hop.start()
    hop.wait_send()
    remote(held.at[other], hop_land.at[1, at.section], v.t_send.at[1], v.t_recv.at[1], across).wait_recv()
    mine[...] = mine[...] + hop_land[1, at.section]
    for h, device in ((2, place(tensor=1 - at.tensor)), (3, place(dp=at.dp_at(0, 1)))):
        hop = remote(mine, hop_land.at[h, 0], v.t_send.at[h], v.t_recv.at[h], device)
        hop.start()
        hop.wait()
        mine[...] = mine[...] + hop_land[h, 0]
    hops = []
    for k in range(1, at.groups):
        hop = remote(mine, hop_land.at[3 + k, 0], v.t_send.at[3 + k], v.t_recv.at[3 + k], place(dp=at.dp_at(k, 0)))
        hop.start()
        hops.append(hop)
    total = mine[...]
    for k, hop in zip(range(1, at.groups), hops):
        hop.wait()
        total = total + hop_land[3 + k, 0]
    v.gain_sums[...] = total

    for which, rows_sent in ((0, v.second_rows), (1, v.grad_in)):
        target = v.taken_rows if which == 0 else v.taken_grads
        copy = remote(rows_sent, target, v.row_send.at[which], v.row_recv.at[which], across)
        copy.wait_recv()
        copy.wait_send()

    home_copy(0).wait()
    for j in range(slices - 1):
        z_copy(GROUPS - 1, j).wait_send()

        @pl.loop(0, GROUPS)
        def _(e):
            z_copy(e, j).wait_recv()

    @pl.loop(0, GROUPS)
    def _(e):
        @pl.loop(0, slices)
        def _(j):
            x_copy(e, j, v.chip).wait_send()


def backward_layer(layer, grad_out, down, x, gains, tables, masks, saved, gathered, dp_size, later=None, rows_out=None):
    rows, width = x.shape
    length = masks.shape[-1]
    (middle, normed_in_t, query_rot, key_rot, value, unit, inverse, opened, slope_open, merged, normed_mid_t, act, slope,
     hidden) = saved
    vmem = pl.BlockSpec(memory_space=pltpu.VMEM)
    any_spec = pl.BlockSpec(memory_space=pl.ANY)
    final_layer = layer == 0
    slices = dp_size // 2
    slice_rows = width // dp_size
    size = hidden.shape[-1]
    assert value.shape[-1] == size and 2 * query_rot.shape[-1] == size
    block = (slices, slice_rows, size)

    def held(*shape, kind=bf16):
        return pltpu.VMEM(shape, kind)

    def stored(*shape, kind=bf16):
        return jax.ShapeDtypeStruct(shape, kind)

    dma = pltpu.SemaphoreType.DMA
    operands = [grad_out, gains, tables, masks]
    operands += [x, middle, normed_in_t, query_rot, key_rot, value, unit, inverse, opened, slope_open, merged, normed_mid_t,
                 act, slope, hidden]
    operands += [*gathered, down]
    in_specs = [vmem] * 4 + [any_spec] * (len(operands) - 4)
    out_shape = [stored(rows, width), stored(GROUPS, *block), stored(GROUPS, *block)]
    out_specs = [vmem, any_spec, any_spec]
    if final_layer:
        later_chip, later_terms = later
        operands += [later_chip, later_terms, *rows_out]
        in_specs += [any_spec, vmem, any_spec, any_spec]
        out_shape += [stored(GROUPS, *block), stored(GROUPS, dp_size // 4, slice_rows, 2 * size), stored(2, width, kind=f32),
                      stored(rows, width), stored(rows, width)]
        out_specs += [any_spec, any_spec, vmem, any_spec, any_spec]
    else:
        out_shape += [stored(2, width, kind=f32), stored(rows, width), stored(2, length, width)]
        out_specs += [vmem, vmem, any_spec]
    scratch = [
        held(width, 3 * size),
        held(width, size),
        held(*query_rot.shape),
        held(*key_rot.shape),
        held(*value.shape),
        held(2, length, size),
        held(2, length, size),
        held(2, length, size),
        held(*inverse.shape, kind=f32),
        held(rows, width),
        held(rows, width, kind=f32),
        held(width, 2 * length),
        held(2, length, size),
        held(2, length, width),
        held(2, length, 2 * size),
        held(2, length, width),
        held(2, length, 3 * size),
        held(width, 2 * length),
        held(2, length, width),
        held(3, rows, width),
        held(rows, width, kind=f32),
        held(2, *block),
        held(*block),
        held(*block),
        dma((15,)),
        dma((3,)),
        dma((3,)),
        dma((3, 3)),
        dma((3, 3)),
        dma((GROUPS,)),
        dma((GROUPS,)),
        dma((2,)),
    ]
    if final_layer:
        hops = 3 + dp_size // 4
        scratch += [
            held(2, slice_rows, size),
            held(2, slice_rows, size),
            held(*block),
            dma((3, 2)),
            dma((GROUPS, slices)),
            dma((GROUPS, slices)),
            dma((GROUPS, slices - 1)),
            dma((GROUPS, slices - 1)),
            held(2, width, kind=f32),
            held(2, 2, width, kind=f32),
            held(hops, 2, 2, width, kind=f32),
            dma((hops,)),
            dma((hops,)),
            dma((2,)),
            dma((2,)),
        ]
    else:
        scratch += [held(2, length, width), held(3, rows, width), dma((3,)), dma((3,)), dma]
    return pl.pallas_call(
        functools.partial(backward_kernel, dp_size, layer),
        out_shape=out_shape,
        in_specs=in_specs,
        out_specs=out_specs,
        scratch_shapes=scratch,
        compiler_params=pltpu.CompilerParams(
            collective_id=4 + layer, has_side_effects=True, vmem_limit_bytes=VMEM_LIMIT
        ),
        name="backward_layer",
    )(*operands)


def nested(outs):
    return (*outs[:5], outs[5:-2], *outs[-2:])


def on_device(
    dp_size,
    layer_input,
    segment_ids,
    output_grad,
    query_weight,
    key_weight,
    value_weight,
    swish_weight,
    output_weight,
    gate_weight,
    up_weight,
    down_weight,
    mixer_gain,
    ffn_gain,
):
    at = Place(dp_size)
    section_first = at.section == 0
    rows_here, width = layer_input.shape[1:]
    length = segment_ids.shape[1]
    score_scale = HEAD_K ** (-0.5)

    quarter_k = query_weight.shape[2] // 2
    quarter_v = value_weight.shape[2] // 2
    quarter_f = gate_weight.shape[2] // 2
    heads_here = quarter_k // HEAD_K
    first_head = (at.tensor * 2 + at.low) * heads_here
    cosine, sine, growth = rotation_tables(length, HEAD_K // 2)

    ids_mine = lax.dynamic_index_in_dim(segment_ids, at.section, 0, keepdims=False)
    ids_pair = lax.ppermute(ids_mine, "dp", [(i, i ^ 2) for i in range(dp_size)])
    ids = jnp.where(at.low == 0, jnp.stack([ids_mine, ids_pair]), jnp.stack([ids_pair, ids_mine]))
    masks = decay_mask(ids, first_head, heads_here) * score_scale
    tables = jnp.stack([cosine, sine, growth, 1.0 / growth])

    first_in = lax.dynamic_index_in_dim(layer_input, at.section, 0, keepdims=False)
    out_grad = lax.dynamic_index_in_dim(output_grad, at.section, 0, keepdims=False)
    shards = (query_weight[0], key_weight[0], value_weight[0], swish_weight[0], output_weight[0].T, gate_weight[0],
              up_weight[0], down_weight[0].T)
    own_gains = jnp.concatenate([mixer_gain, ffn_gain], axis=0)
    *gathered, all_gains, first_saved, second_down, first_sent = nested(
        forward_layer(0, first_in, own_gains, tables, masks, shards, dp_size, out_grad)
    )
    second_saved = forward_layer(1, first_sent, all_gains, tables, masks, gathered, dp_size)
    gathered = [g.reshape(2, width, g.shape[-1]) for g in gathered]
    second_grad, later_chip, _, later_terms, second_sent, first_down = backward_layer(
        1, out_grad, second_down, first_sent, all_gains, tables, masks, second_saved, gathered, dp_size
    )
    first_grad, _, _, _, landed, my_gains, taken_rows, taken_grads = backward_layer(
        0, second_grad, first_down, first_in, all_gains, tables, masks, first_saved, gathered, dp_size,
        (later_chip, later_terms), (first_sent, second_sent),
    )

    def by_layer(first, second, taken):
        return jnp.where(section_first, jnp.stack([first, taken]), jnp.stack([taken, second]))[None]

    def shard(e):
        return jnp.sum(landed[e].astype(f32), axis=0)

    def columns(e, start, size):
        step = landed.shape[-1] // 2
        part = jnp.concatenate([landed[e, :, :, p * step + start : p * step + start + size] for p in range(2)], axis=-1)
        return jnp.sum(part.astype(f32), axis=0)

    return (
        by_layer(first_sent, second_sent, taken_rows),
        by_layer(first_grad, second_grad, taken_grads),
        columns(4, 0, quarter_k)[None],
        columns(4, quarter_k, quarter_k)[None],
        shard(5)[None],
        shard(6)[None],
        shard(3).T[None],
        shard(1)[None],
        shard(2)[None],
        shard(0).T[None],
        my_gains[0][None],
        my_gains[1][None],
    )


def solution(mesh):
    in_specs = (
        P(None, ("dp", "tensor"), None),
        P(None, "dp"),
        P(None, ("dp", "tensor"), None),
        P("section", "dp", "tensor"),
        P("section", "dp", "tensor"),
        P("section", "dp", "tensor"),
        P("section", "dp", "tensor"),
        P("section", "tensor", "dp"),
        P("section", "dp", "tensor"),
        P("section", "dp", "tensor"),
        P("section", "tensor", "dp"),
        P("section", None),
        P("section", None),
    )
    out_specs = (
        P("section", None, ("dp", "tensor"), None),
        P("section", None, ("dp", "tensor"), None),
        P("section", "dp", "tensor"),
        P("section", "dp", "tensor"),
        P("section", "dp", "tensor"),
        P("section", "dp", "tensor"),
        P("section", "tensor", "dp"),
        P("section", "dp", "tensor"),
        P("section", "dp", "tensor"),
        P("section", "tensor", "dp"),
        P("section", None),
        P("section", None),
    )
    return jax.shard_map(
        functools.partial(on_device, mesh.shape["dp"]),
        mesh=mesh,
        in_specs=in_specs,
        out_specs=out_specs,
        check_vma=False,
    )
```

```python
import functools

import jax
import jax.numpy as jnp
from jax import lax
from jax.experimental import pallas as pl
from jax.experimental.pallas import tpu as pltpu
from jax.sharding import PartitionSpec as P

HEAD_K = 256
HEAD_V = 512
MESH = pl.DeviceIdType.MESH

epsilon = 1e-05
group_guard = 1.0
bf16 = jnp.bfloat16
f32 = jnp.float32


def rotation_tables(length, half_width):
    pair_index = jnp.arange(half_width).astype(f32)
    position = jnp.arange(length).astype(f32)[:, None]
    angle = position * jnp.exp(-jnp.log(10000.0) * pair_index / half_width)
    zeta = (pair_index / half_width + 0.4) / 1.4
    growth = jnp.exp(position / 512.0 * jnp.log(zeta))
    return (jnp.cos(angle), jnp.sin(angle), growth)


def decay_mask(segments, first_head, heads):
    length = segments.shape[-1]
    position = jnp.arange(length)
    earlier = position[:, None] >= position[None, :]
    same_doc = (segments[:, :, None] == segments[:, None, :]) & earlier[None]
    distance = jnp.maximum(position[:, None] - position[None, :], 0).astype(f32)
    head_index = (first_head + jnp.arange(heads)).astype(f32)
    log_rate = jnp.log(1.0 - jnp.exp2(-5.0 - head_index))
    decay = jnp.exp(log_rate[:, None, None] * distance[None])
    return jnp.where(same_doc[:, None], decay[None], 0.0)


class Place:
    def __init__(self, dp_size):
        self.groups = dp_size // 4
        self.section = lax.axis_index("section")
        self.dp = lax.axis_index("dp")
        self.tensor = lax.axis_index("tensor")
        self.core = self.dp % 2
        self.low = (self.dp // 2) % 2
        self.group = self.dp // 4

    def dp_at(self, group_step, low_step):
        group = (self.group + group_step + self.groups) % self.groups
        return (group * 2 + (self.low + low_step) % 2) * 2 + self.core

    def sibling(self):
        return self.dp + 1 - 2 * self.core


SQUARE = ((0, 1), (1, 0), (1, 1))
TILE = 512
VMEM_LIMIT = 63 * 1024 * 1024


def mm(left, right):
    return lax.dot_general(left, right, (((1,), (0,)), ((), ())), preferred_element_type=f32)


def mm_nt(left, right):
    return lax.dot_general(left, right, (((1,), (1,)), ((), ())), preferred_element_type=f32)


def mm_tn(left, right):
    return lax.dot_general(left, right, (((0,), (0,)), ((), ())), preferred_element_type=f32)


class Square:
    def __init__(self, dp_size, rows):
        self.at = Place(dp_size)
        self.rows = rows
        self.own = self.at.low
        self.next = 1 - self.at.low

    def device(self, low_step, tensor_step):
        return (self.at.section, self.at.dp_at(0, low_step), (self.at.tensor + tensor_step) % 2)

    def barrier(self):
        barrier = pltpu.get_barrier_semaphore()
        for step in SQUARE:
            pl.semaphore_signal(barrier, inc=1, device_id=self.device(*step), device_id_type=MESH)
        pl.semaphore_wait(barrier, len(SQUARE))

    def chunk(self, ref, low_step=0, tensor_step=0):
        start = pl.multiple_of((self.at.tensor + tensor_step) % 2 * self.rows, self.rows)
        return ref.at[(self.at.low + low_step) % 2, pl.ds(start, self.rows)]

    def copy(self, src, dst, send, recv, step):
        return pltpu.make_async_remote_copy(
            src_ref=src,
            dst_ref=dst,
            send_sem=send,
            recv_sem=recv,
            device_id=self.device(*step),
            device_id_type=MESH,
        )

    def spread(self, ref, send, recv):
        pushes = []
        for j, step in enumerate(SQUARE):
            push = self.copy(self.chunk(ref), self.chunk(ref), send.at[j], recv.at[j], step)
            push.start()
            pushes.append(push)
        return pushes

    def spread_from(self, own, ref, send, recv, here):
        local = pltpu.make_async_copy(own, self.chunk(ref), here)
        local.start()
        pushes = [local]
        for j, step in enumerate(SQUARE):
            push = self.copy(own, self.chunk(ref), send.at[j], recv.at[j], step)
            push.start()
            pushes.append(push)
        return pushes

    def give(self, parts, landed, send, recv, j):
        push = self.copy(self.chunk(parts, *SQUARE[j]), landed.at[j], send.at[j], recv.at[j], SQUARE[j])
        push.start()
        return push


def row_blocks(rows, body, block=32):
    block = min(block, rows)

    @pl.loop(0, rows // block)
    def _(i):
        body(pl.ds(pl.multiple_of(i * block, block), block))


def norm_parts(values):
    centred = values - jnp.mean(values, axis=-1, keepdims=True)
    scale = lax.rsqrt(jnp.mean(centred * centred, axis=-1, keepdims=True) + epsilon)
    return centred * scale, scale


def norm_grad(normed, scale, upstream, gain):
    through = upstream * gain
    return scale * (
        through
        - jnp.mean(through, axis=-1, keepdims=True)
        - normed * jnp.mean(through * normed, axis=-1, keepdims=True)
    )


def turn(values, cosine, sine, scale):
    half = values.shape[-1] // 2
    a, b = values[:, :half], values[:, half:]
    return jnp.concatenate([(a * cosine - b * sine) * scale, (a * sine + b * cosine) * scale], axis=-1)


def turn_back(values, cosine, sine, scale):
    half = values.shape[-1] // 2
    a, b = values[:, :half] * scale, values[:, half:] * scale
    return jnp.concatenate([a * cosine + b * sine, b * cosine - a * sine], axis=-1)


def transpose_into(target, source):
    _, length, width = source.shape
    for s in range(2):
        for start in range(0, width, TILE):
            target[start : start + TILE, s * length : (s + 1) * length] = source[s, :, start : start + TILE].T


def forward_kernel(dp_size, layer, *refs):
    streams = layer == 0
    v = Refs()
    if streams:
        (v.x, v.own_gains, v.tables, v.masks, v.out_grad, *refs) = refs
        shards, refs = refs[:8], refs[8:]
        stored, refs = refs[:4], refs[4:]
        (v.gains, *refs) = refs
    else:
        (v.x, v.gains, v.tables, v.masks, *refs) = refs
        stored, refs = refs[:4], refs[4:]
    (middle, normed_in_t, query_rot, key_rot, value, unit, inverse, opened, slope_open, merged, normed_mid_t, act, slope,
     hidden, *refs) = refs
    if streams:
        (v.grad_down, result, *refs) = refs
    held, refs = refs[:4], refs[4:]
    (w_sem, normed_in, normed_mid, parts, landed, s_send, s_recv, g_send, g_recv, *refs) = refs
    x, tables, masks = v.x, v.tables, v.masks
    rows, width = x.shape
    sq = Square(dp_size, rows)
    at = sq.at
    qkvs, out_t, gate_up, down_t = held
    wide_k = query_rot.shape[-1]
    wide_v = value.shape[-1]
    wide_f = hidden.shape[-1]
    heads = wide_k // HEAD_K
    slices = dp_size // 2
    other = 1 - at.section
    groups = [(0, 0, wide_k), (0, wide_k, wide_k), (0, 2 * wide_k, wide_v), (0, 2 * wide_k + wide_v, wide_v),
              (1, 0, wide_v), (2, 0, wide_f), (2, wide_f, wide_f), (3, 0, wide_f)]
    loads = {}

    def load(i):
        which, first, size = groups[i]
        columns = pl.ds(first, size)
        loads[i] = pltpu.make_async_copy(
            stored[which].at[layer, :, :, :, columns], held[which].at[:, :, :, columns], w_sem.at[i]
        )
        loads[i].start()

    def weight(which, first, size):
        return held[which][:, :, :, first : first + size].reshape(width, size)

    def first_norm(block):
        unit_rows, _ = norm_parts(x[block].astype(f32))
        sq.chunk(normed_in)[block] = (unit_rows * v.gains[layer, 0:1]).astype(bf16)

    def project(i, s):
        loads_wait(i)
        first, size = groups[i][1:]
        tokens = normed_in[s]
        for start in range(0, size, TILE):
            wide = mm(tokens, weight(0, first + start, TILE))
            cols = slice(start, start + TILE)
            if i < 2:
                dest = (query_rot, key_rot)[i]
                for head in range(TILE // HEAD_K):
                    part = wide[:, head * HEAD_K : (head + 1) * HEAD_K]
                    dest[s, :, start + head * HEAD_K : start + (head + 1) * HEAD_K] = turn(
                        part, tables[0], tables[1], tables[2 + i]
                    ).astype(bf16)
            elif i == 2:
                value[s, :, cols] = wide.astype(bf16)
            else:
                sigmoid = 1.0 / (1.0 + jnp.exp(-wide))
                opened[s, :, cols] = (wide * sigmoid).astype(bf16)
                slope_open[s, :, cols] = (sigmoid * (1.0 + wide * (1.0 - sigmoid))).astype(bf16)

    waited = []

    def loads_wait(i):
        if i not in waited:
            waited.append(i)
            loads[i].wait()

    def retain(s):
        for head in range(heads):
            cols_k = slice(head * HEAD_K, (head + 1) * HEAD_K)
            cols_v = slice(head * HEAD_V, (head + 1) * HEAD_V)
            product = mm_nt(query_rot[s, :, cols_k], key_rot[s, :, cols_k])
            weights = (product * masks[s, head]).astype(bf16)
            mixed = mm(weights, value[s, :, cols_v])
            centred = mixed - jnp.mean(mixed, axis=-1, keepdims=True)
            scale = lax.rsqrt(jnp.mean(centred * centred, axis=-1, keepdims=True) + group_guard)
            unit_rows = centred * scale
            inverse[s, head] = scale
            unit[s, :, cols_v] = unit_rows.astype(bf16)
            merged[s, :, cols_v] = (unit_rows * opened[s, :, cols_v].astype(f32)).astype(bf16)

    def give_back(s, source, weight_t):
        tokens = source[s]
        step = width // slices
        for i in range(slices):
            parts[s, :, i * step : (i + 1) * step] = mm_nt(tokens, weight_t[i].reshape(step, -1)).astype(bf16)

    def collected(block, which):
        total = sq.chunk(parts)[block].astype(f32)
        for j in range(len(SQUARE)):
            total = total + landed[which, j, block].astype(f32)
        return total

    def give(s, which):
        send, recv = g_send.at[which], g_recv.at[which]
        return [sq.give(parts, landed.at[which], send, recv, j) for j in ((1, 2) if s == 1 else (0,))]

    def second_norm(block):
        middle_rows = x[block].astype(f32) + collected(block, 0)
        middle[block] = middle_rows
        unit_rows, _ = norm_parts(middle_rows)
        sq.chunk(normed_mid)[block] = (unit_rows * v.gains[layer, 1:2]).astype(bf16)

    def feed(s):
        loads_wait(5)
        loads_wait(6)
        tokens = normed_mid[s]
        for start in range(0, wide_f, TILE):
            cols = slice(start, start + TILE)
            gate = mm(tokens, weight(2, start, TILE))
            up = mm(tokens, weight(2, wide_f + start, TILE))
            square = gate * gate
            bend = jnp.tanh(0.7978845608028654 * gate * (1.0 + 0.044715 * square))
            half = 0.5 * (1.0 + bend)
            gelu = gate * half
            slope_gelu = half + 0.5 * gate * (1.0 - bend * bend) * (
                0.7978845608028654 * (1.0 + 3 * 0.044715 * square)
            )
            act[s, :, cols] = gelu.astype(bf16)
            slope[s, :, cols] = (slope_gelu * up).astype(bf16)
            hidden[s, :, cols] = (gelu * up).astype(bf16)

    def turn_if(condition, target, source):
        @pl.when(condition)
        def _():
            transpose_into(target, source)

    if not streams:
        for i in range(7):
            load(i)
        row_blocks(rows, first_norm)
        sq.barrier()
        ins = sq.spread(normed_in, s_send.at[0], s_recv.at[0])
        ins[0].wait_recv()
        for i in range(4):
            project(i, sq.own)
        ins[1].wait_recv()
        ins[2].wait_recv()
        turn_if(at.core == at.section, normed_in_t, normed_in)
        for i in range(4):
            project(i, sq.next)
        retain(sq.next)
        loads_wait(4)
        give_back(sq.next, merged, out_t)
        gives = give(1, 0)
        retain(sq.own)
        give_back(sq.own, merged, out_t)
        gives += give(0, 0)
        turn_if(at.core != at.section, normed_in_t, normed_in)
        for push in gives:
            push.wait_recv()
        row_blocks(rows, second_norm)
        mids = sq.spread(normed_mid, s_send.at[1], s_recv.at[1])
        mids[0].wait_recv()
        feed(sq.own)
        mids[1].wait_recv()
        mids[2].wait_recv()
        feed(sq.next)
        transpose_into(normed_mid_t, normed_mid)
        for push in ins + mids + gives:
            push.wait_send()
        return

    (z_send, z_recv, x_send, x_recv, c_send, c_recv, o_send, o_recv, here_sem, gain_send, gain_recv, d_send, d_recv,
     d_sem) = refs
    steps = [(k, b) for k in range(at.groups) for b in range(2)][1:]

    def place(section=None, dp=None):
        return (at.section if section is None else section, at.dp if dp is None else dp, at.tensor)

    def copy(src, dst, send, recv, device):
        return pltpu.make_async_remote_copy(
            src_ref=src, dst_ref=dst, send_sem=send, recv_sem=recv, device_id=device, device_id_type=MESH
        )

    partners = [sq.device(*step) for step in SQUARE] + [place(dp=at.sibling()), place(section=other)]
    partners += [place(dp=at.dp_at(k, b)) for k, b in steps if (k, b) != (0, 1)]
    barrier = pltpu.get_barrier_semaphore()
    for partner in partners:
        pl.semaphore_signal(barrier, inc=1, device_id=partner, device_id_type=MESH)
    pl.semaphore_wait(barrier, len(partners))

    gain_copy = copy(v.own_gains, v.gains.at[at.section], gain_send, gain_recv, place(section=other))
    gain_copy.start()
    v.gains[at.section] = v.own_gains[...]

    def slot(i, section, dp):
        which, first, size = groups[i]
        return stored[which].at[section, dp // 2, dp % 2, :, pl.ds(first, size)]

    def block(i, section, core):
        which, first, size = groups[i]
        return stored[which].at[section, :, core, :, pl.ds(first, size)]

    def part(i, b):
        size = groups[i][2]
        return shards[i].at[:, pl.ds(pl.multiple_of((at.low + b) % 2 * size, size), size)]

    z_copies, x_copies, here, core_own, core_other = {}, {}, {}, {}, {}

    def push_own(i):
        mine = slot(i, at.section, at.dp)
        for j, (k, b) in enumerate(steps):
            z_copies[i, j] = copy(part(i, b), mine, z_send.at[i, j], z_recv.at[i, j], place(dp=at.dp_at(k, b)))
            z_copies[i, j].start()
        x_copies[i, 0] = copy(part(i, 0), mine, x_send.at[i, 0], x_recv.at[i, 0], place(section=other))
        x_copies[i, 0].start()
        here[i] = pltpu.make_async_copy(part(i, 0), mine, here_sem.at[i])
        here[i].start()

    def pass_on(i):
        for j, (k, b) in enumerate(steps):
            z_copies[i, j].wait_recv()
            arrived = slot(i, at.section, at.dp_at(-k, b))
            x_copies[i, j + 1] = copy(arrived, arrived, x_send.at[i, j + 1], x_recv.at[i, j + 1], place(section=other))
            x_copies[i, j + 1].start()
        here[i].wait()
        mine = block(i, at.section, at.core)
        core_own[i] = copy(mine, mine, c_send.at[i], c_recv.at[i], place(dp=at.sibling()))
        core_own[i].start()

    def share_other(i):
        for j in range(slices):
            x_copies[i, j].wait_recv()
        theirs = block(i, other, at.core)
        core_other[i] = copy(theirs, theirs, o_send.at[i], o_recv.at[i], place(dp=at.sibling()))
        core_other[i].start()

    def arrive(i):
        @pl.when(at.section == 0)
        def _():
            core_own[i].wait_recv()

        @pl.when(at.section == 1)
        def _():
            core_other[i].wait_recv()

        load(i)

    ahead = 3
    for i in range(ahead):
        push_own(i)
    gain_copy.wait_recv()
    row_blocks(rows, first_norm)
    ins = sq.spread(normed_in, s_send.at[0], s_recv.at[0])

    def advance(i):
        pass_on(i)
        if i + ahead < 8:
            push_own(i + ahead)
        if i > 0:
            share_other(i - 1)
            arrive(i - 1)

    advance(0)
    downs = sq.spread_from(v.out_grad, v.grad_down, d_send, d_recv, d_sem)
    advance(1)
    for push in ins:
        push.wait_recv()
    transpose_into(normed_in_t, normed_in)
    for i in range(2, 5):
        advance(i)
        for s in (sq.own, sq.next):
            project(i - 2, s)
    advance(5)
    for s in (sq.own, sq.next):
        project(3, s)
    retain(sq.next)
    loads_wait(4)
    give_back(sq.next, merged, out_t)
    gives = give(1, 0)
    retain(sq.own)
    give_back(sq.own, merged, out_t)
    gives += give(0, 0)
    advance(6)
    for push in gives:
        push.wait_recv()
    row_blocks(rows, second_norm)
    mids = sq.spread(normed_mid, s_send.at[1], s_recv.at[1])
    advance(7)
    for push in mids:
        push.wait_recv()
    turn_if(at.core == at.section, normed_mid_t, normed_mid)
    feed(sq.next)
    feed(sq.own)
    for push in gives:
        push.wait_send()

    def last_group():
        for j in range(slices):
            x_copies[7, j].wait_recv()
        core_other[7].start()

    theirs = block(7, other, at.core)
    core_other[7] = copy(theirs, theirs, o_send.at[7], o_recv.at[7], place(dp=at.sibling()))

    @pl.when(at.section == 1)
    def _():
        last_group()

    arrive(7)
    loads_wait(7)
    give_back(sq.next, hidden, down_t)
    ends = give(1, 1)
    give_back(sq.own, hidden, down_t)
    ends += give(0, 1)
    turn_if(at.core != at.section, normed_mid_t, normed_mid)

    @pl.when(at.section == 0)
    def _():
        last_group()

    for push in ends:
        push.wait_recv()

    def last(block):
        result[block] = (middle[block] + collected(block, 1)).astype(bf16)

    row_blocks(rows, last)

    @pl.when(at.section == 0)
    def _():
        for i in range(8):
            core_other[i].wait_recv()

    @pl.when(at.section == 1)
    def _():
        for i in range(8):
            core_own[i].wait_recv()

    for push in downs:
        push.wait()
    for push in ins + mids + ends + list(z_copies.values()) + list(x_copies.values()):
        push.wait_send()
    for i in range(8):
        core_own[i].wait_send()
        core_other[i].wait_send()
    gain_copy.wait_send()


def forward_layer(layer, x, gains, tables, masks, weights, dp_size, out_grad=None):
    rows, width = x.shape
    length = masks.shape[-1]
    heads = masks.shape[1]
    streams = layer == 0
    slices = dp_size // 2
    quarter_k = heads * HEAD_K
    quarter_v = heads * HEAD_V
    quarter_f = weights[-1].shape[-1] // 2 if streams else weights[-1].shape[-1]
    vmem = pl.BlockSpec(memory_space=pltpu.VMEM)
    any_spec = pl.BlockSpec(memory_space=pl.ANY)
    wides = (2 * quarter_k + 2 * quarter_v, quarter_v, 2 * quarter_f, quarter_f)

    def tokens(wide, kind=bf16):
        return jax.ShapeDtypeStruct((2, length, wide), kind)

    turned = jax.ShapeDtypeStruct((width, 2 * length), bf16)
    dma = pltpu.SemaphoreType.DMA
    out_shape = [
        jax.ShapeDtypeStruct((rows, width), f32),
        turned,
        tokens(quarter_k),
        tokens(quarter_k),
        tokens(quarter_v),
        tokens(quarter_v),
        jax.ShapeDtypeStruct((2, heads, length, 1), f32),
        tokens(quarter_v),
        tokens(quarter_v),
        tokens(quarter_v),
        turned,
        tokens(quarter_f),
        tokens(quarter_f),
        tokens(quarter_f),
    ]
    out_specs = [vmem] * len(out_shape)
    scratch = [pltpu.VMEM((slices, 2, width // dp_size, wide), bf16) for wide in wides] + [
        dma((8,)),
        pltpu.VMEM((2, length, width), bf16),
        pltpu.VMEM((2, length, width), bf16),
        pltpu.VMEM((2, length, width), bf16),
        pltpu.VMEM((2, 3, rows, width), bf16),
        dma((2, 3)),
        dma((2, 3)),
        dma((2, 3)),
        dma((2, 3)),
    ]
    if streams:
        out_shape = (
            [jax.ShapeDtypeStruct((2, slices, 2, width // dp_size, wide), bf16) for wide in wides]
            + [jax.ShapeDtypeStruct((2,) + gains.shape, f32)]
            + out_shape
            + [tokens(width), jax.ShapeDtypeStruct((rows, width), bf16)]
        )
        out_specs = [any_spec] * 4 + [vmem] + out_specs + [any_spec, vmem]
        scratch += [
            dma((8, slices - 1)),
            dma((8, slices - 1)),
            dma((8, slices)),
            dma((8, slices)),
            dma((8,)),
            dma((8,)),
            dma((8,)),
            dma((8,)),
            dma((8,)),
            dma,
            dma,
            dma((3,)),
            dma((3,)),
            dma,
        ]
    operands = [x, gains, tables, masks] + ([out_grad] if streams else [])
    return pl.pallas_call(
        functools.partial(forward_kernel, dp_size, layer),
        out_shape=out_shape,
        in_specs=[vmem] * len(operands) + [any_spec] * len(weights),
        out_specs=out_specs,
        scratch_shapes=scratch,
        compiler_params=pltpu.CompilerParams(
            collective_id=1 + layer, has_side_effects=True, vmem_limit_bytes=VMEM_LIMIT
        ),
        name="forward_layer",
    )(*operands, *weights)


class Refs:
    pass


KEPT = 5
GROUPS = 7


def backward_kernel(dp_size, layer, *refs):
    final_layer = layer == 0
    v = Refs()
    (v.grad_out, v.gains, v.tables, v.masks, v.x, v.middle, v.normed_in_t, v.query_rot, v.key_rot, v.value, v.unit,
     v.inverse, v.opened, v.slope_open, v.merged, v.normed_mid_t, v.act, v.slope, v.hidden,
     v.qkvs_all, v.out_all, v.gate_up_all, v.down_all, v.down_in, *refs) = refs
    if final_layer:
        (v.later_chip, v.later_terms, v.first_rows, v.later_normed_in_t, v.later_qkvs, v.later_hidden, v.later_middle,
         *refs) = refs
    v.grad_in, v.chip, v.core_land, *refs = refs
    if final_layer:
        v.x_land, v.final, v.gain_sums, v.result, v.taken_rows, v.taken_grads, *refs = refs
    else:
        v.terms, v.next_down, v.kept_qkvs, *refs = refs
    (v.big, v.out_t, v.query_v, v.key_v, v.value_v, v.wide_a, v.wide_b, v.wide_c, v.inverse_v, v.x_v, v.middle_v,
     v.normed_t, v.outer, v.grad_down, v.grad_gate_up, v.grad_branch, v.grad_qkvs, v.turned, v.parts, v.landed,
     v.grad_middle, v.stage_given, v.stage_own, v.core_part, v.load_sem, v.s_send, v.s_recv, v.g_send, v.g_recv,
     v.c_send, v.c_recv, v.local_sem, *refs) = refs
    if final_layer:
        (v.left, v.right, v.sums, v.r_sem, v.x_send, v.x_recv, v.z_send, v.z_recv, v.terms, v.held, v.hop_land,
         v.t_send, v.t_recv, v.row_send, v.row_recv, v.landed_y) = refs
    else:
        v.d_send, v.d_recv, v.d_sem, v.kept_sem = refs
    at = Place(dp_size)
    rows, width = v.x.shape
    sq = Square(dp_size, rows)
    masks, tables, gains = v.masks, v.tables, v.gains
    query_v, key_v, value_v = v.query_v, v.key_v, v.value_v
    wide_a, wide_b, wide_c = v.wide_a, v.wide_b, v.wide_c
    grad_down, grad_gate_up, grad_branch, grad_qkvs = v.grad_down, v.grad_gate_up, v.grad_branch, v.grad_qkvs
    big, out_t, outer, parts, landed, terms = v.big, v.out_t, v.outer, v.parts, v.landed, v.terms
    wide_k = query_v.shape[-1]
    wide_v = value_v.shape[-1]
    wide_f = outer.shape[-1]
    heads = wide_k // HEAD_K
    slices = dp_size // 2
    slice_rows = width // dp_size
    gain_in = gains[layer, 0:1]
    gain_mid = gains[layer, 1:2]
    other = 1 - at.section
    steps = [(k, b) for k in range(at.groups) for b in range(2)]
    steps = steps[1:] + steps[:1]

    def load(index, source, target):
        copy = pltpu.make_async_copy(source, target, v.load_sem.at[index])
        copy.start()
        return copy

    def remote(src, dst, send, recv, device):
        return pltpu.make_async_remote_copy(
            src_ref=src, dst_ref=dst, send_sem=send, recv_sem=recv, device_id=device, device_id_type=MESH
        )

    def place(section=None, dp=None, tensor=None):
        return (
            at.section if section is None else section,
            at.dp if dp is None else dp,
            at.tensor if tensor is None else tensor,
        )

    sibling = place(dp=at.sibling())
    across = place(section=other)

    token_load = load(14, v.down_in, grad_down)
    down_load = load(0, v.down_all.at[layer], big.at[:, pl.ds(2 * wide_f, wide_f)])
    act_load = load(1, v.act, wide_a)
    slope_load = load(2, v.slope, wide_b)
    gate_load = load(3, v.gate_up_all.at[layer], big.at[:, pl.ds(0, 2 * wide_f)])
    hidden_load = load(4, v.hidden, outer)
    mid_load = load(5, v.normed_mid_t, v.normed_t)
    early = [
        load(6, v.middle, v.middle_v),
        load(7, v.x, v.x_v),
        load(8, v.out_all.at[layer], out_t),
        load(9, v.query_rot, query_v),
        load(10, v.key_rot, key_v),
        load(11, v.value, value_v),
        load(12, v.inverse, v.inverse_v),
        load(13, v.opened, wide_c),
    ]
    terms[...] = jnp.zeros_like(terms)

    partners = [sq.device(*step) for step in SQUARE] + [sibling]
    if final_layer:
        partners.append(across)
        partners += [place(dp=at.dp_at(k, b)) for k, b in steps[:-1] if (k, b) != (0, 1)]
    barrier = pltpu.get_barrier_semaphore()
    for partner in partners:
        pl.semaphore_signal(barrier, inc=1, device_id=partner, device_id_type=MESH)
    pl.semaphore_wait(barrier, len(partners))

    def x_copy(e, at_source, j, source):
        block = source.at[at_source, j]
        return remote(block, v.x_land.at[e, j], v.x_send.at[e, j], v.x_recv.at[e, j], across)

    def start_x(e, at_source, source):
        @pl.loop(0, slices)
        def _(j):
            x_copy(e, at_source, j, source).start()

    row_copies = []
    if final_layer:

        @pl.when(at.section == 0)
        def _():
            @pl.loop(0, KEPT)
            def _(e):
                start_x(e, e, v.later_chip)

            remote(v.grad_out, v.taken_grads, v.row_send.at[1], v.row_recv.at[1], across).start()

        @pl.when(at.section == 1)
        def _():
            remote(v.first_rows, v.taken_rows, v.row_send.at[0], v.row_recv.at[0], across).start()

    def through_down(s):
        tokens = grad_down[s]
        for start in range(0, wide_f, TILE):
            cols = slice(start, start + TILE)
            grad_hidden = mm(tokens, big[:, 2 * wide_f + start : 2 * wide_f + start + TILE])
            grad_gate_up[s, :, cols] = (grad_hidden * wide_b[s, :, cols].astype(f32)).astype(bf16)
            grad_gate_up[s, :, wide_f + start : wide_f + start + TILE] = (
                grad_hidden * wide_a[s, :, cols].astype(f32)
            ).astype(bf16)

    def give_back(s, source, weight, first, size, target):
        tokens = source[s]
        for start in range(0, width, TILE):
            target[s, :, start : start + TILE] = mm_nt(
                tokens, weight[start : start + TILE, first : first + size]
            ).astype(bf16)

    def collected(block, given, land):
        total = sq.chunk(given)[block].astype(f32)
        for j in range(len(SQUARE)):
            total = total + land[j, block].astype(f32)
        return total

    def exchange(source, weight, first, size, target, land, which):
        give_back(sq.next, source, weight, first, size, target)
        send, recv = v.g_send.at[which], v.g_recv.at[which]
        pushes = [sq.give(target, land, send, recv, j) for j in (1, 2)]
        give_back(sq.own, source, weight, first, size, target)
        pushes.append(sq.give(target, land, send, recv, 0))
        return pushes

    members = [
        (v.turned, outer, 0, wide_f),
        (v.normed_t, grad_gate_up, 0, wide_f),
        (v.normed_t, grad_gate_up, wide_f, wide_f),
        (v.turned, outer, 0, wide_v),
        (v.normed_t, grad_qkvs, 0, 2 * wide_k),
        (v.normed_t, grad_qkvs, 2 * wide_k, wide_v),
        (v.normed_t, grad_qkvs, 2 * wide_k + wide_v, wide_v),
    ]
    members += members[KEPT:]
    given_copies, own_copies, fetches = {}, {}, {}

    def product(e, dp):
        left, right, first, size = members[e]
        start = pl.multiple_of(dp * slice_rows, slice_rows)
        wide = right[:, :, first : first + size].reshape(-1, size)
        return mm(left[pl.ds(start, slice_rows), :], wide)

    def given(e):
        if e >= 2:
            given_copies[e - 2].wait_send()
        stage = v.stage_given.at[e % 2]

        @pl.loop(0, slices)
        def _(j):
            stage[j] = product(e, j * 2 + 1 - at.core).astype(bf16)

        given_copies[e] = remote(stage, v.core_land.at[e], v.c_send.at[e], v.c_recv.at[e], sibling)
        given_copies[e].start()

    def fetch(e):
        given_copies[e].wait_recv()
        fetches[e] = pltpu.make_async_copy(v.core_land.at[e], v.core_part, v.local_sem.at[0])
        fetches[e].start()

    def settle(e):
        if e in settled:
            return
        settled.append(e)
        own_copies[e].wait()
        if final_layer:

            @pl.when(at.section == (1 if e < GROUPS else 0))
            def _():
                start_x(e if e < GROUPS else e - GROUPS + KEPT, e, v.chip)

    def own(e):
        if e >= 1:
            settle(e - 1)
        fetches[e].wait()

        @pl.loop(0, slices)
        def _(j):
            v.stage_own[j] = (product(e, j * 2 + at.core) + v.core_part[j].astype(f32)).astype(bf16)

        own_copies[e] = pltpu.make_async_copy(v.stage_own, v.chip.at[e], v.local_sem.at[1])
        own_copies[e].start()

    settled = []

    def index(k, b):
        return ((at.group + k) % at.groups) * 2 + (at.low + b) % 2

    def piece(e, k):
        start = pl.multiple_of(at.low * wide_f, wide_f)
        return v.final.at[e, k, :, pl.ds(start, wide_f)]

    def z_copy(e, j):
        k, b = steps[j]
        return remote(v.sums.at[j], piece(e, k), v.z_send.at[e, j], v.z_recv.at[e, j], place(dp=at.dp_at(k, b)))

    def home_copy(e):
        return pltpu.make_async_copy(v.sums.at[slices - 1], piece(e, 0), v.r_sem.at[2, 0])

    def reduce_slices(e, at_source, source, first, stop, wait_previous):
        def loads(j):
            here = index(*steps[j])
            return (
                pltpu.make_async_copy(source.at[at_source, here], v.left.at[j % 2], v.r_sem.at[0, j % 2]),
                pltpu.make_async_copy(v.x_land.at[e, here], v.right.at[j % 2], v.r_sem.at[1, j % 2]),
            )

        def begin(j):
            x_copy(e, at_source, index(*steps[j]), source).wait_recv()
            for copy in loads(j):
                copy.start()

        begin(first)
        for j in range(first, stop):
            if j + 1 < stop:
                begin(j + 1)
            for copy in loads(j):
                copy.wait()

            @pl.when(wait_previous)
            def _():
                if j == slices - 1:
                    home_copy(e).wait()
                else:
                    z_copy(e - 1, j).wait_send()

            v.sums[j] = (v.left[j % 2].astype(f32) + v.right[j % 2].astype(f32)).astype(bf16)
            if j == slices - 1:
                home_copy(e).start()
            else:
                z_copy(e, j).start()

    reduced = [0, 0]

    def source_of(section, e):
        if section == 0:
            return e, v.chip
        return (e, v.later_chip) if e < KEPT else (e + GROUPS - KEPT, v.chip)

    def reduce_some(section, count):
        if not final_layer:
            return

        @pl.when(at.section == section)
        def _():
            done = reduced[section]
            while done < reduced[section] + count:
                e, first = divmod(done, slices)
                stop = min(slices, first + reduced[section] + count - done)
                reduce_slices(e, *source_of(section, e), first, stop, e > 0)
                done += stop - first

        reduced[section] += count

    def reduce_rest(section):
        e, first = divmod(reduced[section], slices)

        @pl.when(at.section == section)
        def _():
            begin = e
            if first > 0:
                reduce_slices(e, *source_of(section, e), first, slices, e > 0)
                begin = e + 1
            same = KEPT if section == 1 else GROUPS

            @pl.loop(begin, same)
            def _(i):
                reduce_slices(i, i, source_of(section, 0)[1], 0, slices, i > 0)

            for i in range(same, GROUPS):
                reduce_slices(i, *source_of(section, i), 0, slices, True)

    token_load.wait()
    if final_layer:
        hidden_load.wait()
        transpose_into(v.turned, grad_down)
        given(0)
    down_load.wait()
    act_load.wait()
    slope_load.wait()
    through_down(sq.next)
    through_down(sq.own)
    unit_load = load(1, v.unit, wide_a)
    bend_load = load(2, v.slope_open, wide_b)
    gate_load.wait()
    gives = exchange(grad_gate_up, big, 0, 2 * wide_f, parts, landed, 0)
    if not final_layer:
        hidden_load.wait()
        transpose_into(v.turned, grad_down)
        given(0)
    fetch(0)
    own(0)
    mid_load.wait()
    settle(0)
    given(1)
    qkvs_load = load(3, v.qkvs_all.at[layer], big)
    merged_load = load(4, v.merged, outer)
    for copy in early:
        copy.wait()
    for push in gives:
        push.wait_recv()

    def through_mid(block):
        upstream = collected(block, parts, landed)
        normed, scale = norm_parts(v.middle_v[block])
        grad_rows = v.grad_out[block].astype(f32) + norm_grad(normed, scale, upstream, gain_mid)
        v.grad_middle[block] = grad_rows
        sq.chunk(grad_branch)[block] = grad_rows.astype(bf16)
        terms[1:2] = terms[1:2] + jnp.sum(upstream * normed, axis=0, keepdims=True)

    row_blocks(rows, through_mid)
    mids = sq.spread(grad_branch, v.s_send, v.s_recv)
    reduce_some(0, 1)
    given(2)
    fetch(1)
    own(1)
    unit_load.wait()
    bend_load.wait()
    settle(1)
    reduce_some(1, slices)
    reduce_some(0, 1)

    def through_heads(s):
        tokens = grad_branch[s]
        for head in range(heads):
            cols_k = slice(head * HEAD_K, (head + 1) * HEAD_K)
            cols_v = slice(head * HEAD_V, (head + 1) * HEAD_V)
            grad_merged = mm(tokens, out_t[:, cols_v])
            unit_rows = wide_a[s, :, cols_v].astype(f32)
            first = 2 * wide_k + wide_v + head * HEAD_V
            grad_qkvs[s, :, first : first + HEAD_V] = (
                grad_merged * unit_rows * wide_b[s, :, cols_v].astype(f32)
            ).astype(bf16)
            grad_unit = grad_merged * wide_c[s, :, cols_v].astype(f32)
            grad_mixed = (
                v.inverse_v[s, head]
                * (
                    grad_unit
                    - jnp.mean(grad_unit, axis=-1, keepdims=True)
                    - unit_rows * jnp.mean(grad_unit * unit_rows, axis=-1, keepdims=True)
                )
            ).astype(bf16)
            query, key, val = query_v[s, :, cols_k], key_v[s, :, cols_k], value_v[s, :, cols_v]
            mask = masks[s, head]
            weight = (mm_nt(query, key) * mask).astype(bf16)
            grad_product = (mm_nt(grad_mixed, val) * mask).astype(bf16)
            first = 2 * wide_k + head * HEAD_V
            grad_qkvs[s, :, first : first + HEAD_V] = mm_tn(weight, grad_mixed).astype(bf16)
            grad_qkvs[s, :, cols_k] = turn_back(mm(grad_product, key), tables[0], tables[1], tables[2]).astype(bf16)
            first = wide_k + head * HEAD_K
            grad_qkvs[s, :, first : first + HEAD_K] = turn_back(
                mm_tn(grad_product, query), tables[0], tables[1], tables[3]
            ).astype(bf16)

    mids[0].wait_recv()
    through_heads(sq.own)
    mids[1].wait_recv()
    mids[2].wait_recv()
    through_heads(sq.next)
    if not final_layer:
        keep = pltpu.make_async_copy(grad_qkvs, v.kept_qkvs, v.kept_sem)
        keep.start()
    qkvs_load.wait()
    reduce_some(0, 1)
    for push in gives:
        push.wait_send()
    ends = exchange(grad_qkvs, big, 0, grad_qkvs.shape[-1], parts, landed, 1)
    fetch(2)
    own(2)
    in_load = load(5, v.normed_in_t, v.normed_t)
    transpose_into(v.turned, grad_branch)
    settle(2)
    merged_load.wait()
    given(3)
    in_load.wait()
    given(4)
    fetch(3)
    own(3)
    reduce_some(1, slices)
    reduce_some(0, 1)
    settle(3)
    for push in ends:
        push.wait_recv()

    def through_in(block):
        upstream = collected(block, parts, landed)
        normed, scale = norm_parts(v.x_v[block].astype(f32))
        v.grad_in[block] = (v.grad_middle[block] + norm_grad(normed, scale, upstream, gain_in)).astype(bf16)
        terms[0:1] = terms[0:1] + jnp.sum(upstream * normed, axis=0, keepdims=True)

    row_blocks(rows, through_in)
    if final_layer:

        @pl.when(at.section == 1)
        def _():
            remote(v.grad_in, v.taken_grads, v.row_send.at[1], v.row_recv.at[1], across).start()

    else:
        downs = sq.spread_from(v.grad_in, v.next_down, v.d_send, v.d_recv, v.d_sem)

    if not final_layer:
        fetch(4)
        own(4)
        settle(4)
        for push in mids + ends:
            push.wait_send()
        for e in (3, 4):
            given_copies[e].wait_send()
        for push in downs:
            push.wait()
        keep.wait()
        return

    reduce_some(0, 1)
    given(5)
    fetch(4)
    own(4)
    reduce_some(0, 1)
    given(6)
    settle(4)
    reduce_some(1, slices)
    reduce_some(0, 1)
    fetch(5)
    own(5)
    reduce_some(0, 1)
    fetch(6)
    own(6)
    in_load = load(5, v.later_normed_in_t, v.normed_t)
    qkvs_load = load(3, v.later_qkvs, grad_qkvs)
    hidden_load = load(4, v.later_hidden, outer)
    middle_load = load(6, v.later_middle, v.middle_v)
    down_load = load(0, v.down_all.at[1], big.at[:, pl.ds(2 * wide_f, wide_f)])
    settle(6)
    reduce_some(1, slices)
    reduce_some(0, 1)
    in_load.wait()
    qkvs_load.wait()
    given(7)
    reduce_some(0, 1)
    given(8)
    fetch(7)
    own(7)
    reduce_some(0, 1)
    fetch(8)
    own(8)
    settle(7)
    reduce_some(0, 1)
    for push in mids + ends:
        push.wait_send()
    hidden_load.wait()
    down_load.wait()
    settle(8)
    gives_y = exchange(outer, big, 2 * wide_f, wide_f, parts, v.landed_y, 2)
    reduce_some(1, slices)
    reduce_some(0, slices)
    middle_load.wait()
    for push in gives_y:
        push.wait_recv()

    def last(block):
        v.result[block] = (v.middle_v[block] + collected(block, parts, v.landed_y)).astype(bf16)

    row_blocks(rows, last)

    @pl.when(at.section == 0)
    def _():
        remote(v.result, v.taken_rows, v.row_send.at[0], v.row_recv.at[0], across).start()

    for push in gives_y:
        push.wait_send()
    for e in (7, 8):
        given_copies[e].wait_send()
    reduce_rest(1)
    reduce_rest(0)

    held, hop_land, mine = v.held, v.hop_land, v.held.at[at.section]
    held[0] = terms[...]
    held[1] = v.later_terms[...]
    hop = remote(held, hop_land.at[0], v.t_send.at[0], v.t_recv.at[0], sibling)
    hop.start()
    hop.wait()
    held[...] = held[...] + hop_land[0]
    hop = remote(held.at[other], hop_land.at[1, other], v.t_send.at[1], v.t_recv.at[1], across)
    hop.start()
    hop.wait_send()
    remote(held.at[other], hop_land.at[1, at.section], v.t_send.at[1], v.t_recv.at[1], across).wait_recv()
    mine[...] = mine[...] + hop_land[1, at.section]
    for h, device in ((2, place(tensor=1 - at.tensor)), (3, place(dp=at.dp_at(0, 1)))):
        hop = remote(mine, hop_land.at[h, 0], v.t_send.at[h], v.t_recv.at[h], device)
        hop.start()
        hop.wait()
        mine[...] = mine[...] + hop_land[h, 0]
    hops = []
    for k in range(1, at.groups):
        hop = remote(mine, hop_land.at[3 + k, 0], v.t_send.at[3 + k], v.t_recv.at[3 + k], place(dp=at.dp_at(k, 0)))
        hop.start()
        hops.append(hop)
    total = mine[...]
    for k, hop in zip(range(1, at.groups), hops):
        hop.wait()
        total = total + hop_land[3 + k, 0]
    v.gain_sums[...] = total

    for which, rows_sent in ((0, v.result), (1, v.grad_in)):
        target = v.taken_rows if which == 0 else v.taken_grads
        copy = remote(rows_sent, target, v.row_send.at[which], v.row_recv.at[which], across)
        copy.wait_recv()
        copy.wait_send()

    home_copy(0).wait()
    for j in range(slices - 1):
        z_copy(GROUPS - 1, j).wait_send()

        @pl.loop(0, GROUPS)
        def _(e):
            z_copy(e, j).wait_recv()

    @pl.loop(0, GROUPS)
    def _(e):
        @pl.loop(0, slices)
        def _(j):
            x_copy(e, e, j, v.chip).wait_send()


def backward_layer(layer, grad_out, down, x, gains, tables, masks, saved, gathered, dp_size, later=None, x_out=None):
    rows, width = x.shape
    length = masks.shape[-1]
    (middle, normed_in_t, query_rot, key_rot, value, unit, inverse, opened, slope_open, merged, normed_mid_t, act, slope,
     hidden) = saved
    vmem = pl.BlockSpec(memory_space=pltpu.VMEM)
    any_spec = pl.BlockSpec(memory_space=pl.ANY)
    final_layer = layer == 0
    slices = dp_size // 2
    slice_rows = width // dp_size
    size = hidden.shape[-1]
    assert value.shape[-1] == size and 2 * query_rot.shape[-1] == size
    block = (slices, slice_rows, size)

    def held(*shape, kind=bf16):
        return pltpu.VMEM(shape, kind)

    def stored(*shape, kind=bf16):
        return jax.ShapeDtypeStruct(shape, kind)

    dma = pltpu.SemaphoreType.DMA
    operands = [grad_out, gains, tables, masks]
    operands += [x, middle, normed_in_t, query_rot, key_rot, value, unit, inverse, opened, slope_open, merged, normed_mid_t,
                 act, slope, hidden]
    operands += [*gathered, down]
    in_specs = [vmem] * 4 + [any_spec] * (len(operands) - 4)
    count = 2 * GROUPS - KEPT if final_layer else KEPT
    out_shape = [stored(rows, width), stored(count, *block), stored(count, *block)]
    out_specs = [vmem, any_spec, any_spec]
    if final_layer:
        later_chip, later_terms, later_qkvs, later_saved = later
        operands += [later_chip, later_terms, x_out, later_saved[1], later_qkvs, later_saved[-1], later_saved[0]]
        in_specs += [any_spec, vmem] + [any_spec] * 5
        out_shape += [stored(GROUPS, *block), stored(GROUPS, dp_size // 4, slice_rows, 2 * size), stored(2, width, kind=f32),
                      stored(rows, width), stored(rows, width), stored(rows, width)]
        out_specs += [any_spec, any_spec, vmem, vmem, any_spec, any_spec]
    else:
        out_shape += [stored(2, width, kind=f32), stored(2, length, width), stored(2, length, 3 * size)]
        out_specs += [vmem, any_spec, any_spec]
    scratch = [
        held(width, 3 * size),
        held(width, size),
        held(*query_rot.shape),
        held(*key_rot.shape),
        held(*value.shape),
        held(2, length, size),
        held(2, length, size),
        held(2, length, size),
        held(*inverse.shape, kind=f32),
        held(rows, width),
        held(rows, width, kind=f32),
        held(width, 2 * length),
        held(2, length, size),
        held(2, length, width),
        held(2, length, 2 * size),
        held(2, length, width),
        held(2, length, 3 * size),
        held(width, 2 * length),
        held(2, length, width),
        held(3, rows, width),
        held(rows, width, kind=f32),
        held(2, *block),
        held(*block),
        held(*block),
        dma((15,)),
        dma((3,)),
        dma((3,)),
        dma((3, 3)),
        dma((3, 3)),
        dma((count,)),
        dma((count,)),
        dma((2,)),
    ]
    if final_layer:
        hops = 3 + dp_size // 4
        scratch += [
            held(2, slice_rows, size),
            held(2, slice_rows, size),
            held(*block),
            dma((3, 2)),
            dma((GROUPS, slices)),
            dma((GROUPS, slices)),
            dma((GROUPS, slices - 1)),
            dma((GROUPS, slices - 1)),
            held(2, width, kind=f32),
            held(2, 2, width, kind=f32),
            held(hops, 2, 2, width, kind=f32),
            dma((hops,)),
            dma((hops,)),
            dma((2,)),
            dma((2,)),
            held(3, rows, width),
        ]
    else:
        scratch += [dma((3,)), dma((3,)), dma, dma]
    return pl.pallas_call(
        functools.partial(backward_kernel, dp_size, layer),
        out_shape=out_shape,
        in_specs=in_specs,
        out_specs=out_specs,
        scratch_shapes=scratch,
        compiler_params=pltpu.CompilerParams(
            collective_id=4 + layer, has_side_effects=True, vmem_limit_bytes=VMEM_LIMIT
        ),
        name="backward_layer",
    )(*operands)


def nested(outs):
    return (*outs[:5], outs[5:-2], *outs[-2:])


def on_device(
    dp_size,
    layer_input,
    segment_ids,
    output_grad,
    query_weight,
    key_weight,
    value_weight,
    swish_weight,
    output_weight,
    gate_weight,
    up_weight,
    down_weight,
    mixer_gain,
    ffn_gain,
):
    at = Place(dp_size)
    section_first = at.section == 0
    rows_here, width = layer_input.shape[1:]
    length = segment_ids.shape[1]
    score_scale = HEAD_K ** (-0.5)

    quarter_k = query_weight.shape[2] // 2
    quarter_v = value_weight.shape[2] // 2
    quarter_f = gate_weight.shape[2] // 2
    heads_here = quarter_k // HEAD_K
    first_head = (at.tensor * 2 + at.low) * heads_here
    cosine, sine, growth = rotation_tables(length, HEAD_K // 2)

    ids_mine = lax.dynamic_index_in_dim(segment_ids, at.section, 0, keepdims=False)
    ids_pair = lax.ppermute(ids_mine, "dp", [(i, i ^ 2) for i in range(dp_size)])
    ids = jnp.where(at.low == 0, jnp.stack([ids_mine, ids_pair]), jnp.stack([ids_pair, ids_mine]))
    masks = decay_mask(ids, first_head, heads_here) * score_scale
    tables = jnp.stack([cosine, sine, growth, 1.0 / growth])

    first_in = lax.dynamic_index_in_dim(layer_input, at.section, 0, keepdims=False)
    out_grad = lax.dynamic_index_in_dim(output_grad, at.section, 0, keepdims=False)
    shards = (query_weight[0], key_weight[0], value_weight[0], swish_weight[0], output_weight[0].T, gate_weight[0],
              up_weight[0], down_weight[0].T)
    own_gains = jnp.concatenate([mixer_gain, ffn_gain], axis=0)
    *gathered, all_gains, first_saved, second_down, first_sent = nested(
        forward_layer(0, first_in, own_gains, tables, masks, shards, dp_size, out_grad)
    )
    second_saved = forward_layer(1, first_sent, all_gains, tables, masks, gathered, dp_size)
    gathered = [g.reshape(2, width, g.shape[-1]) for g in gathered]
    second_grad, later_chip, _, later_terms, first_down, later_qkvs = backward_layer(
        1, out_grad, second_down, first_sent, all_gains, tables, masks, second_saved, gathered, dp_size
    )
    first_grad, _, _, _, landed, my_gains, second_sent, taken_rows, taken_grads = backward_layer(
        0, second_grad, first_down, first_in, all_gains, tables, masks, first_saved, gathered, dp_size,
        (later_chip, later_terms, later_qkvs, second_saved), first_sent,
    )

    def by_layer(first, second, taken):
        return jnp.where(section_first, jnp.stack([first, taken]), jnp.stack([taken, second]))[None]

    def shard(e):
        return jnp.sum(landed[e].astype(f32), axis=0)

    def columns(e, start, size):
        step = landed.shape[-1] // 2
        part = jnp.concatenate([landed[e, :, :, p * step + start : p * step + start + size] for p in range(2)], axis=-1)
        return jnp.sum(part.astype(f32), axis=0)

    return (
        by_layer(first_sent, second_sent, taken_rows),
        by_layer(first_grad, second_grad, taken_grads),
        columns(4, 0, quarter_k)[None],
        columns(4, quarter_k, quarter_k)[None],
        shard(5)[None],
        shard(6)[None],
        shard(3).T[None],
        shard(1)[None],
        shard(2)[None],
        shard(0).T[None],
        my_gains[0][None],
        my_gains[1][None],
    )


def solution(mesh):
    in_specs = (
        P(None, ("dp", "tensor"), None),
        P(None, "dp"),
        P(None, ("dp", "tensor"), None),
        P("section", "dp", "tensor"),
        P("section", "dp", "tensor"),
        P("section", "dp", "tensor"),
        P("section", "dp", "tensor"),
        P("section", "tensor", "dp"),
        P("section", "dp", "tensor"),
        P("section", "dp", "tensor"),
        P("section", "tensor", "dp"),
        P("section", None),
        P("section", None),
    )
    out_specs = (
        P("section", None, ("dp", "tensor"), None),
        P("section", None, ("dp", "tensor"), None),
        P("section", "dp", "tensor"),
        P("section", "dp", "tensor"),
        P("section", "dp", "tensor"),
        P("section", "dp", "tensor"),
        P("section", "tensor", "dp"),
        P("section", "dp", "tensor"),
        P("section", "dp", "tensor"),
        P("section", "tensor", "dp"),
        P("section", None),
        P("section", None),
    )
    return jax.shard_map(
        functools.partial(on_device, mesh.shape["dp"]),
        mesh=mesh,
        in_specs=in_specs,
        out_specs=out_specs,
        check_vma=False,
    )
```

```python
import functools

import jax
import jax.numpy as jnp
from jax import lax
from jax.experimental import pallas as pl
from jax.experimental.pallas import tpu as pltpu
from jax.sharding import PartitionSpec as P

HEAD_K = 256
HEAD_V = 512
MESH = pl.DeviceIdType.MESH

epsilon = 1e-05
group_guard = 1.0
bf16 = jnp.bfloat16
f32 = jnp.float32


def rotation_tables(length, half_width):
    pair_index = jnp.arange(half_width).astype(f32)
    position = jnp.arange(length).astype(f32)[:, None]
    angle = position * jnp.exp(-jnp.log(10000.0) * pair_index / half_width)
    zeta = (pair_index / half_width + 0.4) / 1.4
    growth = jnp.exp(position / 512.0 * jnp.log(zeta))
    return (jnp.cos(angle), jnp.sin(angle), growth)


def decay_mask(segments, first_head, heads):
    length = segments.shape[-1]
    position = jnp.arange(length)
    earlier = position[:, None] >= position[None, :]
    same_doc = (segments[:, :, None] == segments[:, None, :]) & earlier[None]
    distance = jnp.maximum(position[:, None] - position[None, :], 0).astype(f32)
    head_index = (first_head + jnp.arange(heads)).astype(f32)
    log_rate = jnp.log(1.0 - jnp.exp2(-5.0 - head_index))
    decay = jnp.exp(log_rate[:, None, None] * distance[None])
    return jnp.where(same_doc[:, None], decay[None], 0.0)


class Place:
    def __init__(self, dp_size):
        self.groups = dp_size // 4
        self.section = lax.axis_index("section")
        self.dp = lax.axis_index("dp")
        self.tensor = lax.axis_index("tensor")
        self.core = self.dp % 2
        self.low = (self.dp // 2) % 2
        self.group = self.dp // 4

    def dp_at(self, group_step, low_step):
        group = (self.group + group_step + self.groups) % self.groups
        return (group * 2 + (self.low + low_step) % 2) * 2 + self.core

    def sibling(self):
        return self.dp + 1 - 2 * self.core


SQUARE = ((0, 1), (1, 0), (1, 1))
TILE = 512
VMEM_LIMIT = 63 * 1024 * 1024


def mm(left, right):
    return lax.dot_general(left, right, (((1,), (0,)), ((), ())), preferred_element_type=f32)


def mm_nt(left, right):
    return lax.dot_general(left, right, (((1,), (1,)), ((), ())), preferred_element_type=f32)


def mm_tn(left, right):
    return lax.dot_general(left, right, (((0,), (0,)), ((), ())), preferred_element_type=f32)


class Square:
    def __init__(self, dp_size, rows):
        self.at = Place(dp_size)
        self.rows = rows
        self.own = self.at.low
        self.next = 1 - self.at.low

    def device(self, low_step, tensor_step):
        return (self.at.section, self.at.dp_at(0, low_step), (self.at.tensor + tensor_step) % 2)

    def barrier(self):
        barrier = pltpu.get_barrier_semaphore()
        for step in SQUARE:
            pl.semaphore_signal(barrier, inc=1, device_id=self.device(*step), device_id_type=MESH)
        pl.semaphore_wait(barrier, len(SQUARE))

    def chunk(self, ref, low_step=0, tensor_step=0):
        start = pl.multiple_of((self.at.tensor + tensor_step) % 2 * self.rows, self.rows)
        return ref.at[(self.at.low + low_step) % 2, pl.ds(start, self.rows)]

    def copy(self, src, dst, send, recv, step):
        return pltpu.make_async_remote_copy(
            src_ref=src,
            dst_ref=dst,
            send_sem=send,
            recv_sem=recv,
            device_id=self.device(*step),
            device_id_type=MESH,
        )

    def spread(self, ref, send, recv):
        pushes = []
        for j, step in enumerate(SQUARE):
            push = self.copy(self.chunk(ref), self.chunk(ref), send.at[j], recv.at[j], step)
            push.start()
            pushes.append(push)
        return pushes

    def spread_from(self, own, ref, send, recv, here):
        local = pltpu.make_async_copy(own, self.chunk(ref), here)
        local.start()
        pushes = [local]
        for j, step in enumerate(SQUARE):
            push = self.copy(own, self.chunk(ref), send.at[j], recv.at[j], step)
            push.start()
            pushes.append(push)
        return pushes

    def give(self, parts, landed, send, recv, j):
        push = self.copy(self.chunk(parts, *SQUARE[j]), landed.at[j], send.at[j], recv.at[j], SQUARE[j])
        push.start()
        return push


def row_blocks(rows, body, block=32):
    block = min(block, rows)

    @pl.loop(0, rows // block)
    def _(i):
        body(pl.ds(pl.multiple_of(i * block, block), block))


def norm_parts(values):
    centred = values - jnp.mean(values, axis=-1, keepdims=True)
    scale = lax.rsqrt(jnp.mean(centred * centred, axis=-1, keepdims=True) + epsilon)
    return centred * scale, scale


def norm_grad(normed, scale, upstream, gain):
    through = upstream * gain
    return scale * (
        through
        - jnp.mean(through, axis=-1, keepdims=True)
        - normed * jnp.mean(through * normed, axis=-1, keepdims=True)
    )


def turn(values, cosine, sine, scale):
    half = values.shape[-1] // 2
    a, b = values[:, :half], values[:, half:]
    return jnp.concatenate([(a * cosine - b * sine) * scale, (a * sine + b * cosine) * scale], axis=-1)


def turn_back(values, cosine, sine, scale):
    half = values.shape[-1] // 2
    a, b = values[:, :half] * scale, values[:, half:] * scale
    return jnp.concatenate([a * cosine + b * sine, b * cosine - a * sine], axis=-1)


def transpose_into(target, source):
    _, length, width = source.shape
    for s in range(2):
        for start in range(0, width, TILE):
            target[start : start + TILE, s * length : (s + 1) * length] = source[s, :, start : start + TILE].T


def forward_kernel(dp_size, layer, *refs):
    streams = layer == 0
    v = Refs()
    if streams:
        (v.x, v.own_gains, v.tables, v.masks, v.out_grad, *refs) = refs
        shards, refs = refs[:8], refs[8:]
        stored, refs = refs[:4], refs[4:]
        (v.gains, *refs) = refs
    else:
        (v.x, v.gains, v.tables, v.masks, *refs) = refs
        stored, refs = refs[:4], refs[4:]
    (middle, normed_in_t, query_rot, key_rot, value, unit, inverse, opened, slope_open, merged, normed_mid_t, act, slope,
     hidden, *refs) = refs
    if streams:
        (v.grad_down, result, *refs) = refs
    held, refs = refs[:4], refs[4:]
    (w_sem, normed_in, *refs) = refs
    if streams:
        (normed_mid, *refs) = refs
    else:
        normed_mid = normed_mid_t
    (parts, landed, s_send, s_recv, g_send, g_recv, *refs) = refs
    x, tables, masks = v.x, v.tables, v.masks
    rows, width = x.shape
    sq = Square(dp_size, rows)
    at = sq.at
    qkvs, out_t, gate_up, down_t = held
    wide_k = query_rot.shape[-1]
    wide_v = value.shape[-1]
    wide_f = hidden.shape[-1]
    heads = wide_k // HEAD_K
    slices = dp_size // 2
    other = 1 - at.section
    groups = [(0, 0, wide_k), (0, wide_k, wide_k), (0, 2 * wide_k, wide_v), (0, 2 * wide_k + wide_v, wide_v),
              (1, 0, wide_v), (2, 0, wide_f), (2, wide_f, wide_f), (3, 0, wide_f)]
    loads = {}

    def load(i):
        which, first, size = groups[i]
        columns = pl.ds(first, size)
        loads[i] = pltpu.make_async_copy(
            stored[which].at[layer, :, :, :, columns], held[which].at[:, :, :, columns], w_sem.at[i]
        )
        loads[i].start()

    def weight(which, first, size):
        return held[which][:, :, :, first : first + size].reshape(width, size)

    def first_norm(block):
        unit_rows, _ = norm_parts(x[block].astype(f32))
        sq.chunk(normed_in)[block] = (unit_rows * v.gains[layer, 0:1]).astype(bf16)

    def project(i, s):
        loads_wait(i)
        first, size = groups[i][1:]
        tokens = normed_in[s]
        for start in range(0, size, TILE):
            wide = mm(tokens, weight(0, first + start, TILE))
            cols = slice(start, start + TILE)
            if i < 2:
                dest = (query_rot, key_rot)[i]
                for head in range(TILE // HEAD_K):
                    part = wide[:, head * HEAD_K : (head + 1) * HEAD_K]
                    dest[s, :, start + head * HEAD_K : start + (head + 1) * HEAD_K] = turn(
                        part, tables[0], tables[1], tables[2 + i]
                    ).astype(bf16)
            elif i == 2:
                value[s, :, cols] = wide.astype(bf16)
            else:
                sigmoid = 1.0 / (1.0 + jnp.exp(-wide))
                opened[s, :, cols] = (wide * sigmoid).astype(bf16)
                slope_open[s, :, cols] = (sigmoid * (1.0 + wide * (1.0 - sigmoid))).astype(bf16)

    waited = []

    def loads_wait(i):
        if i not in waited:
            waited.append(i)
            loads[i].wait()

    def retain(s):
        for head in range(heads):
            cols_k = slice(head * HEAD_K, (head + 1) * HEAD_K)
            cols_v = slice(head * HEAD_V, (head + 1) * HEAD_V)
            product = mm_nt(query_rot[s, :, cols_k], key_rot[s, :, cols_k])
            weights = (product * masks[s, head]).astype(bf16)
            mixed = mm(weights, value[s, :, cols_v])
            centred = mixed - jnp.mean(mixed, axis=-1, keepdims=True)
            scale = lax.rsqrt(jnp.mean(centred * centred, axis=-1, keepdims=True) + group_guard)
            unit_rows = centred * scale
            inverse[s, head] = scale
            unit[s, :, cols_v] = unit_rows.astype(bf16)
            merged[s, :, cols_v] = (unit_rows * opened[s, :, cols_v].astype(f32)).astype(bf16)

    def give_back(s, source, weight_t):
        tokens = source[s]
        step = width // slices
        for i in range(slices):
            parts[s, :, i * step : (i + 1) * step] = mm_nt(tokens, weight_t[i].reshape(step, -1)).astype(bf16)

    def collected(block, which):
        total = sq.chunk(parts)[block].astype(f32)
        for j in range(len(SQUARE)):
            total = total + landed[which, j, block].astype(f32)
        return total

    def give(s, which):
        send, recv = g_send.at[which], g_recv.at[which]
        return [sq.give(parts, landed.at[which], send, recv, j) for j in ((1, 2) if s == 1 else (0,))]

    def second_norm(block):
        middle_rows = x[block].astype(f32) + collected(block, 0)
        middle[block] = middle_rows
        unit_rows, _ = norm_parts(middle_rows)
        sq.chunk(normed_mid)[block] = (unit_rows * v.gains[layer, 1:2]).astype(bf16)

    def feed(s):
        loads_wait(5)
        loads_wait(6)
        tokens = normed_mid[s]
        for start in range(0, wide_f, TILE):
            cols = slice(start, start + TILE)
            gate = mm(tokens, weight(2, start, TILE))
            up = mm(tokens, weight(2, wide_f + start, TILE))
            square = gate * gate
            bend = jnp.tanh(0.7978845608028654 * gate * (1.0 + 0.044715 * square))
            half = 0.5 * (1.0 + bend)
            gelu = gate * half
            slope_gelu = half + 0.5 * gate * (1.0 - bend * bend) * (
                0.7978845608028654 * (1.0 + 3 * 0.044715 * square)
            )
            act[s, :, cols] = gelu.astype(bf16)
            slope[s, :, cols] = (slope_gelu * up).astype(bf16)
            hidden[s, :, cols] = (gelu * up).astype(bf16)

    def turn_if(condition, target, source):
        @pl.when(condition)
        def _():
            transpose_into(target, source)

    if not streams:
        for i in range(7):
            load(i)
        row_blocks(rows, first_norm)
        sq.barrier()
        ins = sq.spread(normed_in, s_send.at[0], s_recv.at[0])
        ins[0].wait_recv()
        for i in range(4):
            project(i, sq.own)
        ins[1].wait_recv()
        ins[2].wait_recv()
        turn_if(at.core == at.section, normed_in_t, normed_in)
        for i in range(4):
            project(i, sq.next)
        retain(sq.next)
        loads_wait(4)
        give_back(sq.next, merged, out_t)
        gives = give(1, 0)
        retain(sq.own)
        give_back(sq.own, merged, out_t)
        gives += give(0, 0)
        turn_if(at.core != at.section, normed_in_t, normed_in)
        for push in gives:
            push.wait_recv()
        row_blocks(rows, second_norm)
        mids = sq.spread(normed_mid, s_send.at[1], s_recv.at[1])
        mids[0].wait_recv()
        feed(sq.own)
        mids[1].wait_recv()
        mids[2].wait_recv()
        feed(sq.next)
        for push in ins + mids + gives:
            push.wait_send()
        return

    (z_send, z_recv, x_send, x_recv, c_send, c_recv, o_send, o_recv, here_sem, gain_send, gain_recv, d_send, d_recv,
     d_sem) = refs
    steps = [(k, b) for k in range(at.groups) for b in range(2)][1:]

    def place(section=None, dp=None):
        return (at.section if section is None else section, at.dp if dp is None else dp, at.tensor)

    def copy(src, dst, send, recv, device):
        return pltpu.make_async_remote_copy(
            src_ref=src, dst_ref=dst, send_sem=send, recv_sem=recv, device_id=device, device_id_type=MESH
        )

    partners = [sq.device(*step) for step in SQUARE] + [place(dp=at.sibling()), place(section=other)]
    partners += [place(dp=at.dp_at(k, b)) for k, b in steps if (k, b) != (0, 1)]
    barrier = pltpu.get_barrier_semaphore()
    for partner in partners:
        pl.semaphore_signal(barrier, inc=1, device_id=partner, device_id_type=MESH)
    pl.semaphore_wait(barrier, len(partners))

    gain_copy = copy(v.own_gains, v.gains.at[at.section], gain_send, gain_recv, place(section=other))
    gain_copy.start()
    v.gains[at.section] = v.own_gains[...]

    def slot(i, section, dp):
        which, first, size = groups[i]
        return stored[which].at[section, dp // 2, dp % 2, :, pl.ds(first, size)]

    def block(i, section, core):
        which, first, size = groups[i]
        return stored[which].at[section, :, core, :, pl.ds(first, size)]

    def part(i, b):
        size = groups[i][2]
        return shards[i].at[:, pl.ds(pl.multiple_of((at.low + b) % 2 * size, size), size)]

    z_copies, x_copies, here, core_own, core_other = {}, {}, {}, {}, {}

    def push_own(i):
        mine = slot(i, at.section, at.dp)
        for j, (k, b) in enumerate(steps):
            z_copies[i, j] = copy(part(i, b), mine, z_send.at[i, j], z_recv.at[i, j], place(dp=at.dp_at(k, b)))
            z_copies[i, j].start()
        x_copies[i, 0] = copy(part(i, 0), mine, x_send.at[i, 0], x_recv.at[i, 0], place(section=other))
        x_copies[i, 0].start()
        here[i] = pltpu.make_async_copy(part(i, 0), mine, here_sem.at[i])
        here[i].start()

    def pass_on(i):
        for j, (k, b) in enumerate(steps):
            z_copies[i, j].wait_recv()
            arrived = slot(i, at.section, at.dp_at(-k, b))
            x_copies[i, j + 1] = copy(arrived, arrived, x_send.at[i, j + 1], x_recv.at[i, j + 1], place(section=other))
            x_copies[i, j + 1].start()
        here[i].wait()
        mine = block(i, at.section, at.core)
        core_own[i] = copy(mine, mine, c_send.at[i], c_recv.at[i], place(dp=at.sibling()))
        core_own[i].start()

    def share_other(i):
        for j in range(slices):
            x_copies[i, j].wait_recv()
        theirs = block(i, other, at.core)
        core_other[i] = copy(theirs, theirs, o_send.at[i], o_recv.at[i], place(dp=at.sibling()))
        core_other[i].start()

    def arrive(i):
        @pl.when(at.section == 0)
        def _():
            core_own[i].wait_recv()

        @pl.when(at.section == 1)
        def _():
            core_other[i].wait_recv()

        load(i)

    ahead = 3
    for i in range(ahead):
        push_own(i)
    gain_copy.wait_recv()
    row_blocks(rows, first_norm)
    ins = sq.spread(normed_in, s_send.at[0], s_recv.at[0])

    def advance(i):
        pass_on(i)
        if i + ahead < 8:
            push_own(i + ahead)
        if i > 0:
            share_other(i - 1)
            arrive(i - 1)

    advance(0)
    downs = sq.spread_from(v.out_grad, v.grad_down, d_send, d_recv, d_sem)
    advance(1)
    for push in ins:
        push.wait_recv()
    late = jnp.logical_and(at.section == 1, at.core == 1)
    early = jnp.logical_not(late)
    turn_if(early, normed_in_t, normed_in)
    for i in range(2, 5):
        advance(i)
        for s in (sq.own, sq.next):
            project(i - 2, s)
    advance(5)
    for s in (sq.own, sq.next):
        project(3, s)
    retain(sq.next)
    loads_wait(4)
    give_back(sq.next, merged, out_t)
    gives = give(1, 0)
    retain(sq.own)
    give_back(sq.own, merged, out_t)
    gives += give(0, 0)
    advance(6)
    for push in gives:
        push.wait_recv()
    row_blocks(rows, second_norm)
    mids = sq.spread(normed_mid, s_send.at[1], s_recv.at[1])
    advance(7)
    for push in mids:
        push.wait_recv()
    turn_if(early, normed_mid_t, normed_mid)
    feed(sq.next)
    feed(sq.own)
    for push in gives:
        push.wait_send()

    def last_group():
        for j in range(slices):
            x_copies[7, j].wait_recv()
        core_other[7].start()

    theirs = block(7, other, at.core)
    core_other[7] = copy(theirs, theirs, o_send.at[7], o_recv.at[7], place(dp=at.sibling()))

    @pl.when(at.section == 1)
    def _():
        last_group()

    arrive(7)
    loads_wait(7)
    turn_if(late, normed_in_t, normed_in)
    turn_if(late, normed_mid_t, normed_mid)
    give_back(sq.next, hidden, down_t)
    ends = give(1, 1)
    give_back(sq.own, hidden, down_t)
    ends += give(0, 1)

    @pl.when(at.section == 0)
    def _():
        last_group()

    for push in ends:
        push.wait_recv()

    def last(block):
        result[block] = (middle[block] + collected(block, 1)).astype(bf16)

    row_blocks(rows, last)

    @pl.when(at.section == 0)
    def _():
        for i in range(8):
            core_other[i].wait_recv()

    @pl.when(at.section == 1)
    def _():
        for i in range(8):
            core_own[i].wait_recv()

    for push in downs:
        push.wait()
    for push in ins + mids + ends + list(z_copies.values()) + list(x_copies.values()):
        push.wait_send()
    for i in range(8):
        core_own[i].wait_send()
        core_other[i].wait_send()
    gain_copy.wait_send()


def forward_layer(layer, x, gains, tables, masks, weights, dp_size, out_grad=None):
    rows, width = x.shape
    length = masks.shape[-1]
    heads = masks.shape[1]
    streams = layer == 0
    slices = dp_size // 2
    quarter_k = heads * HEAD_K
    quarter_v = heads * HEAD_V
    quarter_f = weights[-1].shape[-1] // 2 if streams else weights[-1].shape[-1]
    vmem = pl.BlockSpec(memory_space=pltpu.VMEM)
    any_spec = pl.BlockSpec(memory_space=pl.ANY)
    wides = (2 * quarter_k + 2 * quarter_v, quarter_v, 2 * quarter_f, quarter_f)

    def tokens(wide, kind=bf16):
        return jax.ShapeDtypeStruct((2, length, wide), kind)

    turned = jax.ShapeDtypeStruct((width, 2 * length), bf16)
    dma = pltpu.SemaphoreType.DMA
    out_shape = [
        jax.ShapeDtypeStruct((rows, width), f32),
        turned,
        tokens(quarter_k),
        tokens(quarter_k),
        tokens(quarter_v),
        tokens(quarter_v),
        jax.ShapeDtypeStruct((2, heads, length, 1), f32),
        tokens(quarter_v),
        tokens(quarter_v),
        tokens(quarter_v),
        turned if streams else tokens(width),
        tokens(quarter_f),
        tokens(quarter_f),
        tokens(quarter_f),
    ]
    out_specs = [vmem] * len(out_shape)
    scratch = [pltpu.VMEM((slices, 2, width // dp_size, wide), bf16) for wide in wides] + [
        dma((8,)),
    ] + [pltpu.VMEM((2, length, width), bf16)] * (3 if streams else 2) + [
        pltpu.VMEM((2, 3, rows, width), bf16),
        dma((2, 3)),
        dma((2, 3)),
        dma((2, 3)),
        dma((2, 3)),
    ]
    if streams:
        out_shape = (
            [jax.ShapeDtypeStruct((2, slices, 2, width // dp_size, wide), bf16) for wide in wides]
            + [jax.ShapeDtypeStruct((2,) + gains.shape, f32)]
            + out_shape
            + [tokens(width), jax.ShapeDtypeStruct((rows, width), bf16)]
        )
        out_specs = [any_spec] * 4 + [vmem] + out_specs + [any_spec, vmem]
        scratch += [
            dma((8, slices - 1)),
            dma((8, slices - 1)),
            dma((8, slices)),
            dma((8, slices)),
            dma((8,)),
            dma((8,)),
            dma((8,)),
            dma((8,)),
            dma((8,)),
            dma,
            dma,
            dma((3,)),
            dma((3,)),
            dma,
        ]
    operands = [x, gains, tables, masks] + ([out_grad] if streams else [])
    return pl.pallas_call(
        functools.partial(forward_kernel, dp_size, layer),
        out_shape=out_shape,
        in_specs=[vmem] * len(operands) + [any_spec] * len(weights),
        out_specs=out_specs,
        scratch_shapes=scratch,
        compiler_params=pltpu.CompilerParams(
            collective_id=1 + layer, has_side_effects=True, vmem_limit_bytes=VMEM_LIMIT
        ),
        name="forward_layer",
    )(*operands, *weights)


class Refs:
    pass


KEPT = 5
GROUPS = 7


def backward_kernel(dp_size, layer, *refs):
    final_layer = layer == 0
    v = Refs()
    (v.grad_out, v.gains, v.tables, v.masks, v.x, v.middle, v.normed_in_t, v.query_rot, v.key_rot, v.value, v.unit,
     v.inverse, v.opened, v.slope_open, v.merged, v.normed_mid_t, v.act, v.slope, v.hidden,
     v.qkvs_all, v.out_all, v.gate_up_all, v.down_all, v.down_in, *refs) = refs
    if final_layer:
        (v.later_chip, v.later_terms, v.first_rows, v.later_normed_in_t, v.later_qkvs, v.later_hidden, v.later_middle,
         *refs) = refs
    v.grad_in, v.chip, v.core_land, *refs = refs
    if final_layer:
        v.x_land, v.final, v.gain_sums, v.result, v.taken_rows, v.taken_grads, *refs = refs
    else:
        v.terms, v.next_down, v.kept_qkvs, *refs = refs
    (v.big, v.out_t, v.query_v, v.key_v, v.value_v, v.wide_a, v.wide_b, v.wide_c, v.inverse_v, v.x_v, v.middle_v,
     v.normed_t, v.outer, v.grad_down, v.grad_gate_up, v.grad_branch, v.grad_qkvs, v.turned, v.parts, v.landed,
     v.grad_middle, v.stage_given, v.stage_own, v.core_part, v.load_sem, v.s_send, v.s_recv, v.g_send, v.g_recv,
     v.c_send, v.c_recv, v.local_sem, *refs) = refs
    if final_layer:
        (v.left, v.right, v.sums, v.r_sem, v.x_send, v.x_recv, v.z_send, v.z_recv, v.terms, v.held, v.hop_land,
         v.t_send, v.t_recv, v.row_send, v.row_recv, v.landed_y) = refs
    else:
        v.d_send, v.d_recv, v.d_sem, v.kept_sem, v.mid_v = refs
    at = Place(dp_size)
    rows, width = v.x.shape
    sq = Square(dp_size, rows)
    masks, tables, gains = v.masks, v.tables, v.gains
    query_v, key_v, value_v = v.query_v, v.key_v, v.value_v
    wide_a, wide_b, wide_c = v.wide_a, v.wide_b, v.wide_c
    grad_down, grad_gate_up, grad_branch, grad_qkvs = v.grad_down, v.grad_gate_up, v.grad_branch, v.grad_qkvs
    big, out_t, outer, parts, landed, terms = v.big, v.out_t, v.outer, v.parts, v.landed, v.terms
    wide_k = query_v.shape[-1]
    wide_v = value_v.shape[-1]
    wide_f = outer.shape[-1]
    heads = wide_k // HEAD_K
    slices = dp_size // 2
    slice_rows = width // dp_size
    gain_in = gains[layer, 0:1]
    gain_mid = gains[layer, 1:2]
    other = 1 - at.section
    steps = [(k, b) for k in range(at.groups) for b in range(2)]
    steps = steps[1:] + steps[:1]

    def load(index, source, target):
        copy = pltpu.make_async_copy(source, target, v.load_sem.at[index])
        copy.start()
        return copy

    def remote(src, dst, send, recv, device):
        return pltpu.make_async_remote_copy(
            src_ref=src, dst_ref=dst, send_sem=send, recv_sem=recv, device_id=device, device_id_type=MESH
        )

    def place(section=None, dp=None, tensor=None):
        return (
            at.section if section is None else section,
            at.dp if dp is None else dp,
            at.tensor if tensor is None else tensor,
        )

    sibling = place(dp=at.sibling())
    across = place(section=other)

    token_load = load(14, v.down_in, grad_down)
    down_load = load(0, v.down_all.at[layer], big.at[:, pl.ds(2 * wide_f, wide_f)])
    act_load = load(1, v.act, wide_a)
    slope_load = load(2, v.slope, wide_b)
    gate_load = load(3, v.gate_up_all.at[layer], big.at[:, pl.ds(0, 2 * wide_f)])
    hidden_load = load(4, v.hidden, outer)
    mid_load = load(5, v.normed_mid_t, v.normed_t if final_layer else v.mid_v)
    early = [
        load(6, v.middle, v.middle_v),
        load(7, v.x, v.x_v),
        load(8, v.out_all.at[layer], out_t),
        load(9, v.query_rot, query_v),
        load(10, v.key_rot, key_v),
        load(11, v.value, value_v),
        load(12, v.inverse, v.inverse_v),
        load(13, v.opened, wide_c),
    ]
    terms[...] = jnp.zeros_like(terms)

    partners = [sq.device(*step) for step in SQUARE] + [sibling]
    if final_layer:
        partners.append(across)
        partners += [place(dp=at.dp_at(k, b)) for k, b in steps[:-1] if (k, b) != (0, 1)]
    barrier = pltpu.get_barrier_semaphore()
    for partner in partners:
        pl.semaphore_signal(barrier, inc=1, device_id=partner, device_id_type=MESH)
    pl.semaphore_wait(barrier, len(partners))

    def x_copy(e, at_source, j, source):
        block = source.at[at_source, j]
        return remote(block, v.x_land.at[e, j], v.x_send.at[e, j], v.x_recv.at[e, j], across)

    def start_x(e, at_source, source):
        @pl.loop(0, slices)
        def _(j):
            x_copy(e, at_source, j, source).start()

    row_copies = []
    if final_layer:

        @pl.when(at.section == 0)
        def _():
            @pl.loop(0, KEPT)
            def _(e):
                start_x(e, e, v.later_chip)

            remote(v.grad_out, v.taken_grads, v.row_send.at[1], v.row_recv.at[1], across).start()

        @pl.when(at.section == 1)
        def _():
            remote(v.first_rows, v.taken_rows, v.row_send.at[0], v.row_recv.at[0], across).start()

    def through_down(s):
        tokens = grad_down[s]
        for start in range(0, wide_f, TILE):
            cols = slice(start, start + TILE)
            grad_hidden = mm(tokens, big[:, 2 * wide_f + start : 2 * wide_f + start + TILE])
            grad_gate_up[s, :, cols] = (grad_hidden * wide_b[s, :, cols].astype(f32)).astype(bf16)
            grad_gate_up[s, :, wide_f + start : wide_f + start + TILE] = (
                grad_hidden * wide_a[s, :, cols].astype(f32)
            ).astype(bf16)

    def give_back(s, source, weight, first, size, target):
        tokens = source[s]
        for start in range(0, width, TILE):
            target[s, :, start : start + TILE] = mm_nt(
                tokens, weight[start : start + TILE, first : first + size]
            ).astype(bf16)

    def collected(block, given, land):
        total = sq.chunk(given)[block].astype(f32)
        for j in range(len(SQUARE)):
            total = total + land[j, block].astype(f32)
        return total

    def exchange(source, weight, first, size, target, land, which):
        give_back(sq.next, source, weight, first, size, target)
        send, recv = v.g_send.at[which], v.g_recv.at[which]
        pushes = [sq.give(target, land, send, recv, j) for j in (1, 2)]
        give_back(sq.own, source, weight, first, size, target)
        pushes.append(sq.give(target, land, send, recv, 0))
        return pushes

    members = [
        (v.turned, outer, 0, wide_f),
        (v.normed_t, grad_gate_up, 0, wide_f),
        (v.normed_t, grad_gate_up, wide_f, wide_f),
        (v.turned, outer, 0, wide_v),
        (v.normed_t, grad_qkvs, 0, 2 * wide_k),
        (v.normed_t, grad_qkvs, 2 * wide_k, wide_v),
        (v.normed_t, grad_qkvs, 2 * wide_k + wide_v, wide_v),
    ]
    members += members[KEPT:]
    given_copies, own_copies, fetches = {}, {}, {}

    def product(e, dp):
        left, right, first, size = members[e]
        start = pl.multiple_of(dp * slice_rows, slice_rows)
        wide = right[:, :, first : first + size].reshape(-1, size)
        return mm(left[pl.ds(start, slice_rows), :], wide)

    def given(e):
        if e >= 2:
            given_copies[e - 2].wait_send()
        stage = v.stage_given.at[e % 2]

        @pl.loop(0, slices)
        def _(j):
            stage[j] = product(e, j * 2 + 1 - at.core).astype(bf16)

        given_copies[e] = remote(stage, v.core_land.at[e], v.c_send.at[e], v.c_recv.at[e], sibling)
        given_copies[e].start()

    def fetch(e):
        given_copies[e].wait_recv()
        fetches[e] = pltpu.make_async_copy(v.core_land.at[e], v.core_part, v.local_sem.at[0])
        fetches[e].start()

    def settle(e):
        if e in settled:
            return
        settled.append(e)
        own_copies[e].wait()
        if final_layer:

            @pl.when(at.section == (1 if e < GROUPS else 0))
            def _():
                start_x(e if e < GROUPS else e - GROUPS + KEPT, e, v.chip)

    def own(e):
        if e >= 1:
            settle(e - 1)
        fetches[e].wait()

        @pl.loop(0, slices)
        def _(j):
            v.stage_own[j] = (product(e, j * 2 + at.core) + v.core_part[j].astype(f32)).astype(bf16)

        own_copies[e] = pltpu.make_async_copy(v.stage_own, v.chip.at[e], v.local_sem.at[1])
        own_copies[e].start()

    settled = []

    def index(k, b):
        return ((at.group + k) % at.groups) * 2 + (at.low + b) % 2

    def piece(e, k):
        start = pl.multiple_of(at.low * wide_f, wide_f)
        return v.final.at[e, k, :, pl.ds(start, wide_f)]

    def z_copy(e, j):
        k, b = steps[j]
        return remote(v.sums.at[j], piece(e, k), v.z_send.at[e, j], v.z_recv.at[e, j], place(dp=at.dp_at(k, b)))

    def home_copy(e):
        return pltpu.make_async_copy(v.sums.at[slices - 1], piece(e, 0), v.r_sem.at[2, 0])

    def reduce_slices(e, at_source, source, first, stop, wait_previous):
        def loads(j):
            here = index(*steps[j])
            return (
                pltpu.make_async_copy(source.at[at_source, here], v.left.at[j % 2], v.r_sem.at[0, j % 2]),
                pltpu.make_async_copy(v.x_land.at[e, here], v.right.at[j % 2], v.r_sem.at[1, j % 2]),
            )

        def begin(j):
            x_copy(e, at_source, index(*steps[j]), source).wait_recv()
            for copy in loads(j):
                copy.start()

        begin(first)
        for j in range(first, stop):
            if j + 1 < stop:
                begin(j + 1)
            for copy in loads(j):
                copy.wait()

            @pl.when(wait_previous)
            def _():
                if j == slices - 1:
                    home_copy(e).wait()
                else:
                    z_copy(e - 1, j).wait_send()

            v.sums[j] = (v.left[j % 2].astype(f32) + v.right[j % 2].astype(f32)).astype(bf16)
            if j == slices - 1:
                home_copy(e).start()
            else:
                z_copy(e, j).start()

    reduced = [0, 0]

    def source_of(section, e):
        if section == 0:
            return e, v.chip
        return (e, v.later_chip) if e < KEPT else (e + GROUPS - KEPT, v.chip)

    def reduce_some(section, count):
        if not final_layer:
            return

        @pl.when(at.section == section)
        def _():
            done = reduced[section]
            while done < reduced[section] + count:
                e, first = divmod(done, slices)
                stop = min(slices, first + reduced[section] + count - done)
                reduce_slices(e, *source_of(section, e), first, stop, e > 0)
                done += stop - first

        reduced[section] += count

    def reduce_rest(section):
        e, first = divmod(reduced[section], slices)

        @pl.when(at.section == section)
        def _():
            begin = e
            if first > 0:
                reduce_slices(e, *source_of(section, e), first, slices, e > 0)
                begin = e + 1
            same = KEPT if section == 1 else GROUPS

            @pl.loop(begin, same)
            def _(i):
                reduce_slices(i, i, source_of(section, 0)[1], 0, slices, i > 0)

            for i in range(same, GROUPS):
                reduce_slices(i, *source_of(section, i), 0, slices, True)

    token_load.wait()
    if final_layer:
        hidden_load.wait()
        transpose_into(v.turned, grad_down)
        given(0)
    down_load.wait()
    act_load.wait()
    slope_load.wait()
    through_down(sq.next)
    through_down(sq.own)
    if final_layer:
        fetch(0)
        own(0)
        mid_load.wait()
        settle(0)
    unit_load = load(1, v.unit, wide_a)
    bend_load = load(2, v.slope_open, wide_b)
    gate_load.wait()
    gives = exchange(grad_gate_up, big, 0, 2 * wide_f, parts, landed, 0)
    if not final_layer:
        hidden_load.wait()
        transpose_into(v.turned, grad_down)
        given(0)
        fetch(0)
        own(0)
        mid_load.wait()
        transpose_into(v.normed_t, v.mid_v)
        settle(0)
    given(1)
    qkvs_load = load(3, v.qkvs_all.at[layer], big)
    merged_load = load(4, v.merged, outer)
    for copy in early:
        copy.wait()
    for push in gives:
        push.wait_recv()

    def through_mid(block):
        upstream = collected(block, parts, landed)
        normed, scale = norm_parts(v.middle_v[block])
        grad_rows = v.grad_out[block].astype(f32) + norm_grad(normed, scale, upstream, gain_mid)
        v.grad_middle[block] = grad_rows
        sq.chunk(grad_branch)[block] = grad_rows.astype(bf16)
        terms[1:2] = terms[1:2] + jnp.sum(upstream * normed, axis=0, keepdims=True)

    row_blocks(rows, through_mid)
    mids = sq.spread(grad_branch, v.s_send, v.s_recv)
    reduce_some(0, 1)
    given(2)
    fetch(1)
    own(1)
    unit_load.wait()
    bend_load.wait()
    settle(1)
    reduce_some(1, slices)
    reduce_some(0, 1)

    def through_heads(s):
        tokens = grad_branch[s]
        for head in range(heads):
            cols_k = slice(head * HEAD_K, (head + 1) * HEAD_K)
            cols_v = slice(head * HEAD_V, (head + 1) * HEAD_V)
            grad_merged = mm(tokens, out_t[:, cols_v])
            unit_rows = wide_a[s, :, cols_v].astype(f32)
            first = 2 * wide_k + wide_v + head * HEAD_V
            grad_qkvs[s, :, first : first + HEAD_V] = (
                grad_merged * unit_rows * wide_b[s, :, cols_v].astype(f32)
            ).astype(bf16)
            grad_unit = grad_merged * wide_c[s, :, cols_v].astype(f32)
            grad_mixed = (
                v.inverse_v[s, head]
                * (
                    grad_unit
                    - jnp.mean(grad_unit, axis=-1, keepdims=True)
                    - unit_rows * jnp.mean(grad_unit * unit_rows, axis=-1, keepdims=True)
                )
            ).astype(bf16)
            query, key, val = query_v[s, :, cols_k], key_v[s, :, cols_k], value_v[s, :, cols_v]
            mask = masks[s, head]
            weight = (mm_nt(query, key) * mask).astype(bf16)
            grad_product = (mm_nt(grad_mixed, val) * mask).astype(bf16)
            first = 2 * wide_k + head * HEAD_V
            grad_qkvs[s, :, first : first + HEAD_V] = mm_tn(weight, grad_mixed).astype(bf16)
            grad_qkvs[s, :, cols_k] = turn_back(mm(grad_product, key), tables[0], tables[1], tables[2]).astype(bf16)
            first = wide_k + head * HEAD_K
            grad_qkvs[s, :, first : first + HEAD_K] = turn_back(
                mm_tn(grad_product, query), tables[0], tables[1], tables[3]
            ).astype(bf16)

    mids[0].wait_recv()
    through_heads(sq.own)
    mids[1].wait_recv()
    mids[2].wait_recv()
    through_heads(sq.next)
    if not final_layer:
        keep = pltpu.make_async_copy(grad_qkvs, v.kept_qkvs, v.kept_sem)
        keep.start()
    qkvs_load.wait()
    reduce_some(0, 1)
    for push in gives:
        push.wait_send()
    ends = exchange(grad_qkvs, big, 0, grad_qkvs.shape[-1], parts, landed, 1)
    fetch(2)
    own(2)
    in_load = load(5, v.normed_in_t, v.normed_t)
    transpose_into(v.turned, grad_branch)
    settle(2)
    merged_load.wait()
    given(3)
    in_load.wait()
    given(4)
    fetch(3)
    own(3)
    reduce_some(1, slices)
    reduce_some(0, 1)
    settle(3)
    for push in ends:
        push.wait_recv()

    def through_in(block):
        upstream = collected(block, parts, landed)
        normed, scale = norm_parts(v.x_v[block].astype(f32))
        v.grad_in[block] = (v.grad_middle[block] + norm_grad(normed, scale, upstream, gain_in)).astype(bf16)
        terms[0:1] = terms[0:1] + jnp.sum(upstream * normed, axis=0, keepdims=True)

    row_blocks(rows, through_in)
    if final_layer:

        @pl.when(at.section == 1)
        def _():
            remote(v.grad_in, v.taken_grads, v.row_send.at[1], v.row_recv.at[1], across).start()

    else:
        downs = sq.spread_from(v.grad_in, v.next_down, v.d_send, v.d_recv, v.d_sem)

    if not final_layer:
        fetch(4)
        own(4)
        settle(4)
        for push in mids + ends:
            push.wait_send()
        for e in (3, 4):
            given_copies[e].wait_send()
        for push in downs:
            push.wait()
        keep.wait()
        return

    reduce_some(0, 1)
    given(5)
    fetch(4)
    own(4)
    reduce_some(0, 1)
    given(6)
    settle(4)
    reduce_some(1, slices)
    reduce_some(0, 1)
    fetch(5)
    own(5)
    reduce_some(0, 1)
    fetch(6)
    own(6)
    in_load = load(5, v.later_normed_in_t, v.normed_t)
    qkvs_load = load(3, v.later_qkvs, grad_qkvs)
    hidden_load = load(4, v.later_hidden, outer)
    middle_load = load(6, v.later_middle, v.middle_v)
    down_load = load(0, v.down_all.at[1], big.at[:, pl.ds(2 * wide_f, wide_f)])
    settle(6)
    reduce_some(1, slices)
    reduce_some(0, 1)
    in_load.wait()
    qkvs_load.wait()
    given(7)
    reduce_some(0, 1)
    given(8)
    fetch(7)
    own(7)
    reduce_some(0, 1)
    fetch(8)
    own(8)
    settle(7)
    reduce_some(0, 1)
    for push in mids + ends:
        push.wait_send()
    hidden_load.wait()
    down_load.wait()
    settle(8)
    gives_y = exchange(outer, big, 2 * wide_f, wide_f, parts, v.landed_y, 2)
    reduce_some(1, slices)
    reduce_some(0, slices)
    middle_load.wait()
    for push in gives_y:
        push.wait_recv()

    def last(block):
        v.result[block] = (v.middle_v[block] + collected(block, parts, v.landed_y)).astype(bf16)

    row_blocks(rows, last)

    @pl.when(at.section == 0)
    def _():
        remote(v.result, v.taken_rows, v.row_send.at[0], v.row_recv.at[0], across).start()

    for push in gives_y:
        push.wait_send()
    for e in (7, 8):
        given_copies[e].wait_send()
    reduce_rest(1)
    reduce_rest(0)

    held, hop_land, mine = v.held, v.hop_land, v.held.at[at.section]
    held[0] = terms[...]
    held[1] = v.later_terms[...]
    hop = remote(held, hop_land.at[0], v.t_send.at[0], v.t_recv.at[0], sibling)
    hop.start()
    hop.wait()
    held[...] = held[...] + hop_land[0]
    hop = remote(held.at[other], hop_land.at[1, other], v.t_send.at[1], v.t_recv.at[1], across)
    hop.start()
    hop.wait_send()
    remote(held.at[other], hop_land.at[1, at.section], v.t_send.at[1], v.t_recv.at[1], across).wait_recv()
    mine[...] = mine[...] + hop_land[1, at.section]
    for h, device in ((2, place(tensor=1 - at.tensor)), (3, place(dp=at.dp_at(0, 1)))):
        hop = remote(mine, hop_land.at[h, 0], v.t_send.at[h], v.t_recv.at[h], device)
        hop.start()
        hop.wait()
        mine[...] = mine[...] + hop_land[h, 0]
    hops = []
    for k in range(1, at.groups):
        hop = remote(mine, hop_land.at[3 + k, 0], v.t_send.at[3 + k], v.t_recv.at[3 + k], place(dp=at.dp_at(k, 0)))
        hop.start()
        hops.append(hop)
    total = mine[...]
    for k, hop in zip(range(1, at.groups), hops):
        hop.wait()
        total = total + hop_land[3 + k, 0]
    v.gain_sums[...] = total

    for which, rows_sent in ((0, v.result), (1, v.grad_in)):
        target = v.taken_rows if which == 0 else v.taken_grads
        copy = remote(rows_sent, target, v.row_send.at[which], v.row_recv.at[which], across)
        copy.wait_recv()
        copy.wait_send()

    home_copy(0).wait()
    for j in range(slices - 1):
        z_copy(GROUPS - 1, j).wait_send()

        @pl.loop(0, GROUPS)
        def _(e):
            z_copy(e, j).wait_recv()

    @pl.loop(0, GROUPS)
    def _(e):
        @pl.loop(0, slices)
        def _(j):
            x_copy(e, e, j, v.chip).wait_send()


def backward_layer(layer, grad_out, down, x, gains, tables, masks, saved, gathered, dp_size, later=None, x_out=None):
    rows, width = x.shape
    length = masks.shape[-1]
    (middle, normed_in_t, query_rot, key_rot, value, unit, inverse, opened, slope_open, merged, normed_mid_t, act, slope,
     hidden) = saved
    vmem = pl.BlockSpec(memory_space=pltpu.VMEM)
    any_spec = pl.BlockSpec(memory_space=pl.ANY)
    final_layer = layer == 0
    slices = dp_size // 2
    slice_rows = width // dp_size
    size = hidden.shape[-1]
    assert value.shape[-1] == size and 2 * query_rot.shape[-1] == size
    block = (slices, slice_rows, size)

    def held(*shape, kind=bf16):
        return pltpu.VMEM(shape, kind)

    def stored(*shape, kind=bf16):
        return jax.ShapeDtypeStruct(shape, kind)

    dma = pltpu.SemaphoreType.DMA
    operands = [grad_out, gains, tables, masks]
    operands += [x, middle, normed_in_t, query_rot, key_rot, value, unit, inverse, opened, slope_open, merged, normed_mid_t,
                 act, slope, hidden]
    operands += [*gathered, down]
    in_specs = [vmem] * 4 + [any_spec] * (len(operands) - 4)
    count = 2 * GROUPS - KEPT if final_layer else KEPT
    out_shape = [stored(rows, width), stored(count, *block), stored(count, *block)]
    out_specs = [vmem, any_spec, any_spec]
    if final_layer:
        later_chip, later_terms, later_qkvs, later_saved = later
        operands += [later_chip, later_terms, x_out, later_saved[1], later_qkvs, later_saved[-1], later_saved[0]]
        in_specs += [any_spec, vmem] + [any_spec] * 5
        out_shape += [stored(GROUPS, *block), stored(GROUPS, dp_size // 4, slice_rows, 2 * size), stored(2, width, kind=f32),
                      stored(rows, width), stored(rows, width), stored(rows, width)]
        out_specs += [any_spec, any_spec, vmem, vmem, any_spec, any_spec]
    else:
        out_shape += [stored(2, width, kind=f32), stored(2, length, width), stored(2, length, 3 * size)]
        out_specs += [vmem, any_spec, any_spec]
    scratch = [
        held(width, 3 * size),
        held(width, size),
        held(*query_rot.shape),
        held(*key_rot.shape),
        held(*value.shape),
        held(2, length, size),
        held(2, length, size),
        held(2, length, size),
        held(*inverse.shape, kind=f32),
        held(rows, width),
        held(rows, width, kind=f32),
        held(width, 2 * length),
        held(2, length, size),
        held(2, length, width),
        held(2, length, 2 * size),
        held(2, length, width),
        held(2, length, 3 * size),
        held(width, 2 * length),
        held(2, length, width),
        held(3, rows, width),
        held(rows, width, kind=f32),
        held(2, *block),
        held(*block),
        held(*block),
        dma((15,)),
        dma((3,)),
        dma((3,)),
        dma((3, 3)),
        dma((3, 3)),
        dma((count,)),
        dma((count,)),
        dma((2,)),
    ]
    if final_layer:
        hops = 3 + dp_size // 4
        scratch += [
            held(2, slice_rows, size),
            held(2, slice_rows, size),
            held(*block),
            dma((3, 2)),
            dma((GROUPS, slices)),
            dma((GROUPS, slices)),
            dma((GROUPS, slices - 1)),
            dma((GROUPS, slices - 1)),
            held(2, width, kind=f32),
            held(2, 2, width, kind=f32),
            held(hops, 2, 2, width, kind=f32),
            dma((hops,)),
            dma((hops,)),
            dma((2,)),
            dma((2,)),
            held(3, rows, width),
        ]
    else:
        scratch += [dma((3,)), dma((3,)), dma, dma, held(2, length, width)]
    return pl.pallas_call(
        functools.partial(backward_kernel, dp_size, layer),
        out_shape=out_shape,
        in_specs=in_specs,
        out_specs=out_specs,
        scratch_shapes=scratch,
        compiler_params=pltpu.CompilerParams(
            collective_id=4 + layer, has_side_effects=True, vmem_limit_bytes=VMEM_LIMIT
        ),
        name="backward_layer",
    )(*operands)


def nested(outs):
    return (*outs[:5], outs[5:-2], *outs[-2:])


def on_device(
    dp_size,
    layer_input,
    segment_ids,
    output_grad,
    query_weight,
    key_weight,
    value_weight,
    swish_weight,
    output_weight,
    gate_weight,
    up_weight,
    down_weight,
    mixer_gain,
    ffn_gain,
):
    at = Place(dp_size)
    section_first = at.section == 0
    rows_here, width = layer_input.shape[1:]
    length = segment_ids.shape[1]
    score_scale = HEAD_K ** (-0.5)

    quarter_k = query_weight.shape[2] // 2
    quarter_v = value_weight.shape[2] // 2
    quarter_f = gate_weight.shape[2] // 2
    heads_here = quarter_k // HEAD_K
    first_head = (at.tensor * 2 + at.low) * heads_here
    cosine, sine, growth = rotation_tables(length, HEAD_K // 2)

    ids_mine = lax.dynamic_index_in_dim(segment_ids, at.section, 0, keepdims=False)
    ids_pair = lax.ppermute(ids_mine, "dp", [(i, i ^ 2) for i in range(dp_size)])
    ids = jnp.where(at.low == 0, jnp.stack([ids_mine, ids_pair]), jnp.stack([ids_pair, ids_mine]))
    masks = decay_mask(ids, first_head, heads_here) * score_scale
    tables = jnp.stack([cosine, sine, growth, 1.0 / growth])

    first_in = lax.dynamic_index_in_dim(layer_input, at.section, 0, keepdims=False)
    out_grad = lax.dynamic_index_in_dim(output_grad, at.section, 0, keepdims=False)
    shards = (query_weight[0], key_weight[0], value_weight[0], swish_weight[0], output_weight[0].T, gate_weight[0],
              up_weight[0], down_weight[0].T)
    own_gains = jnp.concatenate([mixer_gain, ffn_gain], axis=0)
    *gathered, all_gains, first_saved, second_down, first_sent = nested(
        forward_layer(0, first_in, own_gains, tables, masks, shards, dp_size, out_grad)
    )
    second_saved = forward_layer(1, first_sent, all_gains, tables, masks, gathered, dp_size)
    gathered = [g.reshape(2, width, g.shape[-1]) for g in gathered]
    second_grad, later_chip, _, later_terms, first_down, later_qkvs = backward_layer(
        1, out_grad, second_down, first_sent, all_gains, tables, masks, second_saved, gathered, dp_size
    )
    first_grad, _, _, _, landed, my_gains, second_sent, taken_rows, taken_grads = backward_layer(
        0, second_grad, first_down, first_in, all_gains, tables, masks, first_saved, gathered, dp_size,
        (later_chip, later_terms, later_qkvs, second_saved), first_sent,
    )

    def by_layer(first, second, taken):
        return jnp.where(section_first, jnp.stack([first, taken]), jnp.stack([taken, second]))[None]

    def shard(e):
        return jnp.sum(landed[e].astype(f32), axis=0)

    def columns(e, start, size):
        step = landed.shape[-1] // 2
        part = jnp.concatenate([landed[e, :, :, p * step + start : p * step + start + size] for p in range(2)], axis=-1)
        return jnp.sum(part.astype(f32), axis=0)

    return (
        by_layer(first_sent, second_sent, taken_rows),
        by_layer(first_grad, second_grad, taken_grads),
        columns(4, 0, quarter_k)[None],
        columns(4, quarter_k, quarter_k)[None],
        shard(5)[None],
        shard(6)[None],
        shard(3).T[None],
        shard(1)[None],
        shard(2)[None],
        shard(0).T[None],
        my_gains[0][None],
        my_gains[1][None],
    )


def solution(mesh):
    in_specs = (
        P(None, ("dp", "tensor"), None),
        P(None, "dp"),
        P(None, ("dp", "tensor"), None),
        P("section", "dp", "tensor"),
        P("section", "dp", "tensor"),
        P("section", "dp", "tensor"),
        P("section", "dp", "tensor"),
        P("section", "tensor", "dp"),
        P("section", "dp", "tensor"),
        P("section", "dp", "tensor"),
        P("section", "tensor", "dp"),
        P("section", None),
        P("section", None),
    )
    out_specs = (
        P("section", None, ("dp", "tensor"), None),
        P("section", None, ("dp", "tensor"), None),
        P("section", "dp", "tensor"),
        P("section", "dp", "tensor"),
        P("section", "dp", "tensor"),
        P("section", "dp", "tensor"),
        P("section", "tensor", "dp"),
        P("section", "dp", "tensor"),
        P("section", "dp", "tensor"),
        P("section", "tensor", "dp"),
        P("section", None),
        P("section", None),
    )
    return jax.shard_map(
        functools.partial(on_device, mesh.shape["dp"]),
        mesh=mesh,
        in_specs=in_specs,
        out_specs=out_specs,
        check_vma=False,
    )
```

```python
import functools

import jax
import jax.numpy as jnp
from jax import lax
from jax.experimental import pallas as pl
from jax.experimental.pallas import tpu as pltpu
from jax.sharding import PartitionSpec as P

HEAD_K = 256
HEAD_V = 512
MESH = pl.DeviceIdType.MESH

epsilon = 1e-05
group_guard = 1.0
bf16 = jnp.bfloat16
f32 = jnp.float32


def rotation_tables(length, half_width):
    pair_index = jnp.arange(half_width).astype(f32)
    position = jnp.arange(length).astype(f32)[:, None]
    angle = position * jnp.exp(-jnp.log(10000.0) * pair_index / half_width)
    zeta = (pair_index / half_width + 0.4) / 1.4
    growth = jnp.exp(position / 512.0 * jnp.log(zeta))
    return (jnp.cos(angle), jnp.sin(angle), growth)


def decay_mask(segments, first_head, heads):
    length = segments.shape[-1]
    position = jnp.arange(length)
    earlier = position[:, None] >= position[None, :]
    same_doc = (segments[:, :, None] == segments[:, None, :]) & earlier[None]
    distance = jnp.maximum(position[:, None] - position[None, :], 0).astype(f32)
    head_index = (first_head + jnp.arange(heads)).astype(f32)
    log_rate = jnp.log(1.0 - jnp.exp2(-5.0 - head_index))
    decay = jnp.exp(log_rate[:, None, None] * distance[None])
    return jnp.where(same_doc[:, None], decay[None], 0.0)


class Place:
    def __init__(self, dp_size):
        self.groups = dp_size // 4
        self.section = lax.axis_index("section")
        self.dp = lax.axis_index("dp")
        self.tensor = lax.axis_index("tensor")
        self.core = self.dp % 2
        self.low = (self.dp // 2) % 2
        self.group = self.dp // 4

    def dp_at(self, group_step, low_step):
        group = (self.group + group_step + self.groups) % self.groups
        return (group * 2 + (self.low + low_step) % 2) * 2 + self.core

    def sibling(self):
        return self.dp + 1 - 2 * self.core


SQUARE = ((0, 1), (1, 0), (1, 1))
TILE = 512
VMEM_LIMIT = 63 * 1024 * 1024


def mm(left, right):
    return lax.dot_general(left, right, (((1,), (0,)), ((), ())), preferred_element_type=f32)


def mm_nt(left, right):
    return lax.dot_general(left, right, (((1,), (1,)), ((), ())), preferred_element_type=f32)


def mm_tn(left, right):
    return lax.dot_general(left, right, (((0,), (0,)), ((), ())), preferred_element_type=f32)


class Square:
    def __init__(self, dp_size, rows):
        self.at = Place(dp_size)
        self.rows = rows
        self.own = self.at.low
        self.next = 1 - self.at.low

    def device(self, low_step, tensor_step):
        return (self.at.section, self.at.dp_at(0, low_step), (self.at.tensor + tensor_step) % 2)

    def barrier(self):
        barrier = pltpu.get_barrier_semaphore()
        for step in SQUARE:
            pl.semaphore_signal(barrier, inc=1, device_id=self.device(*step), device_id_type=MESH)
        pl.semaphore_wait(barrier, len(SQUARE))

    def chunk(self, ref, low_step=0, tensor_step=0):
        start = pl.multiple_of((self.at.tensor + tensor_step) % 2 * self.rows, self.rows)
        return ref.at[(self.at.low + low_step) % 2, pl.ds(start, self.rows)]

    def copy(self, src, dst, send, recv, step):
        return pltpu.make_async_remote_copy(
            src_ref=src,
            dst_ref=dst,
            send_sem=send,
            recv_sem=recv,
            device_id=self.device(*step),
            device_id_type=MESH,
        )

    def spread(self, ref, send, recv):
        pushes = []
        for j, step in enumerate(SQUARE):
            push = self.copy(self.chunk(ref), self.chunk(ref), send.at[j], recv.at[j], step)
            push.start()
            pushes.append(push)
        return pushes

    def spread_from(self, own, ref, send, recv, here):
        local = pltpu.make_async_copy(own, self.chunk(ref), here)
        local.start()
        pushes = [local]
        for j, step in enumerate(SQUARE):
            push = self.copy(own, self.chunk(ref), send.at[j], recv.at[j], step)
            push.start()
            pushes.append(push)
        return pushes

    def give(self, parts, landed, send, recv, j):
        push = self.copy(self.chunk(parts, *SQUARE[j]), landed.at[j], send.at[j], recv.at[j], SQUARE[j])
        push.start()
        return push


def row_blocks(rows, body, block=32):
    block = min(block, rows)

    @pl.loop(0, rows // block)
    def _(i):
        body(pl.ds(pl.multiple_of(i * block, block), block))


def norm_parts(values):
    centred = values - jnp.mean(values, axis=-1, keepdims=True)
    scale = lax.rsqrt(jnp.mean(centred * centred, axis=-1, keepdims=True) + epsilon)
    return centred * scale, scale


def norm_grad(normed, scale, upstream, gain):
    through = upstream * gain
    return scale * (
        through
        - jnp.mean(through, axis=-1, keepdims=True)
        - normed * jnp.mean(through * normed, axis=-1, keepdims=True)
    )


def turn(values, cosine, sine, scale):
    half = values.shape[-1] // 2
    a, b = values[:, :half], values[:, half:]
    return jnp.concatenate([(a * cosine - b * sine) * scale, (a * sine + b * cosine) * scale], axis=-1)


def turn_back(values, cosine, sine, scale):
    half = values.shape[-1] // 2
    a, b = values[:, :half] * scale, values[:, half:] * scale
    return jnp.concatenate([a * cosine + b * sine, b * cosine - a * sine], axis=-1)


def transpose_into(target, source):
    _, length, width = source.shape
    for s in range(2):
        for start in range(0, width, TILE):
            target[start : start + TILE, s * length : (s + 1) * length] = source[s, :, start : start + TILE].T


def forward_kernel(dp_size, layer, *refs):
    streams = layer == 0
    v = Refs()
    if streams:
        (v.x, v.own_gains, v.tables, v.masks, v.out_grad, *refs) = refs
        shards, refs = refs[:8], refs[8:]
        stored, refs = refs[:4], refs[4:]
        (v.gains, *refs) = refs
    else:
        (v.x, v.gains, v.tables, v.masks, *refs) = refs
        stored, refs = refs[:4], refs[4:]
    saved, refs = refs[:14], refs[14:]
    if streams:
        (v.grad_down, result, *refs) = refs
    scratch, refs = refs[:14], refs[14:]
    (middle, normed_in_t, query_rot, key_rot, value, unit, inverse, opened, slope_open, merged, normed_mid_t, act, slope,
     hidden) = scratch
    save_sem, x_v, masks, tables, in_sem, *refs = refs
    held, refs = refs[:4], refs[4:]
    (w_sem, normed_in, *refs) = refs
    if streams:
        (normed_mid, *refs) = refs
    else:
        normed_mid = normed_mid_t
    (parts, landed, s_send, s_recv, g_send, g_recv, *refs) = refs
    x = x_v
    rows, width = x.shape
    sq = Square(dp_size, rows)
    at = sq.at
    operand_copies = [
        pltpu.make_async_copy(source, target, in_sem.at[i])
        for i, (source, target) in enumerate(((v.x, x_v), (v.tables, tables), (v.masks, masks)))
    ]
    for copy in operand_copies:
        copy.start()
    operand_copies[0].wait()
    saves = []

    def save(*which):
        for i in which:
            copy = pltpu.make_async_copy(scratch[i], saved[i], save_sem.at[i])
            copy.start()
            saves.append(copy)

    qkvs, out_t, gate_up, down_t = held
    wide_k = query_rot.shape[-1]
    wide_v = value.shape[-1]
    wide_f = hidden.shape[-1]
    heads = wide_k // HEAD_K
    slices = dp_size // 2
    other = 1 - at.section
    groups = [(0, 0, wide_k), (0, wide_k, wide_k), (0, 2 * wide_k, wide_v), (0, 2 * wide_k + wide_v, wide_v),
              (1, 0, wide_v), (2, 0, wide_f), (2, wide_f, wide_f), (3, 0, wide_f)]
    loads = {}

    def load(i):
        which, first, size = groups[i]
        columns = pl.ds(first, size)
        loads[i] = pltpu.make_async_copy(
            stored[which].at[layer, :, :, :, columns], held[which].at[:, :, :, columns], w_sem.at[i]
        )
        loads[i].start()

    def weight(which, first, size):
        return held[which][:, :, :, first : first + size].reshape(width, size)

    def first_norm(block):
        unit_rows, _ = norm_parts(x[block].astype(f32))
        sq.chunk(normed_in)[block] = (unit_rows * v.gains[layer, 0:1]).astype(bf16)

    def project(i, s):
        loads_wait(i)
        first, size = groups[i][1:]
        tokens = normed_in[s]
        for start in range(0, size, TILE):
            wide = mm(tokens, weight(0, first + start, TILE))
            cols = slice(start, start + TILE)
            if i < 2:
                dest = (query_rot, key_rot)[i]
                for head in range(TILE // HEAD_K):
                    part = wide[:, head * HEAD_K : (head + 1) * HEAD_K]
                    dest[s, :, start + head * HEAD_K : start + (head + 1) * HEAD_K] = turn(
                        part, tables[0], tables[1], tables[2 + i]
                    ).astype(bf16)
            elif i == 2:
                value[s, :, cols] = wide.astype(bf16)
            else:
                sigmoid = 1.0 / (1.0 + jnp.exp(-wide))
                opened[s, :, cols] = (wide * sigmoid).astype(bf16)
                slope_open[s, :, cols] = (sigmoid * (1.0 + wide * (1.0 - sigmoid))).astype(bf16)

    waited = []

    def loads_wait(i):
        if i not in waited:
            waited.append(i)
            loads[i].wait()

    def retain(s):
        for head in range(heads):
            cols_k = slice(head * HEAD_K, (head + 1) * HEAD_K)
            cols_v = slice(head * HEAD_V, (head + 1) * HEAD_V)
            product = mm_nt(query_rot[s, :, cols_k], key_rot[s, :, cols_k])
            weights = (product * masks[s, head]).astype(bf16)
            mixed = mm(weights, value[s, :, cols_v])
            centred = mixed - jnp.mean(mixed, axis=-1, keepdims=True)
            scale = lax.rsqrt(jnp.mean(centred * centred, axis=-1, keepdims=True) + group_guard)
            unit_rows = centred * scale
            inverse[s, head] = scale
            unit[s, :, cols_v] = unit_rows.astype(bf16)
            merged[s, :, cols_v] = (unit_rows * opened[s, :, cols_v].astype(f32)).astype(bf16)

    def give_back(s, source, weight_t):
        tokens = source[s]
        step = width // slices
        for i in range(slices):
            parts[s, :, i * step : (i + 1) * step] = mm_nt(tokens, weight_t[i].reshape(step, -1)).astype(bf16)

    def collected(block, which):
        total = sq.chunk(parts)[block].astype(f32)
        for j in range(len(SQUARE)):
            total = total + landed[which, j, block].astype(f32)
        return total

    def give(s, which):
        send, recv = g_send.at[which], g_recv.at[which]
        return [sq.give(parts, landed.at[which], send, recv, j) for j in ((1, 2) if s == 1 else (0,))]

    def second_norm(block):
        middle_rows = x[block].astype(f32) + collected(block, 0)
        middle[block] = middle_rows
        unit_rows, _ = norm_parts(middle_rows)
        sq.chunk(normed_mid)[block] = (unit_rows * v.gains[layer, 1:2]).astype(bf16)

    def feed(s):
        loads_wait(5)
        loads_wait(6)
        tokens = normed_mid[s]
        for start in range(0, wide_f, TILE):
            cols = slice(start, start + TILE)
            gate = mm(tokens, weight(2, start, TILE))
            up = mm(tokens, weight(2, wide_f + start, TILE))
            square = gate * gate
            bend = jnp.tanh(0.7978845608028654 * gate * (1.0 + 0.044715 * square))
            half = 0.5 * (1.0 + bend)
            gelu = gate * half
            slope_gelu = half + 0.5 * gate * (1.0 - bend * bend) * (
                0.7978845608028654 * (1.0 + 3 * 0.044715 * square)
            )
            act[s, :, cols] = gelu.astype(bf16)
            slope[s, :, cols] = (slope_gelu * up).astype(bf16)
            hidden[s, :, cols] = (gelu * up).astype(bf16)

    def turn_if(condition, target, source):
        @pl.when(condition)
        def _():
            transpose_into(target, source)

    if not streams:
        for i in range(7):
            load(i)
        row_blocks(rows, first_norm)
        sq.barrier()
        ins = sq.spread(normed_in, s_send.at[0], s_recv.at[0])
        operand_copies[1].wait()
        operand_copies[2].wait()
        ins[0].wait_recv()
        for i in range(4):
            project(i, sq.own)
        ins[1].wait_recv()
        ins[2].wait_recv()
        turn_if(at.core == at.section, normed_in_t, normed_in)
        for i in range(4):
            project(i, sq.next)
        save(2, 3, 4, 7, 8)
        retain(sq.next)
        loads_wait(4)
        give_back(sq.next, merged, out_t)
        gives = give(1, 0)
        retain(sq.own)
        give_back(sq.own, merged, out_t)
        gives += give(0, 0)
        save(5, 6, 9)
        turn_if(at.core != at.section, normed_in_t, normed_in)
        save(1)
        for push in gives:
            push.wait_recv()
        row_blocks(rows, second_norm)
        save(0)
        mids = sq.spread(normed_mid, s_send.at[1], s_recv.at[1])
        mids[0].wait_recv()
        feed(sq.own)
        mids[1].wait_recv()
        mids[2].wait_recv()
        save(10)
        feed(sq.next)
        save(11, 12, 13)
        for push in ins + mids + gives:
            push.wait_send()
        for copy in saves:
            copy.wait()
        return

    (z_send, z_recv, x_send, x_recv, c_send, c_recv, o_send, o_recv, here_sem, gain_send, gain_recv, d_send, d_recv,
     d_sem) = refs
    steps = [(k, b) for k in range(at.groups) for b in range(2)][1:]

    def place(section=None, dp=None):
        return (at.section if section is None else section, at.dp if dp is None else dp, at.tensor)

    def copy(src, dst, send, recv, device):
        return pltpu.make_async_remote_copy(
            src_ref=src, dst_ref=dst, send_sem=send, recv_sem=recv, device_id=device, device_id_type=MESH
        )

    partners = [sq.device(*step) for step in SQUARE] + [place(dp=at.sibling()), place(section=other)]
    partners += [place(dp=at.dp_at(k, b)) for k, b in steps if (k, b) != (0, 1)]
    barrier = pltpu.get_barrier_semaphore()
    for partner in partners:
        pl.semaphore_signal(barrier, inc=1, device_id=partner, device_id_type=MESH)
    pl.semaphore_wait(barrier, len(partners))

    gain_copy = copy(v.own_gains, v.gains.at[at.section], gain_send, gain_recv, place(section=other))
    gain_copy.start()
    v.gains[at.section] = v.own_gains[...]

    def slot(i, section, dp):
        which, first, size = groups[i]
        return stored[which].at[section, dp // 2, dp % 2, :, pl.ds(first, size)]

    def block(i, section, core):
        which, first, size = groups[i]
        return stored[which].at[section, :, core, :, pl.ds(first, size)]

    def part(i, b):
        size = groups[i][2]
        return shards[i].at[:, pl.ds(pl.multiple_of((at.low + b) % 2 * size, size), size)]

    z_copies, x_copies, here, core_own, core_other = {}, {}, {}, {}, {}

    def push_own(i):
        mine = slot(i, at.section, at.dp)
        for j, (k, b) in enumerate(steps):
            z_copies[i, j] = copy(part(i, b), mine, z_send.at[i, j], z_recv.at[i, j], place(dp=at.dp_at(k, b)))
            z_copies[i, j].start()
        x_copies[i, 0] = copy(part(i, 0), mine, x_send.at[i, 0], x_recv.at[i, 0], place(section=other))
        x_copies[i, 0].start()
        here[i] = pltpu.make_async_copy(part(i, 0), mine, here_sem.at[i])
        here[i].start()

    def pass_on(i):
        for j, (k, b) in enumerate(steps):
            z_copies[i, j].wait_recv()
            arrived = slot(i, at.section, at.dp_at(-k, b))
            x_copies[i, j + 1] = copy(arrived, arrived, x_send.at[i, j + 1], x_recv.at[i, j + 1], place(section=other))
            x_copies[i, j + 1].start()
        here[i].wait()
        mine = block(i, at.section, at.core)
        core_own[i] = copy(mine, mine, c_send.at[i], c_recv.at[i], place(dp=at.sibling()))
        core_own[i].start()

    def share_other(i):
        for j in range(slices):
            x_copies[i, j].wait_recv()
        theirs = block(i, other, at.core)
        core_other[i] = copy(theirs, theirs, o_send.at[i], o_recv.at[i], place(dp=at.sibling()))
        core_other[i].start()

    def arrive(i):
        @pl.when(at.section == 0)
        def _():
            core_own[i].wait_recv()

        @pl.when(at.section == 1)
        def _():
            core_other[i].wait_recv()

        load(i)

    ahead = 3
    for i in range(ahead):
        push_own(i)
    gain_copy.wait_recv()
    row_blocks(rows, first_norm)
    ins = sq.spread(normed_in, s_send.at[0], s_recv.at[0])

    def advance(i):
        pass_on(i)
        if i + ahead < 8:
            push_own(i + ahead)
        if i > 0:
            share_other(i - 1)
            arrive(i - 1)

    advance(0)
    downs = sq.spread_from(v.out_grad, v.grad_down, d_send, d_recv, d_sem)
    advance(1)
    for push in ins:
        push.wait_recv()
    transpose_into(normed_in_t, normed_in)
    save(1)
    operand_copies[1].wait()
    operand_copies[2].wait()
    for i in range(2, 5):
        advance(i)
        for s in (sq.own, sq.next):
            project(i - 2, s)
    advance(5)
    for s in (sq.own, sq.next):
        project(3, s)
    retain(sq.next)
    loads_wait(4)
    give_back(sq.next, merged, out_t)
    gives = give(1, 0)
    retain(sq.own)
    give_back(sq.own, merged, out_t)
    gives += give(0, 0)
    advance(6)
    for push in gives:
        push.wait_recv()
    row_blocks(rows, second_norm)
    mids = sq.spread(normed_mid, s_send.at[1], s_recv.at[1])
    advance(7)
    for push in mids:
        push.wait_recv()
    transpose_into(normed_mid_t, normed_mid)
    save(0, 2, 3, 4, 5, 6, 7, 8, 9, 10)
    feed(sq.next)
    feed(sq.own)
    save(11, 12, 13)
    for push in gives:
        push.wait_send()

    def last_group():
        for j in range(slices):
            x_copies[7, j].wait_recv()
        core_other[7].start()

    theirs = block(7, other, at.core)
    core_other[7] = copy(theirs, theirs, o_send.at[7], o_recv.at[7], place(dp=at.sibling()))

    @pl.when(at.section == 1)
    def _():
        last_group()

    arrive(7)
    loads_wait(7)
    give_back(sq.next, hidden, down_t)
    ends = give(1, 1)
    give_back(sq.own, hidden, down_t)
    ends += give(0, 1)

    @pl.when(at.section == 0)
    def _():
        last_group()

    for push in ends:
        push.wait_recv()

    def last(block):
        result[block] = (middle[block] + collected(block, 1)).astype(bf16)

    row_blocks(rows, last)

    @pl.when(at.section == 0)
    def _():
        for i in range(8):
            core_other[i].wait_recv()

    @pl.when(at.section == 1)
    def _():
        for i in range(8):
            core_own[i].wait_recv()

    for push in downs:
        push.wait()
    for push in ins + mids + ends + list(z_copies.values()) + list(x_copies.values()):
        push.wait_send()
    for i in range(8):
        core_own[i].wait_send()
        core_other[i].wait_send()
    gain_copy.wait_send()
    for copy in saves:
        copy.wait()


def forward_layer(layer, x, gains, tables, masks, weights, dp_size, out_grad=None):
    rows, width = x.shape
    length = masks.shape[-1]
    heads = masks.shape[1]
    streams = layer == 0
    slices = dp_size // 2
    quarter_k = heads * HEAD_K
    quarter_v = heads * HEAD_V
    quarter_f = weights[-1].shape[-1] // 2 if streams else weights[-1].shape[-1]
    vmem = pl.BlockSpec(memory_space=pltpu.VMEM)
    any_spec = pl.BlockSpec(memory_space=pl.ANY)
    wides = (2 * quarter_k + 2 * quarter_v, quarter_v, 2 * quarter_f, quarter_f)

    def tokens(wide, kind=bf16):
        return jax.ShapeDtypeStruct((2, length, wide), kind)

    turned = jax.ShapeDtypeStruct((width, 2 * length), bf16)
    dma = pltpu.SemaphoreType.DMA
    out_shape = [
        jax.ShapeDtypeStruct((rows, width), f32),
        turned,
        tokens(quarter_k),
        tokens(quarter_k),
        tokens(quarter_v),
        tokens(quarter_v),
        jax.ShapeDtypeStruct((2, heads, length, 1), f32),
        tokens(quarter_v),
        tokens(quarter_v),
        tokens(quarter_v),
        turned if streams else tokens(width),
        tokens(quarter_f),
        tokens(quarter_f),
        tokens(quarter_f),
    ]
    out_specs = [any_spec] * len(out_shape)
    scratch = [pltpu.VMEM(out.shape, out.dtype) for out in out_shape]
    scratch += [dma((14,))] + [pltpu.VMEM(a.shape, a.dtype) for a in (x, masks, tables)] + [dma((3,))]
    scratch += [pltpu.VMEM((slices, 2, width // dp_size, wide), bf16) for wide in wides] + [
        dma((8,)),
    ] + [pltpu.VMEM((2, length, width), bf16)] * (3 if streams else 2) + [
        pltpu.VMEM((2, 3, rows, width), bf16),
        dma((2, 3)),
        dma((2, 3)),
        dma((2, 3)),
        dma((2, 3)),
    ]
    if streams:
        out_shape = (
            [jax.ShapeDtypeStruct((2, slices, 2, width // dp_size, wide), bf16) for wide in wides]
            + [jax.ShapeDtypeStruct((2,) + gains.shape, f32)]
            + out_shape
            + [tokens(width), jax.ShapeDtypeStruct((rows, width), bf16)]
        )
        out_specs = [any_spec] * 4 + [vmem] + out_specs + [any_spec, vmem]
        scratch += [
            dma((8, slices - 1)),
            dma((8, slices - 1)),
            dma((8, slices)),
            dma((8, slices)),
            dma((8,)),
            dma((8,)),
            dma((8,)),
            dma((8,)),
            dma((8,)),
            dma,
            dma,
            dma((3,)),
            dma((3,)),
            dma,
        ]
    operands = [x, gains, tables, masks] + ([out_grad] if streams else [])
    return pl.pallas_call(
        functools.partial(forward_kernel, dp_size, layer),
        out_shape=out_shape,
        in_specs=[any_spec, vmem, any_spec, any_spec] + [vmem] * (len(operands) - 4) + [any_spec] * len(weights),
        out_specs=out_specs,
        scratch_shapes=scratch,
        compiler_params=pltpu.CompilerParams(
            collective_id=1 + layer, has_side_effects=True, vmem_limit_bytes=VMEM_LIMIT
        ),
        name="forward_layer",
    )(*operands, *weights)


class Refs:
    pass


KEPT = 5
GROUPS = 7


def backward_kernel(dp_size, layer, *refs):
    final_layer = layer == 0
    v = Refs()
    (v.grad_out, v.gains, v.tables, v.masks, v.x, v.middle, v.normed_in_t, v.query_rot, v.key_rot, v.value, v.unit,
     v.inverse, v.opened, v.slope_open, v.merged, v.normed_mid_t, v.act, v.slope, v.hidden,
     v.qkvs_all, v.out_all, v.gate_up_all, v.down_all, v.down_in, *refs) = refs
    if final_layer:
        (v.later_chip, v.later_terms, v.first_rows, v.later_normed_in_t, v.later_qkvs, v.later_hidden, v.later_middle,
         *refs) = refs
    v.grad_in, v.chip, v.core_land, *refs = refs
    if final_layer:
        v.x_land, v.final, v.gain_sums, v.result, v.taken_rows, v.taken_grads, *refs = refs
    else:
        v.terms, v.next_down, v.kept_qkvs, *refs = refs
    (v.big, v.out_t, v.query_v, v.key_v, v.value_v, v.wide_a, v.wide_b, v.wide_c, v.inverse_v, v.x_v, v.middle_v,
     v.normed_t, v.outer, v.grad_down, v.grad_gate_up, v.grad_branch, v.grad_qkvs, v.turned, v.parts, v.landed,
     v.grad_middle, v.stage_given, v.stage_own, v.core_part, v.load_sem, v.s_send, v.s_recv, v.g_send, v.g_recv,
     v.c_send, v.c_recv, v.local_sem, v.masks_v, v.tables_v, v.grad_out_v, *refs) = refs
    if final_layer:
        (v.left, v.right, v.sums, v.r_sem, v.x_send, v.x_recv, v.z_send, v.z_recv, v.terms, v.held, v.hop_land,
         v.t_send, v.t_recv, v.row_send, v.row_recv, v.landed_y) = refs
    else:
        v.d_send, v.d_recv, v.d_sem, v.kept_sem, v.mid_v = refs
    at = Place(dp_size)
    rows, width = v.x.shape
    sq = Square(dp_size, rows)
    masks, tables, gains = v.masks_v, v.tables_v, v.gains
    query_v, key_v, value_v = v.query_v, v.key_v, v.value_v
    wide_a, wide_b, wide_c = v.wide_a, v.wide_b, v.wide_c
    grad_down, grad_gate_up, grad_branch, grad_qkvs = v.grad_down, v.grad_gate_up, v.grad_branch, v.grad_qkvs
    big, out_t, outer, parts, landed, terms = v.big, v.out_t, v.outer, v.parts, v.landed, v.terms
    wide_k = query_v.shape[-1]
    wide_v = value_v.shape[-1]
    wide_f = outer.shape[-1]
    heads = wide_k // HEAD_K
    slices = dp_size // 2
    slice_rows = width // dp_size
    gain_in = gains[layer, 0:1]
    gain_mid = gains[layer, 1:2]
    other = 1 - at.section
    steps = [(k, b) for k in range(at.groups) for b in range(2)]
    steps = steps[1:] + steps[:1]

    def load(index, source, target):
        copy = pltpu.make_async_copy(source, target, v.load_sem.at[index])
        copy.start()
        return copy

    def remote(src, dst, send, recv, device):
        return pltpu.make_async_remote_copy(
            src_ref=src, dst_ref=dst, send_sem=send, recv_sem=recv, device_id=device, device_id_type=MESH
        )

    def place(section=None, dp=None, tensor=None):
        return (
            at.section if section is None else section,
            at.dp if dp is None else dp,
            at.tensor if tensor is None else tensor,
        )

    sibling = place(dp=at.sibling())
    across = place(section=other)

    token_load = load(14, v.down_in, grad_down)
    down_load = load(0, v.down_all.at[layer], big.at[:, pl.ds(2 * wide_f, wide_f)])
    act_load = load(1, v.act, wide_a)
    slope_load = load(2, v.slope, wide_b)
    gate_load = load(3, v.gate_up_all.at[layer], big.at[:, pl.ds(0, 2 * wide_f)])
    hidden_load = load(4, v.hidden, outer)
    mid_load = load(5, v.normed_mid_t, v.normed_t if final_layer else v.mid_v)
    early = [
        load(6, v.middle, v.middle_v),
        load(7, v.x, v.x_v),
        load(8, v.out_all.at[layer], out_t),
        load(9, v.query_rot, query_v),
        load(10, v.key_rot, key_v),
        load(11, v.value, value_v),
        load(12, v.inverse, v.inverse_v),
        load(13, v.opened, wide_c),
        load(15, v.masks, masks),
        load(16, v.tables, tables),
        load(17, v.grad_out, v.grad_out_v),
    ]
    terms[...] = jnp.zeros_like(terms)

    partners = [sq.device(*step) for step in SQUARE] + [sibling]
    if final_layer:
        partners.append(across)
        partners += [place(dp=at.dp_at(k, b)) for k, b in steps[:-1] if (k, b) != (0, 1)]
    barrier = pltpu.get_barrier_semaphore()
    for partner in partners:
        pl.semaphore_signal(barrier, inc=1, device_id=partner, device_id_type=MESH)
    pl.semaphore_wait(barrier, len(partners))

    def x_copy(e, at_source, j, source):
        block = source.at[at_source, j]
        return remote(block, v.x_land.at[e, j], v.x_send.at[e, j], v.x_recv.at[e, j], across)

    def start_x(e, at_source, source):
        @pl.loop(0, slices)
        def _(j):
            x_copy(e, at_source, j, source).start()

    row_copies = []
    if final_layer:

        @pl.when(at.section == 0)
        def _():
            @pl.loop(0, KEPT)
            def _(e):
                start_x(e, e, v.later_chip)

            remote(v.grad_out, v.taken_grads, v.row_send.at[1], v.row_recv.at[1], across).start()

        @pl.when(at.section == 1)
        def _():
            remote(v.first_rows, v.taken_rows, v.row_send.at[0], v.row_recv.at[0], across).start()

    def through_down(s):
        tokens = grad_down[s]
        for start in range(0, wide_f, TILE):
            cols = slice(start, start + TILE)
            grad_hidden = mm(tokens, big[:, 2 * wide_f + start : 2 * wide_f + start + TILE])
            grad_gate_up[s, :, cols] = (grad_hidden * wide_b[s, :, cols].astype(f32)).astype(bf16)
            grad_gate_up[s, :, wide_f + start : wide_f + start + TILE] = (
                grad_hidden * wide_a[s, :, cols].astype(f32)
            ).astype(bf16)

    def give_back(s, source, weight, first, size, target):
        tokens = source[s]
        for start in range(0, width, TILE):
            target[s, :, start : start + TILE] = mm_nt(
                tokens, weight[start : start + TILE, first : first + size]
            ).astype(bf16)

    def collected(block, given, land):
        total = sq.chunk(given)[block].astype(f32)
        for j in range(len(SQUARE)):
            total = total + land[j, block].astype(f32)
        return total

    def exchange(source, weight, first, size, target, land, which):
        give_back(sq.next, source, weight, first, size, target)
        send, recv = v.g_send.at[which], v.g_recv.at[which]
        pushes = [sq.give(target, land, send, recv, j) for j in (1, 2)]
        give_back(sq.own, source, weight, first, size, target)
        pushes.append(sq.give(target, land, send, recv, 0))
        return pushes

    members = [
        (v.turned, outer, 0, wide_f),
        (v.normed_t, grad_gate_up, 0, wide_f),
        (v.normed_t, grad_gate_up, wide_f, wide_f),
        (v.turned, outer, 0, wide_v),
        (v.normed_t, grad_qkvs, 0, 2 * wide_k),
        (v.normed_t, grad_qkvs, 2 * wide_k, wide_v),
        (v.normed_t, grad_qkvs, 2 * wide_k + wide_v, wide_v),
    ]
    members += members[KEPT:]
    given_copies, own_copies, fetches = {}, {}, {}

    def product(e, dp):
        left, right, first, size = members[e]
        start = pl.multiple_of(dp * slice_rows, slice_rows)
        wide = right[:, :, first : first + size].reshape(-1, size)
        return mm(left[pl.ds(start, slice_rows), :], wide)

    def given(e):
        if e >= 2:
            given_copies[e - 2].wait_send()
        stage = v.stage_given.at[e % 2]

        @pl.loop(0, slices)
        def _(j):
            stage[j] = product(e, j * 2 + 1 - at.core).astype(bf16)

        given_copies[e] = remote(stage, v.core_land.at[e], v.c_send.at[e], v.c_recv.at[e], sibling)
        given_copies[e].start()

    def fetch(e):
        given_copies[e].wait_recv()
        fetches[e] = pltpu.make_async_copy(v.core_land.at[e], v.core_part, v.local_sem.at[0])
        fetches[e].start()

    def settle(e):
        if e in settled:
            return
        settled.append(e)
        own_copies[e].wait()
        if final_layer:

            @pl.when(at.section == (1 if e < GROUPS else 0))
            def _():
                start_x(e if e < GROUPS else e - GROUPS + KEPT, e, v.chip)

    def own(e):
        if e >= 1:
            settle(e - 1)
        fetches[e].wait()

        @pl.loop(0, slices)
        def _(j):
            v.stage_own[j] = (product(e, j * 2 + at.core) + v.core_part[j].astype(f32)).astype(bf16)

        own_copies[e] = pltpu.make_async_copy(v.stage_own, v.chip.at[e], v.local_sem.at[1])
        own_copies[e].start()

    settled = []

    def index(k, b):
        return ((at.group + k) % at.groups) * 2 + (at.low + b) % 2

    def piece(e, k):
        start = pl.multiple_of(at.low * wide_f, wide_f)
        return v.final.at[e, k, :, pl.ds(start, wide_f)]

    def z_copy(e, j):
        k, b = steps[j]
        return remote(v.sums.at[j], piece(e, k), v.z_send.at[e, j], v.z_recv.at[e, j], place(dp=at.dp_at(k, b)))

    def home_copy(e):
        return pltpu.make_async_copy(v.sums.at[slices - 1], piece(e, 0), v.r_sem.at[2, 0])

    def reduce_slices(e, at_source, source, first, stop, wait_previous):
        def loads(j):
            here = index(*steps[j])
            return (
                pltpu.make_async_copy(source.at[at_source, here], v.left.at[j % 2], v.r_sem.at[0, j % 2]),
                pltpu.make_async_copy(v.x_land.at[e, here], v.right.at[j % 2], v.r_sem.at[1, j % 2]),
            )

        def begin(j):
            x_copy(e, at_source, index(*steps[j]), source).wait_recv()
            for copy in loads(j):
                copy.start()

        begin(first)
        for j in range(first, stop):
            if j + 1 < stop:
                begin(j + 1)
            for copy in loads(j):
                copy.wait()

            @pl.when(wait_previous)
            def _():
                if j == slices - 1:
                    home_copy(e).wait()
                else:
                    z_copy(e - 1, j).wait_send()

            v.sums[j] = (v.left[j % 2].astype(f32) + v.right[j % 2].astype(f32)).astype(bf16)
            if j == slices - 1:
                home_copy(e).start()
            else:
                z_copy(e, j).start()

    reduced = [0, 0]

    def source_of(section, e):
        if section == 0:
            return e, v.chip
        return (e, v.later_chip) if e < KEPT else (e + GROUPS - KEPT, v.chip)

    def reduce_some(section, count):
        if not final_layer:
            return

        @pl.when(at.section == section)
        def _():
            done = reduced[section]
            while done < reduced[section] + count:
                e, first = divmod(done, slices)
                stop = min(slices, first + reduced[section] + count - done)
                reduce_slices(e, *source_of(section, e), first, stop, e > 0)
                done += stop - first

        reduced[section] += count

    def reduce_rest(section):
        e, first = divmod(reduced[section], slices)

        @pl.when(at.section == section)
        def _():
            begin = e
            if first > 0:
                reduce_slices(e, *source_of(section, e), first, slices, e > 0)
                begin = e + 1
            same = KEPT if section == 1 else GROUPS

            @pl.loop(begin, same)
            def _(i):
                reduce_slices(i, i, source_of(section, 0)[1], 0, slices, i > 0)

            for i in range(same, GROUPS):
                reduce_slices(i, *source_of(section, i), 0, slices, True)

    token_load.wait()
    if final_layer:
        hidden_load.wait()
        transpose_into(v.turned, grad_down)
        given(0)
    down_load.wait()
    act_load.wait()
    slope_load.wait()
    through_down(sq.next)
    through_down(sq.own)
    unit_load = load(1, v.unit, wide_a)
    bend_load = load(2, v.slope_open, wide_b)
    gate_load.wait()
    gives = exchange(grad_gate_up, big, 0, 2 * wide_f, parts, landed, 0)
    if not final_layer:
        hidden_load.wait()
        transpose_into(v.turned, grad_down)
        given(0)
    fetch(0)
    own(0)
    mid_load.wait()
    if not final_layer:
        transpose_into(v.normed_t, v.mid_v)
    settle(0)
    given(1)
    qkvs_load = load(3, v.qkvs_all.at[layer], big)
    merged_load = load(4, v.merged, outer)
    for copy in early:
        copy.wait()
    for push in gives:
        push.wait_recv()

    def through_mid(block):
        upstream = collected(block, parts, landed)
        normed, scale = norm_parts(v.middle_v[block])
        grad_rows = v.grad_out_v[block].astype(f32) + norm_grad(normed, scale, upstream, gain_mid)
        v.grad_middle[block] = grad_rows
        sq.chunk(grad_branch)[block] = grad_rows.astype(bf16)
        terms[1:2] = terms[1:2] + jnp.sum(upstream * normed, axis=0, keepdims=True)

    row_blocks(rows, through_mid)
    mids = sq.spread(grad_branch, v.s_send, v.s_recv)
    reduce_some(0, 1)
    given(2)
    fetch(1)
    own(1)
    unit_load.wait()
    bend_load.wait()
    settle(1)
    reduce_some(1, slices)
    reduce_some(0, 1)

    def through_heads(s):
        tokens = grad_branch[s]
        for head in range(heads):
            cols_k = slice(head * HEAD_K, (head + 1) * HEAD_K)
            cols_v = slice(head * HEAD_V, (head + 1) * HEAD_V)
            grad_merged = mm(tokens, out_t[:, cols_v])
            unit_rows = wide_a[s, :, cols_v].astype(f32)
            first = 2 * wide_k + wide_v + head * HEAD_V
            grad_qkvs[s, :, first : first + HEAD_V] = (
                grad_merged * unit_rows * wide_b[s, :, cols_v].astype(f32)
            ).astype(bf16)
            grad_unit = grad_merged * wide_c[s, :, cols_v].astype(f32)
            grad_mixed = (
                v.inverse_v[s, head]
                * (
                    grad_unit
                    - jnp.mean(grad_unit, axis=-1, keepdims=True)
                    - unit_rows * jnp.mean(grad_unit * unit_rows, axis=-1, keepdims=True)
                )
            ).astype(bf16)
            query, key, val = query_v[s, :, cols_k], key_v[s, :, cols_k], value_v[s, :, cols_v]
            mask = masks[s, head]
            weight = (mm_nt(query, key) * mask).astype(bf16)
            grad_product = (mm_nt(grad_mixed, val) * mask).astype(bf16)
            first = 2 * wide_k + head * HEAD_V
            grad_qkvs[s, :, first : first + HEAD_V] = mm_tn(weight, grad_mixed).astype(bf16)
            grad_qkvs[s, :, cols_k] = turn_back(mm(grad_product, key), tables[0], tables[1], tables[2]).astype(bf16)
            first = wide_k + head * HEAD_K
            grad_qkvs[s, :, first : first + HEAD_K] = turn_back(
                mm_tn(grad_product, query), tables[0], tables[1], tables[3]
            ).astype(bf16)

    mids[0].wait_recv()
    through_heads(sq.own)
    mids[1].wait_recv()
    mids[2].wait_recv()
    through_heads(sq.next)
    if not final_layer:
        keep = pltpu.make_async_copy(grad_qkvs, v.kept_qkvs, v.kept_sem)
        keep.start()
    qkvs_load.wait()
    reduce_some(0, 1)
    for push in gives:
        push.wait_send()
    ends = exchange(grad_qkvs, big, 0, grad_qkvs.shape[-1], parts, landed, 1)
    fetch(2)
    own(2)
    in_load = load(5, v.normed_in_t, v.normed_t)
    transpose_into(v.turned, grad_branch)
    settle(2)
    merged_load.wait()
    given(3)
    in_load.wait()
    given(4)
    fetch(3)
    own(3)
    reduce_some(1, slices)
    reduce_some(0, 1)
    settle(3)
    for push in ends:
        push.wait_recv()

    def through_in(block):
        upstream = collected(block, parts, landed)
        normed, scale = norm_parts(v.x_v[block].astype(f32))
        v.grad_in[block] = (v.grad_middle[block] + norm_grad(normed, scale, upstream, gain_in)).astype(bf16)
        terms[0:1] = terms[0:1] + jnp.sum(upstream * normed, axis=0, keepdims=True)

    row_blocks(rows, through_in)
    if final_layer:

        @pl.when(at.section == 1)
        def _():
            remote(v.grad_in, v.taken_grads, v.row_send.at[1], v.row_recv.at[1], across).start()

    else:
        downs = sq.spread_from(v.grad_in, v.next_down, v.d_send, v.d_recv, v.d_sem)

    if not final_layer:
        fetch(4)
        own(4)
        settle(4)
        for push in mids + ends:
            push.wait_send()
        for e in (3, 4):
            given_copies[e].wait_send()
        for push in downs:
            push.wait()
        keep.wait()
        return

    reduce_some(0, 1)
    given(5)
    fetch(4)
    own(4)
    reduce_some(0, 1)
    given(6)
    settle(4)
    reduce_some(1, slices)
    reduce_some(0, 1)
    fetch(5)
    own(5)
    reduce_some(0, 1)
    fetch(6)
    own(6)
    in_load = load(5, v.later_normed_in_t, v.normed_t)
    qkvs_load = load(3, v.later_qkvs, grad_qkvs)
    hidden_load = load(4, v.later_hidden, outer)
    middle_load = load(6, v.later_middle, v.middle_v)
    down_load = load(0, v.down_all.at[1], big.at[:, pl.ds(2 * wide_f, wide_f)])
    settle(6)
    reduce_some(1, slices)
    reduce_some(0, 1)
    in_load.wait()
    qkvs_load.wait()
    given(7)
    reduce_some(0, 1)
    given(8)
    fetch(7)
    own(7)
    reduce_some(0, 1)
    fetch(8)
    own(8)
    settle(7)
    reduce_some(0, 1)
    for push in mids + ends:
        push.wait_send()
    hidden_load.wait()
    down_load.wait()
    settle(8)
    gives_y = exchange(outer, big, 2 * wide_f, wide_f, parts, v.landed_y, 2)
    reduce_some(1, slices)
    reduce_some(0, slices)
    middle_load.wait()
    for push in gives_y:
        push.wait_recv()

    def last(block):
        v.result[block] = (v.middle_v[block] + collected(block, parts, v.landed_y)).astype(bf16)

    row_blocks(rows, last)

    @pl.when(at.section == 0)
    def _():
        remote(v.result, v.taken_rows, v.row_send.at[0], v.row_recv.at[0], across).start()

    for push in gives_y:
        push.wait_send()
    for e in (7, 8):
        given_copies[e].wait_send()
    reduce_rest(1)
    reduce_rest(0)

    held, hop_land, mine = v.held, v.hop_land, v.held.at[at.section]
    held[0] = terms[...]
    held[1] = v.later_terms[...]
    hop = remote(held, hop_land.at[0], v.t_send.at[0], v.t_recv.at[0], sibling)
    hop.start()
    hop.wait()
    held[...] = held[...] + hop_land[0]
    hop = remote(held.at[other], hop_land.at[1, other], v.t_send.at[1], v.t_recv.at[1], across)
    hop.start()
    hop.wait_send()
    remote(held.at[other], hop_land.at[1, at.section], v.t_send.at[1], v.t_recv.at[1], across).wait_recv()
    mine[...] = mine[...] + hop_land[1, at.section]
    for h, device in ((2, place(tensor=1 - at.tensor)), (3, place(dp=at.dp_at(0, 1)))):
        hop = remote(mine, hop_land.at[h, 0], v.t_send.at[h], v.t_recv.at[h], device)
        hop.start()
        hop.wait()
        mine[...] = mine[...] + hop_land[h, 0]
    hops = []
    for k in range(1, at.groups):
        hop = remote(mine, hop_land.at[3 + k, 0], v.t_send.at[3 + k], v.t_recv.at[3 + k], place(dp=at.dp_at(k, 0)))
        hop.start()
        hops.append(hop)
    total = mine[...]
    for k, hop in zip(range(1, at.groups), hops):
        hop.wait()
        total = total + hop_land[3 + k, 0]
    v.gain_sums[...] = total

    for which, rows_sent in ((0, v.result), (1, v.grad_in)):
        target = v.taken_rows if which == 0 else v.taken_grads
        copy = remote(rows_sent, target, v.row_send.at[which], v.row_recv.at[which], across)
        copy.wait_recv()
        copy.wait_send()

    home_copy(0).wait()
    for j in range(slices - 1):
        z_copy(GROUPS - 1, j).wait_send()

        @pl.loop(0, GROUPS)
        def _(e):
            z_copy(e, j).wait_recv()

    @pl.loop(0, GROUPS)
    def _(e):
        @pl.loop(0, slices)
        def _(j):
            x_copy(e, e, j, v.chip).wait_send()


def backward_layer(layer, grad_out, down, x, gains, tables, masks, saved, gathered, dp_size, later=None, x_out=None):
    rows, width = x.shape
    length = masks.shape[-1]
    (middle, normed_in_t, query_rot, key_rot, value, unit, inverse, opened, slope_open, merged, normed_mid_t, act, slope,
     hidden) = saved
    vmem = pl.BlockSpec(memory_space=pltpu.VMEM)
    any_spec = pl.BlockSpec(memory_space=pl.ANY)
    final_layer = layer == 0
    slices = dp_size // 2
    slice_rows = width // dp_size
    size = hidden.shape[-1]
    assert value.shape[-1] == size and 2 * query_rot.shape[-1] == size
    block = (slices, slice_rows, size)

    def held(*shape, kind=bf16):
        return pltpu.VMEM(shape, kind)

    def stored(*shape, kind=bf16):
        return jax.ShapeDtypeStruct(shape, kind)

    dma = pltpu.SemaphoreType.DMA
    operands = [grad_out, gains, tables, masks]
    operands += [x, middle, normed_in_t, query_rot, key_rot, value, unit, inverse, opened, slope_open, merged, normed_mid_t,
                 act, slope, hidden]
    operands += [*gathered, down]
    in_specs = [any_spec, vmem] + [any_spec] * (len(operands) - 2)
    count = 2 * GROUPS - KEPT if final_layer else KEPT
    out_shape = [stored(rows, width), stored(count, *block), stored(count, *block)]
    out_specs = [vmem, any_spec, any_spec]
    if final_layer:
        later_chip, later_terms, later_qkvs, later_saved = later
        operands += [later_chip, later_terms, x_out, later_saved[1], later_qkvs, later_saved[-1], later_saved[0]]
        in_specs += [any_spec, vmem] + [any_spec] * 5
        out_shape += [stored(GROUPS, *block), stored(GROUPS, dp_size // 4, slice_rows, 2 * size), stored(2, width, kind=f32),
                      stored(rows, width), stored(rows, width), stored(rows, width)]
        out_specs += [any_spec, any_spec, vmem, vmem, any_spec, any_spec]
    else:
        out_shape += [stored(2, width, kind=f32), stored(2, length, width), stored(2, length, 3 * size)]
        out_specs += [vmem, any_spec, any_spec]
    scratch = [
        held(width, 3 * size),
        held(width, size),
        held(*query_rot.shape),
        held(*key_rot.shape),
        held(*value.shape),
        held(2, length, size),
        held(2, length, size),
        held(2, length, size),
        held(*inverse.shape, kind=f32),
        held(rows, width),
        held(rows, width, kind=f32),
        held(width, 2 * length),
        held(2, length, size),
        held(2, length, width),
        held(2, length, 2 * size),
        held(2, length, width),
        held(2, length, 3 * size),
        held(width, 2 * length),
        held(2, length, width),
        held(3, rows, width),
        held(rows, width, kind=f32),
        held(2, *block),
        held(*block),
        held(*block),
        dma((18,)),
        dma((3,)),
        dma((3,)),
        dma((3, 3)),
        dma((3, 3)),
        dma((count,)),
        dma((count,)),
        dma((2,)),
        held(*masks.shape, kind=f32),
        held(*tables.shape, kind=f32),
        held(rows, width),
    ]
    if final_layer:
        hops = 3 + dp_size // 4
        scratch += [
            held(2, slice_rows, size),
            held(2, slice_rows, size),
            held(*block),
            dma((3, 2)),
            dma((GROUPS, slices)),
            dma((GROUPS, slices)),
            dma((GROUPS, slices - 1)),
            dma((GROUPS, slices - 1)),
            held(2, width, kind=f32),
            held(2, 2, width, kind=f32),
            held(hops, 2, 2, width, kind=f32),
            dma((hops,)),
            dma((hops,)),
            dma((2,)),
            dma((2,)),
            held(3, rows, width),
        ]
    else:
        scratch += [dma((3,)), dma((3,)), dma, dma, held(2, length, width)]
    return pl.pallas_call(
        functools.partial(backward_kernel, dp_size, layer),
        out_shape=out_shape,
        in_specs=in_specs,
        out_specs=out_specs,
        scratch_shapes=scratch,
        compiler_params=pltpu.CompilerParams(
            collective_id=4 + layer, has_side_effects=True, vmem_limit_bytes=VMEM_LIMIT
        ),
        name="backward_layer",
    )(*operands)


def nested(outs):
    return (*outs[:5], outs[5:-2], *outs[-2:])


def on_device(
    dp_size,
    layer_input,
    segment_ids,
    output_grad,
    query_weight,
    key_weight,
    value_weight,
    swish_weight,
    output_weight,
    gate_weight,
    up_weight,
    down_weight,
    mixer_gain,
    ffn_gain,
):
    at = Place(dp_size)
    section_first = at.section == 0
    rows_here, width = layer_input.shape[1:]
    length = segment_ids.shape[1]
    score_scale = HEAD_K ** (-0.5)

    quarter_k = query_weight.shape[2] // 2
    quarter_v = value_weight.shape[2] // 2
    quarter_f = gate_weight.shape[2] // 2
    heads_here = quarter_k // HEAD_K
    first_head = (at.tensor * 2 + at.low) * heads_here
    cosine, sine, growth = rotation_tables(length, HEAD_K // 2)

    ids_mine = lax.dynamic_index_in_dim(segment_ids, at.section, 0, keepdims=False)
    ids_pair = lax.ppermute(ids_mine, "dp", [(i, i ^ 2) for i in range(dp_size)])
    ids = jnp.where(at.low == 0, jnp.stack([ids_mine, ids_pair]), jnp.stack([ids_pair, ids_mine]))
    masks = decay_mask(ids, first_head, heads_here) * score_scale
    tables = jnp.stack([cosine, sine, growth, 1.0 / growth])

    first_in = lax.dynamic_index_in_dim(layer_input, at.section, 0, keepdims=False)
    out_grad = lax.dynamic_index_in_dim(output_grad, at.section, 0, keepdims=False)
    shards = (query_weight[0], key_weight[0], value_weight[0], swish_weight[0], output_weight[0].T, gate_weight[0],
              up_weight[0], down_weight[0].T)
    own_gains = jnp.concatenate([mixer_gain, ffn_gain], axis=0)
    *gathered, all_gains, first_saved, second_down, first_sent = nested(
        forward_layer(0, first_in, own_gains, tables, masks, shards, dp_size, out_grad)
    )
    second_saved = forward_layer(1, first_sent, all_gains, tables, masks, gathered, dp_size)
    gathered = [g.reshape(2, width, g.shape[-1]) for g in gathered]
    second_grad, later_chip, _, later_terms, first_down, later_qkvs = backward_layer(
        1, out_grad, second_down, first_sent, all_gains, tables, masks, second_saved, gathered, dp_size
    )
    first_grad, _, _, _, landed, my_gains, second_sent, taken_rows, taken_grads = backward_layer(
        0, second_grad, first_down, first_in, all_gains, tables, masks, first_saved, gathered, dp_size,
        (later_chip, later_terms, later_qkvs, second_saved), first_sent,
    )

    def by_layer(first, second, taken):
        return jnp.where(section_first, jnp.stack([first, taken]), jnp.stack([taken, second]))[None]

    def shard(e):
        return jnp.sum(landed[e].astype(f32), axis=0)

    def columns(e, start, size):
        step = landed.shape[-1] // 2
        part = jnp.concatenate([landed[e, :, :, p * step + start : p * step + start + size] for p in range(2)], axis=-1)
        return jnp.sum(part.astype(f32), axis=0)

    return (
        by_layer(first_sent, second_sent, taken_rows),
        by_layer(first_grad, second_grad, taken_grads),
        columns(4, 0, quarter_k)[None],
        columns(4, quarter_k, quarter_k)[None],
        shard(5)[None],
        shard(6)[None],
        shard(3).T[None],
        shard(1)[None],
        shard(2)[None],
        shard(0).T[None],
        my_gains[0][None],
        my_gains[1][None],
    )


def solution(mesh):
    in_specs = (
        P(None, ("dp", "tensor"), None),
        P(None, "dp"),
        P(None, ("dp", "tensor"), None),
        P("section", "dp", "tensor"),
        P("section", "dp", "tensor"),
        P("section", "dp", "tensor"),
        P("section", "dp", "tensor"),
        P("section", "tensor", "dp"),
        P("section", "dp", "tensor"),
        P("section", "dp", "tensor"),
        P("section", "tensor", "dp"),
        P("section", None),
        P("section", None),
    )
    out_specs = (
        P("section", None, ("dp", "tensor"), None),
        P("section", None, ("dp", "tensor"), None),
        P("section", "dp", "tensor"),
        P("section", "dp", "tensor"),
        P("section", "dp", "tensor"),
        P("section", "dp", "tensor"),
        P("section", "tensor", "dp"),
        P("section", "dp", "tensor"),
        P("section", "dp", "tensor"),
        P("section", "tensor", "dp"),
        P("section", None),
        P("section", None),
    )
    return jax.shard_map(
        functools.partial(on_device, mesh.shape["dp"]),
        mesh=mesh,
        in_specs=in_specs,
        out_specs=out_specs,
        check_vma=False,
    )
```

```python
import functools

import jax
import jax.numpy as jnp
from jax import lax
from jax.experimental import pallas as pl
from jax.experimental.pallas import tpu as pltpu
from jax.sharding import PartitionSpec as P

HEAD_K = 256
HEAD_V = 512
MESH = pl.DeviceIdType.MESH

epsilon = 1e-05
group_guard = 1.0
bf16 = jnp.bfloat16
f32 = jnp.float32


def rotation_tables(length, half_width):
    pair_index = jnp.arange(half_width).astype(f32)
    position = jnp.arange(length).astype(f32)[:, None]
    angle = position * jnp.exp(-jnp.log(10000.0) * pair_index / half_width)
    zeta = (pair_index / half_width + 0.4) / 1.4
    growth = jnp.exp(position / 512.0 * jnp.log(zeta))
    return (jnp.cos(angle), jnp.sin(angle), growth)


class Place:
    def __init__(self, dp_size):
        self.groups = dp_size // 4
        self.section = lax.axis_index("section")
        self.dp = lax.axis_index("dp")
        self.tensor = lax.axis_index("tensor")
        self.core = self.dp % 2
        self.low = (self.dp // 2) % 2
        self.group = self.dp // 4

    def dp_at(self, group_step, low_step):
        group = (self.group + group_step + self.groups) % self.groups
        return (group * 2 + (self.low + low_step) % 2) * 2 + self.core

    def sibling(self):
        return self.dp + 1 - 2 * self.core


SQUARE = ((0, 1), (1, 0), (1, 1))
TILE = 512
VMEM_LIMIT = 63 * 1024 * 1024


def mm(left, right):
    return lax.dot_general(left, right, (((1,), (0,)), ((), ())), preferred_element_type=f32)


def mm_nt(left, right):
    return lax.dot_general(left, right, (((1,), (1,)), ((), ())), preferred_element_type=f32)


def mm_tn(left, right):
    return lax.dot_general(left, right, (((0,), (0,)), ((), ())), preferred_element_type=f32)


class Square:
    def __init__(self, dp_size, rows):
        self.at = Place(dp_size)
        self.rows = rows
        self.own = self.at.low
        self.next = 1 - self.at.low

    def device(self, low_step, tensor_step):
        return (self.at.section, self.at.dp_at(0, low_step), (self.at.tensor + tensor_step) % 2)

    def barrier(self):
        barrier = pltpu.get_barrier_semaphore()
        for step in SQUARE:
            pl.semaphore_signal(barrier, inc=1, device_id=self.device(*step), device_id_type=MESH)
        pl.semaphore_wait(barrier, len(SQUARE))

    def chunk(self, ref, low_step=0, tensor_step=0):
        start = pl.multiple_of((self.at.tensor + tensor_step) % 2 * self.rows, self.rows)
        return ref.at[(self.at.low + low_step) % 2, pl.ds(start, self.rows)]

    def copy(self, src, dst, send, recv, step):
        return pltpu.make_async_remote_copy(
            src_ref=src,
            dst_ref=dst,
            send_sem=send,
            recv_sem=recv,
            device_id=self.device(*step),
            device_id_type=MESH,
        )

    def spread(self, ref, send, recv):
        pushes = []
        for j, step in enumerate(SQUARE):
            push = self.copy(self.chunk(ref), self.chunk(ref), send.at[j], recv.at[j], step)
            push.start()
            pushes.append(push)
        return pushes

    def spread_from(self, own, ref, send, recv, here):
        local = pltpu.make_async_copy(own, self.chunk(ref), here)
        local.start()
        pushes = [local]
        for j, step in enumerate(SQUARE):
            push = self.copy(own, self.chunk(ref), send.at[j], recv.at[j], step)
            push.start()
            pushes.append(push)
        return pushes

    def give(self, parts, landed, send, recv, j):
        push = self.copy(self.chunk(parts, *SQUARE[j]), landed.at[j], send.at[j], recv.at[j], SQUARE[j])
        push.start()
        return push


def row_blocks(rows, body, block=32):
    block = min(block, rows)

    @pl.loop(0, rows // block)
    def _(i):
        body(pl.ds(pl.multiple_of(i * block, block), block))


def norm_parts(values):
    centred = values - jnp.mean(values, axis=-1, keepdims=True)
    scale = lax.rsqrt(jnp.mean(centred * centred, axis=-1, keepdims=True) + epsilon)
    return centred * scale, scale


def norm_grad(normed, scale, upstream, gain):
    through = upstream * gain
    return scale * (
        through
        - jnp.mean(through, axis=-1, keepdims=True)
        - normed * jnp.mean(through * normed, axis=-1, keepdims=True)
    )


def turn(values, cosine, sine, scale):
    half = values.shape[-1] // 2
    a, b = values[:, :half], values[:, half:]
    return jnp.concatenate([(a * cosine - b * sine) * scale, (a * sine + b * cosine) * scale], axis=-1)


def turn_back(values, cosine, sine, scale):
    half = values.shape[-1] // 2
    a, b = values[:, :half] * scale, values[:, half:] * scale
    return jnp.concatenate([a * cosine + b * sine, b * cosine - a * sine], axis=-1)


def transpose_into(target, source):
    _, length, width = source.shape
    for s in range(2):
        for start in range(0, width, TILE):
            target[start : start + TILE, s * length : (s + 1) * length] = source[s, :, start : start + TILE].T


def forward_kernel(dp_size, layer, *refs):
    streams = layer == 0
    v = Refs()
    if streams:
        (v.x, v.mixer_gain, v.ffn_gain, v.ids, v.tables, v.out_grad, *refs) = refs
        shards, refs = refs[:8], refs[8:]
        stored, refs = refs[:4], refs[4:]
        (v.gains, v.masks, *refs) = refs
    else:
        (v.x, v.gains, v.tables, v.masks, v.down, *refs) = refs
        stored, refs = refs[:4], refs[4:]
    saved, refs = refs[:14], refs[14:]
    if streams:
        (v.grad_down, result, *refs) = refs
    else:
        (v.turned_down, *refs) = refs
    scratch, refs = refs[:14], refs[14:]
    (middle, normed_in_t, query_rot, key_rot, value, unit, inverse, opened, slope_open, merged, normed_mid_t, act, slope,
     hidden) = scratch
    save_sem, x_v, masks, tables, in_sem, *refs = refs
    held, refs = refs[:4], refs[4:]
    (w_sem, normed_in, *refs) = refs
    if streams:
        (normed_mid, *refs) = refs
    else:
        normed_mid = normed_mid_t
    (parts, landed, s_send, s_recv, g_send, g_recv, *refs) = refs
    x = x_v
    rows, width = x.shape
    sq = Square(dp_size, rows)
    at = sq.at
    sources = [(v.x.at[at.section] if streams else v.x, x_v), (v.tables, tables)]
    if not streams:
        sources.append((v.masks, masks))
    operand_copies = [
        pltpu.make_async_copy(source, target, in_sem.at[i]) for i, (source, target) in enumerate(sources)
    ]
    for copy in operand_copies:
        copy.start()
    operand_copies[0].wait()
    saves = []

    def save(*which):
        for i in which:
            copy = pltpu.make_async_copy(scratch[i], saved[i], save_sem.at[i])
            copy.start()
            saves.append(copy)

    qkvs, out_t, gate_up, down_t = held
    wide_k = query_rot.shape[-1]
    wide_v = value.shape[-1]
    wide_f = hidden.shape[-1]
    heads = wide_k // HEAD_K
    slices = dp_size // 2
    other = 1 - at.section
    groups = [(0, 0, wide_k), (0, wide_k, wide_k), (0, 2 * wide_k, wide_v), (0, 2 * wide_k + wide_v, wide_v),
              (1, 0, wide_v), (2, 0, wide_f), (2, wide_f, wide_f), (3, 0, wide_f)]
    loads = {}

    def load(i):
        which, first, size = groups[i]
        columns = pl.ds(first, size)
        loads[i] = pltpu.make_async_copy(
            stored[which].at[layer, :, :, :, columns], held[which].at[:, :, :, columns], w_sem.at[i]
        )
        loads[i].start()

    def weight(which, first, size):
        return held[which][:, :, :, first : first + size].reshape(width, size)

    def first_norm(block):
        unit_rows, _ = norm_parts(x[block].astype(f32))
        sq.chunk(normed_in)[block] = (unit_rows * v.gains[layer, 0:1]).astype(bf16)

    def project(i, s):
        loads_wait(i)
        first, size = groups[i][1:]
        tokens = normed_in[s]
        for start in range(0, size, TILE):
            wide = mm(tokens, weight(0, first + start, TILE))
            cols = slice(start, start + TILE)
            if i < 2:
                dest = (query_rot, key_rot)[i]
                for head in range(TILE // HEAD_K):
                    part = wide[:, head * HEAD_K : (head + 1) * HEAD_K]
                    dest[s, :, start + head * HEAD_K : start + (head + 1) * HEAD_K] = turn(
                        part, tables[0], tables[1], tables[2 + i]
                    ).astype(bf16)
            elif i == 2:
                value[s, :, cols] = wide.astype(bf16)
            else:
                sigmoid = 1.0 / (1.0 + jnp.exp(-wide))
                opened[s, :, cols] = (wide * sigmoid).astype(bf16)
                slope_open[s, :, cols] = (sigmoid * (1.0 + wide * (1.0 - sigmoid))).astype(bf16)

    waited = []

    def loads_wait(i):
        if i not in waited:
            waited.append(i)
            loads[i].wait()

    def retain(s):
        for head in range(heads):
            cols_k = slice(head * HEAD_K, (head + 1) * HEAD_K)
            cols_v = slice(head * HEAD_V, (head + 1) * HEAD_V)
            product = mm_nt(query_rot[s, :, cols_k], key_rot[s, :, cols_k])
            weights = (product * masks[s, head]).astype(bf16)
            mixed = mm(weights, value[s, :, cols_v])
            centred = mixed - jnp.mean(mixed, axis=-1, keepdims=True)
            scale = lax.rsqrt(jnp.mean(centred * centred, axis=-1, keepdims=True) + group_guard)
            unit_rows = centred * scale
            inverse[s, head] = scale
            unit[s, :, cols_v] = unit_rows.astype(bf16)
            merged[s, :, cols_v] = (unit_rows * opened[s, :, cols_v].astype(f32)).astype(bf16)

    def give_back(s, source, weight_t):
        tokens = source[s]
        step = width // slices
        for i in range(slices):
            parts[s, :, i * step : (i + 1) * step] = mm_nt(tokens, weight_t[i].reshape(step, -1)).astype(bf16)

    def collected(block, which):
        total = sq.chunk(parts)[block].astype(f32)
        for j in range(len(SQUARE)):
            total = total + landed[which, j, block].astype(f32)
        return total

    def give(s, which):
        send, recv = g_send.at[which], g_recv.at[which]
        return [sq.give(parts, landed.at[which], send, recv, j) for j in ((1, 2) if s == 1 else (0,))]

    def second_norm(block):
        middle_rows = x[block].astype(f32) + collected(block, 0)
        middle[block] = middle_rows
        unit_rows, _ = norm_parts(middle_rows)
        sq.chunk(normed_mid)[block] = (unit_rows * v.gains[layer, 1:2]).astype(bf16)

    def feed(s):
        loads_wait(5)
        loads_wait(6)
        tokens = normed_mid[s]
        for start in range(0, wide_f, TILE):
            cols = slice(start, start + TILE)
            gate = mm(tokens, weight(2, start, TILE))
            up = mm(tokens, weight(2, wide_f + start, TILE))
            square = gate * gate
            bend = jnp.tanh(0.7978845608028654 * gate * (1.0 + 0.044715 * square))
            half = 0.5 * (1.0 + bend)
            gelu = gate * half
            slope_gelu = half + 0.5 * gate * (1.0 - bend * bend) * (
                0.7978845608028654 * (1.0 + 3 * 0.044715 * square)
            )
            act[s, :, cols] = gelu.astype(bf16)
            slope[s, :, cols] = (slope_gelu * up).astype(bf16)
            hidden[s, :, cols] = (gelu * up).astype(bf16)

    def turn_if(condition, target, source):
        @pl.when(condition)
        def _():
            transpose_into(target, source)

    if not streams:
        (down_v, turned_v, down_sem) = refs
        down_load = pltpu.make_async_copy(v.down, down_v, down_sem.at[0])
        down_load.start()
        down_save = pltpu.make_async_copy(turned_v, v.turned_down, down_sem.at[1])

        def turn_down(condition):
            @pl.when(condition)
            def _():
                down_load.wait()
                transpose_into(turned_v, down_v)
                down_save.start()

        for i in range(7):
            load(i)
        turn_down(at.core == at.section)
        row_blocks(rows, first_norm)
        sq.barrier()
        ins = sq.spread(normed_in, s_send.at[0], s_recv.at[0])
        operand_copies[1].wait()
        operand_copies[2].wait()
        ins[0].wait_recv()
        for i in range(4):
            project(i, sq.own)
        ins[1].wait_recv()
        ins[2].wait_recv()
        turn_if(at.core == at.section, normed_in_t, normed_in)
        for i in range(4):
            project(i, sq.next)
        save(2, 3, 4, 7, 8)
        retain(sq.next)
        loads_wait(4)
        give_back(sq.next, merged, out_t)
        gives = give(1, 0)
        retain(sq.own)
        give_back(sq.own, merged, out_t)
        gives += give(0, 0)
        save(5, 6, 9)
        turn_if(at.core != at.section, normed_in_t, normed_in)
        save(1)
        turn_down(at.core != at.section)
        for push in gives:
            push.wait_recv()
        row_blocks(rows, second_norm)
        save(0)
        mids = sq.spread(normed_mid, s_send.at[1], s_recv.at[1])
        mids[0].wait_recv()
        feed(sq.own)
        mids[1].wait_recv()
        mids[2].wait_recv()
        save(10)
        feed(sq.next)
        save(11, 12, 13)
        for push in ins + mids + gives:
            push.wait_send()
        for copy in saves:
            copy.wait()
        down_save.wait()
        return

    (z_send, z_recv, x_send, x_recv, c_send, c_recv, o_send, o_recv, here_sem, gain_send, gain_recv, d_send, d_recv,
     d_sem, own_gains, ids_land, id_send, id_recv, mask_sem) = refs
    steps = [(k, b) for k in range(at.groups) for b in range(2)][1:]

    def place(section=None, dp=None):
        return (at.section if section is None else section, at.dp if dp is None else dp, at.tensor)

    def copy(src, dst, send, recv, device):
        return pltpu.make_async_remote_copy(
            src_ref=src, dst_ref=dst, send_sem=send, recv_sem=recv, device_id=device, device_id_type=MESH
        )

    partners = [sq.device(*step) for step in SQUARE] + [place(dp=at.sibling()), place(section=other)]
    partners += [place(dp=at.dp_at(k, b)) for k, b in steps if (k, b) != (0, 1)]
    barrier = pltpu.get_barrier_semaphore()
    for partner in partners:
        pl.semaphore_signal(barrier, inc=1, device_id=partner, device_id_type=MESH)
    pl.semaphore_wait(barrier, len(partners))

    own_gains[0:1] = v.mixer_gain[...]
    own_gains[1:2] = v.ffn_gain[...]
    gain_copy = copy(own_gains, v.gains.at[at.section], gain_send, gain_recv, place(section=other))
    gain_copy.start()
    v.gains[at.section] = own_gains[...]
    id_copy = copy(v.ids, ids_land, id_send, id_recv, sq.device(1, 0))
    id_copy.start()

    def make_masks():
        length = masks.shape[-1]
        t = lax.broadcasted_iota(jnp.int32, (length, length), 0).astype(f32)
        s = lax.broadcasted_iota(jnp.int32, (length, length), 1).astype(f32)
        distance = jnp.maximum(t - s, 0.0)
        decays = []
        for head in range(heads):
            number = jnp.full((1, 1), ((at.tensor * 2 + at.low) * heads + head).astype(f32))
            rate = jnp.log(1.0 - jnp.exp2(-5.0 - number))
            decays.append(jnp.exp(rate * distance) * HEAD_K ** (-0.5))
        for sequence, ids in ((sq.own, v.ids), (sq.next, ids_land)):
            row = ids[pl.ds(at.section, 1), :]
            same = t >= s
            for document in (1, 2):
                start = jnp.sum(jnp.where(row < document, 1.0, 0.0), axis=1, keepdims=True)
                same = jnp.logical_and(same, (t >= start) == (s >= start))
            for head in range(heads):
                masks[sequence, head] = jnp.where(same, decays[head], 0.0)

    def slot(i, section, dp):
        which, first, size = groups[i]
        return stored[which].at[section, dp // 2, dp % 2, :, pl.ds(first, size)]

    def block(i, section, core):
        which, first, size = groups[i]
        return stored[which].at[section, :, core, :, pl.ds(first, size)]

    def part(i, b):
        size = groups[i][2]
        return shards[i].at[:, pl.ds(pl.multiple_of((at.low + b) % 2 * size, size), size)]

    z_copies, x_copies, here, core_own, core_other = {}, {}, {}, {}, {}

    def push_own(i):
        mine = slot(i, at.section, at.dp)
        for j, (k, b) in enumerate(steps):
            z_copies[i, j] = copy(part(i, b), mine, z_send.at[i, j], z_recv.at[i, j], place(dp=at.dp_at(k, b)))
            z_copies[i, j].start()
        x_copies[i, 0] = copy(part(i, 0), mine, x_send.at[i, 0], x_recv.at[i, 0], place(section=other))
        x_copies[i, 0].start()
        here[i] = pltpu.make_async_copy(part(i, 0), mine, here_sem.at[i])
        here[i].start()

    def pass_on(i):
        for j, (k, b) in enumerate(steps):
            z_copies[i, j].wait_recv()
            arrived = slot(i, at.section, at.dp_at(-k, b))
            x_copies[i, j + 1] = copy(arrived, arrived, x_send.at[i, j + 1], x_recv.at[i, j + 1], place(section=other))
            x_copies[i, j + 1].start()
        here[i].wait()
        mine = block(i, at.section, at.core)
        core_own[i] = copy(mine, mine, c_send.at[i], c_recv.at[i], place(dp=at.sibling()))
        core_own[i].start()

    def share_other(i):
        for j in range(slices):
            x_copies[i, j].wait_recv()
        theirs = block(i, other, at.core)
        core_other[i] = copy(theirs, theirs, o_send.at[i], o_recv.at[i], place(dp=at.sibling()))
        core_other[i].start()

    def arrive(i):
        @pl.when(at.section == 0)
        def _():
            core_own[i].wait_recv()

        @pl.when(at.section == 1)
        def _():
            core_other[i].wait_recv()

        load(i)

    ahead = 3
    for i in range(ahead):
        push_own(i)
    gain_copy.wait_recv()
    row_blocks(rows, first_norm)
    ins = sq.spread(normed_in, s_send.at[0], s_recv.at[0])

    def advance(i):
        pass_on(i)
        if i + ahead < 8:
            push_own(i + ahead)
        if i > 0:
            share_other(i - 1)
            arrive(i - 1)

    advance(0)
    downs = sq.spread_from(v.out_grad.at[at.section], v.grad_down, d_send, d_recv, d_sem)
    id_copy.wait_recv()
    make_masks()
    mask_save = pltpu.make_async_copy(masks, v.masks, mask_sem)
    mask_save.start()
    advance(1)
    for push in ins:
        push.wait_recv()
    transpose_into(normed_in_t, normed_in)
    save(1)
    operand_copies[1].wait()
    for i in range(2, 5):
        advance(i)
        for s in (sq.own, sq.next):
            project(i - 2, s)
    advance(5)
    for s in (sq.own, sq.next):
        project(3, s)
    retain(sq.next)
    loads_wait(4)
    give_back(sq.next, merged, out_t)
    gives = give(1, 0)
    retain(sq.own)
    give_back(sq.own, merged, out_t)
    gives += give(0, 0)
    advance(6)
    for push in gives:
        push.wait_recv()
    row_blocks(rows, second_norm)
    mids = sq.spread(normed_mid, s_send.at[1], s_recv.at[1])
    advance(7)
    for push in mids:
        push.wait_recv()
    transpose_into(normed_mid_t, normed_mid)
    save(0, 2, 3, 4, 5, 6, 7, 8, 9, 10)
    feed(sq.next)
    feed(sq.own)
    save(11, 12, 13)
    for push in gives:
        push.wait_send()

    def last_group():
        for j in range(slices):
            x_copies[7, j].wait_recv()
        core_other[7].start()

    theirs = block(7, other, at.core)
    core_other[7] = copy(theirs, theirs, o_send.at[7], o_recv.at[7], place(dp=at.sibling()))

    @pl.when(at.section == 1)
    def _():
        last_group()

    arrive(7)
    loads_wait(7)
    give_back(sq.next, hidden, down_t)
    ends = give(1, 1)
    give_back(sq.own, hidden, down_t)
    ends += give(0, 1)

    @pl.when(at.section == 0)
    def _():
        last_group()

    for push in ends:
        push.wait_recv()

    def last(block):
        result[block] = (middle[block] + collected(block, 1)).astype(bf16)

    row_blocks(rows, last)

    @pl.when(at.section == 0)
    def _():
        for i in range(8):
            core_other[i].wait_recv()

    @pl.when(at.section == 1)
    def _():
        for i in range(8):
            core_own[i].wait_recv()

    for push in downs:
        push.wait()
    for push in ins + mids + ends + list(z_copies.values()) + list(x_copies.values()):
        push.wait_send()
    for i in range(8):
        core_own[i].wait_send()
        core_other[i].wait_send()
    gain_copy.wait_send()
    id_copy.wait_send()
    mask_save.wait()
    for copy in saves:
        copy.wait()


def forward_layer(layer, operands, weights, length, heads, dp_size):
    rows, width = operands[0].shape[-2:]
    streams = layer == 0
    slices = dp_size // 2
    quarter_k = heads * HEAD_K
    quarter_v = heads * HEAD_V
    quarter_f = weights[-1].shape[-1] // 2 if streams else weights[-1].shape[-1]
    vmem = pl.BlockSpec(memory_space=pltpu.VMEM)
    any_spec = pl.BlockSpec(memory_space=pl.ANY)
    wides = (2 * quarter_k + 2 * quarter_v, quarter_v, 2 * quarter_f, quarter_f)

    def tokens(wide, kind=bf16):
        return jax.ShapeDtypeStruct((2, length, wide), kind)

    turned = jax.ShapeDtypeStruct((width, 2 * length), bf16)
    dma = pltpu.SemaphoreType.DMA
    out_shape = [
        jax.ShapeDtypeStruct((rows, width), f32),
        turned,
        tokens(quarter_k),
        tokens(quarter_k),
        tokens(quarter_v),
        tokens(quarter_v),
        jax.ShapeDtypeStruct((2, heads, length, 1), f32),
        tokens(quarter_v),
        tokens(quarter_v),
        tokens(quarter_v),
        turned if streams else tokens(width),
        tokens(quarter_f),
        tokens(quarter_f),
        tokens(quarter_f),
    ]
    out_specs = [any_spec] * len(out_shape)
    scratch = [pltpu.VMEM(out.shape, out.dtype) for out in out_shape]
    mask_shape = (2, heads, length, length)
    scratch += [
        dma((14,)),
        pltpu.VMEM((rows, width), bf16),
        pltpu.VMEM(mask_shape, f32),
        pltpu.VMEM((4, length, HEAD_K // 2), f32),
        dma((3,)),
    ]
    scratch += [pltpu.VMEM((slices, 2, width // dp_size, wide), bf16) for wide in wides] + [
        dma((8,)),
    ] + [pltpu.VMEM((2, length, width), bf16)] * (3 if streams else 2) + [
        pltpu.VMEM((2, 3, rows, width), bf16),
        dma((2, 3)),
        dma((2, 3)),
        dma((2, 3)),
        dma((2, 3)),
    ]
    if streams:
        out_shape = (
            [jax.ShapeDtypeStruct((2, slices, 2, width // dp_size, wide), bf16) for wide in wides]
            + [jax.ShapeDtypeStruct((2, 2, width), f32), jax.ShapeDtypeStruct(mask_shape, f32)]
            + out_shape
            + [tokens(width), jax.ShapeDtypeStruct((rows, width), bf16)]
        )
        out_specs = [any_spec] * 4 + [vmem, any_spec] + out_specs + [any_spec, vmem]
        scratch += [
            dma((8, slices - 1)),
            dma((8, slices - 1)),
            dma((8, slices)),
            dma((8, slices)),
            dma((8,)),
            dma((8,)),
            dma((8,)),
            dma((8,)),
            dma((8,)),
            dma,
            dma,
            dma((3,)),
            dma((3,)),
            dma,
            pltpu.VMEM((2, width), f32),
            pltpu.VMEM((2, length), jnp.int32),
            dma,
            dma,
            dma,
        ]
        in_specs = [any_spec, vmem, vmem, vmem, any_spec, any_spec]
    else:
        out_shape = out_shape + [turned]
        out_specs = out_specs + [any_spec]
        scratch += [pltpu.VMEM((2, length, width), bf16), pltpu.VMEM(turned.shape, bf16), dma((2,))]
        in_specs = [any_spec, vmem, any_spec, any_spec, any_spec]
    return pl.pallas_call(
        functools.partial(forward_kernel, dp_size, layer),
        out_shape=out_shape,
        in_specs=in_specs + [any_spec] * len(weights),
        out_specs=out_specs,
        scratch_shapes=scratch,
        compiler_params=pltpu.CompilerParams(
            collective_id=1 + layer, has_side_effects=True, vmem_limit_bytes=VMEM_LIMIT
        ),
        name="forward_layer",
    )(*operands, *weights)


class Refs:
    pass


KEPT = 5
GROUPS = 7


def backward_kernel(dp_size, layer, *refs):
    final_layer = layer == 0
    v = Refs()
    (v.grad_out, v.gains, v.tables, v.masks, v.x, v.middle, v.normed_in_t, v.query_rot, v.key_rot, v.value, v.unit,
     v.inverse, v.opened, v.slope_open, v.merged, v.normed_mid_t, v.act, v.slope, v.hidden,
     v.qkvs_all, v.out_all, v.gate_up_all, v.down_all, v.down_in, *refs) = refs
    if not final_layer:
        v.down_turned, *refs = refs
    if final_layer:
        (v.later_chip, v.later_terms, v.first_rows, v.later_normed_in_t, v.later_qkvs, v.later_hidden, v.later_middle,
         *refs) = refs
    v.grad_in, v.chip, v.core_land, *refs = refs
    if final_layer:
        v.x_land, v.final, v.gain_sums, v.result, v.taken_rows, v.taken_grads, *refs = refs
    else:
        v.terms, v.next_down, v.kept_qkvs, *refs = refs
    (v.big, v.out_t, v.query_v, v.key_v, v.value_v, v.wide_a, v.wide_b, v.wide_c, v.inverse_v, v.x_v, v.middle_v,
     v.normed_t, v.outer, v.grad_down, v.grad_gate_up, v.grad_branch, v.grad_qkvs, v.turned, v.parts, v.landed,
     v.grad_middle, v.stage_given, v.stage_own, v.core_part, v.load_sem, v.s_send, v.s_recv, v.g_send, v.g_recv,
     v.c_send, v.c_recv, v.local_sem, v.masks_v, v.tables_v, v.grad_out_v, *refs) = refs
    if final_layer:
        (v.left, v.right, v.sums, v.r_sem, v.x_send, v.x_recv, v.z_send, v.z_recv, v.terms, v.held, v.hop_land,
         v.t_send, v.t_recv, v.row_send, v.row_recv, v.landed_y) = refs
    else:
        v.d_send, v.d_recv, v.d_sem, v.kept_sem, v.mid_v = refs
    at = Place(dp_size)
    rows, width = v.x.shape[-2:]
    sq = Square(dp_size, rows)
    masks, tables, gains = v.masks_v, v.tables_v, v.gains
    query_v, key_v, value_v = v.query_v, v.key_v, v.value_v
    wide_a, wide_b, wide_c = v.wide_a, v.wide_b, v.wide_c
    grad_down, grad_gate_up, grad_branch, grad_qkvs = v.grad_down, v.grad_gate_up, v.grad_branch, v.grad_qkvs
    big, out_t, outer, parts, landed, terms = v.big, v.out_t, v.outer, v.parts, v.landed, v.terms
    wide_k = query_v.shape[-1]
    wide_v = value_v.shape[-1]
    wide_f = outer.shape[-1]
    heads = wide_k // HEAD_K
    slices = dp_size // 2
    slice_rows = width // dp_size
    gain_in = gains[layer, 0:1]
    gain_mid = gains[layer, 1:2]
    other = 1 - at.section
    steps = [(k, b) for k in range(at.groups) for b in range(2)]
    steps = steps[1:] + steps[:1]

    def load(index, source, target):
        copy = pltpu.make_async_copy(source, target, v.load_sem.at[index])
        copy.start()
        return copy

    def remote(src, dst, send, recv, device):
        return pltpu.make_async_remote_copy(
            src_ref=src, dst_ref=dst, send_sem=send, recv_sem=recv, device_id=device, device_id_type=MESH
        )

    def place(section=None, dp=None, tensor=None):
        return (
            at.section if section is None else section,
            at.dp if dp is None else dp,
            at.tensor if tensor is None else tensor,
        )

    sibling = place(dp=at.sibling())
    across = place(section=other)

    token_load = load(14, v.down_in, grad_down)
    down_load = load(0, v.down_all.at[layer], big.at[:, pl.ds(2 * wide_f, wide_f)])
    act_load = load(1, v.act, wide_a)
    slope_load = load(2, v.slope, wide_b)
    gate_load = load(3, v.gate_up_all.at[layer], big.at[:, pl.ds(0, 2 * wide_f)])
    hidden_load = load(4, v.hidden, outer)
    if not final_layer:
        turned_load = load(18, v.down_turned, v.turned)
    mid_load = load(5, v.normed_mid_t, v.normed_t if final_layer else v.mid_v)
    early = [
        load(6, v.middle, v.middle_v),
        load(7, v.x.at[at.section] if final_layer else v.x, v.x_v),
        load(8, v.out_all.at[layer], out_t),
        load(9, v.query_rot, query_v),
        load(10, v.key_rot, key_v),
        load(11, v.value, value_v),
        load(12, v.inverse, v.inverse_v),
        load(13, v.opened, wide_c),
        load(15, v.masks, masks),
        load(16, v.tables, tables),
        load(17, v.grad_out if final_layer else v.grad_out.at[at.section], v.grad_out_v),
    ]
    terms[...] = jnp.zeros_like(terms)

    partners = [sq.device(*step) for step in SQUARE] + [sibling]
    if final_layer:
        partners.append(across)
        partners += [place(dp=at.dp_at(k, b)) for k, b in steps[:-1] if (k, b) != (0, 1)]
    barrier = pltpu.get_barrier_semaphore()
    for partner in partners:
        pl.semaphore_signal(barrier, inc=1, device_id=partner, device_id_type=MESH)
    pl.semaphore_wait(barrier, len(partners))

    def x_copy(e, at_source, j, source):
        block = source.at[at_source, j]
        return remote(block, v.x_land.at[e, j], v.x_send.at[e, j], v.x_recv.at[e, j], across)

    def start_x(e, at_source, source):
        @pl.loop(0, slices)
        def _(j):
            x_copy(e, at_source, j, source).start()

    row_copies = []
    if final_layer:

        @pl.when(at.section == 0)
        def _():
            @pl.loop(0, KEPT)
            def _(e):
                start_x(e, e, v.later_chip)

            remote(v.grad_out, v.taken_grads, v.row_send.at[1], v.row_recv.at[1], across).start()

        @pl.when(at.section == 1)
        def _():
            remote(v.first_rows, v.taken_rows, v.row_send.at[0], v.row_recv.at[0], across).start()

    def through_down(s):
        tokens = grad_down[s]
        for start in range(0, wide_f, TILE):
            cols = slice(start, start + TILE)
            grad_hidden = mm(tokens, big[:, 2 * wide_f + start : 2 * wide_f + start + TILE])
            grad_gate_up[s, :, cols] = (grad_hidden * wide_b[s, :, cols].astype(f32)).astype(bf16)
            grad_gate_up[s, :, wide_f + start : wide_f + start + TILE] = (
                grad_hidden * wide_a[s, :, cols].astype(f32)
            ).astype(bf16)

    def give_back(s, source, weight, first, size, target):
        tokens = source[s]
        for start in range(0, width, TILE):
            target[s, :, start : start + TILE] = mm_nt(
                tokens, weight[start : start + TILE, first : first + size]
            ).astype(bf16)

    def collected(block, given, land):
        total = sq.chunk(given)[block].astype(f32)
        for j in range(len(SQUARE)):
            total = total + land[j, block].astype(f32)
        return total

    def exchange(source, weight, first, size, target, land, which):
        give_back(sq.next, source, weight, first, size, target)
        send, recv = v.g_send.at[which], v.g_recv.at[which]
        pushes = [sq.give(target, land, send, recv, j) for j in (1, 2)]
        give_back(sq.own, source, weight, first, size, target)
        pushes.append(sq.give(target, land, send, recv, 0))
        return pushes

    members = [
        (v.turned, outer, 0, wide_f),
        (v.normed_t, grad_gate_up, 0, wide_f),
        (v.normed_t, grad_gate_up, wide_f, wide_f),
        (v.turned, outer, 0, wide_v),
        (v.normed_t, grad_qkvs, 0, 2 * wide_k),
        (v.normed_t, grad_qkvs, 2 * wide_k, wide_v),
        (v.normed_t, grad_qkvs, 2 * wide_k + wide_v, wide_v),
    ]
    members += members[KEPT:]
    given_copies, own_copies, fetches = {}, {}, {}

    def product(e, dp):
        left, right, first, size = members[e]
        start = pl.multiple_of(dp * slice_rows, slice_rows)
        wide = right[:, :, first : first + size].reshape(-1, size)
        return mm(left[pl.ds(start, slice_rows), :], wide)

    def given(e):
        if e >= 2:
            given_copies[e - 2].wait_send()
        stage = v.stage_given.at[e % 2]

        @pl.loop(0, slices)
        def _(j):
            stage[j] = product(e, j * 2 + 1 - at.core).astype(bf16)

        given_copies[e] = remote(stage, v.core_land.at[e], v.c_send.at[e], v.c_recv.at[e], sibling)
        given_copies[e].start()

    def fetch(e):
        given_copies[e].wait_recv()
        fetches[e] = pltpu.make_async_copy(v.core_land.at[e], v.core_part, v.local_sem.at[0])
        fetches[e].start()

    def settle(e):
        if e in settled:
            return
        settled.append(e)
        own_copies[e].wait()
        if final_layer:

            @pl.when(at.section == (1 if e < GROUPS else 0))
            def _():
                start_x(e if e < GROUPS else e - GROUPS + KEPT, e, v.chip)

    def own(e):
        if e >= 1:
            settle(e - 1)
        fetches[e].wait()

        @pl.loop(0, slices)
        def _(j):
            v.stage_own[j] = (product(e, j * 2 + at.core) + v.core_part[j].astype(f32)).astype(bf16)

        own_copies[e] = pltpu.make_async_copy(v.stage_own, v.chip.at[e], v.local_sem.at[1])
        own_copies[e].start()

    settled = []

    def index(k, b):
        return ((at.group + k) % at.groups) * 2 + (at.low + b) % 2

    def piece(e, k):
        start = pl.multiple_of(at.low * wide_f, wide_f)
        return v.final.at[e, k, :, pl.ds(start, wide_f)]

    def z_copy(e, j):
        k, b = steps[j]
        return remote(v.sums.at[j], piece(e, k), v.z_send.at[e, j], v.z_recv.at[e, j], place(dp=at.dp_at(k, b)))

    def home_copy(e):
        return pltpu.make_async_copy(v.sums.at[slices - 1], piece(e, 0), v.r_sem.at[2, 0])

    def reduce_slices(e, at_source, source, first, stop, wait_previous):
        def loads(j):
            here = index(*steps[j])
            return (
                pltpu.make_async_copy(source.at[at_source, here], v.left.at[j % 2], v.r_sem.at[0, j % 2]),
                pltpu.make_async_copy(v.x_land.at[e, here], v.right.at[j % 2], v.r_sem.at[1, j % 2]),
            )

        def begin(j):
            x_copy(e, at_source, index(*steps[j]), source).wait_recv()
            for copy in loads(j):
                copy.start()

        begin(first)
        for j in range(first, stop):
            if j + 1 < stop:
                begin(j + 1)
            for copy in loads(j):
                copy.wait()

            @pl.when(wait_previous)
            def _():
                if j == slices - 1:
                    home_copy(e).wait()
                else:
                    z_copy(e - 1, j).wait_send()

            v.sums[j] = (v.left[j % 2].astype(f32) + v.right[j % 2].astype(f32)).astype(bf16)
            if j == slices - 1:
                home_copy(e).start()
            else:
                z_copy(e, j).start()

    reduced = [0, 0]

    def source_of(section, e):
        if section == 0:
            return e, v.chip
        return (e, v.later_chip) if e < KEPT else (e + GROUPS - KEPT, v.chip)

    def reduce_some(section, count):
        if not final_layer:
            return

        @pl.when(at.section == section)
        def _():
            done = reduced[section]
            while done < reduced[section] + count:
                e, first = divmod(done, slices)
                stop = min(slices, first + reduced[section] + count - done)
                reduce_slices(e, *source_of(section, e), first, stop, e > 0)
                done += stop - first

        reduced[section] += count

    def reduce_rest(section):
        e, first = divmod(reduced[section], slices)

        @pl.when(at.section == section)
        def _():
            begin = e
            if first > 0:
                reduce_slices(e, *source_of(section, e), first, slices, e > 0)
                begin = e + 1
            same = KEPT if section == 1 else GROUPS

            @pl.loop(begin, same)
            def _(i):
                reduce_slices(i, i, source_of(section, 0)[1], 0, slices, i > 0)

            for i in range(same, GROUPS):
                reduce_slices(i, *source_of(section, i), 0, slices, True)

    token_load.wait()
    if final_layer:
        hidden_load.wait()
        transpose_into(v.turned, grad_down)
        given(0)
    down_load.wait()
    act_load.wait()
    slope_load.wait()
    through_down(sq.next)
    through_down(sq.own)
    unit_load = load(1, v.unit, wide_a)
    bend_load = load(2, v.slope_open, wide_b)
    gate_load.wait()
    gives = exchange(grad_gate_up, big, 0, 2 * wide_f, parts, landed, 0)
    if not final_layer:
        hidden_load.wait()
        turned_load.wait()
        given(0)
    fetch(0)
    own(0)
    mid_load.wait()
    if not final_layer:
        transpose_into(v.normed_t, v.mid_v)
    settle(0)
    given(1)
    qkvs_load = load(3, v.qkvs_all.at[layer], big)
    merged_load = load(4, v.merged, outer)
    for copy in early:
        copy.wait()
    for push in gives:
        push.wait_recv()

    def through_mid(block):
        upstream = collected(block, parts, landed)
        normed, scale = norm_parts(v.middle_v[block])
        grad_rows = v.grad_out_v[block].astype(f32) + norm_grad(normed, scale, upstream, gain_mid)
        v.grad_middle[block] = grad_rows
        sq.chunk(grad_branch)[block] = grad_rows.astype(bf16)
        terms[1:2] = terms[1:2] + jnp.sum(upstream * normed, axis=0, keepdims=True)

    row_blocks(rows, through_mid)
    mids = sq.spread(grad_branch, v.s_send, v.s_recv)
    reduce_some(0, 1)
    given(2)
    fetch(1)
    own(1)
    unit_load.wait()
    bend_load.wait()
    settle(1)
    reduce_some(1, slices)
    reduce_some(0, 1)

    def through_heads(s):
        tokens = grad_branch[s]
        for head in range(heads):
            cols_k = slice(head * HEAD_K, (head + 1) * HEAD_K)
            cols_v = slice(head * HEAD_V, (head + 1) * HEAD_V)
            grad_merged = mm(tokens, out_t[:, cols_v])
            unit_rows = wide_a[s, :, cols_v].astype(f32)
            first = 2 * wide_k + wide_v + head * HEAD_V
            grad_qkvs[s, :, first : first + HEAD_V] = (
                grad_merged * unit_rows * wide_b[s, :, cols_v].astype(f32)
            ).astype(bf16)
            grad_unit = grad_merged * wide_c[s, :, cols_v].astype(f32)
            grad_mixed = (
                v.inverse_v[s, head]
                * (
                    grad_unit
                    - jnp.mean(grad_unit, axis=-1, keepdims=True)
                    - unit_rows * jnp.mean(grad_unit * unit_rows, axis=-1, keepdims=True)
                )
            ).astype(bf16)
            query, key, val = query_v[s, :, cols_k], key_v[s, :, cols_k], value_v[s, :, cols_v]
            mask = masks[s, head]
            weight = (mm_nt(query, key) * mask).astype(bf16)
            grad_product = (mm_nt(grad_mixed, val) * mask).astype(bf16)
            first = 2 * wide_k + head * HEAD_V
            grad_qkvs[s, :, first : first + HEAD_V] = mm_tn(weight, grad_mixed).astype(bf16)
            grad_qkvs[s, :, cols_k] = turn_back(mm(grad_product, key), tables[0], tables[1], tables[2]).astype(bf16)
            first = wide_k + head * HEAD_K
            grad_qkvs[s, :, first : first + HEAD_K] = turn_back(
                mm_tn(grad_product, query), tables[0], tables[1], tables[3]
            ).astype(bf16)

    mids[0].wait_recv()
    through_heads(sq.own)
    mids[1].wait_recv()
    mids[2].wait_recv()
    through_heads(sq.next)
    if not final_layer:
        keep = pltpu.make_async_copy(grad_qkvs, v.kept_qkvs, v.kept_sem)
        keep.start()
    qkvs_load.wait()
    reduce_some(0, 1)
    for push in gives:
        push.wait_send()
    ends = exchange(grad_qkvs, big, 0, grad_qkvs.shape[-1], parts, landed, 1)
    fetch(2)
    own(2)
    in_load = load(5, v.normed_in_t, v.normed_t)
    transpose_into(v.turned, grad_branch)
    settle(2)
    merged_load.wait()
    given(3)
    in_load.wait()
    given(4)
    fetch(3)
    own(3)
    reduce_some(1, slices)
    reduce_some(0, 1)
    settle(3)
    for push in ends:
        push.wait_recv()

    def through_in(block):
        upstream = collected(block, parts, landed)
        normed, scale = norm_parts(v.x_v[block].astype(f32))
        v.grad_in[block] = (v.grad_middle[block] + norm_grad(normed, scale, upstream, gain_in)).astype(bf16)
        terms[0:1] = terms[0:1] + jnp.sum(upstream * normed, axis=0, keepdims=True)

    row_blocks(rows, through_in)
    if final_layer:

        @pl.when(at.section == 1)
        def _():
            remote(v.grad_in, v.taken_grads, v.row_send.at[1], v.row_recv.at[1], across).start()

    else:
        downs = sq.spread_from(v.grad_in, v.next_down, v.d_send, v.d_recv, v.d_sem)

    if not final_layer:
        fetch(4)
        own(4)
        settle(4)
        for push in mids + ends:
            push.wait_send()
        for e in (3, 4):
            given_copies[e].wait_send()
        for push in downs:
            push.wait()
        keep.wait()
        return

    reduce_some(0, 1)
    given(5)
    fetch(4)
    own(4)
    reduce_some(0, 1)
    given(6)
    settle(4)
    reduce_some(1, slices)
    reduce_some(0, 1)
    fetch(5)
    own(5)
    reduce_some(0, 1)
    fetch(6)
    own(6)
    in_load = load(5, v.later_normed_in_t, v.normed_t)
    qkvs_load = load(3, v.later_qkvs, grad_qkvs)
    hidden_load = load(4, v.later_hidden, outer)
    middle_load = load(6, v.later_middle, v.middle_v)
    down_load = load(0, v.down_all.at[1], big.at[:, pl.ds(2 * wide_f, wide_f)])
    settle(6)
    reduce_some(1, slices)
    reduce_some(0, 1)
    in_load.wait()
    qkvs_load.wait()
    given(7)
    reduce_some(0, 1)
    given(8)
    fetch(7)
    own(7)
    reduce_some(0, 1)
    fetch(8)
    own(8)
    settle(7)
    reduce_some(0, 1)
    for push in mids + ends:
        push.wait_send()
    hidden_load.wait()
    down_load.wait()
    settle(8)
    gives_y = exchange(outer, big, 2 * wide_f, wide_f, parts, v.landed_y, 2)
    reduce_some(1, slices)
    reduce_some(0, slices)
    middle_load.wait()
    for push in gives_y:
        push.wait_recv()

    def last(block):
        v.result[block] = (v.middle_v[block] + collected(block, parts, v.landed_y)).astype(bf16)

    row_blocks(rows, last)

    @pl.when(at.section == 0)
    def _():
        remote(v.result, v.taken_rows, v.row_send.at[0], v.row_recv.at[0], across).start()

    for push in gives_y:
        push.wait_send()
    for e in (7, 8):
        given_copies[e].wait_send()
    reduce_rest(1)
    reduce_rest(0)

    held, hop_land, mine = v.held, v.hop_land, v.held.at[at.section]
    held[0] = terms[...]
    held[1] = v.later_terms[...]
    hop = remote(held, hop_land.at[0], v.t_send.at[0], v.t_recv.at[0], sibling)
    hop.start()
    hop.wait()
    held[...] = held[...] + hop_land[0]
    hop = remote(held.at[other], hop_land.at[1, other], v.t_send.at[1], v.t_recv.at[1], across)
    hop.start()
    hop.wait_send()
    remote(held.at[other], hop_land.at[1, at.section], v.t_send.at[1], v.t_recv.at[1], across).wait_recv()
    mine[...] = mine[...] + hop_land[1, at.section]
    for h, device in ((2, place(tensor=1 - at.tensor)), (3, place(dp=at.dp_at(0, 1)))):
        hop = remote(mine, hop_land.at[h, 0], v.t_send.at[h], v.t_recv.at[h], device)
        hop.start()
        hop.wait()
        mine[...] = mine[...] + hop_land[h, 0]
    hops = []
    for k in range(1, at.groups):
        hop = remote(mine, hop_land.at[3 + k, 0], v.t_send.at[3 + k], v.t_recv.at[3 + k], place(dp=at.dp_at(k, 0)))
        hop.start()
        hops.append(hop)
    total = mine[...]
    for k, hop in zip(range(1, at.groups), hops):
        hop.wait()
        total = total + hop_land[3 + k, 0]
    v.gain_sums[...] = total

    for which, rows_sent in ((0, v.result), (1, v.grad_in)):
        target = v.taken_rows if which == 0 else v.taken_grads
        copy = remote(rows_sent, target, v.row_send.at[which], v.row_recv.at[which], across)
        copy.wait_recv()
        copy.wait_send()

    home_copy(0).wait()
    for j in range(slices - 1):
        z_copy(GROUPS - 1, j).wait_send()

        @pl.loop(0, GROUPS)
        def _(e):
            z_copy(e, j).wait_recv()

    @pl.loop(0, GROUPS)
    def _(e):
        @pl.loop(0, slices)
        def _(j):
            x_copy(e, e, j, v.chip).wait_send()


def backward_layer(layer, grad_out, down, turned_down, x, gains, tables, masks, saved, gathered, dp_size, later=None, x_out=None):
    rows, width = x.shape[-2:]
    length = masks.shape[-1]
    (middle, normed_in_t, query_rot, key_rot, value, unit, inverse, opened, slope_open, merged, normed_mid_t, act, slope,
     hidden) = saved
    vmem = pl.BlockSpec(memory_space=pltpu.VMEM)
    any_spec = pl.BlockSpec(memory_space=pl.ANY)
    final_layer = layer == 0
    slices = dp_size // 2
    slice_rows = width // dp_size
    size = hidden.shape[-1]
    assert value.shape[-1] == size and 2 * query_rot.shape[-1] == size
    block = (slices, slice_rows, size)

    def held(*shape, kind=bf16):
        return pltpu.VMEM(shape, kind)

    def stored(*shape, kind=bf16):
        return jax.ShapeDtypeStruct(shape, kind)

    dma = pltpu.SemaphoreType.DMA
    operands = [grad_out, gains, tables, masks]
    operands += [x, middle, normed_in_t, query_rot, key_rot, value, unit, inverse, opened, slope_open, merged, normed_mid_t,
                 act, slope, hidden]
    operands += [*gathered, down]
    if not final_layer:
        operands += [turned_down]
    in_specs = [any_spec, vmem] + [any_spec] * (len(operands) - 2)
    count = 2 * GROUPS - KEPT if final_layer else KEPT
    out_shape = [stored(rows, width), stored(count, *block), stored(count, *block)]
    out_specs = [vmem, any_spec, any_spec]
    if final_layer:
        later_chip, later_terms, later_qkvs, later_saved = later
        operands += [later_chip, later_terms, x_out, later_saved[1], later_qkvs, later_saved[-1], later_saved[0]]
        in_specs += [any_spec, vmem] + [any_spec] * 5
        out_shape += [stored(GROUPS, *block), stored(GROUPS, dp_size // 4, slice_rows, 2 * size), stored(2, width, kind=f32),
                      stored(rows, width), stored(rows, width), stored(rows, width)]
        out_specs += [any_spec, any_spec, vmem, vmem, any_spec, any_spec]
    else:
        out_shape += [stored(2, width, kind=f32), stored(2, length, width), stored(2, length, 3 * size)]
        out_specs += [vmem, any_spec, any_spec]
    scratch = [
        held(width, 3 * size),
        held(width, size),
        held(*query_rot.shape),
        held(*key_rot.shape),
        held(*value.shape),
        held(2, length, size),
        held(2, length, size),
        held(2, length, size),
        held(*inverse.shape, kind=f32),
        held(rows, width),
        held(rows, width, kind=f32),
        held(width, 2 * length),
        held(2, length, size),
        held(2, length, width),
        held(2, length, 2 * size),
        held(2, length, width),
        held(2, length, 3 * size),
        held(width, 2 * length),
        held(2, length, width),
        held(3, rows, width),
        held(rows, width, kind=f32),
        held(2, *block),
        held(*block),
        held(*block),
        dma((19,)),
        dma((3,)),
        dma((3,)),
        dma((3, 3)),
        dma((3, 3)),
        dma((count,)),
        dma((count,)),
        dma((2,)),
        held(*masks.shape, kind=f32),
        held(*tables.shape, kind=f32),
        held(rows, width),
    ]
    if final_layer:
        hops = 3 + dp_size // 4
        scratch += [
            held(2, slice_rows, size),
            held(2, slice_rows, size),
            held(*block),
            dma((3, 2)),
            dma((GROUPS, slices)),
            dma((GROUPS, slices)),
            dma((GROUPS, slices - 1)),
            dma((GROUPS, slices - 1)),
            held(2, width, kind=f32),
            held(2, 2, width, kind=f32),
            held(hops, 2, 2, width, kind=f32),
            dma((hops,)),
            dma((hops,)),
            dma((2,)),
            dma((2,)),
            held(3, rows, width),
        ]
    else:
        scratch += [dma((3,)), dma((3,)), dma, dma, held(2, length, width)]
    return pl.pallas_call(
        functools.partial(backward_kernel, dp_size, layer),
        out_shape=out_shape,
        in_specs=in_specs,
        out_specs=out_specs,
        scratch_shapes=scratch,
        compiler_params=pltpu.CompilerParams(
            collective_id=4 + layer, has_side_effects=True, vmem_limit_bytes=VMEM_LIMIT
        ),
        name="backward_layer",
    )(*operands)


def nested(outs):
    return (*outs[:6], outs[6:-2], *outs[-2:])


def on_device(
    dp_size,
    layer_input,
    segment_ids,
    output_grad,
    query_weight,
    key_weight,
    value_weight,
    swish_weight,
    output_weight,
    gate_weight,
    up_weight,
    down_weight,
    mixer_gain,
    ffn_gain,
):
    at = Place(dp_size)
    section_first = at.section == 0
    width = layer_input.shape[2]
    length = segment_ids.shape[1]
    quarter_k = query_weight.shape[2] // 2
    heads_here = quarter_k // HEAD_K
    cosine, sine, growth = rotation_tables(length, HEAD_K // 2)
    tables = jnp.stack([cosine, sine, growth, 1.0 / growth])

    shards = (query_weight[0], key_weight[0], value_weight[0], swish_weight[0], output_weight[0].T, gate_weight[0],
              up_weight[0], down_weight[0].T)
    *gathered, all_gains, masks, first_saved, second_down, first_sent = nested(
        forward_layer(
            0, (layer_input, mixer_gain, ffn_gain, segment_ids, tables, output_grad), shards, length, heads_here, dp_size
        )
    )
    *second_saved, turned_down = forward_layer(
        1, (first_sent, all_gains, tables, masks, second_down), gathered, length, heads_here, dp_size
    )
    gathered = [g.reshape(2, width, g.shape[-1]) for g in gathered]
    second_grad, later_chip, _, later_terms, first_down, later_qkvs = backward_layer(
        1, output_grad, second_down, turned_down, first_sent, all_gains, tables, masks, second_saved, gathered, dp_size
    )
    first_grad, _, _, _, landed, my_gains, second_sent, taken_rows, taken_grads = backward_layer(
        0, second_grad, first_down, None, layer_input, all_gains, tables, masks, first_saved, gathered, dp_size,
        (later_chip, later_terms, later_qkvs, second_saved), first_sent,
    )

    def by_layer(first, second, taken):
        return jnp.where(section_first, jnp.stack([first, taken]), jnp.stack([taken, second]))[None]

    def shard(e):
        return jnp.sum(landed[e].astype(f32), axis=0)

    def columns(e, start, size):
        step = landed.shape[-1] // 2
        part = jnp.concatenate([landed[e, :, :, p * step + start : p * step + start + size] for p in range(2)], axis=-1)
        return jnp.sum(part.astype(f32), axis=0)

    return (
        by_layer(first_sent, second_sent, taken_rows),
        by_layer(first_grad, second_grad, taken_grads),
        columns(4, 0, quarter_k)[None],
        columns(4, quarter_k, quarter_k)[None],
        shard(5)[None],
        shard(6)[None],
        shard(3).T[None],
        shard(1)[None],
        shard(2)[None],
        shard(0).T[None],
        my_gains[0][None],
        my_gains[1][None],
    )


def solution(mesh):
    in_specs = (
        P(None, ("dp", "tensor"), None),
        P(None, "dp"),
        P(None, ("dp", "tensor"), None),
        P("section", "dp", "tensor"),
        P("section", "dp", "tensor"),
        P("section", "dp", "tensor"),
        P("section", "dp", "tensor"),
        P("section", "tensor", "dp"),
        P("section", "dp", "tensor"),
        P("section", "dp", "tensor"),
        P("section", "tensor", "dp"),
        P("section", None),
        P("section", None),
    )
    out_specs = (
        P("section", None, ("dp", "tensor"), None),
        P("section", None, ("dp", "tensor"), None),
        P("section", "dp", "tensor"),
        P("section", "dp", "tensor"),
        P("section", "dp", "tensor"),
        P("section", "dp", "tensor"),
        P("section", "tensor", "dp"),
        P("section", "dp", "tensor"),
        P("section", "dp", "tensor"),
        P("section", "tensor", "dp"),
        P("section", None),
        P("section", None),
    )
    return jax.shard_map(
        functools.partial(on_device, mesh.shape["dp"]),
        mesh=mesh,
        in_specs=in_specs,
        out_specs=out_specs,
        check_vma=False,
    )
```

```python
import functools

import jax
import jax.numpy as jnp
from jax import lax
from jax.experimental import pallas as pl
from jax.experimental.pallas import tpu as pltpu
from jax.sharding import PartitionSpec as P

HEAD_K = 256
HEAD_V = 512
MESH = pl.DeviceIdType.MESH

epsilon = 1e-05
group_guard = 1.0
bf16 = jnp.bfloat16
f32 = jnp.float32


def rotation_tables(length, half_width):
    pair_index = jnp.arange(half_width).astype(f32)
    position = jnp.arange(length).astype(f32)[:, None]
    angle = position * jnp.exp(-jnp.log(10000.0) * pair_index / half_width)
    zeta = (pair_index / half_width + 0.4) / 1.4
    growth = jnp.exp(position / 512.0 * jnp.log(zeta))
    return (jnp.cos(angle), jnp.sin(angle), growth)


class Place:
    def __init__(self, dp_size):
        self.groups = dp_size // 4
        self.section = lax.axis_index("section")
        self.dp = lax.axis_index("dp")
        self.tensor = lax.axis_index("tensor")
        self.core = self.dp % 2
        self.low = (self.dp // 2) % 2
        self.group = self.dp // 4

    def dp_at(self, group_step, low_step):
        group = (self.group + group_step + self.groups) % self.groups
        return (group * 2 + (self.low + low_step) % 2) * 2 + self.core

    def sibling(self):
        return self.dp + 1 - 2 * self.core


SQUARE = ((0, 1), (1, 0), (1, 1))
TILE = 512
VMEM_LIMIT = 63 * 1024 * 1024


def mm(left, right):
    return lax.dot_general(left, right, (((1,), (0,)), ((), ())), preferred_element_type=f32)


def mm_nt(left, right):
    return lax.dot_general(left, right, (((1,), (1,)), ((), ())), preferred_element_type=f32)


def mm_tn(left, right):
    return lax.dot_general(left, right, (((0,), (0,)), ((), ())), preferred_element_type=f32)


class Square:
    def __init__(self, dp_size, rows):
        self.at = Place(dp_size)
        self.rows = rows
        self.own = self.at.low
        self.next = 1 - self.at.low

    def device(self, low_step, tensor_step):
        return (self.at.section, self.at.dp_at(0, low_step), (self.at.tensor + tensor_step) % 2)

    def barrier(self):
        barrier = pltpu.get_barrier_semaphore()
        for step in SQUARE:
            pl.semaphore_signal(barrier, inc=1, device_id=self.device(*step), device_id_type=MESH)
        pl.semaphore_wait(barrier, len(SQUARE))

    def chunk(self, ref, low_step=0, tensor_step=0):
        start = pl.multiple_of((self.at.tensor + tensor_step) % 2 * self.rows, self.rows)
        return ref.at[(self.at.low + low_step) % 2, pl.ds(start, self.rows)]

    def copy(self, src, dst, send, recv, step):
        return pltpu.make_async_remote_copy(
            src_ref=src,
            dst_ref=dst,
            send_sem=send,
            recv_sem=recv,
            device_id=self.device(*step),
            device_id_type=MESH,
        )

    def spread(self, ref, send, recv, own=None, here=None):
        return Spread(self, ref, send, recv, own, here)

    def give(self, parts, landed, send, recv, j):
        push = self.copy(self.chunk(parts, *SQUARE[j]), landed.at[j], send.at[j], recv.at[j], SQUARE[j])
        push.start()
        return push


class Spread:
    def __init__(self, sq, ref, send, recv, own, here):
        self.sq, self.ref, self.send, self.recv = sq, ref, send, recv
        self.half = sq.rows // 2
        source = sq.chunk(ref) if own is None else own
        self.local = None
        if own is not None:
            self.local = pltpu.make_async_copy(own, sq.chunk(ref), here)
            self.local.start()
        beside, below = (0, 1), (1, 0)
        self.first = [
            self.push(source, sq.chunk(ref), half, j, step)
            for j, (half, step) in enumerate(((0, beside), (1, below), (1, beside), (0, below)))
        ]
        from_beside, from_below = sq.chunk(ref, *beside), sq.chunk(ref, *below)
        self.onward = [
            self.push(from_beside, from_beside, 0, 4, below, start=False),
            self.push(from_below, from_below, 1, 5, beside, start=False),
        ]

    def push(self, source, target, half, j, step, start=True):
        block = pl.ds(half * self.half, self.half)
        copy = self.sq.copy(source.at[block], target.at[block], self.send.at[j], self.recv.at[j], step)
        if start:
            copy.start()
        return copy

    def wait_own(self):
        for came, onward in zip(self.first[:2], self.onward):
            came.wait_recv()
            onward.start()
        self.first[2].wait_recv()

    def wait_next(self):
        self.first[3].wait_recv()
        for onward in self.onward:
            onward.wait_recv()

    def wait_recv(self):
        self.wait_own()
        self.wait_next()

    def wait_send(self):
        for copy in self.first + self.onward:
            copy.wait_send()
        if self.local is not None:
            self.local.wait()


def row_blocks(rows, body, block=32):
    block = min(block, rows)

    @pl.loop(0, rows // block)
    def _(i):
        body(pl.ds(pl.multiple_of(i * block, block), block))


def norm_parts(values):
    centred = values - jnp.mean(values, axis=-1, keepdims=True)
    scale = lax.rsqrt(jnp.mean(centred * centred, axis=-1, keepdims=True) + epsilon)
    return centred * scale, scale


def norm_grad(normed, scale, upstream, gain):
    through = upstream * gain
    return scale * (
        through
        - jnp.mean(through, axis=-1, keepdims=True)
        - normed * jnp.mean(through * normed, axis=-1, keepdims=True)
    )


def turn(values, cosine, sine, scale):
    half = values.shape[-1] // 2
    a, b = values[:, :half], values[:, half:]
    return jnp.concatenate([(a * cosine - b * sine) * scale, (a * sine + b * cosine) * scale], axis=-1)


def turn_back(values, cosine, sine, scale):
    half = values.shape[-1] // 2
    a, b = values[:, :half] * scale, values[:, half:] * scale
    return jnp.concatenate([a * cosine + b * sine, b * cosine - a * sine], axis=-1)


def transpose_into(target, source):
    _, length, width = source.shape
    for s in range(2):
        for start in range(0, width, TILE):
            target[start : start + TILE, s * length : (s + 1) * length] = source[s, :, start : start + TILE].T


def forward_kernel(dp_size, layer, *refs):
    streams = layer == 0
    v = Refs()
    if streams:
        (v.x, v.mixer_gain, v.ffn_gain, v.ids, v.tables, v.out_grad, *refs) = refs
        shards, refs = refs[:8], refs[8:]
        stored, refs = refs[:4], refs[4:]
        (v.gains, v.masks, *refs) = refs
    else:
        (v.x, v.gains, v.tables, v.masks, v.down, *refs) = refs
        stored, refs = refs[:4], refs[4:]
    saved, refs = refs[:14], refs[14:]
    if streams:
        (v.grad_down, result, *refs) = refs
    else:
        (v.turned_down, *refs) = refs
    scratch, refs = refs[:14], refs[14:]
    (middle, normed_in_t, query_rot, key_rot, value, unit, inverse, opened, slope_open, merged, normed_mid_t, act, slope,
     hidden) = scratch
    save_sem, x_v, masks, tables, in_sem, *refs = refs
    held, refs = refs[:4], refs[4:]
    (w_sem, normed_in, *refs) = refs
    if streams:
        (normed_mid, *refs) = refs
    else:
        normed_mid = normed_mid_t
    (parts, landed, s_send, s_recv, g_send, g_recv, *refs) = refs
    x = x_v
    rows, width = x.shape
    sq = Square(dp_size, rows)
    at = sq.at
    sources = [(v.x.at[at.section] if streams else v.x, x_v), (v.tables, tables)]
    if not streams:
        sources.append((v.masks, masks))
    operand_copies = [
        pltpu.make_async_copy(source, target, in_sem.at[i]) for i, (source, target) in enumerate(sources)
    ]
    for copy in operand_copies:
        copy.start()
    operand_copies[0].wait()
    saves = []

    def save(*which):
        for i in which:
            copy = pltpu.make_async_copy(scratch[i], saved[i], save_sem.at[i])
            copy.start()
            saves.append(copy)

    qkvs, out_t, gate_up, down_t = held
    wide_k = query_rot.shape[-1]
    wide_v = value.shape[-1]
    wide_f = hidden.shape[-1]
    heads = wide_k // HEAD_K
    slices = dp_size // 2
    other = 1 - at.section
    groups = [(0, 0, wide_k), (0, wide_k, wide_k), (0, 2 * wide_k, wide_v), (0, 2 * wide_k + wide_v, wide_v),
              (1, 0, wide_v), (2, 0, wide_f), (2, wide_f, wide_f), (3, 0, wide_f)]
    loads = {}

    def load(i):
        which, first, size = groups[i]
        columns = pl.ds(first, size)
        loads[i] = pltpu.make_async_copy(
            stored[which].at[layer, :, :, :, columns], held[which].at[:, :, :, columns], w_sem.at[i]
        )
        loads[i].start()

    def weight(which, first, size):
        return held[which][:, :, :, first : first + size].reshape(width, size)

    def first_norm(block):
        unit_rows, _ = norm_parts(x[block].astype(f32))
        sq.chunk(normed_in)[block] = (unit_rows * v.gains[layer, 0:1]).astype(bf16)

    def project(i, s):
        loads_wait(i)
        first, size = groups[i][1:]
        tokens = normed_in[s]
        for start in range(0, size, TILE):
            wide = mm(tokens, weight(0, first + start, TILE))
            cols = slice(start, start + TILE)
            if i < 2:
                dest = (query_rot, key_rot)[i]
                for head in range(TILE // HEAD_K):
                    part = wide[:, head * HEAD_K : (head + 1) * HEAD_K]
                    dest[s, :, start + head * HEAD_K : start + (head + 1) * HEAD_K] = turn(
                        part, tables[0], tables[1], tables[2 + i]
                    ).astype(bf16)
            elif i == 2:
                value[s, :, cols] = wide.astype(bf16)
            else:
                sigmoid = 1.0 / (1.0 + jnp.exp(-wide))
                opened[s, :, cols] = (wide * sigmoid).astype(bf16)
                slope_open[s, :, cols] = (sigmoid * (1.0 + wide * (1.0 - sigmoid))).astype(bf16)

    waited = []

    def loads_wait(i):
        if i not in waited:
            waited.append(i)
            loads[i].wait()

    def retain(s):
        for head in range(heads):
            cols_k = slice(head * HEAD_K, (head + 1) * HEAD_K)
            cols_v = slice(head * HEAD_V, (head + 1) * HEAD_V)
            product = mm_nt(query_rot[s, :, cols_k], key_rot[s, :, cols_k])
            weights = (product * masks[s, head]).astype(bf16)
            mixed = mm(weights, value[s, :, cols_v])
            centred = mixed - jnp.mean(mixed, axis=-1, keepdims=True)
            scale = lax.rsqrt(jnp.mean(centred * centred, axis=-1, keepdims=True) + group_guard)
            unit_rows = centred * scale
            inverse[s, head] = scale
            unit[s, :, cols_v] = unit_rows.astype(bf16)
            merged[s, :, cols_v] = (unit_rows * opened[s, :, cols_v].astype(f32)).astype(bf16)

    def give_back(s, source, weight_t):
        tokens = source[s]
        step = width // slices
        for i in range(slices):
            parts[s, :, i * step : (i + 1) * step] = mm_nt(tokens, weight_t[i].reshape(step, -1)).astype(bf16)

    def collected(block, which):
        total = sq.chunk(parts)[block].astype(f32)
        for j in range(len(SQUARE)):
            total = total + landed[which, j, block].astype(f32)
        return total

    def give(s, which):
        send, recv = g_send.at[which], g_recv.at[which]
        return [sq.give(parts, landed.at[which], send, recv, j) for j in ((1, 2) if s == 1 else (0,))]

    def second_norm(block):
        middle_rows = x[block].astype(f32) + collected(block, 0)
        middle[block] = middle_rows
        unit_rows, _ = norm_parts(middle_rows)
        sq.chunk(normed_mid)[block] = (unit_rows * v.gains[layer, 1:2]).astype(bf16)

    def feed(s):
        loads_wait(5)
        loads_wait(6)
        tokens = normed_mid[s]
        for start in range(0, wide_f, TILE):
            cols = slice(start, start + TILE)
            gate = mm(tokens, weight(2, start, TILE))
            up = mm(tokens, weight(2, wide_f + start, TILE))
            square = gate * gate
            bend = jnp.tanh(0.7978845608028654 * gate * (1.0 + 0.044715 * square))
            half = 0.5 * (1.0 + bend)
            gelu = gate * half
            slope_gelu = half + 0.5 * gate * (1.0 - bend * bend) * (
                0.7978845608028654 * (1.0 + 3 * 0.044715 * square)
            )
            act[s, :, cols] = gelu.astype(bf16)
            slope[s, :, cols] = (slope_gelu * up).astype(bf16)
            hidden[s, :, cols] = (gelu * up).astype(bf16)

    if not streams:
        (down_v, turned_v, down_sem) = refs
        down_load = pltpu.make_async_copy(v.down, down_v, down_sem.at[0])
        down_load.start()
        down_save = pltpu.make_async_copy(turned_v, v.turned_down, down_sem.at[1])

        def turn_down(condition):
            @pl.when(condition)
            def _():
                down_load.wait()
                transpose_into(turned_v, down_v)
                down_save.start()

        for i in range(7):
            load(i)
        turn_down(at.core == at.section)
        row_blocks(rows, first_norm)
        sq.barrier()
        ins = sq.spread(normed_in, s_send.at[0], s_recv.at[0])
        operand_copies[1].wait()
        operand_copies[2].wait()
        ins.wait_own()
        for i in range(4):
            project(i, sq.own)
        ins.wait_next()
        for i in range(4):
            project(i, sq.next)
        save(2, 3, 4, 7, 8)
        retain(sq.next)
        loads_wait(4)
        give_back(sq.next, merged, out_t)
        gives = give(1, 0)
        retain(sq.own)
        give_back(sq.own, merged, out_t)
        gives += give(0, 0)
        save(5, 6, 9)
        transpose_into(normed_in_t, normed_in)
        save(1)
        turn_down(at.core != at.section)
        for push in gives:
            push.wait_recv()
        row_blocks(rows, second_norm)
        save(0)
        mids = sq.spread(normed_mid, s_send.at[1], s_recv.at[1])
        mids.wait_own()
        feed(sq.own)
        mids.wait_next()
        save(10)
        feed(sq.next)
        save(11, 12, 13)
        for push in [ins, mids] + gives:
            push.wait_send()
        for copy in saves:
            copy.wait()
        down_save.wait()
        return

    (z_send, z_recv, x_send, x_recv, c_send, c_recv, o_send, o_recv, here_sem, gain_send, gain_recv, d_send, d_recv,
     d_sem, own_gains, ids_land, id_send, id_recv, mask_sem) = refs
    steps = [(k, b) for k in range(at.groups) for b in range(2)][1:]

    def place(section=None, dp=None):
        return (at.section if section is None else section, at.dp if dp is None else dp, at.tensor)

    def copy(src, dst, send, recv, device):
        return pltpu.make_async_remote_copy(
            src_ref=src, dst_ref=dst, send_sem=send, recv_sem=recv, device_id=device, device_id_type=MESH
        )

    partners = [sq.device(*step) for step in SQUARE] + [place(dp=at.sibling()), place(section=other)]
    partners += [place(dp=at.dp_at(k, b)) for k, b in steps if (k, b) != (0, 1)]
    barrier = pltpu.get_barrier_semaphore()
    for partner in partners:
        pl.semaphore_signal(barrier, inc=1, device_id=partner, device_id_type=MESH)
    pl.semaphore_wait(barrier, len(partners))

    own_gains[0:1] = v.mixer_gain[...]
    own_gains[1:2] = v.ffn_gain[...]
    gain_copy = copy(own_gains, v.gains.at[at.section], gain_send, gain_recv, place(section=other))
    gain_copy.start()
    v.gains[at.section] = own_gains[...]
    id_copy = copy(v.ids, ids_land, id_send, id_recv, sq.device(1, 0))
    id_copy.start()

    def make_masks():
        length = masks.shape[-1]
        t = lax.broadcasted_iota(jnp.int32, (length, length), 0).astype(f32)
        s = lax.broadcasted_iota(jnp.int32, (length, length), 1).astype(f32)
        distance = jnp.maximum(t - s, 0.0)
        decays = []
        for head in range(heads):
            number = jnp.full((1, 1), ((at.tensor * 2 + at.low) * heads + head).astype(f32))
            rate = jnp.log(1.0 - jnp.exp2(-5.0 - number))
            decays.append(jnp.exp(rate * distance) * HEAD_K ** (-0.5))
        for sequence, ids in ((sq.own, v.ids), (sq.next, ids_land)):
            row = ids[pl.ds(at.section, 1), :]
            same = t >= s
            for document in (1, 2):
                start = jnp.sum(jnp.where(row < document, 1.0, 0.0), axis=1, keepdims=True)
                same = jnp.logical_and(same, (t >= start) == (s >= start))
            for head in range(heads):
                masks[sequence, head] = jnp.where(same, decays[head], 0.0)

    def slot(i, section, dp):
        which, first, size = groups[i]
        return stored[which].at[section, dp // 2, dp % 2, :, pl.ds(first, size)]

    def block(i, section, core):
        which, first, size = groups[i]
        return stored[which].at[section, :, core, :, pl.ds(first, size)]

    def part(i, b):
        size = groups[i][2]
        return shards[i].at[:, pl.ds(pl.multiple_of((at.low + b) % 2 * size, size), size)]

    z_copies, x_copies, here, core_own, core_other = {}, {}, {}, {}, {}

    def push_own(i):
        mine = slot(i, at.section, at.dp)
        for j, (k, b) in enumerate(steps):
            z_copies[i, j] = copy(part(i, b), mine, z_send.at[i, j], z_recv.at[i, j], place(dp=at.dp_at(k, b)))
            z_copies[i, j].start()
        x_copies[i, 0] = copy(part(i, 0), mine, x_send.at[i, 0], x_recv.at[i, 0], place(section=other))
        x_copies[i, 0].start()
        here[i] = pltpu.make_async_copy(part(i, 0), mine, here_sem.at[i])
        here[i].start()

    def pass_on(i):
        for j, (k, b) in enumerate(steps):
            z_copies[i, j].wait_recv()
            arrived = slot(i, at.section, at.dp_at(-k, b))
            x_copies[i, j + 1] = copy(arrived, arrived, x_send.at[i, j + 1], x_recv.at[i, j + 1], place(section=other))
            x_copies[i, j + 1].start()
        here[i].wait()
        mine = block(i, at.section, at.core)
        core_own[i] = copy(mine, mine, c_send.at[i], c_recv.at[i], place(dp=at.sibling()))
        core_own[i].start()

    def share_other(i):
        for j in range(slices):
            x_copies[i, j].wait_recv()
        theirs = block(i, other, at.core)
        core_other[i] = copy(theirs, theirs, o_send.at[i], o_recv.at[i], place(dp=at.sibling()))
        core_other[i].start()

    def arrive(i):
        @pl.when(at.section == 0)
        def _():
            core_own[i].wait_recv()

        @pl.when(at.section == 1)
        def _():
            core_other[i].wait_recv()

        load(i)

    ahead = 3
    for i in range(ahead):
        push_own(i)
    gain_copy.wait_recv()
    row_blocks(rows, first_norm)
    ins = sq.spread(normed_in, s_send.at[0], s_recv.at[0])

    def advance(i):
        pass_on(i)
        if i + ahead < 8:
            push_own(i + ahead)
        if i > 0:
            share_other(i - 1)
            arrive(i - 1)

    advance(0)
    downs = sq.spread(v.grad_down, d_send, d_recv, v.out_grad.at[at.section], d_sem)
    id_copy.wait_recv()
    make_masks()
    mask_save = pltpu.make_async_copy(masks, v.masks, mask_sem)
    mask_save.start()
    ins.wait_recv()
    advance(1)
    downs.wait_recv()
    transpose_into(normed_in_t, normed_in)
    save(1)
    operand_copies[1].wait()
    for i in range(2, 5):
        advance(i)
        for s in (sq.own, sq.next):
            project(i - 2, s)
    advance(5)
    for s in (sq.own, sq.next):
        project(3, s)
    retain(sq.next)
    loads_wait(4)
    give_back(sq.next, merged, out_t)
    gives = give(1, 0)
    retain(sq.own)
    give_back(sq.own, merged, out_t)
    gives += give(0, 0)
    advance(6)
    for push in gives:
        push.wait_recv()
    row_blocks(rows, second_norm)
    mids = sq.spread(normed_mid, s_send.at[1], s_recv.at[1])
    mids.wait_recv()
    advance(7)
    transpose_into(normed_mid_t, normed_mid)
    save(0, 2, 3, 4, 5, 6, 7, 8, 9, 10)
    feed(sq.next)
    feed(sq.own)
    save(11, 12, 13)
    for push in gives:
        push.wait_send()

    def last_group():
        for j in range(slices):
            x_copies[7, j].wait_recv()
        core_other[7].start()

    theirs = block(7, other, at.core)
    core_other[7] = copy(theirs, theirs, o_send.at[7], o_recv.at[7], place(dp=at.sibling()))

    @pl.when(at.section == 1)
    def _():
        last_group()

    arrive(7)
    loads_wait(7)
    give_back(sq.next, hidden, down_t)
    ends = give(1, 1)
    give_back(sq.own, hidden, down_t)
    ends += give(0, 1)

    @pl.when(at.section == 0)
    def _():
        last_group()

    for push in ends:
        push.wait_recv()

    def last(block):
        result[block] = (middle[block] + collected(block, 1)).astype(bf16)

    row_blocks(rows, last)

    @pl.when(at.section == 0)
    def _():
        for i in range(8):
            core_other[i].wait_recv()

    @pl.when(at.section == 1)
    def _():
        for i in range(8):
            core_own[i].wait_recv()

    for push in [downs, ins, mids] + ends + list(z_copies.values()) + list(x_copies.values()):
        push.wait_send()
    for i in range(8):
        core_own[i].wait_send()
        core_other[i].wait_send()
    gain_copy.wait_send()
    id_copy.wait_send()
    mask_save.wait()
    for copy in saves:
        copy.wait()


def forward_layer(layer, operands, weights, length, heads, dp_size):
    rows, width = operands[0].shape[-2:]
    streams = layer == 0
    slices = dp_size // 2
    quarter_k = heads * HEAD_K
    quarter_v = heads * HEAD_V
    quarter_f = weights[-1].shape[-1] // 2 if streams else weights[-1].shape[-1]
    vmem = pl.BlockSpec(memory_space=pltpu.VMEM)
    any_spec = pl.BlockSpec(memory_space=pl.ANY)
    wides = (2 * quarter_k + 2 * quarter_v, quarter_v, 2 * quarter_f, quarter_f)

    def tokens(wide, kind=bf16):
        return jax.ShapeDtypeStruct((2, length, wide), kind)

    turned = jax.ShapeDtypeStruct((width, 2 * length), bf16)
    dma = pltpu.SemaphoreType.DMA
    out_shape = [
        jax.ShapeDtypeStruct((rows, width), f32),
        turned,
        tokens(quarter_k),
        tokens(quarter_k),
        tokens(quarter_v),
        tokens(quarter_v),
        jax.ShapeDtypeStruct((2, heads, length, 1), f32),
        tokens(quarter_v),
        tokens(quarter_v),
        tokens(quarter_v),
        turned if streams else tokens(width),
        tokens(quarter_f),
        tokens(quarter_f),
        tokens(quarter_f),
    ]
    out_specs = [any_spec] * len(out_shape)
    scratch = [pltpu.VMEM(out.shape, out.dtype) for out in out_shape]
    mask_shape = (2, heads, length, length)
    scratch += [
        dma((14,)),
        pltpu.VMEM((rows, width), bf16),
        pltpu.VMEM(mask_shape, f32),
        pltpu.VMEM((4, length, HEAD_K // 2), f32),
        dma((3,)),
    ]
    scratch += [pltpu.VMEM((slices, 2, width // dp_size, wide), bf16) for wide in wides] + [
        dma((8,)),
    ] + [pltpu.VMEM((2, length, width), bf16)] * (3 if streams else 2) + [
        pltpu.VMEM((2, 3, rows, width), bf16),
        dma((2, 6)),
        dma((2, 6)),
        dma((2, 3)),
        dma((2, 3)),
    ]
    if streams:
        out_shape = (
            [jax.ShapeDtypeStruct((2, slices, 2, width // dp_size, wide), bf16) for wide in wides]
            + [jax.ShapeDtypeStruct((2, 2, width), f32), jax.ShapeDtypeStruct(mask_shape, f32)]
            + out_shape
            + [tokens(width), jax.ShapeDtypeStruct((rows, width), bf16)]
        )
        out_specs = [any_spec] * 4 + [vmem, any_spec] + out_specs + [any_spec, vmem]
        scratch += [
            dma((8, slices - 1)),
            dma((8, slices - 1)),
            dma((8, slices)),
            dma((8, slices)),
            dma((8,)),
            dma((8,)),
            dma((8,)),
            dma((8,)),
            dma((8,)),
            dma,
            dma,
            dma((6,)),
            dma((6,)),
            dma,
            pltpu.VMEM((2, width), f32),
            pltpu.VMEM((2, length), jnp.int32),
            dma,
            dma,
            dma,
        ]
        in_specs = [any_spec, vmem, vmem, vmem, any_spec, any_spec]
    else:
        out_shape = out_shape + [turned]
        out_specs = out_specs + [any_spec]
        scratch += [pltpu.VMEM((2, length, width), bf16), pltpu.VMEM(turned.shape, bf16), dma((2,))]
        in_specs = [any_spec, vmem, any_spec, any_spec, any_spec]
    return pl.pallas_call(
        functools.partial(forward_kernel, dp_size, layer),
        out_shape=out_shape,
        in_specs=in_specs + [any_spec] * len(weights),
        out_specs=out_specs,
        scratch_shapes=scratch,
        compiler_params=pltpu.CompilerParams(
            collective_id=1 + layer, has_side_effects=True, vmem_limit_bytes=VMEM_LIMIT
        ),
        name="forward_layer",
    )(*operands, *weights)


class Refs:
    pass


KEPT = 5
GROUPS = 7


def backward_kernel(dp_size, layer, *refs):
    final_layer = layer == 0
    v = Refs()
    (v.grad_out, v.gains, v.tables, v.masks, v.x, v.middle, v.normed_in_t, v.query_rot, v.key_rot, v.value, v.unit,
     v.inverse, v.opened, v.slope_open, v.merged, v.normed_mid_t, v.act, v.slope, v.hidden,
     v.qkvs_all, v.out_all, v.gate_up_all, v.down_all, v.down_in, *refs) = refs
    if not final_layer:
        v.down_turned, *refs = refs
    if final_layer:
        (v.later_chip, v.later_terms, v.first_rows, v.later_normed_in_t, v.later_qkvs, v.later_hidden, v.later_middle,
         *refs) = refs
    v.grad_in, v.chip, v.core_land, *refs = refs
    if final_layer:
        v.x_land, v.final, v.gain_sums, v.result, v.taken_rows, v.taken_grads, *refs = refs
    else:
        v.terms, v.next_down, v.kept_qkvs, *refs = refs
    (v.big, v.out_t, v.query_v, v.key_v, v.value_v, v.wide_a, v.wide_b, v.wide_c, v.inverse_v, v.x_v, v.middle_v,
     v.normed_t, v.outer, v.grad_down, v.grad_gate_up, v.grad_branch, v.grad_qkvs, v.turned, v.parts, v.landed,
     v.grad_middle, v.stage_given, v.stage_own, v.core_part, v.load_sem, v.s_send, v.s_recv, v.g_send, v.g_recv,
     v.c_send, v.c_recv, v.local_sem, v.masks_v, v.tables_v, v.grad_out_v, *refs) = refs
    if final_layer:
        (v.left, v.right, v.sums, v.r_sem, v.x_send, v.x_recv, v.z_send, v.z_recv, v.terms, v.held, v.hop_land,
         v.t_send, v.t_recv, v.row_send, v.row_recv, v.landed_y) = refs
    else:
        v.d_send, v.d_recv, v.d_sem, v.kept_sem, v.mid_v = refs
    at = Place(dp_size)
    rows, width = v.x.shape[-2:]
    sq = Square(dp_size, rows)
    masks, tables, gains = v.masks_v, v.tables_v, v.gains
    query_v, key_v, value_v = v.query_v, v.key_v, v.value_v
    wide_a, wide_b, wide_c = v.wide_a, v.wide_b, v.wide_c
    grad_down, grad_gate_up, grad_branch, grad_qkvs = v.grad_down, v.grad_gate_up, v.grad_branch, v.grad_qkvs
    big, out_t, outer, parts, landed, terms = v.big, v.out_t, v.outer, v.parts, v.landed, v.terms
    wide_k = query_v.shape[-1]
    wide_v = value_v.shape[-1]
    wide_f = outer.shape[-1]
    heads = wide_k // HEAD_K
    slices = dp_size // 2
    slice_rows = width // dp_size
    gain_in = gains[layer, 0:1]
    gain_mid = gains[layer, 1:2]
    other = 1 - at.section
    steps = [(k, b) for k in range(at.groups) for b in range(2)]
    steps = steps[1:] + steps[:1]

    def load(index, source, target):
        copy = pltpu.make_async_copy(source, target, v.load_sem.at[index])
        copy.start()
        return copy

    def remote(src, dst, send, recv, device):
        return pltpu.make_async_remote_copy(
            src_ref=src, dst_ref=dst, send_sem=send, recv_sem=recv, device_id=device, device_id_type=MESH
        )

    def place(section=None, dp=None, tensor=None):
        return (
            at.section if section is None else section,
            at.dp if dp is None else dp,
            at.tensor if tensor is None else tensor,
        )

    sibling = place(dp=at.sibling())
    across = place(section=other)

    token_load = load(14, v.down_in, grad_down)
    down_load = load(0, v.down_all.at[layer], big.at[:, pl.ds(2 * wide_f, wide_f)])
    act_load = load(1, v.act, wide_a)
    slope_load = load(2, v.slope, wide_b)
    gate_load = load(3, v.gate_up_all.at[layer], big.at[:, pl.ds(0, 2 * wide_f)])
    hidden_load = load(4, v.hidden, outer)
    if not final_layer:
        turned_load = load(18, v.down_turned, v.turned)
    mid_load = load(5, v.normed_mid_t, v.normed_t if final_layer else v.mid_v)
    early = [
        load(6, v.middle, v.middle_v),
        load(7, v.x.at[at.section] if final_layer else v.x, v.x_v),
        load(8, v.out_all.at[layer], out_t),
        load(9, v.query_rot, query_v),
        load(10, v.key_rot, key_v),
        load(11, v.value, value_v),
        load(12, v.inverse, v.inverse_v),
        load(13, v.opened, wide_c),
        load(15, v.masks, masks),
        load(16, v.tables, tables),
        load(17, v.grad_out if final_layer else v.grad_out.at[at.section], v.grad_out_v),
    ]
    terms[...] = jnp.zeros_like(terms)

    partners = [sq.device(*step) for step in SQUARE] + [sibling]
    if final_layer:
        partners.append(across)
        partners += [place(dp=at.dp_at(k, b)) for k, b in steps[:-1] if (k, b) != (0, 1)]
    barrier = pltpu.get_barrier_semaphore()
    for partner in partners:
        pl.semaphore_signal(barrier, inc=1, device_id=partner, device_id_type=MESH)
    pl.semaphore_wait(barrier, len(partners))

    def x_copy(e, at_source, j, source):
        block = source.at[at_source, j]
        return remote(block, v.x_land.at[e, j], v.x_send.at[e, j], v.x_recv.at[e, j], across)

    def start_x(e, at_source, source):
        @pl.loop(0, slices)
        def _(j):
            x_copy(e, at_source, j, source).start()

    row_copies = []
    if final_layer:

        @pl.when(at.section == 0)
        def _():
            @pl.loop(0, KEPT)
            def _(e):
                start_x(e, e, v.later_chip)

            remote(v.grad_out, v.taken_grads, v.row_send.at[1], v.row_recv.at[1], across).start()

        @pl.when(at.section == 1)
        def _():
            remote(v.first_rows, v.taken_rows, v.row_send.at[0], v.row_recv.at[0], across).start()

    def through_down(s):
        tokens = grad_down[s]
        for start in range(0, wide_f, TILE):
            cols = slice(start, start + TILE)
            grad_hidden = mm(tokens, big[:, 2 * wide_f + start : 2 * wide_f + start + TILE])
            grad_gate_up[s, :, cols] = (grad_hidden * wide_b[s, :, cols].astype(f32)).astype(bf16)
            grad_gate_up[s, :, wide_f + start : wide_f + start + TILE] = (
                grad_hidden * wide_a[s, :, cols].astype(f32)
            ).astype(bf16)

    def give_back(s, source, weight, first, size, target):
        tokens = source[s]
        for start in range(0, width, TILE):
            target[s, :, start : start + TILE] = mm_nt(
                tokens, weight[start : start + TILE, first : first + size]
            ).astype(bf16)

    def collected(block, given, land):
        total = sq.chunk(given)[block].astype(f32)
        for j in range(len(SQUARE)):
            total = total + land[j, block].astype(f32)
        return total

    def exchange(source, weight, first, size, target, land, which):
        give_back(sq.next, source, weight, first, size, target)
        send, recv = v.g_send.at[which], v.g_recv.at[which]
        pushes = [sq.give(target, land, send, recv, j) for j in (1, 2)]
        give_back(sq.own, source, weight, first, size, target)
        pushes.append(sq.give(target, land, send, recv, 0))
        return pushes

    members = [
        (v.turned, outer, 0, wide_f),
        (v.normed_t, grad_gate_up, 0, wide_f),
        (v.normed_t, grad_gate_up, wide_f, wide_f),
        (v.turned, outer, 0, wide_v),
        (v.normed_t, grad_qkvs, 0, 2 * wide_k),
        (v.normed_t, grad_qkvs, 2 * wide_k, wide_v),
        (v.normed_t, grad_qkvs, 2 * wide_k + wide_v, wide_v),
    ]
    members += members[KEPT:]
    given_copies, own_copies, fetches = {}, {}, {}

    def product(e, dp):
        left, right, first, size = members[e]
        start = pl.multiple_of(dp * slice_rows, slice_rows)
        wide = right[:, :, first : first + size].reshape(-1, size)
        return mm(left[pl.ds(start, slice_rows), :], wide)

    def given(e):
        if e >= 2:
            given_copies[e - 2].wait_send()
        stage = v.stage_given.at[e % 2]

        @pl.loop(0, slices)
        def _(j):
            stage[j] = product(e, j * 2 + 1 - at.core).astype(bf16)

        given_copies[e] = remote(stage, v.core_land.at[e], v.c_send.at[e], v.c_recv.at[e], sibling)
        given_copies[e].start()

    def fetch(e):
        given_copies[e].wait_recv()
        fetches[e] = pltpu.make_async_copy(v.core_land.at[e], v.core_part, v.local_sem.at[0])
        fetches[e].start()

    def settle(e):
        if e in settled:
            return
        settled.append(e)
        own_copies[e].wait()
        if final_layer:

            @pl.when(at.section == (1 if e < GROUPS else 0))
            def _():
                start_x(e if e < GROUPS else e - GROUPS + KEPT, e, v.chip)

    def own(e):
        if e >= 1:
            settle(e - 1)
        fetches[e].wait()

        @pl.loop(0, slices)
        def _(j):
            v.stage_own[j] = (product(e, j * 2 + at.core) + v.core_part[j].astype(f32)).astype(bf16)

        own_copies[e] = pltpu.make_async_copy(v.stage_own, v.chip.at[e], v.local_sem.at[1])
        own_copies[e].start()

    settled = []

    def index(k, b):
        return ((at.group + k) % at.groups) * 2 + (at.low + b) % 2

    def piece(e, k):
        start = pl.multiple_of(at.low * wide_f, wide_f)
        return v.final.at[e, k, :, pl.ds(start, wide_f)]

    def z_copy(e, j):
        k, b = steps[j]
        return remote(v.sums.at[j], piece(e, k), v.z_send.at[e, j], v.z_recv.at[e, j], place(dp=at.dp_at(k, b)))

    def home_copy(e):
        return pltpu.make_async_copy(v.sums.at[slices - 1], piece(e, 0), v.r_sem.at[2, 0])

    def reduce_slices(e, at_source, source, first, stop, wait_previous):
        def loads(j):
            here = index(*steps[j])
            return (
                pltpu.make_async_copy(source.at[at_source, here], v.left.at[j % 2], v.r_sem.at[0, j % 2]),
                pltpu.make_async_copy(v.x_land.at[e, here], v.right.at[j % 2], v.r_sem.at[1, j % 2]),
            )

        def begin(j):
            x_copy(e, at_source, index(*steps[j]), source).wait_recv()
            for copy in loads(j):
                copy.start()

        begin(first)
        for j in range(first, stop):
            if j + 1 < stop:
                begin(j + 1)
            for copy in loads(j):
                copy.wait()

            @pl.when(wait_previous)
            def _():
                if j == slices - 1:
                    home_copy(e).wait()
                else:
                    z_copy(e - 1, j).wait_send()

            v.sums[j] = (v.left[j % 2].astype(f32) + v.right[j % 2].astype(f32)).astype(bf16)
            if j == slices - 1:
                home_copy(e).start()
            else:
                z_copy(e, j).start()

    reduced = [0, 0]

    def source_of(section, e):
        if section == 0:
            return e, v.chip
        return (e, v.later_chip) if e < KEPT else (e + GROUPS - KEPT, v.chip)

    def reduce_some(section, count):
        if not final_layer:
            return

        @pl.when(at.section == section)
        def _():
            done = reduced[section]
            while done < reduced[section] + count:
                e, first = divmod(done, slices)
                stop = min(slices, first + reduced[section] + count - done)
                reduce_slices(e, *source_of(section, e), first, stop, e > 0)
                done += stop - first

        reduced[section] += count

    def reduce_rest(section):
        e, first = divmod(reduced[section], slices)

        @pl.when(at.section == section)
        def _():
            begin = e
            if first > 0:
                reduce_slices(e, *source_of(section, e), first, slices, e > 0)
                begin = e + 1
            same = KEPT if section == 1 else GROUPS

            @pl.loop(begin, same)
            def _(i):
                reduce_slices(i, i, source_of(section, 0)[1], 0, slices, i > 0)

            for i in range(same, GROUPS):
                reduce_slices(i, *source_of(section, i), 0, slices, True)

    token_load.wait()
    if final_layer:
        hidden_load.wait()
        transpose_into(v.turned, grad_down)
        given(0)
    down_load.wait()
    act_load.wait()
    slope_load.wait()
    through_down(sq.next)
    through_down(sq.own)
    unit_load = load(1, v.unit, wide_a)
    bend_load = load(2, v.slope_open, wide_b)
    gate_load.wait()
    gives = exchange(grad_gate_up, big, 0, 2 * wide_f, parts, landed, 0)
    if not final_layer:
        hidden_load.wait()
        turned_load.wait()
        given(0)
    fetch(0)
    own(0)
    mid_load.wait()
    if not final_layer:
        transpose_into(v.normed_t, v.mid_v)
    settle(0)
    given(1)
    qkvs_load = load(3, v.qkvs_all.at[layer], big)
    merged_load = load(4, v.merged, outer)
    for copy in early:
        copy.wait()
    for push in gives:
        push.wait_recv()

    def through_mid(block):
        upstream = collected(block, parts, landed)
        normed, scale = norm_parts(v.middle_v[block])
        grad_rows = v.grad_out_v[block].astype(f32) + norm_grad(normed, scale, upstream, gain_mid)
        v.grad_middle[block] = grad_rows
        sq.chunk(grad_branch)[block] = grad_rows.astype(bf16)
        terms[1:2] = terms[1:2] + jnp.sum(upstream * normed, axis=0, keepdims=True)

    row_blocks(rows, through_mid)
    mids = sq.spread(grad_branch, v.s_send, v.s_recv)
    reduce_some(0, 1)
    given(2)
    fetch(1)
    own(1)
    unit_load.wait()
    bend_load.wait()
    settle(1)
    reduce_some(1, slices)
    reduce_some(0, 1)

    def through_heads(s):
        tokens = grad_branch[s]
        for head in range(heads):
            cols_k = slice(head * HEAD_K, (head + 1) * HEAD_K)
            cols_v = slice(head * HEAD_V, (head + 1) * HEAD_V)
            grad_merged = mm(tokens, out_t[:, cols_v])
            unit_rows = wide_a[s, :, cols_v].astype(f32)
            first = 2 * wide_k + wide_v + head * HEAD_V
            grad_qkvs[s, :, first : first + HEAD_V] = (
                grad_merged * unit_rows * wide_b[s, :, cols_v].astype(f32)
            ).astype(bf16)
            grad_unit = grad_merged * wide_c[s, :, cols_v].astype(f32)
            grad_mixed = (
                v.inverse_v[s, head]
                * (
                    grad_unit
                    - jnp.mean(grad_unit, axis=-1, keepdims=True)
                    - unit_rows * jnp.mean(grad_unit * unit_rows, axis=-1, keepdims=True)
                )
            ).astype(bf16)
            query, key, val = query_v[s, :, cols_k], key_v[s, :, cols_k], value_v[s, :, cols_v]
            mask = masks[s, head]
            weight = (mm_nt(query, key) * mask).astype(bf16)
            grad_product = (mm_nt(grad_mixed, val) * mask).astype(bf16)
            first = 2 * wide_k + head * HEAD_V
            grad_qkvs[s, :, first : first + HEAD_V] = mm_tn(weight, grad_mixed).astype(bf16)
            grad_qkvs[s, :, cols_k] = turn_back(mm(grad_product, key), tables[0], tables[1], tables[2]).astype(bf16)
            first = wide_k + head * HEAD_K
            grad_qkvs[s, :, first : first + HEAD_K] = turn_back(
                mm_tn(grad_product, query), tables[0], tables[1], tables[3]
            ).astype(bf16)

    mids.wait_own()
    through_heads(sq.own)
    mids.wait_next()
    through_heads(sq.next)
    if not final_layer:
        keep = pltpu.make_async_copy(grad_qkvs, v.kept_qkvs, v.kept_sem)
        keep.start()
    qkvs_load.wait()
    reduce_some(0, 1)
    for push in gives:
        push.wait_send()
    ends = exchange(grad_qkvs, big, 0, grad_qkvs.shape[-1], parts, landed, 1)
    fetch(2)
    own(2)
    in_load = load(5, v.normed_in_t, v.normed_t)
    transpose_into(v.turned, grad_branch)
    settle(2)
    merged_load.wait()
    given(3)
    in_load.wait()
    given(4)
    fetch(3)
    own(3)
    reduce_some(1, slices)
    reduce_some(0, 1)
    settle(3)
    for push in ends:
        push.wait_recv()

    def through_in(block):
        upstream = collected(block, parts, landed)
        normed, scale = norm_parts(v.x_v[block].astype(f32))
        v.grad_in[block] = (v.grad_middle[block] + norm_grad(normed, scale, upstream, gain_in)).astype(bf16)
        terms[0:1] = terms[0:1] + jnp.sum(upstream * normed, axis=0, keepdims=True)

    row_blocks(rows, through_in)
    if final_layer:

        @pl.when(at.section == 1)
        def _():
            remote(v.grad_in, v.taken_grads, v.row_send.at[1], v.row_recv.at[1], across).start()

    else:
        downs = sq.spread(v.next_down, v.d_send, v.d_recv, v.grad_in, v.d_sem)

    if not final_layer:
        fetch(4)
        downs.wait_own()
        own(4)
        settle(4)
        downs.wait_next()
        for push in [downs, mids] + ends:
            push.wait_send()
        for e in (3, 4):
            given_copies[e].wait_send()
        keep.wait()
        return

    reduce_some(0, 1)
    given(5)
    fetch(4)
    own(4)
    reduce_some(0, 1)
    given(6)
    settle(4)
    reduce_some(1, slices)
    reduce_some(0, 1)
    fetch(5)
    own(5)
    reduce_some(0, 1)
    fetch(6)
    own(6)
    in_load = load(5, v.later_normed_in_t, v.normed_t)
    qkvs_load = load(3, v.later_qkvs, grad_qkvs)
    hidden_load = load(4, v.later_hidden, outer)
    middle_load = load(6, v.later_middle, v.middle_v)
    down_load = load(0, v.down_all.at[1], big.at[:, pl.ds(2 * wide_f, wide_f)])
    settle(6)
    reduce_some(1, slices)
    reduce_some(0, 1)
    in_load.wait()
    qkvs_load.wait()
    given(7)
    reduce_some(0, 1)
    given(8)
    fetch(7)
    own(7)
    reduce_some(0, 1)
    fetch(8)
    own(8)
    settle(7)
    reduce_some(0, 1)
    for push in [mids] + ends:
        push.wait_send()
    hidden_load.wait()
    down_load.wait()
    settle(8)
    gives_y = exchange(outer, big, 2 * wide_f, wide_f, parts, v.landed_y, 2)
    reduce_some(1, slices)
    reduce_some(0, slices)
    middle_load.wait()
    for push in gives_y:
        push.wait_recv()

    def last(block):
        v.result[block] = (v.middle_v[block] + collected(block, parts, v.landed_y)).astype(bf16)

    row_blocks(rows, last)

    @pl.when(at.section == 0)
    def _():
        remote(v.result, v.taken_rows, v.row_send.at[0], v.row_recv.at[0], across).start()

    for push in gives_y:
        push.wait_send()
    for e in (7, 8):
        given_copies[e].wait_send()
    reduce_rest(1)
    reduce_rest(0)

    held, hop_land, mine = v.held, v.hop_land, v.held.at[at.section]
    held[0] = terms[...]
    held[1] = v.later_terms[...]
    hop = remote(held, hop_land.at[0], v.t_send.at[0], v.t_recv.at[0], sibling)
    hop.start()
    hop.wait()
    held[...] = held[...] + hop_land[0]
    hop = remote(held.at[other], hop_land.at[1, other], v.t_send.at[1], v.t_recv.at[1], across)
    hop.start()
    hop.wait_send()
    remote(held.at[other], hop_land.at[1, at.section], v.t_send.at[1], v.t_recv.at[1], across).wait_recv()
    mine[...] = mine[...] + hop_land[1, at.section]
    for h, device in ((2, place(tensor=1 - at.tensor)), (3, place(dp=at.dp_at(0, 1)))):
        hop = remote(mine, hop_land.at[h, 0], v.t_send.at[h], v.t_recv.at[h], device)
        hop.start()
        hop.wait()
        mine[...] = mine[...] + hop_land[h, 0]
    hops = []
    for k in range(1, at.groups):
        hop = remote(mine, hop_land.at[3 + k, 0], v.t_send.at[3 + k], v.t_recv.at[3 + k], place(dp=at.dp_at(k, 0)))
        hop.start()
        hops.append(hop)
    total = mine[...]
    for k, hop in zip(range(1, at.groups), hops):
        hop.wait()
        total = total + hop_land[3 + k, 0]
    v.gain_sums[...] = total

    for which, rows_sent in ((0, v.result), (1, v.grad_in)):
        target = v.taken_rows if which == 0 else v.taken_grads
        copy = remote(rows_sent, target, v.row_send.at[which], v.row_recv.at[which], across)
        copy.wait_recv()
        copy.wait_send()

    home_copy(0).wait()
    for j in range(slices - 1):
        z_copy(GROUPS - 1, j).wait_send()

        @pl.loop(0, GROUPS)
        def _(e):
            z_copy(e, j).wait_recv()

    @pl.loop(0, GROUPS)
    def _(e):
        @pl.loop(0, slices)
        def _(j):
            x_copy(e, e, j, v.chip).wait_send()


def backward_layer(layer, grad_out, down, turned_down, x, gains, tables, masks, saved, gathered, dp_size, later=None, x_out=None):
    rows, width = x.shape[-2:]
    length = masks.shape[-1]
    (middle, normed_in_t, query_rot, key_rot, value, unit, inverse, opened, slope_open, merged, normed_mid_t, act, slope,
     hidden) = saved
    vmem = pl.BlockSpec(memory_space=pltpu.VMEM)
    any_spec = pl.BlockSpec(memory_space=pl.ANY)
    final_layer = layer == 0
    slices = dp_size // 2
    slice_rows = width // dp_size
    size = hidden.shape[-1]
    assert value.shape[-1] == size and 2 * query_rot.shape[-1] == size
    block = (slices, slice_rows, size)

    def held(*shape, kind=bf16):
        return pltpu.VMEM(shape, kind)

    def stored(*shape, kind=bf16):
        return jax.ShapeDtypeStruct(shape, kind)

    dma = pltpu.SemaphoreType.DMA
    operands = [grad_out, gains, tables, masks]
    operands += [x, middle, normed_in_t, query_rot, key_rot, value, unit, inverse, opened, slope_open, merged, normed_mid_t,
                 act, slope, hidden]
    operands += [*gathered, down]
    if not final_layer:
        operands += [turned_down]
    in_specs = [any_spec, vmem] + [any_spec] * (len(operands) - 2)
    count = 2 * GROUPS - KEPT if final_layer else KEPT
    out_shape = [stored(rows, width), stored(count, *block), stored(count, *block)]
    out_specs = [vmem, any_spec, any_spec]
    if final_layer:
        later_chip, later_terms, later_qkvs, later_saved = later
        operands += [later_chip, later_terms, x_out, later_saved[1], later_qkvs, later_saved[-1], later_saved[0]]
        in_specs += [any_spec, vmem] + [any_spec] * 5
        out_shape += [stored(GROUPS, *block), stored(GROUPS, dp_size // 4, slice_rows, 2 * size), stored(2, width, kind=f32),
                      stored(rows, width), stored(rows, width), stored(rows, width)]
        out_specs += [any_spec, any_spec, vmem, vmem, any_spec, any_spec]
    else:
        out_shape += [stored(2, width, kind=f32), stored(2, length, width), stored(2, length, 3 * size)]
        out_specs += [vmem, any_spec, any_spec]
    scratch = [
        held(width, 3 * size),
        held(width, size),
        held(*query_rot.shape),
        held(*key_rot.shape),
        held(*value.shape),
        held(2, length, size),
        held(2, length, size),
        held(2, length, size),
        held(*inverse.shape, kind=f32),
        held(rows, width),
        held(rows, width, kind=f32),
        held(width, 2 * length),
        held(2, length, size),
        held(2, length, width),
        held(2, length, 2 * size),
        held(2, length, width),
        held(2, length, 3 * size),
        held(width, 2 * length),
        held(2, length, width),
        held(3, rows, width),
        held(rows, width, kind=f32),
        held(2, *block),
        held(*block),
        held(*block),
        dma((19,)),
        dma((6,)),
        dma((6,)),
        dma((3, 3)),
        dma((3, 3)),
        dma((count,)),
        dma((count,)),
        dma((2,)),
        held(*masks.shape, kind=f32),
        held(*tables.shape, kind=f32),
        held(rows, width),
    ]
    if final_layer:
        hops = 3 + dp_size // 4
        scratch += [
            held(2, slice_rows, size),
            held(2, slice_rows, size),
            held(*block),
            dma((3, 2)),
            dma((GROUPS, slices)),
            dma((GROUPS, slices)),
            dma((GROUPS, slices - 1)),
            dma((GROUPS, slices - 1)),
            held(2, width, kind=f32),
            held(2, 2, width, kind=f32),
            held(hops, 2, 2, width, kind=f32),
            dma((hops,)),
            dma((hops,)),
            dma((2,)),
            dma((2,)),
            held(3, rows, width),
        ]
    else:
        scratch += [dma((6,)), dma((6,)), dma, dma, held(2, length, width)]
    return pl.pallas_call(
        functools.partial(backward_kernel, dp_size, layer),
        out_shape=out_shape,
        in_specs=in_specs,
        out_specs=out_specs,
        scratch_shapes=scratch,
        compiler_params=pltpu.CompilerParams(
            collective_id=4 + layer, has_side_effects=True, vmem_limit_bytes=VMEM_LIMIT
        ),
        name="backward_layer",
    )(*operands)


def nested(outs):
    return (*outs[:6], outs[6:-2], *outs[-2:])


def on_device(
    dp_size,
    layer_input,
    segment_ids,
    output_grad,
    query_weight,
    key_weight,
    value_weight,
    swish_weight,
    output_weight,
    gate_weight,
    up_weight,
    down_weight,
    mixer_gain,
    ffn_gain,
):
    at = Place(dp_size)
    section_first = at.section == 0
    width = layer_input.shape[2]
    length = segment_ids.shape[1]
    quarter_k = query_weight.shape[2] // 2
    heads_here = quarter_k // HEAD_K
    cosine, sine, growth = rotation_tables(length, HEAD_K // 2)
    tables = jnp.stack([cosine, sine, growth, 1.0 / growth])

    shards = (query_weight[0], key_weight[0], value_weight[0], swish_weight[0], output_weight[0].T, gate_weight[0],
              up_weight[0], down_weight[0].T)
    *gathered, all_gains, masks, first_saved, second_down, first_sent = nested(
        forward_layer(
            0, (layer_input, mixer_gain, ffn_gain, segment_ids, tables, output_grad), shards, length, heads_here, dp_size
        )
    )
    *second_saved, turned_down = forward_layer(
        1, (first_sent, all_gains, tables, masks, second_down), gathered, length, heads_here, dp_size
    )
    gathered = [g.reshape(2, width, g.shape[-1]) for g in gathered]
    second_grad, later_chip, _, later_terms, first_down, later_qkvs = backward_layer(
        1, output_grad, second_down, turned_down, first_sent, all_gains, tables, masks, second_saved, gathered, dp_size
    )
    first_grad, _, _, _, landed, my_gains, second_sent, taken_rows, taken_grads = backward_layer(
        0, second_grad, first_down, None, layer_input, all_gains, tables, masks, first_saved, gathered, dp_size,
        (later_chip, later_terms, later_qkvs, second_saved), first_sent,
    )

    def by_layer(first, second, taken):
        return jnp.where(section_first, jnp.stack([first, taken]), jnp.stack([taken, second]))[None]

    def shard(e):
        return jnp.sum(landed[e].astype(f32), axis=0)

    def columns(e, start, size):
        step = landed.shape[-1] // 2
        part = jnp.concatenate([landed[e, :, :, p * step + start : p * step + start + size] for p in range(2)], axis=-1)
        return jnp.sum(part.astype(f32), axis=0)

    return (
        by_layer(first_sent, second_sent, taken_rows),
        by_layer(first_grad, second_grad, taken_grads),
        columns(4, 0, quarter_k)[None],
        columns(4, quarter_k, quarter_k)[None],
        shard(5)[None],
        shard(6)[None],
        shard(3).T[None],
        shard(1)[None],
        shard(2)[None],
        shard(0).T[None],
        my_gains[0][None],
        my_gains[1][None],
    )


def solution(mesh):
    in_specs = (
        P(None, ("dp", "tensor"), None),
        P(None, "dp"),
        P(None, ("dp", "tensor"), None),
        P("section", "dp", "tensor"),
        P("section", "dp", "tensor"),
        P("section", "dp", "tensor"),
        P("section", "dp", "tensor"),
        P("section", "tensor", "dp"),
        P("section", "dp", "tensor"),
        P("section", "dp", "tensor"),
        P("section", "tensor", "dp"),
        P("section", None),
        P("section", None),
    )
    out_specs = (
        P("section", None, ("dp", "tensor"), None),
        P("section", None, ("dp", "tensor"), None),
        P("section", "dp", "tensor"),
        P("section", "dp", "tensor"),
        P("section", "dp", "tensor"),
        P("section", "dp", "tensor"),
        P("section", "tensor", "dp"),
        P("section", "dp", "tensor"),
        P("section", "dp", "tensor"),
        P("section", "tensor", "dp"),
        P("section", None),
        P("section", None),
    )
    return jax.shard_map(
        functools.partial(on_device, mesh.shape["dp"]),
        mesh=mesh,
        in_specs=in_specs,
        out_specs=out_specs,
        check_vma=False,
    )
```

```python
import functools

import jax
import jax.numpy as jnp
from jax import lax
from jax.experimental import pallas as pl
from jax.experimental.pallas import tpu as pltpu
from jax.sharding import PartitionSpec as P

HEAD_K = 256
HEAD_V = 512
MESH = pl.DeviceIdType.MESH

epsilon = 1e-05
group_guard = 1.0
bf16 = jnp.bfloat16
f32 = jnp.float32


def rotation_tables(length, half_width):
    pair_index = jnp.arange(half_width).astype(f32)
    position = jnp.arange(length).astype(f32)[:, None]
    angle = position * jnp.exp(-jnp.log(10000.0) * pair_index / half_width)
    zeta = (pair_index / half_width + 0.4) / 1.4
    growth = jnp.exp(position / 512.0 * jnp.log(zeta))
    return (jnp.cos(angle), jnp.sin(angle), growth)


class Place:
    def __init__(self, dp_size):
        self.groups = dp_size // 4
        self.section = lax.axis_index("section")
        self.dp = lax.axis_index("dp")
        self.tensor = lax.axis_index("tensor")
        self.core = self.dp % 2
        self.low = (self.dp // 2) % 2
        self.group = self.dp // 4

    def dp_at(self, group_step, low_step):
        group = (self.group + group_step + self.groups) % self.groups
        return (group * 2 + (self.low + low_step) % 2) * 2 + self.core

    def sibling(self):
        return self.dp + 1 - 2 * self.core


SQUARE = ((0, 1), (1, 0), (1, 1))
TILE = 512
VMEM_LIMIT = 63 * 1024 * 1024


def mm(left, right):
    return lax.dot_general(left, right, (((1,), (0,)), ((), ())), preferred_element_type=f32)


def mm_nt(left, right):
    return lax.dot_general(left, right, (((1,), (1,)), ((), ())), preferred_element_type=f32)


def mm_tn(left, right):
    return lax.dot_general(left, right, (((0,), (0,)), ((), ())), preferred_element_type=f32)


class Square:
    def __init__(self, dp_size, rows):
        self.at = Place(dp_size)
        self.rows = rows
        self.own = self.at.low
        self.next = 1 - self.at.low

    def device(self, low_step, tensor_step):
        return (self.at.section, self.at.dp_at(0, low_step), (self.at.tensor + tensor_step) % 2)

    def barrier(self):
        barrier = pltpu.get_barrier_semaphore()
        for step in SQUARE:
            pl.semaphore_signal(barrier, inc=1, device_id=self.device(*step), device_id_type=MESH)
        pl.semaphore_wait(barrier, len(SQUARE))

    def chunk(self, ref, low_step=0, tensor_step=0):
        start = pl.multiple_of((self.at.tensor + tensor_step) % 2 * self.rows, self.rows)
        return ref.at[(self.at.low + low_step) % 2, pl.ds(start, self.rows)]

    def copy(self, src, dst, send, recv, step):
        return pltpu.make_async_remote_copy(
            src_ref=src,
            dst_ref=dst,
            send_sem=send,
            recv_sem=recv,
            device_id=self.device(*step),
            device_id_type=MESH,
        )

    def spread(self, ref, send, recv, direct, own=None, here=None):
        return (DirectSpread if direct else Spread)(self, ref, send, recv, own, here)

    def give(self, parts, landed, send, recv, j):
        push = self.copy(self.chunk(parts, *SQUARE[j]), landed.at[j], send.at[j], recv.at[j], SQUARE[j])
        push.start()
        return push


class Spread:
    def __init__(self, sq, ref, send, recv, own, here):
        self.sq, self.ref, self.send, self.recv = sq, ref, send, recv
        self.half = sq.rows // 2
        source = self.source(own, here)
        beside, below = (0, 1), (1, 0)
        self.first = [
            self.push(source, sq.chunk(ref), half, j, step)
            for j, (half, step) in enumerate(((0, beside), (1, below), (1, beside), (0, below)))
        ]
        from_beside, from_below = sq.chunk(ref, *beside), sq.chunk(ref, *below)
        self.onward = [
            self.push(from_beside, from_beside, 0, 4, below, start=False),
            self.push(from_below, from_below, 1, 5, beside, start=False),
        ]

    def source(self, own, here):
        self.local = None
        if own is None:
            return self.sq.chunk(self.ref)
        self.local = pltpu.make_async_copy(own, self.sq.chunk(self.ref), here)
        self.local.start()
        return own

    def push(self, source, target, half, j, step, start=True):
        block = pl.ds(half * self.half, self.half)
        copy = self.sq.copy(source.at[block], target.at[block], self.send.at[j], self.recv.at[j], step)
        if start:
            copy.start()
        return copy

    def wait_own(self):
        for came, onward in zip(self.first[:2], self.onward):
            came.wait_recv()
            onward.start()
        self.first[2].wait_recv()

    def wait_next(self):
        self.first[3].wait_recv()
        for onward in self.onward:
            onward.wait_recv()

    def wait_recv(self):
        self.wait_own()
        self.wait_next()

    def wait_send(self):
        for copy in self.first + self.onward:
            copy.wait_send()
        if self.local is not None:
            self.local.wait()


class DirectSpread(Spread):
    def __init__(self, sq, ref, send, recv, own, here):
        self.sq, self.ref = sq, ref
        source = self.source(own, here)
        self.first, self.onward = [], []
        for j, step in enumerate(SQUARE):
            copy = sq.copy(source, sq.chunk(ref), send.at[j], recv.at[j], step)
            copy.start()
            self.first.append(copy)

    def wait_own(self):
        self.first[0].wait_recv()

    def wait_next(self):
        self.first[1].wait_recv()
        self.first[2].wait_recv()


def row_blocks(rows, body, block=32):
    block = min(block, rows)

    @pl.loop(0, rows // block)
    def _(i):
        body(pl.ds(pl.multiple_of(i * block, block), block))


def norm_parts(values):
    centred = values - jnp.mean(values, axis=-1, keepdims=True)
    scale = lax.rsqrt(jnp.mean(centred * centred, axis=-1, keepdims=True) + epsilon)
    return centred * scale, scale


def norm_grad(normed, scale, upstream, gain):
    through = upstream * gain
    return scale * (
        through
        - jnp.mean(through, axis=-1, keepdims=True)
        - normed * jnp.mean(through * normed, axis=-1, keepdims=True)
    )


def turn(values, cosine, sine, scale):
    half = values.shape[-1] // 2
    a, b = values[:, :half], values[:, half:]
    return jnp.concatenate([(a * cosine - b * sine) * scale, (a * sine + b * cosine) * scale], axis=-1)


def turn_back(values, cosine, sine, scale):
    half = values.shape[-1] // 2
    a, b = values[:, :half] * scale, values[:, half:] * scale
    return jnp.concatenate([a * cosine + b * sine, b * cosine - a * sine], axis=-1)


def transpose_into(target, source):
    _, length, width = source.shape
    for s in range(2):
        for start in range(0, width, TILE):
            target[start : start + TILE, s * length : (s + 1) * length] = source[s, :, start : start + TILE].T


def forward_kernel(dp_size, layer, *refs):
    streams = layer == 0
    v = Refs()
    if streams:
        (v.x, v.mixer_gain, v.ffn_gain, v.ids, v.tables, v.out_grad, *refs) = refs
        shards, refs = refs[:8], refs[8:]
        stored, refs = refs[:4], refs[4:]
        (v.gains, v.masks, *refs) = refs
    else:
        (v.x, v.gains, v.tables, v.masks, v.down, *refs) = refs
        stored, refs = refs[:4], refs[4:]
    saved, refs = refs[:14], refs[14:]
    if streams:
        (v.grad_down, result, *refs) = refs
    else:
        (v.turned_down, *refs) = refs
    scratch, refs = refs[:14], refs[14:]
    (middle, normed_in_t, query_rot, key_rot, value, unit, inverse, opened, slope_open, merged, normed_mid_t, act, slope,
     hidden) = scratch
    save_sem, x_v, masks, tables, in_sem, *refs = refs
    held, refs = refs[:4], refs[4:]
    (w_sem, normed_in, *refs) = refs
    if streams:
        (normed_mid, *refs) = refs
    else:
        normed_mid = normed_mid_t
    (parts, landed, s_send, s_recv, g_send, g_recv, *refs) = refs
    x = x_v
    rows, width = x.shape
    sq = Square(dp_size, rows)
    at = sq.at
    sources = [(v.x.at[at.section] if streams else v.x, x_v), (v.tables, tables)]
    if not streams:
        sources.append((v.masks, masks))
    operand_copies = [
        pltpu.make_async_copy(source, target, in_sem.at[i]) for i, (source, target) in enumerate(sources)
    ]
    for copy in operand_copies:
        copy.start()
    operand_copies[0].wait()
    saves = []

    def save(*which):
        for i in which:
            copy = pltpu.make_async_copy(scratch[i], saved[i], save_sem.at[i])
            copy.start()
            saves.append(copy)

    qkvs, out_t, gate_up, down_t = held
    wide_k = query_rot.shape[-1]
    wide_v = value.shape[-1]
    wide_f = hidden.shape[-1]
    heads = wide_k // HEAD_K
    slices = dp_size // 2
    other = 1 - at.section
    groups = [(0, 0, wide_k), (0, wide_k, wide_k), (0, 2 * wide_k, wide_v), (0, 2 * wide_k + wide_v, wide_v),
              (1, 0, wide_v), (2, 0, wide_f), (2, wide_f, wide_f), (3, 0, wide_f)]
    loads = {}

    def load(i):
        which, first, size = groups[i]
        columns = pl.ds(first, size)
        loads[i] = pltpu.make_async_copy(
            stored[which].at[layer, :, :, :, columns], held[which].at[:, :, :, columns], w_sem.at[i]
        )
        loads[i].start()

    def weight(which, first, size):
        return held[which][:, :, :, first : first + size].reshape(width, size)

    def first_norm(block):
        unit_rows, _ = norm_parts(x[block].astype(f32))
        sq.chunk(normed_in)[block] = (unit_rows * v.gains[layer, 0:1]).astype(bf16)

    def project(i, s):
        loads_wait(i)
        first, size = groups[i][1:]
        tokens = normed_in[s]
        for start in range(0, size, TILE):
            wide = mm(tokens, weight(0, first + start, TILE))
            cols = slice(start, start + TILE)
            if i < 2:
                dest = (query_rot, key_rot)[i]
                for head in range(TILE // HEAD_K):
                    part = wide[:, head * HEAD_K : (head + 1) * HEAD_K]
                    dest[s, :, start + head * HEAD_K : start + (head + 1) * HEAD_K] = turn(
                        part, tables[0], tables[1], tables[2 + i]
                    ).astype(bf16)
            elif i == 2:
                value[s, :, cols] = wide.astype(bf16)
            else:
                sigmoid = 1.0 / (1.0 + jnp.exp(-wide))
                opened[s, :, cols] = (wide * sigmoid).astype(bf16)
                slope_open[s, :, cols] = (sigmoid * (1.0 + wide * (1.0 - sigmoid))).astype(bf16)

    waited = []

    def loads_wait(i):
        if i not in waited:
            waited.append(i)
            loads[i].wait()

    def retain(s):
        for head in range(heads):
            cols_k = slice(head * HEAD_K, (head + 1) * HEAD_K)
            cols_v = slice(head * HEAD_V, (head + 1) * HEAD_V)
            product = mm_nt(query_rot[s, :, cols_k], key_rot[s, :, cols_k])
            weights = (product * masks[s, head]).astype(bf16)
            mixed = mm(weights, value[s, :, cols_v])
            centred = mixed - jnp.mean(mixed, axis=-1, keepdims=True)
            scale = lax.rsqrt(jnp.mean(centred * centred, axis=-1, keepdims=True) + group_guard)
            unit_rows = centred * scale
            inverse[s, head] = scale
            unit[s, :, cols_v] = unit_rows.astype(bf16)
            merged[s, :, cols_v] = (unit_rows * opened[s, :, cols_v].astype(f32)).astype(bf16)

    def give_back(s, source, weight_t):
        tokens = source[s]
        step = width // slices
        for i in range(slices):
            parts[s, :, i * step : (i + 1) * step] = mm_nt(tokens, weight_t[i].reshape(step, -1)).astype(bf16)

    def collected(block, which):
        total = sq.chunk(parts)[block].astype(f32)
        for j in range(len(SQUARE)):
            total = total + landed[which, j, block].astype(f32)
        return total

    def give(s, which):
        send, recv = g_send.at[which], g_recv.at[which]
        return [sq.give(parts, landed.at[which], send, recv, j) for j in ((1, 2) if s == 1 else (0,))]

    def second_norm(block):
        middle_rows = x[block].astype(f32) + collected(block, 0)
        middle[block] = middle_rows
        unit_rows, _ = norm_parts(middle_rows)
        sq.chunk(normed_mid)[block] = (unit_rows * v.gains[layer, 1:2]).astype(bf16)

    def feed(s):
        loads_wait(5)
        loads_wait(6)
        tokens = normed_mid[s]
        for start in range(0, wide_f, TILE):
            cols = slice(start, start + TILE)
            gate = mm(tokens, weight(2, start, TILE))
            up = mm(tokens, weight(2, wide_f + start, TILE))
            square = gate * gate
            bend = jnp.tanh(0.7978845608028654 * gate * (1.0 + 0.044715 * square))
            half = 0.5 * (1.0 + bend)
            gelu = gate * half
            slope_gelu = half + 0.5 * gate * (1.0 - bend * bend) * (
                0.7978845608028654 * (1.0 + 3 * 0.044715 * square)
            )
            act[s, :, cols] = gelu.astype(bf16)
            slope[s, :, cols] = (slope_gelu * up).astype(bf16)
            hidden[s, :, cols] = (gelu * up).astype(bf16)

    if not streams:
        (down_v, turned_v, down_sem) = refs
        down_load = pltpu.make_async_copy(v.down, down_v, down_sem.at[0])
        down_load.start()
        down_save = pltpu.make_async_copy(turned_v, v.turned_down, down_sem.at[1])

        def turn_down(condition):
            @pl.when(condition)
            def _():
                down_load.wait()
                transpose_into(turned_v, down_v)
                down_save.start()

        for i in range(7):
            load(i)
        turn_down(at.core == at.section)
        row_blocks(rows, first_norm)
        sq.barrier()
        ins = sq.spread(normed_in, s_send.at[0], s_recv.at[0], False)
        operand_copies[1].wait()
        operand_copies[2].wait()
        ins.wait_own()
        for i in range(4):
            project(i, sq.own)
        ins.wait_next()
        for i in range(4):
            project(i, sq.next)
        save(2, 3, 4, 7, 8)
        retain(sq.next)
        loads_wait(4)
        give_back(sq.next, merged, out_t)
        gives = give(1, 0)
        retain(sq.own)
        give_back(sq.own, merged, out_t)
        gives += give(0, 0)
        save(5, 6, 9)
        transpose_into(normed_in_t, normed_in)
        save(1)
        turn_down(at.core != at.section)
        for push in gives:
            push.wait_recv()
        row_blocks(rows, second_norm)
        save(0)
        mids = sq.spread(normed_mid, s_send.at[1], s_recv.at[1], False)
        mids.wait_own()
        feed(sq.own)
        mids.wait_next()
        save(10)
        feed(sq.next)
        save(11, 12, 13)
        for push in [ins, mids] + gives:
            push.wait_send()
        for copy in saves:
            copy.wait()
        down_save.wait()
        return

    (z_send, z_recv, x_send, x_recv, c_send, c_recv, o_send, o_recv, here_sem, gain_send, gain_recv, d_send, d_recv,
     d_sem, own_gains, ids_land, id_send, id_recv, mask_sem) = refs
    steps = [(k, b) for k in range(at.groups) for b in range(2)][1:]

    def place(section=None, dp=None):
        return (at.section if section is None else section, at.dp if dp is None else dp, at.tensor)

    def copy(src, dst, send, recv, device):
        return pltpu.make_async_remote_copy(
            src_ref=src, dst_ref=dst, send_sem=send, recv_sem=recv, device_id=device, device_id_type=MESH
        )

    partners = [sq.device(*step) for step in SQUARE] + [place(dp=at.sibling()), place(section=other)]
    partners += [place(dp=at.dp_at(k, b)) for k, b in steps if (k, b) != (0, 1)]
    barrier = pltpu.get_barrier_semaphore()
    for partner in partners:
        pl.semaphore_signal(barrier, inc=1, device_id=partner, device_id_type=MESH)
    pl.semaphore_wait(barrier, len(partners))

    own_gains[0:1] = v.mixer_gain[...]
    own_gains[1:2] = v.ffn_gain[...]
    gain_copy = copy(own_gains, v.gains.at[at.section], gain_send, gain_recv, place(section=other))
    gain_copy.start()
    v.gains[at.section] = own_gains[...]
    id_copy = copy(v.ids, ids_land, id_send, id_recv, sq.device(1, 0))
    id_copy.start()

    def make_masks():
        length = masks.shape[-1]
        t = lax.broadcasted_iota(jnp.int32, (length, length), 0).astype(f32)
        s = lax.broadcasted_iota(jnp.int32, (length, length), 1).astype(f32)
        distance = jnp.maximum(t - s, 0.0)
        decays = []
        for head in range(heads):
            number = jnp.full((1, 1), ((at.tensor * 2 + at.low) * heads + head).astype(f32))
            rate = jnp.log(1.0 - jnp.exp2(-5.0 - number))
            decays.append(jnp.exp(rate * distance) * HEAD_K ** (-0.5))
        for sequence, ids in ((sq.own, v.ids), (sq.next, ids_land)):
            row = ids[pl.ds(at.section, 1), :]
            same = t >= s
            for document in (1, 2):
                start = jnp.sum(jnp.where(row < document, 1.0, 0.0), axis=1, keepdims=True)
                same = jnp.logical_and(same, (t >= start) == (s >= start))
            for head in range(heads):
                masks[sequence, head] = jnp.where(same, decays[head], 0.0)

    def slot(i, section, dp):
        which, first, size = groups[i]
        return stored[which].at[section, dp // 2, dp % 2, :, pl.ds(first, size)]

    def block(i, section, core):
        which, first, size = groups[i]
        return stored[which].at[section, :, core, :, pl.ds(first, size)]

    def part(i, b):
        size = groups[i][2]
        return shards[i].at[:, pl.ds(pl.multiple_of((at.low + b) % 2 * size, size), size)]

    z_copies, x_copies, here, core_own, core_other = {}, {}, {}, {}, {}

    def push_own(i):
        mine = slot(i, at.section, at.dp)
        for j, (k, b) in enumerate(steps):
            z_copies[i, j] = copy(part(i, b), mine, z_send.at[i, j], z_recv.at[i, j], place(dp=at.dp_at(k, b)))
            z_copies[i, j].start()
        x_copies[i, 0] = copy(part(i, 0), mine, x_send.at[i, 0], x_recv.at[i, 0], place(section=other))
        x_copies[i, 0].start()
        here[i] = pltpu.make_async_copy(part(i, 0), mine, here_sem.at[i])
        here[i].start()

    def pass_on(i):
        for j, (k, b) in enumerate(steps):
            z_copies[i, j].wait_recv()
            arrived = slot(i, at.section, at.dp_at(-k, b))
            x_copies[i, j + 1] = copy(arrived, arrived, x_send.at[i, j + 1], x_recv.at[i, j + 1], place(section=other))
            x_copies[i, j + 1].start()
        here[i].wait()
        mine = block(i, at.section, at.core)
        core_own[i] = copy(mine, mine, c_send.at[i], c_recv.at[i], place(dp=at.sibling()))
        core_own[i].start()

    def share_other(i):
        for j in range(slices):
            x_copies[i, j].wait_recv()
        theirs = block(i, other, at.core)
        core_other[i] = copy(theirs, theirs, o_send.at[i], o_recv.at[i], place(dp=at.sibling()))
        core_other[i].start()

    def arrive(i):
        @pl.when(at.section == 0)
        def _():
            core_own[i].wait_recv()

        @pl.when(at.section == 1)
        def _():
            core_other[i].wait_recv()

        load(i)

    ahead = 3
    for i in range(ahead):
        push_own(i)
    gain_copy.wait_recv()
    row_blocks(rows, first_norm)
    ins = sq.spread(normed_in, s_send.at[0], s_recv.at[0], True)

    def advance(i):
        pass_on(i)
        if i + ahead < 8:
            push_own(i + ahead)
        if i > 0:
            share_other(i - 1)
            arrive(i - 1)

    advance(0)
    downs = sq.spread(v.grad_down, d_send, d_recv, True, v.out_grad.at[at.section], d_sem)
    id_copy.wait_recv()
    make_masks()
    mask_save = pltpu.make_async_copy(masks, v.masks, mask_sem)
    mask_save.start()
    advance(1)
    ins.wait_recv()
    transpose_into(normed_in_t, normed_in)
    save(1)
    operand_copies[1].wait()
    for i in range(2, 5):
        advance(i)
        for s in (sq.own, sq.next):
            project(i - 2, s)
    advance(5)
    for s in (sq.own, sq.next):
        project(3, s)
    retain(sq.next)
    loads_wait(4)
    give_back(sq.next, merged, out_t)
    gives = give(1, 0)
    retain(sq.own)
    give_back(sq.own, merged, out_t)
    gives += give(0, 0)
    advance(6)
    for push in gives:
        push.wait_recv()
    row_blocks(rows, second_norm)
    mids = sq.spread(normed_mid, s_send.at[1], s_recv.at[1], True)
    advance(7)
    mids.wait_recv()
    transpose_into(normed_mid_t, normed_mid)
    save(0, 2, 3, 4, 5, 6, 7, 8, 9, 10)
    feed(sq.next)
    feed(sq.own)
    save(11, 12, 13)
    for push in gives:
        push.wait_send()

    def last_group():
        for j in range(slices):
            x_copies[7, j].wait_recv()
        core_other[7].start()

    theirs = block(7, other, at.core)
    core_other[7] = copy(theirs, theirs, o_send.at[7], o_recv.at[7], place(dp=at.sibling()))

    @pl.when(at.section == 1)
    def _():
        last_group()

    arrive(7)
    loads_wait(7)
    give_back(sq.next, hidden, down_t)
    ends = give(1, 1)
    give_back(sq.own, hidden, down_t)
    ends += give(0, 1)

    @pl.when(at.section == 0)
    def _():
        last_group()

    for push in ends:
        push.wait_recv()

    def last(block):
        result[block] = (middle[block] + collected(block, 1)).astype(bf16)

    row_blocks(rows, last)

    @pl.when(at.section == 0)
    def _():
        for i in range(8):
            core_other[i].wait_recv()

    @pl.when(at.section == 1)
    def _():
        for i in range(8):
            core_own[i].wait_recv()

    downs.wait_recv()
    for push in [downs, ins, mids] + ends + list(z_copies.values()) + list(x_copies.values()):
        push.wait_send()
    for i in range(8):
        core_own[i].wait_send()
        core_other[i].wait_send()
    gain_copy.wait_send()
    id_copy.wait_send()
    mask_save.wait()
    for copy in saves:
        copy.wait()


def forward_layer(layer, operands, weights, length, heads, dp_size):
    rows, width = operands[0].shape[-2:]
    streams = layer == 0
    slices = dp_size // 2
    quarter_k = heads * HEAD_K
    quarter_v = heads * HEAD_V
    quarter_f = weights[-1].shape[-1] // 2 if streams else weights[-1].shape[-1]
    vmem = pl.BlockSpec(memory_space=pltpu.VMEM)
    any_spec = pl.BlockSpec(memory_space=pl.ANY)
    wides = (2 * quarter_k + 2 * quarter_v, quarter_v, 2 * quarter_f, quarter_f)

    def tokens(wide, kind=bf16):
        return jax.ShapeDtypeStruct((2, length, wide), kind)

    turned = jax.ShapeDtypeStruct((width, 2 * length), bf16)
    dma = pltpu.SemaphoreType.DMA
    out_shape = [
        jax.ShapeDtypeStruct((rows, width), f32),
        turned,
        tokens(quarter_k),
        tokens(quarter_k),
        tokens(quarter_v),
        tokens(quarter_v),
        jax.ShapeDtypeStruct((2, heads, length, 1), f32),
        tokens(quarter_v),
        tokens(quarter_v),
        tokens(quarter_v),
        turned if streams else tokens(width),
        tokens(quarter_f),
        tokens(quarter_f),
        tokens(quarter_f),
    ]
    out_specs = [any_spec] * len(out_shape)
    scratch = [pltpu.VMEM(out.shape, out.dtype) for out in out_shape]
    mask_shape = (2, heads, length, length)
    scratch += [
        dma((14,)),
        pltpu.VMEM((rows, width), bf16),
        pltpu.VMEM(mask_shape, f32),
        pltpu.VMEM((4, length, HEAD_K // 2), f32),
        dma((3,)),
    ]
    scratch += [pltpu.VMEM((slices, 2, width // dp_size, wide), bf16) for wide in wides] + [
        dma((8,)),
    ] + [pltpu.VMEM((2, length, width), bf16)] * (3 if streams else 2) + [
        pltpu.VMEM((2, 3, rows, width), bf16),
        dma((2, 6)),
        dma((2, 6)),
        dma((2, 3)),
        dma((2, 3)),
    ]
    if streams:
        out_shape = (
            [jax.ShapeDtypeStruct((2, slices, 2, width // dp_size, wide), bf16) for wide in wides]
            + [jax.ShapeDtypeStruct((2, 2, width), f32), jax.ShapeDtypeStruct(mask_shape, f32)]
            + out_shape
            + [tokens(width), jax.ShapeDtypeStruct((rows, width), bf16)]
        )
        out_specs = [any_spec] * 4 + [vmem, any_spec] + out_specs + [any_spec, vmem]
        scratch += [
            dma((8, slices - 1)),
            dma((8, slices - 1)),
            dma((8, slices)),
            dma((8, slices)),
            dma((8,)),
            dma((8,)),
            dma((8,)),
            dma((8,)),
            dma((8,)),
            dma,
            dma,
            dma((6,)),
            dma((6,)),
            dma,
            pltpu.VMEM((2, width), f32),
            pltpu.VMEM((2, length), jnp.int32),
            dma,
            dma,
            dma,
        ]
        in_specs = [any_spec, vmem, vmem, vmem, any_spec, any_spec]
    else:
        out_shape = out_shape + [turned]
        out_specs = out_specs + [any_spec]
        scratch += [pltpu.VMEM((2, length, width), bf16), pltpu.VMEM(turned.shape, bf16), dma((2,))]
        in_specs = [any_spec, vmem, any_spec, any_spec, any_spec]
    return pl.pallas_call(
        functools.partial(forward_kernel, dp_size, layer),
        out_shape=out_shape,
        in_specs=in_specs + [any_spec] * len(weights),
        out_specs=out_specs,
        scratch_shapes=scratch,
        compiler_params=pltpu.CompilerParams(
            collective_id=1 + layer, has_side_effects=True, vmem_limit_bytes=VMEM_LIMIT
        ),
        name="forward_layer",
    )(*operands, *weights)


class Refs:
    pass


KEPT = 5
GROUPS = 7


def backward_kernel(dp_size, layer, *refs):
    final_layer = layer == 0
    v = Refs()
    (v.grad_out, v.gains, v.tables, v.masks, v.x, v.middle, v.normed_in_t, v.query_rot, v.key_rot, v.value, v.unit,
     v.inverse, v.opened, v.slope_open, v.merged, v.normed_mid_t, v.act, v.slope, v.hidden,
     v.qkvs_all, v.out_all, v.gate_up_all, v.down_all, v.down_in, *refs) = refs
    if not final_layer:
        v.down_turned, *refs = refs
    if final_layer:
        (v.later_chip, v.later_terms, v.first_rows, v.later_normed_in_t, v.later_qkvs, v.later_hidden, v.later_middle,
         *refs) = refs
    v.grad_in, v.chip, v.core_land, *refs = refs
    if final_layer:
        v.x_land, v.final, v.gain_sums, v.result, v.taken_rows, v.taken_grads, *refs = refs
    else:
        v.terms, v.next_down, v.kept_qkvs, *refs = refs
    (v.big, v.out_t, v.query_v, v.key_v, v.value_v, v.wide_a, v.wide_b, v.wide_c, v.inverse_v, v.x_v, v.middle_v,
     v.normed_t, v.outer, v.grad_down, v.grad_gate_up, v.grad_branch, v.grad_qkvs, v.turned, v.parts, v.landed,
     v.grad_middle, v.stage_given, v.stage_own, v.core_part, v.load_sem, v.s_send, v.s_recv, v.g_send, v.g_recv,
     v.c_send, v.c_recv, v.local_sem, v.masks_v, v.tables_v, v.grad_out_v, *refs) = refs
    if final_layer:
        (v.left, v.right, v.sums, v.r_sem, v.x_send, v.x_recv, v.z_send, v.z_recv, v.terms, v.held, v.hop_land,
         v.t_send, v.t_recv, v.row_send, v.row_recv, v.landed_y) = refs
    else:
        v.d_send, v.d_recv, v.d_sem, v.kept_sem, v.mid_v = refs
    at = Place(dp_size)
    rows, width = v.x.shape[-2:]
    sq = Square(dp_size, rows)
    masks, tables, gains = v.masks_v, v.tables_v, v.gains
    query_v, key_v, value_v = v.query_v, v.key_v, v.value_v
    wide_a, wide_b, wide_c = v.wide_a, v.wide_b, v.wide_c
    grad_down, grad_gate_up, grad_branch, grad_qkvs = v.grad_down, v.grad_gate_up, v.grad_branch, v.grad_qkvs
    big, out_t, outer, parts, landed, terms = v.big, v.out_t, v.outer, v.parts, v.landed, v.terms
    wide_k = query_v.shape[-1]
    wide_v = value_v.shape[-1]
    wide_f = outer.shape[-1]
    heads = wide_k // HEAD_K
    slices = dp_size // 2
    slice_rows = width // dp_size
    gain_in = gains[layer, 0:1]
    gain_mid = gains[layer, 1:2]
    other = 1 - at.section
    steps = [(k, b) for k in range(at.groups) for b in range(2)]
    steps = steps[1:] + steps[:1]

    def load(index, source, target):
        copy = pltpu.make_async_copy(source, target, v.load_sem.at[index])
        copy.start()
        return copy

    def remote(src, dst, send, recv, device):
        return pltpu.make_async_remote_copy(
            src_ref=src, dst_ref=dst, send_sem=send, recv_sem=recv, device_id=device, device_id_type=MESH
        )

    def place(section=None, dp=None, tensor=None):
        return (
            at.section if section is None else section,
            at.dp if dp is None else dp,
            at.tensor if tensor is None else tensor,
        )

    sibling = place(dp=at.sibling())
    across = place(section=other)

    token_load = load(14, v.down_in, grad_down)
    down_load = load(0, v.down_all.at[layer], big.at[:, pl.ds(2 * wide_f, wide_f)])
    act_load = load(1, v.act, wide_a)
    slope_load = load(2, v.slope, wide_b)
    gate_load = load(3, v.gate_up_all.at[layer], big.at[:, pl.ds(0, 2 * wide_f)])
    hidden_load = load(4, v.hidden, outer)
    if not final_layer:
        turned_load = load(18, v.down_turned, v.turned)
    mid_load = load(5, v.normed_mid_t, v.normed_t if final_layer else v.mid_v)
    early = [
        load(6, v.middle, v.middle_v),
        load(7, v.x.at[at.section] if final_layer else v.x, v.x_v),
        load(8, v.out_all.at[layer], out_t),
        load(9, v.query_rot, query_v),
        load(10, v.key_rot, key_v),
        load(11, v.value, value_v),
        load(12, v.inverse, v.inverse_v),
        load(13, v.opened, wide_c),
        load(15, v.masks, masks),
        load(16, v.tables, tables),
        load(17, v.grad_out if final_layer else v.grad_out.at[at.section], v.grad_out_v),
    ]
    terms[...] = jnp.zeros_like(terms)

    partners = [sq.device(*step) for step in SQUARE] + [sibling]
    if final_layer:
        partners.append(across)
        partners += [place(dp=at.dp_at(k, b)) for k, b in steps[:-1] if (k, b) != (0, 1)]
    barrier = pltpu.get_barrier_semaphore()
    for partner in partners:
        pl.semaphore_signal(barrier, inc=1, device_id=partner, device_id_type=MESH)
    pl.semaphore_wait(barrier, len(partners))

    def x_copy(e, at_source, j, source):
        block = source.at[at_source, j]
        return remote(block, v.x_land.at[e, j], v.x_send.at[e, j], v.x_recv.at[e, j], across)

    def start_x(e, at_source, source):
        @pl.loop(0, slices)
        def _(j):
            x_copy(e, at_source, j, source).start()

    row_copies = []
    if final_layer:

        @pl.when(at.section == 0)
        def _():
            @pl.loop(0, KEPT)
            def _(e):
                start_x(e, e, v.later_chip)

            remote(v.grad_out, v.taken_grads, v.row_send.at[1], v.row_recv.at[1], across).start()

        @pl.when(at.section == 1)
        def _():
            remote(v.first_rows, v.taken_rows, v.row_send.at[0], v.row_recv.at[0], across).start()

    def through_down(s):
        tokens = grad_down[s]
        for start in range(0, wide_f, TILE):
            cols = slice(start, start + TILE)
            grad_hidden = mm(tokens, big[:, 2 * wide_f + start : 2 * wide_f + start + TILE])
            grad_gate_up[s, :, cols] = (grad_hidden * wide_b[s, :, cols].astype(f32)).astype(bf16)
            grad_gate_up[s, :, wide_f + start : wide_f + start + TILE] = (
                grad_hidden * wide_a[s, :, cols].astype(f32)
            ).astype(bf16)

    def give_back(s, source, weight, first, size, target):
        tokens = source[s]
        for start in range(0, width, TILE):
            target[s, :, start : start + TILE] = mm_nt(
                tokens, weight[start : start + TILE, first : first + size]
            ).astype(bf16)

    def collected(block, given, land):
        total = sq.chunk(given)[block].astype(f32)
        for j in range(len(SQUARE)):
            total = total + land[j, block].astype(f32)
        return total

    def exchange(source, weight, first, size, target, land, which):
        give_back(sq.next, source, weight, first, size, target)
        send, recv = v.g_send.at[which], v.g_recv.at[which]
        pushes = [sq.give(target, land, send, recv, j) for j in (1, 2)]
        give_back(sq.own, source, weight, first, size, target)
        pushes.append(sq.give(target, land, send, recv, 0))
        return pushes

    members = [
        (v.turned, outer, 0, wide_f),
        (v.normed_t, grad_gate_up, 0, wide_f),
        (v.normed_t, grad_gate_up, wide_f, wide_f),
        (v.turned, outer, 0, wide_v),
        (v.normed_t, grad_qkvs, 0, 2 * wide_k),
        (v.normed_t, grad_qkvs, 2 * wide_k, wide_v),
        (v.normed_t, grad_qkvs, 2 * wide_k + wide_v, wide_v),
    ]
    members += members[KEPT:]
    given_copies, own_copies, fetches = {}, {}, {}

    def product(e, dp):
        left, right, first, size = members[e]
        start = pl.multiple_of(dp * slice_rows, slice_rows)
        wide = right[:, :, first : first + size].reshape(-1, size)
        return mm(left[pl.ds(start, slice_rows), :], wide)

    def given(e):
        if e >= 2:
            given_copies[e - 2].wait_send()
        stage = v.stage_given.at[e % 2]

        @pl.loop(0, slices)
        def _(j):
            stage[j] = product(e, j * 2 + 1 - at.core).astype(bf16)

        given_copies[e] = remote(stage, v.core_land.at[e], v.c_send.at[e], v.c_recv.at[e], sibling)
        given_copies[e].start()

    def fetch(e):
        given_copies[e].wait_recv()
        fetches[e] = pltpu.make_async_copy(v.core_land.at[e], v.core_part, v.local_sem.at[0])
        fetches[e].start()

    def settle(e):
        if e in settled:
            return
        settled.append(e)
        own_copies[e].wait()
        if final_layer:

            @pl.when(at.section == (1 if e < GROUPS else 0))
            def _():
                start_x(e if e < GROUPS else e - GROUPS + KEPT, e, v.chip)

    def own(e):
        if e >= 1:
            settle(e - 1)
        fetches[e].wait()

        @pl.loop(0, slices)
        def _(j):
            v.stage_own[j] = (product(e, j * 2 + at.core) + v.core_part[j].astype(f32)).astype(bf16)

        own_copies[e] = pltpu.make_async_copy(v.stage_own, v.chip.at[e], v.local_sem.at[1])
        own_copies[e].start()

    settled = []

    def index(k, b):
        return ((at.group + k) % at.groups) * 2 + (at.low + b) % 2

    def piece(e, k):
        start = pl.multiple_of(at.low * wide_f, wide_f)
        return v.final.at[e, k, :, pl.ds(start, wide_f)]

    def z_copy(e, j):
        k, b = steps[j]
        return remote(v.sums.at[j], piece(e, k), v.z_send.at[e, j], v.z_recv.at[e, j], place(dp=at.dp_at(k, b)))

    def home_copy(e):
        return pltpu.make_async_copy(v.sums.at[slices - 1], piece(e, 0), v.r_sem.at[2, 0])

    def reduce_slices(e, at_source, source, first, stop, wait_previous):
        def loads(j):
            here = index(*steps[j])
            return (
                pltpu.make_async_copy(source.at[at_source, here], v.left.at[j % 2], v.r_sem.at[0, j % 2]),
                pltpu.make_async_copy(v.x_land.at[e, here], v.right.at[j % 2], v.r_sem.at[1, j % 2]),
            )

        def begin(j):
            x_copy(e, at_source, index(*steps[j]), source).wait_recv()
            for copy in loads(j):
                copy.start()

        begin(first)
        for j in range(first, stop):
            if j + 1 < stop:
                begin(j + 1)
            for copy in loads(j):
                copy.wait()

            @pl.when(wait_previous)
            def _():
                if j == slices - 1:
                    home_copy(e).wait()
                else:
                    z_copy(e - 1, j).wait_send()

            v.sums[j] = (v.left[j % 2].astype(f32) + v.right[j % 2].astype(f32)).astype(bf16)
            if j == slices - 1:
                home_copy(e).start()
            else:
                z_copy(e, j).start()

    reduced = [0, 0]

    def source_of(section, e):
        if section == 0:
            return e, v.chip
        return (e, v.later_chip) if e < KEPT else (e + GROUPS - KEPT, v.chip)

    def reduce_some(section, count):
        if not final_layer:
            return

        @pl.when(at.section == section)
        def _():
            done = reduced[section]
            while done < reduced[section] + count:
                e, first = divmod(done, slices)
                stop = min(slices, first + reduced[section] + count - done)
                reduce_slices(e, *source_of(section, e), first, stop, e > 0)
                done += stop - first

        reduced[section] += count

    def reduce_rest(section):
        e, first = divmod(reduced[section], slices)

        @pl.when(at.section == section)
        def _():
            begin = e
            if first > 0:
                reduce_slices(e, *source_of(section, e), first, slices, e > 0)
                begin = e + 1
            same = KEPT if section == 1 else GROUPS

            @pl.loop(begin, same)
            def _(i):
                reduce_slices(i, i, source_of(section, 0)[1], 0, slices, i > 0)

            for i in range(same, GROUPS):
                reduce_slices(i, *source_of(section, i), 0, slices, True)

    token_load.wait()
    if final_layer:
        hidden_load.wait()
        transpose_into(v.turned, grad_down)
        given(0)
    down_load.wait()
    act_load.wait()
    slope_load.wait()
    through_down(sq.next)
    through_down(sq.own)
    unit_load = load(1, v.unit, wide_a)
    bend_load = load(2, v.slope_open, wide_b)
    gate_load.wait()
    gives = exchange(grad_gate_up, big, 0, 2 * wide_f, parts, landed, 0)
    if not final_layer:
        hidden_load.wait()
        turned_load.wait()
        given(0)
    fetch(0)
    own(0)
    mid_load.wait()
    if not final_layer:
        transpose_into(v.normed_t, v.mid_v)
    settle(0)
    given(1)
    qkvs_load = load(3, v.qkvs_all.at[layer], big)
    merged_load = load(4, v.merged, outer)
    for copy in early:
        copy.wait()
    for push in gives:
        push.wait_recv()

    def through_mid(block):
        upstream = collected(block, parts, landed)
        normed, scale = norm_parts(v.middle_v[block])
        grad_rows = v.grad_out_v[block].astype(f32) + norm_grad(normed, scale, upstream, gain_mid)
        v.grad_middle[block] = grad_rows
        sq.chunk(grad_branch)[block] = grad_rows.astype(bf16)
        terms[1:2] = terms[1:2] + jnp.sum(upstream * normed, axis=0, keepdims=True)

    row_blocks(rows, through_mid)
    mids = sq.spread(grad_branch, v.s_send, v.s_recv, final_layer)
    reduce_some(0, 1)
    given(2)
    fetch(1)
    own(1)
    unit_load.wait()
    bend_load.wait()
    settle(1)
    reduce_some(1, slices)
    reduce_some(0, 1)

    def through_heads(s):
        tokens = grad_branch[s]
        for head in range(heads):
            cols_k = slice(head * HEAD_K, (head + 1) * HEAD_K)
            cols_v = slice(head * HEAD_V, (head + 1) * HEAD_V)
            grad_merged = mm(tokens, out_t[:, cols_v])
            unit_rows = wide_a[s, :, cols_v].astype(f32)
            first = 2 * wide_k + wide_v + head * HEAD_V
            grad_qkvs[s, :, first : first + HEAD_V] = (
                grad_merged * unit_rows * wide_b[s, :, cols_v].astype(f32)
            ).astype(bf16)
            grad_unit = grad_merged * wide_c[s, :, cols_v].astype(f32)
            grad_mixed = (
                v.inverse_v[s, head]
                * (
                    grad_unit
                    - jnp.mean(grad_unit, axis=-1, keepdims=True)
                    - unit_rows * jnp.mean(grad_unit * unit_rows, axis=-1, keepdims=True)
                )
            ).astype(bf16)
            query, key, val = query_v[s, :, cols_k], key_v[s, :, cols_k], value_v[s, :, cols_v]
            mask = masks[s, head]
            weight = (mm_nt(query, key) * mask).astype(bf16)
            grad_product = (mm_nt(grad_mixed, val) * mask).astype(bf16)
            first = 2 * wide_k + head * HEAD_V
            grad_qkvs[s, :, first : first + HEAD_V] = mm_tn(weight, grad_mixed).astype(bf16)
            grad_qkvs[s, :, cols_k] = turn_back(mm(grad_product, key), tables[0], tables[1], tables[2]).astype(bf16)
            first = wide_k + head * HEAD_K
            grad_qkvs[s, :, first : first + HEAD_K] = turn_back(
                mm_tn(grad_product, query), tables[0], tables[1], tables[3]
            ).astype(bf16)

    mids.wait_own()
    through_heads(sq.own)
    mids.wait_next()
    through_heads(sq.next)
    if not final_layer:
        keep = pltpu.make_async_copy(grad_qkvs, v.kept_qkvs, v.kept_sem)
        keep.start()
    qkvs_load.wait()
    reduce_some(0, 1)
    for push in gives:
        push.wait_send()
    ends = exchange(grad_qkvs, big, 0, grad_qkvs.shape[-1], parts, landed, 1)
    fetch(2)
    own(2)
    in_load = load(5, v.normed_in_t, v.normed_t)
    transpose_into(v.turned, grad_branch)
    settle(2)
    merged_load.wait()
    given(3)
    in_load.wait()
    given(4)
    fetch(3)
    own(3)
    reduce_some(1, slices)
    reduce_some(0, 1)
    settle(3)
    for push in ends:
        push.wait_recv()

    def through_in(block):
        upstream = collected(block, parts, landed)
        normed, scale = norm_parts(v.x_v[block].astype(f32))
        v.grad_in[block] = (v.grad_middle[block] + norm_grad(normed, scale, upstream, gain_in)).astype(bf16)
        terms[0:1] = terms[0:1] + jnp.sum(upstream * normed, axis=0, keepdims=True)

    row_blocks(rows, through_in)
    if final_layer:

        @pl.when(at.section == 1)
        def _():
            remote(v.grad_in, v.taken_grads, v.row_send.at[1], v.row_recv.at[1], across).start()

    else:
        downs = sq.spread(v.next_down, v.d_send, v.d_recv, False, v.grad_in, v.d_sem)

    if not final_layer:
        fetch(4)
        downs.wait_own()
        own(4)
        settle(4)
        downs.wait_next()
        for push in [downs, mids] + ends:
            push.wait_send()
        for e in (3, 4):
            given_copies[e].wait_send()
        keep.wait()
        return

    reduce_some(0, 1)
    given(5)
    fetch(4)
    own(4)
    reduce_some(0, 1)
    given(6)
    settle(4)
    reduce_some(1, slices)
    reduce_some(0, 1)
    fetch(5)
    own(5)
    reduce_some(0, 1)
    fetch(6)
    own(6)
    in_load = load(5, v.later_normed_in_t, v.normed_t)
    qkvs_load = load(3, v.later_qkvs, grad_qkvs)
    hidden_load = load(4, v.later_hidden, outer)
    middle_load = load(6, v.later_middle, v.middle_v)
    down_load = load(0, v.down_all.at[1], big.at[:, pl.ds(2 * wide_f, wide_f)])
    settle(6)
    reduce_some(1, slices)
    reduce_some(0, 1)
    in_load.wait()
    qkvs_load.wait()
    given(7)
    reduce_some(0, 1)
    given(8)
    fetch(7)
    own(7)
    reduce_some(0, 1)
    fetch(8)
    own(8)
    settle(7)
    reduce_some(0, 1)
    for push in [mids] + ends:
        push.wait_send()
    hidden_load.wait()
    down_load.wait()
    settle(8)
    gives_y = exchange(outer, big, 2 * wide_f, wide_f, parts, v.landed_y, 2)
    reduce_some(1, slices)
    reduce_some(0, slices)
    middle_load.wait()
    for push in gives_y:
        push.wait_recv()

    def last(block):
        v.result[block] = (v.middle_v[block] + collected(block, parts, v.landed_y)).astype(bf16)

    row_blocks(rows, last)

    @pl.when(at.section == 0)
    def _():
        remote(v.result, v.taken_rows, v.row_send.at[0], v.row_recv.at[0], across).start()

    for push in gives_y:
        push.wait_send()
    for e in (7, 8):
        given_copies[e].wait_send()
    reduce_rest(1)
    reduce_rest(0)

    held, hop_land, mine = v.held, v.hop_land, v.held.at[at.section]
    held[0] = terms[...]
    held[1] = v.later_terms[...]
    hop = remote(held, hop_land.at[0], v.t_send.at[0], v.t_recv.at[0], sibling)
    hop.start()
    hop.wait()
    held[...] = held[...] + hop_land[0]
    hop = remote(held.at[other], hop_land.at[1, other], v.t_send.at[1], v.t_recv.at[1], across)
    hop.start()
    hop.wait_send()
    remote(held.at[other], hop_land.at[1, at.section], v.t_send.at[1], v.t_recv.at[1], across).wait_recv()
    mine[...] = mine[...] + hop_land[1, at.section]
    for h, device in ((2, place(tensor=1 - at.tensor)), (3, place(dp=at.dp_at(0, 1)))):
        hop = remote(mine, hop_land.at[h, 0], v.t_send.at[h], v.t_recv.at[h], device)
        hop.start()
        hop.wait()
        mine[...] = mine[...] + hop_land[h, 0]
    hops = []
    for k in range(1, at.groups):
        hop = remote(mine, hop_land.at[3 + k, 0], v.t_send.at[3 + k], v.t_recv.at[3 + k], place(dp=at.dp_at(k, 0)))
        hop.start()
        hops.append(hop)
    total = mine[...]
    for k, hop in zip(range(1, at.groups), hops):
        hop.wait()
        total = total + hop_land[3 + k, 0]
    v.gain_sums[...] = total

    for which, rows_sent in ((0, v.result), (1, v.grad_in)):
        target = v.taken_rows if which == 0 else v.taken_grads
        copy = remote(rows_sent, target, v.row_send.at[which], v.row_recv.at[which], across)
        copy.wait_recv()
        copy.wait_send()

    home_copy(0).wait()
    for j in range(slices - 1):
        z_copy(GROUPS - 1, j).wait_send()

        @pl.loop(0, GROUPS)
        def _(e):
            z_copy(e, j).wait_recv()

    @pl.loop(0, GROUPS)
    def _(e):
        @pl.loop(0, slices)
        def _(j):
            x_copy(e, e, j, v.chip).wait_send()


def backward_layer(layer, grad_out, down, turned_down, x, gains, tables, masks, saved, gathered, dp_size, later=None, x_out=None):
    rows, width = x.shape[-2:]
    length = masks.shape[-1]
    (middle, normed_in_t, query_rot, key_rot, value, unit, inverse, opened, slope_open, merged, normed_mid_t, act, slope,
     hidden) = saved
    vmem = pl.BlockSpec(memory_space=pltpu.VMEM)
    any_spec = pl.BlockSpec(memory_space=pl.ANY)
    final_layer = layer == 0
    slices = dp_size // 2
    slice_rows = width // dp_size
    size = hidden.shape[-1]
    assert value.shape[-1] == size and 2 * query_rot.shape[-1] == size
    block = (slices, slice_rows, size)

    def held(*shape, kind=bf16):
        return pltpu.VMEM(shape, kind)

    def stored(*shape, kind=bf16):
        return jax.ShapeDtypeStruct(shape, kind)

    dma = pltpu.SemaphoreType.DMA
    operands = [grad_out, gains, tables, masks]
    operands += [x, middle, normed_in_t, query_rot, key_rot, value, unit, inverse, opened, slope_open, merged, normed_mid_t,
                 act, slope, hidden]
    operands += [*gathered, down]
    if not final_layer:
        operands += [turned_down]
    in_specs = [any_spec, vmem] + [any_spec] * (len(operands) - 2)
    count = 2 * GROUPS - KEPT if final_layer else KEPT
    out_shape = [stored(rows, width), stored(count, *block), stored(count, *block)]
    out_specs = [vmem, any_spec, any_spec]
    if final_layer:
        later_chip, later_terms, later_qkvs, later_saved = later
        operands += [later_chip, later_terms, x_out, later_saved[1], later_qkvs, later_saved[-1], later_saved[0]]
        in_specs += [any_spec, vmem] + [any_spec] * 5
        out_shape += [stored(GROUPS, *block), stored(GROUPS, dp_size // 4, slice_rows, 2 * size), stored(2, width, kind=f32),
                      stored(rows, width), stored(rows, width), stored(rows, width)]
        out_specs += [any_spec, any_spec, vmem, vmem, any_spec, any_spec]
    else:
        out_shape += [stored(2, width, kind=f32), stored(2, length, width), stored(2, length, 3 * size)]
        out_specs += [vmem, any_spec, any_spec]
    scratch = [
        held(width, 3 * size),
        held(width, size),
        held(*query_rot.shape),
        held(*key_rot.shape),
        held(*value.shape),
        held(2, length, size),
        held(2, length, size),
        held(2, length, size),
        held(*inverse.shape, kind=f32),
        held(rows, width),
        held(rows, width, kind=f32),
        held(width, 2 * length),
        held(2, length, size),
        held(2, length, width),
        held(2, length, 2 * size),
        held(2, length, width),
        held(2, length, 3 * size),
        held(width, 2 * length),
        held(2, length, width),
        held(3, rows, width),
        held(rows, width, kind=f32),
        held(2, *block),
        held(*block),
        held(*block),
        dma((19,)),
        dma((6,)),
        dma((6,)),
        dma((3, 3)),
        dma((3, 3)),
        dma((count,)),
        dma((count,)),
        dma((2,)),
        held(*masks.shape, kind=f32),
        held(*tables.shape, kind=f32),
        held(rows, width),
    ]
    if final_layer:
        hops = 3 + dp_size // 4
        scratch += [
            held(2, slice_rows, size),
            held(2, slice_rows, size),
            held(*block),
            dma((3, 2)),
            dma((GROUPS, slices)),
            dma((GROUPS, slices)),
            dma((GROUPS, slices - 1)),
            dma((GROUPS, slices - 1)),
            held(2, width, kind=f32),
            held(2, 2, width, kind=f32),
            held(hops, 2, 2, width, kind=f32),
            dma((hops,)),
            dma((hops,)),
            dma((2,)),
            dma((2,)),
            held(3, rows, width),
        ]
    else:
        scratch += [dma((6,)), dma((6,)), dma, dma, held(2, length, width)]
    return pl.pallas_call(
        functools.partial(backward_kernel, dp_size, layer),
        out_shape=out_shape,
        in_specs=in_specs,
        out_specs=out_specs,
        scratch_shapes=scratch,
        compiler_params=pltpu.CompilerParams(
            collective_id=4 + layer, has_side_effects=True, vmem_limit_bytes=VMEM_LIMIT
        ),
        name="backward_layer",
    )(*operands)


def nested(outs):
    return (*outs[:6], outs[6:-2], *outs[-2:])


def on_device(
    dp_size,
    layer_input,
    segment_ids,
    output_grad,
    query_weight,
    key_weight,
    value_weight,
    swish_weight,
    output_weight,
    gate_weight,
    up_weight,
    down_weight,
    mixer_gain,
    ffn_gain,
):
    at = Place(dp_size)
    section_first = at.section == 0
    width = layer_input.shape[2]
    length = segment_ids.shape[1]
    quarter_k = query_weight.shape[2] // 2
    heads_here = quarter_k // HEAD_K
    cosine, sine, growth = rotation_tables(length, HEAD_K // 2)
    tables = jnp.stack([cosine, sine, growth, 1.0 / growth])

    shards = (query_weight[0], key_weight[0], value_weight[0], swish_weight[0], output_weight[0].T, gate_weight[0],
              up_weight[0], down_weight[0].T)
    *gathered, all_gains, masks, first_saved, second_down, first_sent = nested(
        forward_layer(
            0, (layer_input, mixer_gain, ffn_gain, segment_ids, tables, output_grad), shards, length, heads_here, dp_size
        )
    )
    *second_saved, turned_down = forward_layer(
        1, (first_sent, all_gains, tables, masks, second_down), gathered, length, heads_here, dp_size
    )
    gathered = [g.reshape(2, width, g.shape[-1]) for g in gathered]
    second_grad, later_chip, _, later_terms, first_down, later_qkvs = backward_layer(
        1, output_grad, second_down, turned_down, first_sent, all_gains, tables, masks, second_saved, gathered, dp_size
    )
    first_grad, _, _, _, landed, my_gains, second_sent, taken_rows, taken_grads = backward_layer(
        0, second_grad, first_down, None, layer_input, all_gains, tables, masks, first_saved, gathered, dp_size,
        (later_chip, later_terms, later_qkvs, second_saved), first_sent,
    )

    def by_layer(first, second, taken):
        return jnp.where(section_first, jnp.stack([first, taken]), jnp.stack([taken, second]))[None]

    def shard(e):
        return jnp.sum(landed[e].astype(f32), axis=0)

    def columns(e, start, size):
        step = landed.shape[-1] // 2
        part = jnp.concatenate([landed[e, :, :, p * step + start : p * step + start + size] for p in range(2)], axis=-1)
        return jnp.sum(part.astype(f32), axis=0)

    return (
        by_layer(first_sent, second_sent, taken_rows),
        by_layer(first_grad, second_grad, taken_grads),
        columns(4, 0, quarter_k)[None],
        columns(4, quarter_k, quarter_k)[None],
        shard(5)[None],
        shard(6)[None],
        shard(3).T[None],
        shard(1)[None],
        shard(2)[None],
        shard(0).T[None],
        my_gains[0][None],
        my_gains[1][None],
    )


def solution(mesh):
    in_specs = (
        P(None, ("dp", "tensor"), None),
        P(None, "dp"),
        P(None, ("dp", "tensor"), None),
        P("section", "dp", "tensor"),
        P("section", "dp", "tensor"),
        P("section", "dp", "tensor"),
        P("section", "dp", "tensor"),
        P("section", "tensor", "dp"),
        P("section", "dp", "tensor"),
        P("section", "dp", "tensor"),
        P("section", "tensor", "dp"),
        P("section", None),
        P("section", None),
    )
    out_specs = (
        P("section", None, ("dp", "tensor"), None),
        P("section", None, ("dp", "tensor"), None),
        P("section", "dp", "tensor"),
        P("section", "dp", "tensor"),
        P("section", "dp", "tensor"),
        P("section", "dp", "tensor"),
        P("section", "tensor", "dp"),
        P("section", "dp", "tensor"),
        P("section", "dp", "tensor"),
        P("section", "tensor", "dp"),
        P("section", None),
        P("section", None),
    )
    return jax.shard_map(
        functools.partial(on_device, mesh.shape["dp"]),
        mesh=mesh,
        in_specs=in_specs,
        out_specs=out_specs,
        check_vma=False,
    )
```

```python
import functools

import jax
import jax.numpy as jnp
from jax import lax
from jax.experimental import pallas as pl
from jax.experimental.pallas import tpu as pltpu
from jax.sharding import PartitionSpec as P

HEAD_K = 256
HEAD_V = 512
MESH = pl.DeviceIdType.MESH

epsilon = 1e-05
group_guard = 1.0
bf16 = jnp.bfloat16
f32 = jnp.float32


def rotation_tables(length, half_width):
    pair_index = jnp.arange(half_width).astype(f32)
    position = jnp.arange(length).astype(f32)[:, None]
    angle = position * jnp.exp(-jnp.log(10000.0) * pair_index / half_width)
    zeta = (pair_index / half_width + 0.4) / 1.4
    growth = jnp.exp(position / 512.0 * jnp.log(zeta))
    return (jnp.cos(angle), jnp.sin(angle), growth)


class Place:
    def __init__(self, dp_size):
        self.groups = dp_size // 4
        self.section = lax.axis_index("section")
        self.dp = lax.axis_index("dp")
        self.tensor = lax.axis_index("tensor")
        self.core = self.dp % 2
        self.low = (self.dp // 2) % 2
        self.group = self.dp // 4

    def dp_at(self, group_step, low_step):
        group = (self.group + group_step + self.groups) % self.groups
        return (group * 2 + (self.low + low_step) % 2) * 2 + self.core

    def sibling(self):
        return self.dp + 1 - 2 * self.core


SQUARE = ((0, 1), (1, 0), (1, 1))
TILE = 512
VMEM_LIMIT = 63 * 1024 * 1024


def mm(left, right):
    return lax.dot_general(left, right, (((1,), (0,)), ((), ())), preferred_element_type=f32)


def mm_nt(left, right):
    return lax.dot_general(left, right, (((1,), (1,)), ((), ())), preferred_element_type=f32)


def mm_tn(left, right):
    return lax.dot_general(left, right, (((0,), (0,)), ((), ())), preferred_element_type=f32)


class Square:
    def __init__(self, dp_size, rows):
        self.at = Place(dp_size)
        self.rows = rows
        self.own = self.at.low
        self.next = 1 - self.at.low

    def device(self, low_step, tensor_step):
        return (self.at.section, self.at.dp_at(0, low_step), (self.at.tensor + tensor_step) % 2)

    def barrier(self):
        barrier = pltpu.get_barrier_semaphore()
        for step in SQUARE:
            pl.semaphore_signal(barrier, inc=1, device_id=self.device(*step), device_id_type=MESH)
        pl.semaphore_wait(barrier, len(SQUARE))

    def chunk(self, ref, low_step=0, tensor_step=0):
        start = pl.multiple_of((self.at.tensor + tensor_step) % 2 * self.rows, self.rows)
        return ref.at[(self.at.low + low_step) % 2, pl.ds(start, self.rows)]

    def copy(self, src, dst, send, recv, step):
        return pltpu.make_async_remote_copy(
            src_ref=src,
            dst_ref=dst,
            send_sem=send,
            recv_sem=recv,
            device_id=self.device(*step),
            device_id_type=MESH,
        )

    def spread(self, ref, send, recv, direct, own=None, here=None):
        return (DirectSpread if direct else Spread)(self, ref, send, recv, own, here)

    def give(self, parts, landed, send, recv, j):
        push = self.copy(self.chunk(parts, *SQUARE[j]), landed.at[j], send.at[j], recv.at[j], SQUARE[j])
        push.start()
        return push


class Spread:
    def __init__(self, sq, ref, send, recv, own, here):
        self.sq, self.ref, self.send, self.recv = sq, ref, send, recv
        self.half = sq.rows // 2
        source = self.source(own, here)
        beside, below = (0, 1), (1, 0)
        self.first = [
            self.push(source, sq.chunk(ref), half, j, step)
            for j, (half, step) in enumerate(((0, beside), (1, below), (1, beside), (0, below)))
        ]
        from_beside, from_below = sq.chunk(ref, *beside), sq.chunk(ref, *below)
        self.onward = [
            self.push(from_beside, from_beside, 0, 4, below, start=False),
            self.push(from_below, from_below, 1, 5, beside, start=False),
        ]

    def source(self, own, here):
        self.local = None
        if own is None:
            return self.sq.chunk(self.ref)
        self.local = pltpu.make_async_copy(own, self.sq.chunk(self.ref), here)
        self.local.start()
        return own

    def push(self, source, target, half, j, step, start=True):
        block = pl.ds(half * self.half, self.half)
        copy = self.sq.copy(source.at[block], target.at[block], self.send.at[j], self.recv.at[j], step)
        if start:
            copy.start()
        return copy

    def wait_own(self):
        for came, onward in zip(self.first[:2], self.onward):
            came.wait_recv()
            onward.start()
        self.first[2].wait_recv()

    def wait_next(self):
        self.first[3].wait_recv()
        for onward in self.onward:
            onward.wait_recv()

    def wait_recv(self):
        self.wait_own()
        self.wait_next()

    def wait_send(self):
        for copy in self.first + self.onward:
            copy.wait_send()
        if self.local is not None:
            self.local.wait()


class DirectSpread(Spread):
    def __init__(self, sq, ref, send, recv, own, here):
        self.sq, self.ref = sq, ref
        source = self.source(own, here)
        self.first, self.onward = [], []
        for j, step in enumerate(SQUARE):
            copy = sq.copy(source, sq.chunk(ref), send.at[j], recv.at[j], step)
            copy.start()
            self.first.append(copy)

    def wait_own(self):
        self.first[0].wait_recv()

    def wait_next(self):
        self.first[1].wait_recv()
        self.first[2].wait_recv()


class Collect:
    def __init__(self, sq, parts, landed, send, recv):
        self.sq, self.parts, self.landed, self.send, self.recv = sq, parts, landed, send, recv
        self.half = sq.rows // 2
        self.pushes = []

    def push(self, source, half, slot, target_half, j, step):
        copy = self.sq.copy(
            source.at[pl.ds(half * self.half, self.half)],
            self.landed.at[slot, pl.ds(target_half * self.half, self.half)],
            self.send.at[j],
            self.recv.at[j],
            step,
        )
        copy.start()
        self.pushes.append(copy)

    def after_next(self):
        across = self.sq.chunk(self.parts, 1, 1)
        self.push(across, 0, 2, 0, 0, (0, 1))
        self.push(across, 1, 2, 1, 1, (1, 0))
        self.push(self.sq.chunk(self.parts, 1, 0), 1, 1, 1, 2, (1, 0))

    def after_own(self):
        beside, below = self.sq.chunk(self.parts, 0, 1), self.sq.chunk(self.parts, 1, 0)
        self.push(beside, 0, 0, 0, 3, (0, 1))
        for half, chunk, slot, j, step in ((0, below, 1, 4, (1, 0)), (1, beside, 0, 5, (0, 1))):
            self.pushes[half].wait_recv()
            rows = pl.ds(half * self.half, self.half)
            chunk[rows] = (chunk[rows].astype(f32) + self.landed[2, rows].astype(f32)).astype(bf16)
            self.push(chunk, half, slot, half, j, step)

    def wait_recv(self):
        for copy in self.pushes[2:]:
            copy.wait_recv()

    def wait_send(self):
        for copy in self.pushes:
            copy.wait_send()


def row_blocks(rows, body, block=32):
    block = min(block, rows)

    @pl.loop(0, rows // block)
    def _(i):
        body(pl.ds(pl.multiple_of(i * block, block), block))


def norm_parts(values):
    centred = values - jnp.mean(values, axis=-1, keepdims=True)
    scale = lax.rsqrt(jnp.mean(centred * centred, axis=-1, keepdims=True) + epsilon)
    return centred * scale, scale


def norm_grad(normed, scale, upstream, gain):
    through = upstream * gain
    return scale * (
        through
        - jnp.mean(through, axis=-1, keepdims=True)
        - normed * jnp.mean(through * normed, axis=-1, keepdims=True)
    )


def turn(values, cosine, sine, scale):
    half = values.shape[-1] // 2
    a, b = values[:, :half], values[:, half:]
    return jnp.concatenate([(a * cosine - b * sine) * scale, (a * sine + b * cosine) * scale], axis=-1)


def turn_back(values, cosine, sine, scale):
    half = values.shape[-1] // 2
    a, b = values[:, :half] * scale, values[:, half:] * scale
    return jnp.concatenate([a * cosine + b * sine, b * cosine - a * sine], axis=-1)


def transpose_into(target, source):
    _, length, width = source.shape
    for s in range(2):
        for start in range(0, width, TILE):
            target[start : start + TILE, s * length : (s + 1) * length] = source[s, :, start : start + TILE].T


def forward_kernel(dp_size, layer, *refs):
    streams = layer == 0
    v = Refs()
    if streams:
        (v.x, v.mixer_gain, v.ffn_gain, v.ids, v.tables, v.out_grad, *refs) = refs
        shards, refs = refs[:8], refs[8:]
        stored, refs = refs[:4], refs[4:]
        (v.gains, v.masks, *refs) = refs
    else:
        (v.x, v.gains, v.tables, v.masks, v.down, *refs) = refs
        stored, refs = refs[:4], refs[4:]
    saved, refs = refs[:14], refs[14:]
    if streams:
        (v.grad_down, result, *refs) = refs
    else:
        (v.turned_down, *refs) = refs
    scratch, refs = refs[:14], refs[14:]
    (middle, normed_in_t, query_rot, key_rot, value, unit, inverse, opened, slope_open, merged, normed_mid_t, act, slope,
     hidden) = scratch
    save_sem, x_v, masks, tables, in_sem, *refs = refs
    held, refs = refs[:4], refs[4:]
    (w_sem, normed_in, *refs) = refs
    if streams:
        (normed_mid, *refs) = refs
    else:
        normed_mid = normed_mid_t
    (parts, landed, s_send, s_recv, g_send, g_recv, *refs) = refs
    x = x_v
    rows, width = x.shape
    sq = Square(dp_size, rows)
    at = sq.at
    sources = [(v.x.at[at.section] if streams else v.x, x_v), (v.tables, tables)]
    if not streams:
        sources.append((v.masks, masks))
    operand_copies = [
        pltpu.make_async_copy(source, target, in_sem.at[i]) for i, (source, target) in enumerate(sources)
    ]
    for copy in operand_copies:
        copy.start()
    operand_copies[0].wait()
    saves = []

    def save(*which):
        for i in which:
            copy = pltpu.make_async_copy(scratch[i], saved[i], save_sem.at[i])
            copy.start()
            saves.append(copy)

    qkvs, out_t, gate_up, down_t = held
    wide_k = query_rot.shape[-1]
    wide_v = value.shape[-1]
    wide_f = hidden.shape[-1]
    heads = wide_k // HEAD_K
    slices = dp_size // 2
    other = 1 - at.section
    groups = [(0, 0, wide_k), (0, wide_k, wide_k), (0, 2 * wide_k, wide_v), (0, 2 * wide_k + wide_v, wide_v),
              (1, 0, wide_v), (2, 0, wide_f), (2, wide_f, wide_f), (3, 0, wide_f)]
    loads = {}

    def load(i):
        which, first, size = groups[i]
        columns = pl.ds(first, size)
        loads[i] = pltpu.make_async_copy(
            stored[which].at[layer, :, :, :, columns], held[which].at[:, :, :, columns], w_sem.at[i]
        )
        loads[i].start()

    def weight(which, first, size):
        return held[which][:, :, :, first : first + size].reshape(width, size)

    def first_norm(block):
        unit_rows, _ = norm_parts(x[block].astype(f32))
        sq.chunk(normed_in)[block] = (unit_rows * v.gains[layer, 0:1]).astype(bf16)

    def project(i, s):
        loads_wait(i)
        first, size = groups[i][1:]
        tokens = normed_in[s]
        for start in range(0, size, TILE):
            wide = mm(tokens, weight(0, first + start, TILE))
            cols = slice(start, start + TILE)
            if i < 2:
                dest = (query_rot, key_rot)[i]
                for head in range(TILE // HEAD_K):
                    part = wide[:, head * HEAD_K : (head + 1) * HEAD_K]
                    dest[s, :, start + head * HEAD_K : start + (head + 1) * HEAD_K] = turn(
                        part, tables[0], tables[1], tables[2 + i]
                    ).astype(bf16)
            elif i == 2:
                value[s, :, cols] = wide.astype(bf16)
            else:
                sigmoid = 1.0 / (1.0 + jnp.exp(-wide))
                opened[s, :, cols] = (wide * sigmoid).astype(bf16)
                slope_open[s, :, cols] = (sigmoid * (1.0 + wide * (1.0 - sigmoid))).astype(bf16)

    waited = []

    def loads_wait(i):
        if i not in waited:
            waited.append(i)
            loads[i].wait()

    def retain(s):
        for head in range(heads):
            cols_k = slice(head * HEAD_K, (head + 1) * HEAD_K)
            cols_v = slice(head * HEAD_V, (head + 1) * HEAD_V)
            product = mm_nt(query_rot[s, :, cols_k], key_rot[s, :, cols_k])
            weights = (product * masks[s, head]).astype(bf16)
            mixed = mm(weights, value[s, :, cols_v])
            centred = mixed - jnp.mean(mixed, axis=-1, keepdims=True)
            scale = lax.rsqrt(jnp.mean(centred * centred, axis=-1, keepdims=True) + group_guard)
            unit_rows = centred * scale
            inverse[s, head] = scale
            unit[s, :, cols_v] = unit_rows.astype(bf16)
            merged[s, :, cols_v] = (unit_rows * opened[s, :, cols_v].astype(f32)).astype(bf16)

    def give_back(s, source, weight_t):
        tokens = source[s]
        step = width // slices
        for i in range(slices):
            parts[s, :, i * step : (i + 1) * step] = mm_nt(tokens, weight_t[i].reshape(step, -1)).astype(bf16)

    def collected(block, which):
        total = sq.chunk(parts)[block].astype(f32)
        for j in range(3 if streams else 2):
            total = total + landed[which, j, block].astype(f32)
        return total

    def give(s, which):
        send, recv = g_send.at[which], g_recv.at[which]
        return [sq.give(parts, landed.at[which], send, recv, j) for j in ((1, 2) if s == 1 else (0,))]

    def second_norm(block):
        middle_rows = x[block].astype(f32) + collected(block, 0)
        middle[block] = middle_rows
        unit_rows, _ = norm_parts(middle_rows)
        sq.chunk(normed_mid)[block] = (unit_rows * v.gains[layer, 1:2]).astype(bf16)

    def feed(s):
        loads_wait(5)
        loads_wait(6)
        tokens = normed_mid[s]
        for start in range(0, wide_f, TILE):
            cols = slice(start, start + TILE)
            gate = mm(tokens, weight(2, start, TILE))
            up = mm(tokens, weight(2, wide_f + start, TILE))
            square = gate * gate
            bend = jnp.tanh(0.7978845608028654 * gate * (1.0 + 0.044715 * square))
            half = 0.5 * (1.0 + bend)
            gelu = gate * half
            slope_gelu = half + 0.5 * gate * (1.0 - bend * bend) * (
                0.7978845608028654 * (1.0 + 3 * 0.044715 * square)
            )
            act[s, :, cols] = gelu.astype(bf16)
            slope[s, :, cols] = (slope_gelu * up).astype(bf16)
            hidden[s, :, cols] = (gelu * up).astype(bf16)

    if not streams:
        (down_v, turned_v, down_sem) = refs
        down_load = pltpu.make_async_copy(v.down, down_v, down_sem.at[0])
        down_load.start()
        down_save = pltpu.make_async_copy(turned_v, v.turned_down, down_sem.at[1])

        def turn_down(condition):
            @pl.when(condition)
            def _():
                down_load.wait()
                transpose_into(turned_v, down_v)
                down_save.start()

        for i in range(7):
            load(i)
        turn_down(at.core == at.section)
        row_blocks(rows, first_norm)
        sq.barrier()
        ins = sq.spread(normed_in, s_send.at[0], s_recv.at[0], False)
        operand_copies[1].wait()
        operand_copies[2].wait()
        ins.wait_own()
        for i in range(4):
            project(i, sq.own)
        ins.wait_next()
        for i in range(4):
            project(i, sq.next)
        save(2, 3, 4, 7, 8)
        retain(sq.next)
        loads_wait(4)
        give_back(sq.next, merged, out_t)
        collect = Collect(sq, parts, landed.at[0], g_send.at[0], g_recv.at[0])
        collect.after_next()
        retain(sq.own)
        give_back(sq.own, merged, out_t)
        collect.after_own()
        gives = [collect]
        save(5, 6, 9)
        transpose_into(normed_in_t, normed_in)
        save(1)
        turn_down(at.core != at.section)
        for push in gives:
            push.wait_recv()
        row_blocks(rows, second_norm)
        save(0)
        mids = sq.spread(normed_mid, s_send.at[1], s_recv.at[1], False)
        mids.wait_own()
        feed(sq.own)
        mids.wait_next()
        save(10)
        feed(sq.next)
        save(11, 12, 13)
        for push in [ins, mids] + gives:
            push.wait_send()
        for copy in saves:
            copy.wait()
        down_save.wait()
        return

    (z_send, z_recv, x_send, x_recv, c_send, c_recv, o_send, o_recv, here_sem, gain_send, gain_recv, d_send, d_recv,
     d_sem, own_gains, ids_land, id_send, id_recv, mask_sem) = refs
    steps = [(k, b) for k in range(at.groups) for b in range(2)][1:]

    def place(section=None, dp=None):
        return (at.section if section is None else section, at.dp if dp is None else dp, at.tensor)

    def copy(src, dst, send, recv, device):
        return pltpu.make_async_remote_copy(
            src_ref=src, dst_ref=dst, send_sem=send, recv_sem=recv, device_id=device, device_id_type=MESH
        )

    partners = [sq.device(*step) for step in SQUARE] + [place(dp=at.sibling()), place(section=other)]
    partners += [place(dp=at.dp_at(k, b)) for k, b in steps if (k, b) != (0, 1)]
    barrier = pltpu.get_barrier_semaphore()
    for partner in partners:
        pl.semaphore_signal(barrier, inc=1, device_id=partner, device_id_type=MESH)
    pl.semaphore_wait(barrier, len(partners))

    own_gains[0:1] = v.mixer_gain[...]
    own_gains[1:2] = v.ffn_gain[...]
    gain_copy = copy(own_gains, v.gains.at[at.section], gain_send, gain_recv, place(section=other))
    gain_copy.start()
    v.gains[at.section] = own_gains[...]
    id_copy = copy(v.ids, ids_land, id_send, id_recv, sq.device(1, 0))
    id_copy.start()

    def make_masks():
        length = masks.shape[-1]
        t = lax.broadcasted_iota(jnp.int32, (length, length), 0).astype(f32)
        s = lax.broadcasted_iota(jnp.int32, (length, length), 1).astype(f32)
        distance = jnp.maximum(t - s, 0.0)
        decays = []
        for head in range(heads):
            number = jnp.full((1, 1), ((at.tensor * 2 + at.low) * heads + head).astype(f32))
            rate = jnp.log(1.0 - jnp.exp2(-5.0 - number))
            decays.append(jnp.exp(rate * distance) * HEAD_K ** (-0.5))
        for sequence, ids in ((sq.own, v.ids), (sq.next, ids_land)):
            row = ids[pl.ds(at.section, 1), :]
            same = t >= s
            for document in (1, 2):
                start = jnp.sum(jnp.where(row < document, 1.0, 0.0), axis=1, keepdims=True)
                same = jnp.logical_and(same, (t >= start) == (s >= start))
            for head in range(heads):
                masks[sequence, head] = jnp.where(same, decays[head], 0.0)

    def slot(i, section, dp):
        which, first, size = groups[i]
        return stored[which].at[section, dp // 2, dp % 2, :, pl.ds(first, size)]

    def block(i, section, core):
        which, first, size = groups[i]
        return stored[which].at[section, :, core, :, pl.ds(first, size)]

    def part(i, b):
        size = groups[i][2]
        return shards[i].at[:, pl.ds(pl.multiple_of((at.low + b) % 2 * size, size), size)]

    z_copies, x_copies, here, core_own, core_other = {}, {}, {}, {}, {}

    def push_own(i):
        mine = slot(i, at.section, at.dp)
        for j, (k, b) in enumerate(steps):
            z_copies[i, j] = copy(part(i, b), mine, z_send.at[i, j], z_recv.at[i, j], place(dp=at.dp_at(k, b)))
            z_copies[i, j].start()
        x_copies[i, 0] = copy(part(i, 0), mine, x_send.at[i, 0], x_recv.at[i, 0], place(section=other))
        x_copies[i, 0].start()
        here[i] = pltpu.make_async_copy(part(i, 0), mine, here_sem.at[i])
        here[i].start()

    def pass_on(i):
        for j, (k, b) in enumerate(steps):
            z_copies[i, j].wait_recv()
            arrived = slot(i, at.section, at.dp_at(-k, b))
            x_copies[i, j + 1] = copy(arrived, arrived, x_send.at[i, j + 1], x_recv.at[i, j + 1], place(section=other))
            x_copies[i, j + 1].start()
        here[i].wait()
        mine = block(i, at.section, at.core)
        core_own[i] = copy(mine, mine, c_send.at[i], c_recv.at[i], place(dp=at.sibling()))
        core_own[i].start()

    def share_other(i):
        for j in range(slices):
            x_copies[i, j].wait_recv()
        theirs = block(i, other, at.core)
        core_other[i] = copy(theirs, theirs, o_send.at[i], o_recv.at[i], place(dp=at.sibling()))
        core_other[i].start()

    def arrive(i):
        @pl.when(at.section == 0)
        def _():
            core_own[i].wait_recv()

        @pl.when(at.section == 1)
        def _():
            core_other[i].wait_recv()

        load(i)

    ahead = 3
    for i in range(ahead):
        push_own(i)
    gain_copy.wait_recv()
    row_blocks(rows, first_norm)
    ins = sq.spread(normed_in, s_send.at[0], s_recv.at[0], True)

    def advance(i):
        pass_on(i)
        if i + ahead < 8:
            push_own(i + ahead)
        if i > 0:
            share_other(i - 1)
            arrive(i - 1)

    advance(0)
    downs = sq.spread(v.grad_down, d_send, d_recv, True, v.out_grad.at[at.section], d_sem)
    id_copy.wait_recv()
    make_masks()
    mask_save = pltpu.make_async_copy(masks, v.masks, mask_sem)
    mask_save.start()
    advance(1)
    ins.wait_recv()
    transpose_into(normed_in_t, normed_in)
    save(1)
    operand_copies[1].wait()
    for i in range(2, 5):
        advance(i)
        for s in (sq.own, sq.next):
            project(i - 2, s)
    advance(5)
    for s in (sq.own, sq.next):
        project(3, s)
    retain(sq.next)
    loads_wait(4)
    give_back(sq.next, merged, out_t)
    gives = give(1, 0)
    retain(sq.own)
    give_back(sq.own, merged, out_t)
    gives += give(0, 0)
    advance(6)
    for push in gives:
        push.wait_recv()
    row_blocks(rows, second_norm)
    mids = sq.spread(normed_mid, s_send.at[1], s_recv.at[1], True)
    advance(7)
    mids.wait_recv()
    transpose_into(normed_mid_t, normed_mid)
    save(0, 2, 3, 4, 5, 6, 7, 8, 9, 10)
    feed(sq.next)
    feed(sq.own)
    save(11, 12, 13)
    for push in gives:
        push.wait_send()

    def last_group():
        for j in range(slices):
            x_copies[7, j].wait_recv()
        core_other[7].start()

    theirs = block(7, other, at.core)
    core_other[7] = copy(theirs, theirs, o_send.at[7], o_recv.at[7], place(dp=at.sibling()))

    @pl.when(at.section == 1)
    def _():
        last_group()

    arrive(7)
    loads_wait(7)
    give_back(sq.next, hidden, down_t)
    ends = give(1, 1)
    give_back(sq.own, hidden, down_t)
    ends += give(0, 1)

    @pl.when(at.section == 0)
    def _():
        last_group()

    for push in ends:
        push.wait_recv()

    def last(block):
        result[block] = (middle[block] + collected(block, 1)).astype(bf16)

    row_blocks(rows, last)

    @pl.when(at.section == 0)
    def _():
        for i in range(8):
            core_other[i].wait_recv()

    @pl.when(at.section == 1)
    def _():
        for i in range(8):
            core_own[i].wait_recv()

    downs.wait_recv()
    for push in [downs, ins, mids] + ends + list(z_copies.values()) + list(x_copies.values()):
        push.wait_send()
    for i in range(8):
        core_own[i].wait_send()
        core_other[i].wait_send()
    gain_copy.wait_send()
    id_copy.wait_send()
    mask_save.wait()
    for copy in saves:
        copy.wait()


def forward_layer(layer, operands, weights, length, heads, dp_size):
    rows, width = operands[0].shape[-2:]
    streams = layer == 0
    slices = dp_size // 2
    quarter_k = heads * HEAD_K
    quarter_v = heads * HEAD_V
    quarter_f = weights[-1].shape[-1] // 2 if streams else weights[-1].shape[-1]
    vmem = pl.BlockSpec(memory_space=pltpu.VMEM)
    any_spec = pl.BlockSpec(memory_space=pl.ANY)
    wides = (2 * quarter_k + 2 * quarter_v, quarter_v, 2 * quarter_f, quarter_f)

    def tokens(wide, kind=bf16):
        return jax.ShapeDtypeStruct((2, length, wide), kind)

    turned = jax.ShapeDtypeStruct((width, 2 * length), bf16)
    dma = pltpu.SemaphoreType.DMA
    out_shape = [
        jax.ShapeDtypeStruct((rows, width), f32),
        turned,
        tokens(quarter_k),
        tokens(quarter_k),
        tokens(quarter_v),
        tokens(quarter_v),
        jax.ShapeDtypeStruct((2, heads, length, 1), f32),
        tokens(quarter_v),
        tokens(quarter_v),
        tokens(quarter_v),
        turned if streams else tokens(width),
        tokens(quarter_f),
        tokens(quarter_f),
        tokens(quarter_f),
    ]
    out_specs = [any_spec] * len(out_shape)
    scratch = [pltpu.VMEM(out.shape, out.dtype) for out in out_shape]
    mask_shape = (2, heads, length, length)
    scratch += [
        dma((14,)),
        pltpu.VMEM((rows, width), bf16),
        pltpu.VMEM(mask_shape, f32),
        pltpu.VMEM((4, length, HEAD_K // 2), f32),
        dma((3,)),
    ]
    scratch += [pltpu.VMEM((slices, 2, width // dp_size, wide), bf16) for wide in wides] + [
        dma((8,)),
    ] + [pltpu.VMEM((2, length, width), bf16)] * (3 if streams else 2) + [
        pltpu.VMEM((2, 3, rows, width), bf16),
        dma((2, 6)),
        dma((2, 6)),
        dma((2, 6)),
        dma((2, 6)),
    ]
    if streams:
        out_shape = (
            [jax.ShapeDtypeStruct((2, slices, 2, width // dp_size, wide), bf16) for wide in wides]
            + [jax.ShapeDtypeStruct((2, 2, width), f32), jax.ShapeDtypeStruct(mask_shape, f32)]
            + out_shape
            + [tokens(width), jax.ShapeDtypeStruct((rows, width), bf16)]
        )
        out_specs = [any_spec] * 4 + [vmem, any_spec] + out_specs + [any_spec, vmem]
        scratch += [
            dma((8, slices - 1)),
            dma((8, slices - 1)),
            dma((8, slices)),
            dma((8, slices)),
            dma((8,)),
            dma((8,)),
            dma((8,)),
            dma((8,)),
            dma((8,)),
            dma,
            dma,
            dma((6,)),
            dma((6,)),
            dma,
            pltpu.VMEM((2, width), f32),
            pltpu.VMEM((2, length), jnp.int32),
            dma,
            dma,
            dma,
        ]
        in_specs = [any_spec, vmem, vmem, vmem, any_spec, any_spec]
    else:
        out_shape = out_shape + [turned]
        out_specs = out_specs + [any_spec]
        scratch += [pltpu.VMEM((2, length, width), bf16), pltpu.VMEM(turned.shape, bf16), dma((2,))]
        in_specs = [any_spec, vmem, any_spec, any_spec, any_spec]
    return pl.pallas_call(
        functools.partial(forward_kernel, dp_size, layer),
        out_shape=out_shape,
        in_specs=in_specs + [any_spec] * len(weights),
        out_specs=out_specs,
        scratch_shapes=scratch,
        compiler_params=pltpu.CompilerParams(
            collective_id=1 + layer, has_side_effects=True, vmem_limit_bytes=VMEM_LIMIT
        ),
        name="forward_layer",
    )(*operands, *weights)


class Refs:
    pass


KEPT = 5
GROUPS = 7


def backward_kernel(dp_size, layer, *refs):
    final_layer = layer == 0
    v = Refs()
    (v.grad_out, v.gains, v.tables, v.masks, v.x, v.middle, v.normed_in_t, v.query_rot, v.key_rot, v.value, v.unit,
     v.inverse, v.opened, v.slope_open, v.merged, v.normed_mid_t, v.act, v.slope, v.hidden,
     v.qkvs_all, v.out_all, v.gate_up_all, v.down_all, v.down_in, *refs) = refs
    if not final_layer:
        v.down_turned, *refs = refs
    if final_layer:
        (v.later_chip, v.later_terms, v.first_rows, v.later_normed_in_t, v.later_qkvs, v.later_hidden, v.later_middle,
         *refs) = refs
    v.grad_in, v.chip, v.core_land, *refs = refs
    if final_layer:
        v.x_land, v.final, v.gain_sums, v.result, v.taken_rows, v.taken_grads, *refs = refs
    else:
        v.terms, v.next_down, v.kept_qkvs, *refs = refs
    (v.big, v.out_t, v.query_v, v.key_v, v.value_v, v.wide_a, v.wide_b, v.wide_c, v.inverse_v, v.x_v, v.middle_v,
     v.normed_t, v.outer, v.grad_down, v.grad_gate_up, v.grad_branch, v.grad_qkvs, v.turned, v.parts, v.landed,
     v.grad_middle, v.stage_given, v.stage_own, v.core_part, v.load_sem, v.s_send, v.s_recv, v.g_send, v.g_recv,
     v.c_send, v.c_recv, v.local_sem, v.masks_v, v.tables_v, v.grad_out_v, *refs) = refs
    if final_layer:
        (v.left, v.right, v.sums, v.r_sem, v.x_send, v.x_recv, v.z_send, v.z_recv, v.terms, v.held, v.hop_land,
         v.t_send, v.t_recv, v.row_send, v.row_recv, v.landed_y) = refs
    else:
        v.d_send, v.d_recv, v.d_sem, v.kept_sem, v.mid_v = refs
    at = Place(dp_size)
    rows, width = v.x.shape[-2:]
    sq = Square(dp_size, rows)
    masks, tables, gains = v.masks_v, v.tables_v, v.gains
    query_v, key_v, value_v = v.query_v, v.key_v, v.value_v
    wide_a, wide_b, wide_c = v.wide_a, v.wide_b, v.wide_c
    grad_down, grad_gate_up, grad_branch, grad_qkvs = v.grad_down, v.grad_gate_up, v.grad_branch, v.grad_qkvs
    big, out_t, outer, parts, landed, terms = v.big, v.out_t, v.outer, v.parts, v.landed, v.terms
    wide_k = query_v.shape[-1]
    wide_v = value_v.shape[-1]
    wide_f = outer.shape[-1]
    heads = wide_k // HEAD_K
    slices = dp_size // 2
    slice_rows = width // dp_size
    gain_in = gains[layer, 0:1]
    gain_mid = gains[layer, 1:2]
    other = 1 - at.section
    steps = [(k, b) for k in range(at.groups) for b in range(2)]
    steps = steps[1:] + steps[:1]

    def load(index, source, target):
        copy = pltpu.make_async_copy(source, target, v.load_sem.at[index])
        copy.start()
        return copy

    def remote(src, dst, send, recv, device):
        return pltpu.make_async_remote_copy(
            src_ref=src, dst_ref=dst, send_sem=send, recv_sem=recv, device_id=device, device_id_type=MESH
        )

    def place(section=None, dp=None, tensor=None):
        return (
            at.section if section is None else section,
            at.dp if dp is None else dp,
            at.tensor if tensor is None else tensor,
        )

    sibling = place(dp=at.sibling())
    across = place(section=other)

    token_load = load(14, v.down_in, grad_down)
    down_load = load(0, v.down_all.at[layer], big.at[:, pl.ds(2 * wide_f, wide_f)])
    act_load = load(1, v.act, wide_a)
    slope_load = load(2, v.slope, wide_b)
    gate_load = load(3, v.gate_up_all.at[layer], big.at[:, pl.ds(0, 2 * wide_f)])
    hidden_load = load(4, v.hidden, outer)
    if not final_layer:
        turned_load = load(18, v.down_turned, v.turned)
    mid_load = load(5, v.normed_mid_t, v.normed_t if final_layer else v.mid_v)
    early = [
        load(6, v.middle, v.middle_v),
        load(7, v.x.at[at.section] if final_layer else v.x, v.x_v),
        load(8, v.out_all.at[layer], out_t),
        load(9, v.query_rot, query_v),
        load(10, v.key_rot, key_v),
        load(11, v.value, value_v),
        load(12, v.inverse, v.inverse_v),
        load(13, v.opened, wide_c),
        load(15, v.masks, masks),
        load(16, v.tables, tables),
        load(17, v.grad_out if final_layer else v.grad_out.at[at.section], v.grad_out_v),
    ]
    terms[...] = jnp.zeros_like(terms)

    partners = [sq.device(*step) for step in SQUARE] + [sibling]
    if final_layer:
        partners.append(across)
        partners += [place(dp=at.dp_at(k, b)) for k, b in steps[:-1] if (k, b) != (0, 1)]
    barrier = pltpu.get_barrier_semaphore()
    for partner in partners:
        pl.semaphore_signal(barrier, inc=1, device_id=partner, device_id_type=MESH)
    pl.semaphore_wait(barrier, len(partners))

    def x_copy(e, at_source, j, source):
        block = source.at[at_source, j]
        return remote(block, v.x_land.at[e, j], v.x_send.at[e, j], v.x_recv.at[e, j], across)

    def start_x(e, at_source, source):
        @pl.loop(0, slices)
        def _(j):
            x_copy(e, at_source, j, source).start()

    row_copies = []
    if final_layer:

        @pl.when(at.section == 0)
        def _():
            @pl.loop(0, KEPT)
            def _(e):
                start_x(e, e, v.later_chip)

            remote(v.grad_out, v.taken_grads, v.row_send.at[1], v.row_recv.at[1], across).start()

        @pl.when(at.section == 1)
        def _():
            remote(v.first_rows, v.taken_rows, v.row_send.at[0], v.row_recv.at[0], across).start()

    def through_down(s):
        tokens = grad_down[s]
        for start in range(0, wide_f, TILE):
            cols = slice(start, start + TILE)
            grad_hidden = mm(tokens, big[:, 2 * wide_f + start : 2 * wide_f + start + TILE])
            grad_gate_up[s, :, cols] = (grad_hidden * wide_b[s, :, cols].astype(f32)).astype(bf16)
            grad_gate_up[s, :, wide_f + start : wide_f + start + TILE] = (
                grad_hidden * wide_a[s, :, cols].astype(f32)
            ).astype(bf16)

    def give_back(s, source, weight, first, size, target):
        tokens = source[s]
        for start in range(0, width, TILE):
            target[s, :, start : start + TILE] = mm_nt(
                tokens, weight[start : start + TILE, first : first + size]
            ).astype(bf16)

    def collected(block, given, land):
        total = sq.chunk(given)[block].astype(f32)
        for j in range(3 if final_layer else 2):
            total = total + land[j, block].astype(f32)
        return total

    def exchange(source, weight, first, size, target, land, which):
        give_back(sq.next, source, weight, first, size, target)
        send, recv = v.g_send.at[which], v.g_recv.at[which]
        if not final_layer:
            collect = Collect(sq, target, land, send, recv)
            collect.after_next()
            give_back(sq.own, source, weight, first, size, target)
            collect.after_own()
            return [collect]
        pushes = [sq.give(target, land, send, recv, j) for j in (1, 2)]
        give_back(sq.own, source, weight, first, size, target)
        pushes.append(sq.give(target, land, send, recv, 0))
        return pushes

    members = [
        (v.turned, outer, 0, wide_f),
        (v.normed_t, grad_gate_up, 0, wide_f),
        (v.normed_t, grad_gate_up, wide_f, wide_f),
        (v.turned, outer, 0, wide_v),
        (v.normed_t, grad_qkvs, 0, 2 * wide_k),
        (v.normed_t, grad_qkvs, 2 * wide_k, wide_v),
        (v.normed_t, grad_qkvs, 2 * wide_k + wide_v, wide_v),
    ]
    members += members[KEPT:]
    given_copies, own_copies, fetches = {}, {}, {}

    def product(e, dp):
        left, right, first, size = members[e]
        start = pl.multiple_of(dp * slice_rows, slice_rows)
        wide = right[:, :, first : first + size].reshape(-1, size)
        return mm(left[pl.ds(start, slice_rows), :], wide)

    def given(e):
        if e >= 2:
            given_copies[e - 2].wait_send()
        stage = v.stage_given.at[e % 2]

        @pl.loop(0, slices)
        def _(j):
            stage[j] = product(e, j * 2 + 1 - at.core).astype(bf16)

        given_copies[e] = remote(stage, v.core_land.at[e], v.c_send.at[e], v.c_recv.at[e], sibling)
        given_copies[e].start()

    def fetch(e):
        given_copies[e].wait_recv()
        fetches[e] = pltpu.make_async_copy(v.core_land.at[e], v.core_part, v.local_sem.at[0])
        fetches[e].start()

    def settle(e):
        if e in settled:
            return
        settled.append(e)
        own_copies[e].wait()
        if final_layer:

            @pl.when(at.section == (1 if e < GROUPS else 0))
            def _():
                start_x(e if e < GROUPS else e - GROUPS + KEPT, e, v.chip)

    def own(e):
        if e >= 1:
            settle(e - 1)
        fetches[e].wait()

        @pl.loop(0, slices)
        def _(j):
            v.stage_own[j] = (product(e, j * 2 + at.core) + v.core_part[j].astype(f32)).astype(bf16)

        own_copies[e] = pltpu.make_async_copy(v.stage_own, v.chip.at[e], v.local_sem.at[1])
        own_copies[e].start()

    settled = []

    def index(k, b):
        return ((at.group + k) % at.groups) * 2 + (at.low + b) % 2

    def piece(e, k):
        start = pl.multiple_of(at.low * wide_f, wide_f)
        return v.final.at[e, k, :, pl.ds(start, wide_f)]

    def z_copy(e, j):
        k, b = steps[j]
        return remote(v.sums.at[j], piece(e, k), v.z_send.at[e, j], v.z_recv.at[e, j], place(dp=at.dp_at(k, b)))

    def home_copy(e):
        return pltpu.make_async_copy(v.sums.at[slices - 1], piece(e, 0), v.r_sem.at[2, 0])

    def reduce_slices(e, at_source, source, first, stop, wait_previous):
        def loads(j):
            here = index(*steps[j])
            return (
                pltpu.make_async_copy(source.at[at_source, here], v.left.at[j % 2], v.r_sem.at[0, j % 2]),
                pltpu.make_async_copy(v.x_land.at[e, here], v.right.at[j % 2], v.r_sem.at[1, j % 2]),
            )

        def begin(j):
            x_copy(e, at_source, index(*steps[j]), source).wait_recv()
            for copy in loads(j):
                copy.start()

        begin(first)
        for j in range(first, stop):
            if j + 1 < stop:
                begin(j + 1)
            for copy in loads(j):
                copy.wait()

            @pl.when(wait_previous)
            def _():
                if j == slices - 1:
                    home_copy(e).wait()
                else:
                    z_copy(e - 1, j).wait_send()

            v.sums[j] = (v.left[j % 2].astype(f32) + v.right[j % 2].astype(f32)).astype(bf16)
            if j == slices - 1:
                home_copy(e).start()
            else:
                z_copy(e, j).start()

    reduced = [0, 0]

    def source_of(section, e):
        if section == 0:
            return e, v.chip
        return (e, v.later_chip) if e < KEPT else (e + GROUPS - KEPT, v.chip)

    def reduce_some(section, count):
        if not final_layer:
            return

        @pl.when(at.section == section)
        def _():
            done = reduced[section]
            while done < reduced[section] + count:
                e, first = divmod(done, slices)
                stop = min(slices, first + reduced[section] + count - done)
                reduce_slices(e, *source_of(section, e), first, stop, e > 0)
                done += stop - first

        reduced[section] += count

    def reduce_rest(section):
        e, first = divmod(reduced[section], slices)

        @pl.when(at.section == section)
        def _():
            begin = e
            if first > 0:
                reduce_slices(e, *source_of(section, e), first, slices, e > 0)
                begin = e + 1
            same = KEPT if section == 1 else GROUPS

            @pl.loop(begin, same)
            def _(i):
                reduce_slices(i, i, source_of(section, 0)[1], 0, slices, i > 0)

            for i in range(same, GROUPS):
                reduce_slices(i, *source_of(section, i), 0, slices, True)

    token_load.wait()
    if final_layer:
        hidden_load.wait()
        transpose_into(v.turned, grad_down)
        given(0)
    down_load.wait()
    act_load.wait()
    slope_load.wait()
    through_down(sq.next)
    through_down(sq.own)
    unit_load = load(1, v.unit, wide_a)
    bend_load = load(2, v.slope_open, wide_b)
    gate_load.wait()
    gives = exchange(grad_gate_up, big, 0, 2 * wide_f, parts, landed, 0)
    if not final_layer:
        hidden_load.wait()
        turned_load.wait()
        given(0)
    fetch(0)
    own(0)
    mid_load.wait()
    if not final_layer:
        transpose_into(v.normed_t, v.mid_v)
    settle(0)
    given(1)
    qkvs_load = load(3, v.qkvs_all.at[layer], big)
    merged_load = load(4, v.merged, outer)
    for copy in early:
        copy.wait()
    for push in gives:
        push.wait_recv()

    def through_mid(block):
        upstream = collected(block, parts, landed)
        normed, scale = norm_parts(v.middle_v[block])
        grad_rows = v.grad_out_v[block].astype(f32) + norm_grad(normed, scale, upstream, gain_mid)
        v.grad_middle[block] = grad_rows
        sq.chunk(grad_branch)[block] = grad_rows.astype(bf16)
        terms[1:2] = terms[1:2] + jnp.sum(upstream * normed, axis=0, keepdims=True)

    row_blocks(rows, through_mid)
    mids = sq.spread(grad_branch, v.s_send, v.s_recv, final_layer)
    reduce_some(0, 1)
    given(2)
    fetch(1)
    own(1)
    unit_load.wait()
    bend_load.wait()
    settle(1)
    reduce_some(1, slices)
    reduce_some(0, 1)

    def through_heads(s):
        tokens = grad_branch[s]
        for head in range(heads):
            cols_k = slice(head * HEAD_K, (head + 1) * HEAD_K)
            cols_v = slice(head * HEAD_V, (head + 1) * HEAD_V)
            grad_merged = mm(tokens, out_t[:, cols_v])
            unit_rows = wide_a[s, :, cols_v].astype(f32)
            first = 2 * wide_k + wide_v + head * HEAD_V
            grad_qkvs[s, :, first : first + HEAD_V] = (
                grad_merged * unit_rows * wide_b[s, :, cols_v].astype(f32)
            ).astype(bf16)
            grad_unit = grad_merged * wide_c[s, :, cols_v].astype(f32)
            grad_mixed = (
                v.inverse_v[s, head]
                * (
                    grad_unit
                    - jnp.mean(grad_unit, axis=-1, keepdims=True)
                    - unit_rows * jnp.mean(grad_unit * unit_rows, axis=-1, keepdims=True)
                )
            ).astype(bf16)
            query, key, val = query_v[s, :, cols_k], key_v[s, :, cols_k], value_v[s, :, cols_v]
            mask = masks[s, head]
            weight = (mm_nt(query, key) * mask).astype(bf16)
            grad_product = (mm_nt(grad_mixed, val) * mask).astype(bf16)
            first = 2 * wide_k + head * HEAD_V
            grad_qkvs[s, :, first : first + HEAD_V] = mm_tn(weight, grad_mixed).astype(bf16)
            grad_qkvs[s, :, cols_k] = turn_back(mm(grad_product, key), tables[0], tables[1], tables[2]).astype(bf16)
            first = wide_k + head * HEAD_K
            grad_qkvs[s, :, first : first + HEAD_K] = turn_back(
                mm_tn(grad_product, query), tables[0], tables[1], tables[3]
            ).astype(bf16)

    mids.wait_own()
    through_heads(sq.own)
    mids.wait_next()
    through_heads(sq.next)
    if not final_layer:
        keep = pltpu.make_async_copy(grad_qkvs, v.kept_qkvs, v.kept_sem)
        keep.start()
    qkvs_load.wait()
    reduce_some(0, 1)
    for push in gives:
        push.wait_send()
    ends = exchange(grad_qkvs, big, 0, grad_qkvs.shape[-1], parts, landed, 1)
    fetch(2)
    own(2)
    in_load = load(5, v.normed_in_t, v.normed_t)
    transpose_into(v.turned, grad_branch)
    settle(2)
    merged_load.wait()
    given(3)
    in_load.wait()
    given(4)
    fetch(3)
    own(3)
    reduce_some(1, slices)
    reduce_some(0, 1)
    settle(3)
    for push in ends:
        push.wait_recv()

    def through_in(block):
        upstream = collected(block, parts, landed)
        normed, scale = norm_parts(v.x_v[block].astype(f32))
        v.grad_in[block] = (v.grad_middle[block] + norm_grad(normed, scale, upstream, gain_in)).astype(bf16)
        terms[0:1] = terms[0:1] + jnp.sum(upstream * normed, axis=0, keepdims=True)

    row_blocks(rows, through_in)
    if final_layer:

        @pl.when(at.section == 1)
        def _():
            remote(v.grad_in, v.taken_grads, v.row_send.at[1], v.row_recv.at[1], across).start()

    else:
        downs = sq.spread(v.next_down, v.d_send, v.d_recv, False, v.grad_in, v.d_sem)

    if not final_layer:
        fetch(4)
        downs.wait_own()
        own(4)
        settle(4)
        downs.wait_next()
        for push in [downs, mids] + ends:
            push.wait_send()
        for e in (3, 4):
            given_copies[e].wait_send()
        keep.wait()
        return

    reduce_some(0, 1)
    given(5)
    fetch(4)
    own(4)
    reduce_some(0, 1)
    given(6)
    settle(4)
    reduce_some(1, slices)
    reduce_some(0, 1)
    fetch(5)
    own(5)
    reduce_some(0, 1)
    fetch(6)
    own(6)
    in_load = load(5, v.later_normed_in_t, v.normed_t)
    qkvs_load = load(3, v.later_qkvs, grad_qkvs)
    hidden_load = load(4, v.later_hidden, outer)
    middle_load = load(6, v.later_middle, v.middle_v)
    down_load = load(0, v.down_all.at[1], big.at[:, pl.ds(2 * wide_f, wide_f)])
    settle(6)
    reduce_some(1, slices)
    reduce_some(0, 1)
    in_load.wait()
    qkvs_load.wait()
    given(7)
    reduce_some(0, 1)
    given(8)
    fetch(7)
    own(7)
    reduce_some(0, 1)
    fetch(8)
    own(8)
    settle(7)
    reduce_some(0, 1)
    for push in [mids] + ends:
        push.wait_send()
    hidden_load.wait()
    down_load.wait()
    settle(8)
    gives_y = exchange(outer, big, 2 * wide_f, wide_f, parts, v.landed_y, 2)
    reduce_some(1, slices)
    reduce_some(0, slices)
    middle_load.wait()
    for push in gives_y:
        push.wait_recv()

    def last(block):
        v.result[block] = (v.middle_v[block] + collected(block, parts, v.landed_y)).astype(bf16)

    row_blocks(rows, last)

    @pl.when(at.section == 0)
    def _():
        remote(v.result, v.taken_rows, v.row_send.at[0], v.row_recv.at[0], across).start()

    for push in gives_y:
        push.wait_send()
    for e in (7, 8):
        given_copies[e].wait_send()
    reduce_rest(1)
    reduce_rest(0)

    held, hop_land, mine = v.held, v.hop_land, v.held.at[at.section]
    held[0] = terms[...]
    held[1] = v.later_terms[...]
    hop = remote(held, hop_land.at[0], v.t_send.at[0], v.t_recv.at[0], sibling)
    hop.start()
    hop.wait()
    held[...] = held[...] + hop_land[0]
    hop = remote(held.at[other], hop_land.at[1, other], v.t_send.at[1], v.t_recv.at[1], across)
    hop.start()
    hop.wait_send()
    remote(held.at[other], hop_land.at[1, at.section], v.t_send.at[1], v.t_recv.at[1], across).wait_recv()
    mine[...] = mine[...] + hop_land[1, at.section]
    for h, device in ((2, place(tensor=1 - at.tensor)), (3, place(dp=at.dp_at(0, 1)))):
        hop = remote(mine, hop_land.at[h, 0], v.t_send.at[h], v.t_recv.at[h], device)
        hop.start()
        hop.wait()
        mine[...] = mine[...] + hop_land[h, 0]
    hops = []
    for k in range(1, at.groups):
        hop = remote(mine, hop_land.at[3 + k, 0], v.t_send.at[3 + k], v.t_recv.at[3 + k], place(dp=at.dp_at(k, 0)))
        hop.start()
        hops.append(hop)
    total = mine[...]
    for k, hop in zip(range(1, at.groups), hops):
        hop.wait()
        total = total + hop_land[3 + k, 0]
    v.gain_sums[...] = total

    for which, rows_sent in ((0, v.result), (1, v.grad_in)):
        target = v.taken_rows if which == 0 else v.taken_grads
        copy = remote(rows_sent, target, v.row_send.at[which], v.row_recv.at[which], across)
        copy.wait_recv()
        copy.wait_send()

    home_copy(0).wait()
    for j in range(slices - 1):
        z_copy(GROUPS - 1, j).wait_send()

        @pl.loop(0, GROUPS)
        def _(e):
            z_copy(e, j).wait_recv()

    @pl.loop(0, GROUPS)
    def _(e):
        @pl.loop(0, slices)
        def _(j):
            x_copy(e, e, j, v.chip).wait_send()


def backward_layer(layer, grad_out, down, turned_down, x, gains, tables, masks, saved, gathered, dp_size, later=None, x_out=None):
    rows, width = x.shape[-2:]
    length = masks.shape[-1]
    (middle, normed_in_t, query_rot, key_rot, value, unit, inverse, opened, slope_open, merged, normed_mid_t, act, slope,
     hidden) = saved
    vmem = pl.BlockSpec(memory_space=pltpu.VMEM)
    any_spec = pl.BlockSpec(memory_space=pl.ANY)
    final_layer = layer == 0
    slices = dp_size // 2
    slice_rows = width // dp_size
    size = hidden.shape[-1]
    assert value.shape[-1] == size and 2 * query_rot.shape[-1] == size
    block = (slices, slice_rows, size)

    def held(*shape, kind=bf16):
        return pltpu.VMEM(shape, kind)

    def stored(*shape, kind=bf16):
        return jax.ShapeDtypeStruct(shape, kind)

    dma = pltpu.SemaphoreType.DMA
    operands = [grad_out, gains, tables, masks]
    operands += [x, middle, normed_in_t, query_rot, key_rot, value, unit, inverse, opened, slope_open, merged, normed_mid_t,
                 act, slope, hidden]
    operands += [*gathered, down]
    if not final_layer:
        operands += [turned_down]
    in_specs = [any_spec, vmem] + [any_spec] * (len(operands) - 2)
    count = 2 * GROUPS - KEPT if final_layer else KEPT
    out_shape = [stored(rows, width), stored(count, *block), stored(count, *block)]
    out_specs = [vmem, any_spec, any_spec]
    if final_layer:
        later_chip, later_terms, later_qkvs, later_saved = later
        operands += [later_chip, later_terms, x_out, later_saved[1], later_qkvs, later_saved[-1], later_saved[0]]
        in_specs += [any_spec, vmem] + [any_spec] * 5
        out_shape += [stored(GROUPS, *block), stored(GROUPS, dp_size // 4, slice_rows, 2 * size), stored(2, width, kind=f32),
                      stored(rows, width), stored(rows, width), stored(rows, width)]
        out_specs += [any_spec, any_spec, vmem, vmem, any_spec, any_spec]
    else:
        out_shape += [stored(2, width, kind=f32), stored(2, length, width), stored(2, length, 3 * size)]
        out_specs += [vmem, any_spec, any_spec]
    scratch = [
        held(width, 3 * size),
        held(width, size),
        held(*query_rot.shape),
        held(*key_rot.shape),
        held(*value.shape),
        held(2, length, size),
        held(2, length, size),
        held(2, length, size),
        held(*inverse.shape, kind=f32),
        held(rows, width),
        held(rows, width, kind=f32),
        held(width, 2 * length),
        held(2, length, size),
        held(2, length, width),
        held(2, length, 2 * size),
        held(2, length, width),
        held(2, length, 3 * size),
        held(width, 2 * length),
        held(2, length, width),
        held(3, rows, width),
        held(rows, width, kind=f32),
        held(2, *block),
        held(*block),
        held(*block),
        dma((19,)),
        dma((6,)),
        dma((6,)),
        dma((3, 6)),
        dma((3, 6)),
        dma((count,)),
        dma((count,)),
        dma((2,)),
        held(*masks.shape, kind=f32),
        held(*tables.shape, kind=f32),
        held(rows, width),
    ]
    if final_layer:
        hops = 3 + dp_size // 4
        scratch += [
            held(2, slice_rows, size),
            held(2, slice_rows, size),
            held(*block),
            dma((3, 2)),
            dma((GROUPS, slices)),
            dma((GROUPS, slices)),
            dma((GROUPS, slices - 1)),
            dma((GROUPS, slices - 1)),
            held(2, width, kind=f32),
            held(2, 2, width, kind=f32),
            held(hops, 2, 2, width, kind=f32),
            dma((hops,)),
            dma((hops,)),
            dma((2,)),
            dma((2,)),
            held(3, rows, width),
        ]
    else:
        scratch += [dma((6,)), dma((6,)), dma, dma, held(2, length, width)]
    return pl.pallas_call(
        functools.partial(backward_kernel, dp_size, layer),
        out_shape=out_shape,
        in_specs=in_specs,
        out_specs=out_specs,
        scratch_shapes=scratch,
        compiler_params=pltpu.CompilerParams(
            collective_id=4 + layer, has_side_effects=True, vmem_limit_bytes=VMEM_LIMIT
        ),
        name="backward_layer",
    )(*operands)


def nested(outs):
    return (*outs[:6], outs[6:-2], *outs[-2:])


def on_device(
    dp_size,
    layer_input,
    segment_ids,
    output_grad,
    query_weight,
    key_weight,
    value_weight,
    swish_weight,
    output_weight,
    gate_weight,
    up_weight,
    down_weight,
    mixer_gain,
    ffn_gain,
):
    at = Place(dp_size)
    section_first = at.section == 0
    width = layer_input.shape[2]
    length = segment_ids.shape[1]
    quarter_k = query_weight.shape[2] // 2
    heads_here = quarter_k // HEAD_K
    cosine, sine, growth = rotation_tables(length, HEAD_K // 2)
    tables = jnp.stack([cosine, sine, growth, 1.0 / growth])

    shards = (query_weight[0], key_weight[0], value_weight[0], swish_weight[0], output_weight[0].T, gate_weight[0],
              up_weight[0], down_weight[0].T)
    *gathered, all_gains, masks, first_saved, second_down, first_sent = nested(
        forward_layer(
            0, (layer_input, mixer_gain, ffn_gain, segment_ids, tables, output_grad), shards, length, heads_here, dp_size
        )
    )
    *second_saved, turned_down = forward_layer(
        1, (first_sent, all_gains, tables, masks, second_down), gathered, length, heads_here, dp_size
    )
    gathered = [g.reshape(2, width, g.shape[-1]) for g in gathered]
    second_grad, later_chip, _, later_terms, first_down, later_qkvs = backward_layer(
        1, output_grad, second_down, turned_down, first_sent, all_gains, tables, masks, second_saved, gathered, dp_size
    )
    first_grad, _, _, _, landed, my_gains, second_sent, taken_rows, taken_grads = backward_layer(
        0, second_grad, first_down, None, layer_input, all_gains, tables, masks, first_saved, gathered, dp_size,
        (later_chip, later_terms, later_qkvs, second_saved), first_sent,
    )

    def by_layer(first, second, taken):
        return jnp.where(section_first, jnp.stack([first, taken]), jnp.stack([taken, second]))[None]

    def shard(e):
        return jnp.sum(landed[e].astype(f32), axis=0)

    def columns(e, start, size):
        step = landed.shape[-1] // 2
        part = jnp.concatenate([landed[e, :, :, p * step + start : p * step + start + size] for p in range(2)], axis=-1)
        return jnp.sum(part.astype(f32), axis=0)

    return (
        by_layer(first_sent, second_sent, taken_rows),
        by_layer(first_grad, second_grad, taken_grads),
        columns(4, 0, quarter_k)[None],
        columns(4, quarter_k, quarter_k)[None],
        shard(5)[None],
        shard(6)[None],
        shard(3).T[None],
        shard(1)[None],
        shard(2)[None],
        shard(0).T[None],
        my_gains[0][None],
        my_gains[1][None],
    )


def solution(mesh):
    in_specs = (
        P(None, ("dp", "tensor"), None),
        P(None, "dp"),
        P(None, ("dp", "tensor"), None),
        P("section", "dp", "tensor"),
        P("section", "dp", "tensor"),
        P("section", "dp", "tensor"),
        P("section", "dp", "tensor"),
        P("section", "tensor", "dp"),
        P("section", "dp", "tensor"),
        P("section", "dp", "tensor"),
        P("section", "tensor", "dp"),
        P("section", None),
        P("section", None),
    )
    out_specs = (
        P("section", None, ("dp", "tensor"), None),
        P("section", None, ("dp", "tensor"), None),
        P("section", "dp", "tensor"),
        P("section", "dp", "tensor"),
        P("section", "dp", "tensor"),
        P("section", "dp", "tensor"),
        P("section", "tensor", "dp"),
        P("section", "dp", "tensor"),
        P("section", "dp", "tensor"),
        P("section", "tensor", "dp"),
        P("section", None),
        P("section", None),
    )
    return jax.shard_map(
        functools.partial(on_device, mesh.shape["dp"]),
        mesh=mesh,
        in_specs=in_specs,
        out_specs=out_specs,
        check_vma=False,
    )
```
